32 devices in a mesh: seq: 8 (over z, y), batch: 2 (over core), head: 2 (over x).
Axes of the slice: x: 2, y: 2, z: 4, core: 2. Of those that a mesh axis runs over, the one named last changes fastest.
Arguments:
- hidden_in: bfloat16 [2, 1024, 2048], P('batch', 'seq'), may hold values from -6 to 6
- log_decay: float32 [2, 8, 1024], P('batch', 'head', 'seq'), may hold values from -1 to 0, as said below
- out_grad: bfloat16 [2, 1024, 2048], P('batch', 'seq'), may hold values from -6 to 6
- ln1_gain: bfloat16 [2048], P(('seq', 'batch')), may hold values from 0.25 to 1.75
- ln1_bias: bfloat16 [2048], P(('seq', 'batch')), may hold values from -2 to 2
- w_query: bfloat16 [2048, 2048], P(('seq', 'batch'), 'head'), may hold values from -0.125 to 0.125
- w_key: bfloat16 [2048, 2048], P(('seq', 'batch'), 'head'), may hold values from -0.125 to 0.125
- w_value: bfloat16 [2048, 4096], P(('seq', 'batch'), 'head'), may hold values from -0.125 to 0.125
- w_gate: bfloat16 [2048, 4096], P(('seq', 'batch'), 'head'), may hold values from -0.125 to 0.125
- w_out: bfloat16 [4096, 2048], P('head', ('seq', 'batch')), may hold values from -0.1875 to 0.1875
- ln2_gain: bfloat16 [2048], P(('seq', 'batch')), may hold values from 0.25 to 1.75
- ln2_bias: bfloat16 [2048], P(('seq', 'batch')), may hold values from -2 to 2
- mlp_gate: bfloat16 [2048, 4096], P(('seq', 'batch'), 'head'), may hold values from -0.125 to 0.125
- mlp_up: bfloat16 [2048, 4096], P(('seq', 'batch'), 'head'), may hold values from -0.125 to 0.125
- mlp_down: bfloat16 [4096, 2048], P('head', ('seq', 'batch')), may hold values from -0.1875 to 0.1875
Outputs:
- hidden_out: bfloat16 [2, 1024, 2048], P('batch', 'seq')
- grad_in: float32 [2, 1024, 2048], P('batch', 'seq')
- grad_ln1_gain: float32 [2048], P(('seq', 'batch'))
- grad_ln1_bias: float32 [2048], P(('seq', 'batch'))
- grad_query: float32 [2048, 2048], P(('seq', 'batch'), 'head')
- grad_key: float32 [2048, 2048], P(('seq', 'batch'), 'head')
- grad_value: float32 [2048, 4096], P(('seq', 'batch'), 'head')
- grad_gate: float32 [2048, 4096], P(('seq', 'batch'), 'head')
- grad_out: float32 [4096, 2048], P('head', ('seq', 'batch'))
- grad_ln2_gain: float32 [2048], P(('seq', 'batch'))
- grad_ln2_bias: float32 [2048], P(('seq', 'batch'))
- grad_mlp_gate: float32 [2048, 4096], P(('seq', 'batch'), 'head')
- grad_mlp_up: float32 [2048, 4096], P(('seq', 'batch'), 'head')
- grad_mlp_down: float32 [4096, 2048], P('head', ('seq', 'batch'))
The draws below stay inside these ranges and needn't reach their ends.
Inputs may be any that keep to these rules, and one draw needn't show every extreme that they name: `log_decay`: every entry is negative; each head keeps its own rate per sequence, varied from position to position.
All inputs are finite; a program needn't handle non-finite values.
Results may differ from the reference program's by a relative error of at most 0.015.
Values may be sent and summed in bfloat16 or wider, within the bound.
No kernel may reach another device: no remote copies, remote signals or barrier semaphores. Data moves between devices by JAX's collectives and lax.ppermute only.
A program may use at most 320 MiB of HBM per device.

```python
import jax
import jax.numpy as jnp
from jax import lax

D = 2048
RETENTION_HEADS = 8
DK = 256
DV = 512
FF = 4096
BLK = 128
SEQUENCE_COUNT = 2
SEQUENCE_LENGTH = 1024


def draw_log_decay(key, part):
    key = jax.random.fold_in(key, 11)
    every_key_row = jax.random.split(key, 6)
    fast_share = 0.5
    fast = jax.random.bernoulli(every_key_row[0], fast_share, (SEQUENCE_COUNT, RETENTION_HEADS, 1))
    fast_rate = 1.0 / jax.random.uniform(every_key_row[1], (SEQUENCE_COUNT, RETENTION_HEADS, 1), jnp.float32, 30.0, 50.0)
    slow_log = jax.random.uniform(every_key_row[2], (SEQUENCE_COUNT, RETENTION_HEADS, 1), jnp.float32, jnp.log(0.05), jnp.log(0.5))
    slow_rate = jnp.exp(slow_log) / SEQUENCE_LENGTH
    baseline_decay_rate = jnp.where(fast, fast_rate, slow_rate)
    coarse_estimate = jax.random.uniform(every_key_row[3], (SEQUENCE_COUNT, RETENTION_HEADS, SEQUENCE_LENGTH), jnp.float32, 0.5, 2.0)
    spike_position = jax.random.bernoulli(every_key_row[4], 2.0 / SEQUENCE_LENGTH, (SEQUENCE_COUNT, 1, SEQUENCE_LENGTH)).astype(jnp.float32)
    spike_magnitude = jax.random.uniform(every_key_row[5], (SEQUENCE_COUNT, RETENTION_HEADS, SEQUENCE_LENGTH), jnp.float32, 0.22, 0.69)
    return -(baseline_decay_rate * coarse_estimate + spike_position * spike_magnitude)


def with_spikes(values, own_key, source, target, parts, factor):
    owner, partner = [(jnp.arange(values.shape[axis_at]) // (values.shape[axis_at] // parts)).reshape([-1 if axis == axis_at else 1 for axis in range(values.ndim)]) for axis_at in (source, target)]
    chosen = jax.random.permutation(own_key, parts)[partner]
    strong = (owner == chosen) | (owner == (partner + parts // 2) % parts)
    return jnp.where(strong, factor * values, values)


def block_scale(own_key, dims, cuts, low, top_value):
    def one(axis_at, shards_of):
        heights = jax.random.uniform(jax.random.fold_in(jax.random.fold_in(own_key, 6), axis_at), (shards_of,), jnp.float32, low / len(cuts), top_value / len(cuts))
        return jnp.repeat(jnp.exp(heights), dims[axis_at] // shards_of).reshape((-1,) + (1,) * (len(dims) - axis_at - 1))

    loudness = one(*cuts[0])
    for cut in cuts[1:]:
        loudness = loudness * one(*cut)
    return loudness


def noise(own_key, shape, scale, reach, cuts=(), kind=jnp.bfloat16):
    entries = jax.random.normal(own_key, shape, jnp.float32) * scale
    if len(cuts) > 0:
        entries = block_scale(own_key, shape, cuts, -0.22, 0.18) * entries
    return jnp.clip(entries, min=-reach, max=reach).astype(kind)


def heavy_noise(own_key, dims, scale, most, pieces, heavy, kind=jnp.bfloat16):
    drawn = scale * jax.random.normal(own_key, dims, jnp.float32)
    if pieces:
        drawn = drawn * block_scale(own_key, dims, pieces, -0.22, 0.18)
    return jnp.clip(with_spikes(drawn, jax.random.fold_in(own_key, 3), *heavy), -most, most).astype(kind)


def setup_inputs(seed: int = 0) -> dict:
    key_list = jax.random.split(jax.random.key(seed), 16)
    return {
        "hidden_in": noise(key_list[0], (SEQUENCE_COUNT, SEQUENCE_LENGTH, D), 1.0, 6.0, ((0, 2), (1, 8))),
        "log_decay": draw_log_decay(jax.random.fold_in(key_list[15], 71), 0),
        "out_grad": heavy_noise(key_list[2], (SEQUENCE_COUNT, SEQUENCE_LENGTH, D), 1.0, 6.0, ((0, 2), (1, 8)), (1, 2, 8, 2.0)),
        "ln1_gain": jnp.clip(1.0 + 0.15 * jax.random.normal(key_list[3], (D,), jnp.float32), 0.25, 1.75).astype(jnp.bfloat16),
        "ln1_bias": noise(key_list[4], (D,), 0.3, 2.0, ((0, 16),)),
        "w_query": noise(key_list[5], (D, RETENTION_HEADS * DK), D ** -0.5, 0.125, ((0, 16), (1, 2))),
        "w_key": noise(key_list[6], (D, RETENTION_HEADS * DK), D ** -0.5, 0.125, ((0, 16), (1, 2))),
        "w_value": noise(key_list[7], (D, RETENTION_HEADS * DV), D ** -0.5, 0.125, ((0, 16), (1, 2))),
        "w_gate": noise(key_list[8], (D, RETENTION_HEADS * DV), D ** -0.5, 0.125, ((0, 16), (1, 2))),
        "w_out": noise(key_list[9], (RETENTION_HEADS * DV, D), (RETENTION_HEADS * DV // 4) ** -0.5, 0.1875, ((0, 2), (1, 16))),
        "ln2_gain": jnp.clip(1.0 + 0.15 * jax.random.normal(key_list[10], (D,), jnp.float32), 0.25, 1.75).astype(jnp.bfloat16),
        "ln2_bias": noise(key_list[11], (D,), 0.3, 2.0, ((0, 16),)),
        "mlp_gate": noise(key_list[12], (D, FF), D ** -0.5, 0.125, ((0, 16), (1, 2))),
        "mlp_up": noise(key_list[13], (D, FF), D ** -0.5, 0.125, ((0, 16), (1, 2))),
        "mlp_down": noise(key_list[14], (FF, D), (FF // 4) ** -0.5, 0.1875, ((0, 2), (1, 16))),
    }


epsilon = 1e-05

@jax.custom_vjp
def low(v):
    return lax.optimization_barrier(v.astype(jnp.bfloat16)).astype(jnp.float32)

@jax.custom_vjp
def low_back(v):
    return v

def low_keep(v):
    return (low(v), None)

def low_pass(kept, grad):
    return (grad,)

def back_keep(v):
    return (v, None)

def back_low(kept, grad):
    return (low(grad),)
low.defvjp(low_keep, low_pass)
low_back.defvjp(back_keep, back_low)

def product(values, weight):
    return jnp.dot(values, weight, precision=lax.Precision.HIGHEST)

def norm_rows(values, gain, offset):
    center = values - lax.optimization_barrier(jnp.mean(values, axis=-1, keepdims=True))
    scaled = center * lax.rsqrt(lax.optimization_barrier(jnp.mean(center * center, axis=-1, keepdims=True)) + epsilon)
    return scaled * gain + offset

def rotate(values, cosines, sines):
    half_dim = values.shape[-1] // 2
    first_half = values[..., :half_dim]
    second_half = values[..., half_dim:]
    return jnp.concatenate([first_half * cosines - second_half * sines, first_half * sines + second_half * cosines], axis=-1)

def tables(positions, head_dim):
    half_dim = head_dim // 2
    freqs = 10000.0 ** (-jnp.arange(half_dim, dtype=jnp.float32) / half_dim)
    angles = positions[:, None] * freqs[None, :]
    return (jnp.cos(angles)[:, None, :], jnp.sin(angles)[:, None, :])

def retain(queries, every_key_row, values, decay):
    blocks = SEQUENCE_LENGTH // BLK
    query_blk = queries.reshape(blocks, BLK, RETENTION_HEADS, DK)
    key_blk = every_key_row.reshape(blocks, BLK, RETENTION_HEADS, DK)
    value_blk = values.reshape(blocks, BLK, RETENTION_HEADS, DV)
    decay_blk = decay.reshape(RETENTION_HEADS, blocks, BLK).transpose(1, 0, 2)
    index_pos = jnp.arange(BLK)
    causal = index_pos[:, None] >= index_pos[None, :]
    highest_precision = lax.Precision.HIGHEST

    def block_step(carried_state, block_items):
        query_segment, key_segment, value_segment, decay_c = block_items
        running_log_decay = jnp.cumsum(decay_c, axis=-1)
        scores = low_back(jnp.einsum('nhk,mhk->hnm', query_segment, key_segment, precision=highest_precision))
        decay_mat = jnp.exp(jnp.where(causal, running_log_decay[:, :, None] - running_log_decay[:, None, :], -jnp.inf))
        weights = low(scores * decay_mat)
        intra = jnp.einsum('hnm,mhv->nhv', weights, value_segment, precision=highest_precision)
        cross_block_output = jnp.exp(running_log_decay).T[:, :, None] * jnp.einsum('rsw,swi->rsi', query_segment, carried_state, precision=highest_precision)
        tail_decay_weight = jnp.exp(running_log_decay[:, -1:] - running_log_decay)
        updated_state = jnp.exp(running_log_decay[:, -1])[:, None, None] * carried_state + jnp.einsum('spe,spt->pet', key_segment * tail_decay_weight.T[:, :, None], value_segment, precision=highest_precision)
        return (updated_state, intra + cross_block_output)
    start = jnp.zeros((RETENTION_HEADS, DK, DV), jnp.float32)
    finish, outputs = lax.scan(jax.checkpoint(block_step), start, (query_blk, key_blk, value_blk, decay_blk))
    return outputs.reshape(SEQUENCE_LENGTH, RETENTION_HEADS, DV)

def layer(params, inputs, decay):
    ln1_gain, ln1_bias, w_query, w_key, w_value, w_gate, w_out, ln2_gain, ln2_bias, mlp_gate, mlp_up, mlp_down = params
    length = inputs.shape[0]
    normed_one = low(norm_rows(inputs, ln1_gain, ln1_bias))
    query_pre = low_back(product(normed_one, w_query))
    key_pre = low_back(product(normed_one, w_key))
    value_all = low(low_back(product(normed_one, w_value)))
    gate_pre = low_back(product(normed_one, w_gate))
    cosines, sines = tables(jnp.arange(length).astype(jnp.float32), DK)
    queries = low(rotate(query_pre.reshape(length, RETENTION_HEADS, DK), cosines, sines))
    every_key_row = low(rotate(key_pre.reshape(length, RETENTION_HEADS, DK), cosines, sines) * DK ** (-0.5))
    retained = low_back(retain(queries, every_key_row, value_all.reshape(length, RETENTION_HEADS, DV), decay))
    centered = retained - lax.optimization_barrier(jnp.mean(retained, axis=-1, keepdims=True))
    grp_norm = centered * lax.rsqrt(lax.optimization_barrier(jnp.mean(centered * centered, axis=-1, keepdims=True)) + epsilon)
    mixed = low((jax.nn.silu(gate_pre.reshape(length, RETENTION_HEADS, DV)) * grp_norm).reshape(length, RETENTION_HEADS * DV))
    middle = inputs + low_back(product(mixed, w_out))
    normed_two = low(norm_rows(middle, ln2_gain, ln2_bias))
    up_gate = low_back(product(normed_two, mlp_gate))
    up_lin = low_back(product(normed_two, mlp_up))
    hidden = low(jax.nn.gelu(up_gate, approximate=False) * up_lin)
    return middle + low_back(product(hidden, mlp_down))

def reference(hidden_in, log_decay, out_grad, ln1_gain, ln1_bias, w_query, w_key, w_value, w_gate, w_out, ln2_gain, ln2_bias, mlp_gate, mlp_up, mlp_down):
    params = tuple((p.astype(jnp.float32) for p in (ln1_gain, ln1_bias, w_query, w_key, w_value, w_gate, w_out, ln2_gain, ln2_bias, mlp_gate, mlp_up, mlp_down)))

    def one_seq(totals, seq_items):
        inputs, cotangent, decay = seq_items
        result, pull_back = jax.vjp(lambda weights, values: layer(weights, values, decay), params, inputs)
        grads_now, grad_inputs = pull_back(cotangent)
        return (tuple((a + b for a, b in zip(totals, grads_now))), (result, grad_inputs))
    zeros_all = tuple((jnp.zeros_like(p) for p in params))
    grads, stacked = lax.scan(one_seq, zeros_all, (hidden_in.astype(jnp.float32), out_grad.astype(jnp.float32), log_decay))
    results, grad_inputs = stacked
    return (results.astype(jnp.bfloat16), grad_inputs, grads[0], grads[1], grads[2], grads[3], grads[4], grads[5], grads[6], grads[7], grads[8], grads[9], grads[10], grads[11])
```

```python
import jax
import jax.numpy as jnp
from jax import lax
from jax.sharding import Mesh
from jax.sharding import PartitionSpec as P

DK = 256
DV = 512

epsilon = 1e-05
f32 = jnp.float32
bf16 = jnp.bfloat16


def swap(values, axis, k):
    count = lax.axis_size(axis)
    return lax.ppermute(values, axis, [(i, i ^ k) for i in range(count)])


def put(buffer, piece, index, axis):
    return lax.dynamic_update_slice_in_dim(buffer, jnp.expand_dims(piece, axis), index, axis)


def pick(values, index, axis):
    return lax.dynamic_index_in_dim(values, index, axis, keepdims=False)


def assemble(pieces, me, axis):
    shape = list(pieces[0].shape)
    shape.insert(axis, len(pieces))
    buffer = jnp.zeros(shape, pieces[0].dtype)
    for k, piece in enumerate(pieces):
        buffer = put(buffer, piece, me ^ k, axis)
    return buffer


def gather(values, name, axis=0):
    me = lax.axis_index(name)
    pieces = [values] + [swap(values, name, k) for k in range(1, lax.axis_size(name))]
    return assemble(pieces, me, axis)


def trade(values, name):
    me = lax.axis_index(name)
    pieces = [pick(values, me, 0)]
    for k in range(1, lax.axis_size(name)):
        pieces.append(swap(pick(values, me ^ k, 0), name, k))
    return assemble(pieces, me, 0)


def reduce_to(values, name, axis):
    me = lax.axis_index(name)
    total = pick(values, me, axis)
    for k in range(1, lax.axis_size(name)):
        total = total + swap(pick(values, me ^ k, axis).astype(bf16), name, k).astype(f32)
    return total


def matmul(values, weight):
    return jnp.dot(values, weight, preferred_element_type=f32)


def matmul_t(values, weight):
    return lax.dot_general(values, weight, (((1,), (1,)), ((), ())), preferred_element_type=f32)


def outer_sum(values, other):
    return lax.dot_general(values, other, (((0,), (0,)), ((), ())), preferred_element_type=f32)


def batched(spec, left, right):
    return jnp.einsum(spec, left, right, preferred_element_type=f32)


def normalize(values):
    center = values - jnp.mean(values, axis=-1, keepdims=True)
    rstd = lax.rsqrt(jnp.mean(center * center, axis=-1, keepdims=True) + epsilon)
    return center * rstd, rstd


def norm_back(scaled_grad, scaled, rstd):
    return rstd * (
        scaled_grad
        - jnp.mean(scaled_grad, axis=-1, keepdims=True)
        - scaled * jnp.mean(scaled_grad * scaled, axis=-1, keepdims=True)
    )


def rotate(values, cosines, sines):
    half_dim = values.shape[-1] // 2
    first_half = values[..., :half_dim]
    second_half = values[..., half_dim:]
    return jnp.concatenate(
        [first_half * cosines - second_half * sines, first_half * sines + second_half * cosines],
        axis=-1,
    )


def collect_weight(weight):
    cols = weight.shape[-1]
    own = trade(weight.transpose(1, 0, 2), "row")
    own = gather(own, "col", 1)
    own = gather(own, "batch", 2)
    return own.reshape(-1, cols)


def return_grad(grad, rows, nz, ny, nb):
    grad = grad.reshape(nz, ny, nb, rows, -1)
    grad = reduce_to(grad, "batch", 2)
    grad = reduce_to(grad, "col", 1)
    return trade(grad.astype(bf16), "row").astype(f32)


def reduce_tokens(partial, nz, nh):
    width = partial.shape[-1]
    partial = partial.reshape(nz, nh, -1, width)
    return reduce_to(reduce_to(partial, "head", 1), "row", 0)


def gather_tokens(values):
    width = values.shape[-1]
    me = lax.axis_index("row")
    pieces = [gather(values, "head")]
    for k in range(1, lax.axis_size("row")):
        pieces.append(gather(swap(values, "row", k), "head"))
    return assemble(pieces, me, 0).reshape(-1, width)


def shards(
    hidden_in,
    log_decay,
    out_grad,
    ln1_gain,
    ln1_bias,
    w_query,
    w_key,
    w_value,
    w_gate,
    w_out,
    ln2_gain,
    ln2_bias,
    mlp_gate,
    mlp_up,
    mlp_down,
):
    nz, ny = lax.axis_size("row"), lax.axis_size("col")
    nb, nh = lax.axis_size("batch"), lax.axis_size("head")
    z, y, x = lax.axis_index("row"), lax.axis_index("col"), lax.axis_index("head")
    block, width = hidden_in.shape[1:]
    rows = ln1_gain.shape[0]
    own_tokens = block // nh

    qkvg_own = jnp.concatenate(
        [w.reshape(rows, nz, -1) for w in (w_key, w_value, w_query, w_gate)], axis=-1
    )
    hidden_all = gather(hidden_in[0], "row").reshape(nz * block, width)
    qkvg_w = collect_weight(qkvg_own)
    out_w = collect_weight(w_out.T.reshape(rows, nz, -1))
    up_own = jnp.concatenate([w.reshape(rows, nz, -1) for w in (mlp_gate, mlp_up)], axis=-1)
    up_w = collect_weight(up_own)
    down_w = collect_weight(mlp_down.T.reshape(rows, nz, -1))
    down_bf = gather(out_grad[0], "row").reshape(nz * block, width)

    params = jnp.stack([ln1_gain, ln1_bias, ln2_gain, ln2_bias]).astype(f32)
    small = jnp.concatenate([params.reshape(-1), log_decay.reshape(-1)])
    small = gather(gather(small, "row"), "col", 1)
    params = gather(small[..., : 4 * rows], "batch", 2).reshape(nz * ny * nb, 4, rows)
    gain_one, bias_one, gain_two, bias_two = params.transpose(1, 0, 2).reshape(4, width)
    decay = pick(small[..., 4 * rows :].reshape(nz * ny, nz, block), z, 1)

    scaled_one, _ = normalize(hidden_all.astype(f32))
    first_bf = (scaled_one * gain_one + bias_one).astype(bf16)
    projected = matmul(first_bf, qkvg_w)
    key_pre = projected[:, :DK]
    value_bf = projected[:, DK : DK + DV].astype(bf16).reshape(nz, block, DV)
    query_pre = projected[:, DK + DV : 2 * DK + DV]
    gate = projected[:, 2 * DK + DV :]

    half_dim = DK // 2
    freqs = 10000.0 ** (-jnp.arange(half_dim, dtype=f32) / half_dim)
    block_at = jnp.arange(nz) * ny + y
    positions = (block_at[:, None] * block + jnp.arange(block)).astype(f32).reshape(-1)
    angles = positions[:, None] * freqs[None, :]
    cosines, sines = jnp.cos(angles), jnp.sin(angles)
    key_scale = DK ** (-0.5)
    query_bf = rotate(query_pre, cosines, sines).astype(bf16).reshape(nz, block, DK)
    key_bf = (rotate(key_pre, cosines, sines) * key_scale).astype(bf16).reshape(nz, block, DK)

    running = jnp.cumsum(decay, axis=-1)
    entry_all = jnp.exp(running)
    tail_all = jnp.exp(running[:, -1:] - running)
    total = jnp.exp(running[:, -1])
    mine = lambda a: pick(a.reshape(nz, ny, *a.shape[1:]), y, 1)
    own_running = mine(running)
    entry, tail = mine(entry_all)[..., None], mine(tail_all)[..., None]
    causal = jnp.arange(block)[:, None] >= jnp.arange(block)[None, :]
    decay_mat = jnp.exp(
        jnp.where(causal, own_running[:, :, None] - own_running[:, None, :], -jnp.inf)
    )
    pair = gather(jnp.concatenate([key_bf, value_bf], axis=-1), "col", 1)
    pair = pair.reshape(nz * ny, block, DK + DV)
    key_tail = (pair[..., :DK].astype(f32) * tail_all[..., None]).astype(bf16)
    local = batched("nmk,nmv->nkv", key_tail, pair[..., DK:])
    states = [jnp.zeros_like(local[0])]
    for j in range(nz * ny - 1):
        states.append(total[j] * states[-1] + local[j])
    carry_in = mine(jnp.stack([s.astype(bf16) for s in states]))
    scores = batched("znk,zmk->znm", query_bf, key_bf)
    weights_bf = (scores * decay_mat).astype(bf16)
    retained = batched("znm,zmv->znv", weights_bf, value_bf) + entry * batched(
        "znk,zkv->znv", query_bf, carry_in
    )
    grp_norm, grp_rstd = normalize(retained.reshape(nz * block, DV))
    gate_sig = jax.nn.sigmoid(gate)
    gate_act = gate * gate_sig
    mixed_bf = (gate_act * grp_norm).astype(bf16)

    inputs = pick(hidden_in.reshape(nh, own_tokens, width), x, 0).astype(f32)
    middle = inputs + reduce_tokens(matmul_t(mixed_bf, out_w), nz, nh)
    scaled_two, rstd_two = normalize(middle)
    second_bf = gather_tokens((scaled_two * gain_two + bias_two).astype(bf16))
    up = matmul(second_bf, up_w)
    units = up.shape[1] // 2
    up_gate, up_lin = up[:, :units], up[:, units:]
    gelu_val, gelu_pull = jax.vjp(lambda v: jax.nn.gelu(v, approximate=False), up_gate)
    hidden_bf = (gelu_val * up_lin).astype(bf16)
    result = middle + reduce_tokens(matmul_t(hidden_bf, down_w), nz, nh)
    hidden_out = gather(result.astype(bf16), "head").reshape(1, block, width)

    grad_hidden = matmul(down_bf, down_w)
    grad_upgate = gelu_pull(grad_hidden * up_lin)[0].astype(bf16)
    grad_uplin = (grad_hidden * gelu_val).astype(bf16)
    grad_up = jnp.concatenate([grad_upgate, grad_uplin], axis=-1)
    grad_two = reduce_tokens(matmul_t(grad_up, up_w), nz, nh)
    cotangent = pick(out_grad.reshape(nh, own_tokens, width), x, 0).astype(f32)
    grad_middle = cotangent + norm_back(grad_two * gain_two, scaled_two, rstd_two)
    attn_bf = gather_tokens(grad_middle.astype(bf16))
    up_sum = return_grad(outer_sum(second_bf, grad_up), rows, nz, ny, nb)
    down_sum = return_grad(outer_sum(down_bf, hidden_bf), rows, nz, ny, nb)

    grad_mixed = matmul(attn_bf, out_w)
    out_sum = return_grad(outer_sum(attn_bf, mixed_bf), rows, nz, ny, nb)
    grad_gate = (grad_mixed * grp_norm * (gate_sig * (1.0 + gate * (1.0 - gate_sig)))).astype(bf16)
    ret_bf = norm_back(grad_mixed * gate_act, grp_norm, grp_rstd).astype(bf16)
    ret_bf = ret_bf.reshape(nz, block, DV)
    pair = gather(jnp.concatenate([query_bf, ret_bf], axis=-1), "col", 1)
    pair = pair.reshape(nz * ny, block, DK + DV)
    query_entry = (pair[..., :DK].astype(f32) * entry_all[..., None]).astype(bf16)
    local = batched("nmk,nmv->nkv", query_entry, pair[..., DK:])
    states = [jnp.zeros_like(local[0])]
    for j in range(nz * ny - 1, 0, -1):
        states.append(total[j] * states[-1] + local[j])
    carry_out = mine(jnp.stack([s.astype(bf16) for s in states[::-1]]))
    grad_weights = batched("znv,zmv->znm", ret_bf, value_bf)
    grad_scores = (grad_weights * decay_mat).astype(bf16)
    grad_query = batched("znm,zmk->znk", grad_scores, key_bf) + entry * batched(
        "znv,zkv->znk", ret_bf, carry_in
    )
    grad_key = batched("znm,znk->zmk", grad_scores, query_bf) + tail * batched(
        "zmv,zkv->zmk", value_bf, carry_out
    )
    grad_value = batched("znm,znv->zmv", weights_bf, ret_bf) + tail * batched(
        "zmk,zkv->zmv", key_bf, carry_out
    )
    tokens = nz * block
    query_gbf = rotate(grad_query.reshape(tokens, DK), cosines, -sines).astype(bf16)
    key_gbf = (rotate(grad_key.reshape(tokens, DK), cosines, -sines) * key_scale).astype(bf16)
    value_gbf = grad_value.reshape(tokens, DV).astype(bf16)
    grad_proj = jnp.concatenate([key_gbf, value_gbf, query_gbf, grad_gate], axis=-1)
    grad_one = reduce_tokens(matmul_t(grad_proj, qkvg_w), nz, nh)
    qkvg_sum = return_grad(outer_sum(first_bf, grad_proj), rows, nz, ny, nb)
    scaled_own, rstd_own = normalize(inputs)
    grad_in = grad_middle + norm_back(grad_one * gain_one, scaled_own, rstd_own)
    grad_in = gather(grad_in, "head").reshape(1, block, width)

    norm_sums = jnp.stack(
        [
            jnp.sum(grad_one * scaled_own, axis=0),
            jnp.sum(grad_one, axis=0),
            jnp.sum(grad_two * scaled_two, axis=0),
            jnp.sum(grad_two, axis=0),
        ]
    )
    norm_sums = norm_sums + swap(norm_sums, "head", 1)
    norm_sums = norm_sums.reshape(4, nz, ny, nb, rows)
    for name, axis in (("batch", 3), ("col", 2), ("row", 1)):
        me = lax.axis_index(name)
        summed = pick(norm_sums, me, axis)
        for k in range(1, lax.axis_size(name)):
            summed = summed + swap(pick(norm_sums, me ^ k, axis), name, k)
        norm_sums = summed

    def columns(part):
        return part.transpose(1, 0, 2).reshape(rows, -1)

    def stacked(part):
        return part.transpose(0, 2, 1).reshape(-1, rows)

    return (
        hidden_out,
        grad_in,
        norm_sums[0],
        norm_sums[1],
        columns(qkvg_sum[..., DK + DV : 2 * DK + DV]),
        columns(qkvg_sum[..., :DK]),
        columns(qkvg_sum[..., DK : DK + DV]),
        columns(qkvg_sum[..., 2 * DK + DV :]),
        stacked(out_sum),
        norm_sums[2],
        norm_sums[3],
        columns(up_sum[..., :units]),
        columns(up_sum[..., units:]),
        stacked(down_sum),
    )


def solution(mesh):
    seq = ("row", "col")
    tokens = P("batch", seq, None)
    params = P((*seq, "batch"))
    by_rows = P((*seq, "batch"), "head")
    by_cols = P("head", (*seq, "batch"))

    def run(*arrays):
        rows = arrays[1].shape[1] // mesh.shape["head"]
        sizes = (rows, mesh.shape["seq"] // rows, mesh.shape["batch"], mesh.shape["head"])
        order = [mesh.axis_names.index(n) for n in ("seq", "batch", "head")]
        fine = Mesh(
            mesh.devices.transpose(order).reshape(sizes), ("row", "col", "batch", "head")
        )
        return jax.shard_map(
            shards,
            mesh=fine,
            in_specs=(
                tokens,
                P("batch", "head", seq),
                tokens,
                params,
                params,
                by_rows,
                by_rows,
                by_rows,
                by_rows,
                by_cols,
                params,
                params,
                by_rows,
                by_rows,
                by_cols,
            ),
            out_specs=(
                tokens,
                tokens,
                params,
                params,
                by_rows,
                by_rows,
                by_rows,
                by_rows,
                by_cols,
                params,
                params,
                by_rows,
                by_rows,
                by_cols,
            ),
            check_vma=False,
        )(*arrays)

    return run
```

```python
import jax
import jax.numpy as jnp
from jax import lax
from jax.experimental import pallas as pl
from jax.experimental.pallas import tpu as pltpu
from jax.sharding import Mesh
from jax.sharding import PartitionSpec as P

DK = 256
DV = 512

epsilon = 1e-05
f32 = jnp.float32
bf16 = jnp.bfloat16
VMEM_LIMIT = 56 * 1024 * 1024

ORDER = (0, 2, 1, 3)


def swap(values, axis, k):
    count = lax.axis_size(axis)
    return lax.ppermute(values, axis, [(i, i ^ k) for i in range(count)])


def pick(values, index, axis):
    return lax.dynamic_index_in_dim(values, index, axis, keepdims=False)


def after(values, *others):
    return lax.optimization_barrier((values, others))[0]


def gather_small(values, names):
    values = values[None]
    for name in reversed(names):
        bit = 1
        while bit < lax.axis_size(name):
            other = swap(values, name, bit)
            low = (lax.axis_index(name) & bit) == 0
            values = jnp.where(
                low, jnp.concatenate([values, other]), jnp.concatenate([other, values])
            )
            bit *= 2
    return values


def matmul(values, weight):
    return jnp.dot(values, weight, preferred_element_type=f32)


def matmul_t(values, weight):
    return lax.dot_general(values, weight, (((1,), (1,)), ((), ())), preferred_element_type=f32)


def outer_sum(values, other):
    return lax.dot_general(values, other, (((0,), (0,)), ((), ())), preferred_element_type=f32)


def normalize(values):
    center = values - jnp.mean(values, axis=-1, keepdims=True)
    rstd = lax.rsqrt(jnp.mean(center * center, axis=-1, keepdims=True) + epsilon)
    return center * rstd, rstd


def norm_back(scaled_grad, scaled, rstd):
    return rstd * (
        scaled_grad
        - jnp.mean(scaled_grad, axis=-1, keepdims=True)
        - scaled * jnp.mean(scaled_grad * scaled, axis=-1, keepdims=True)
    )


def rotate(values, cosines, sines):
    half_dim = values.shape[-1] // 2
    first_half = values[..., :half_dim]
    second_half = values[..., half_dim:]
    return jnp.concatenate(
        [first_half * cosines - second_half * sines, first_half * sines + second_half * cosines],
        axis=-1,
    )


SMEM = pl.BlockSpec(memory_space=pltpu.SMEM)
WHOLE = pl.BlockSpec(memory_space=pltpu.VMEM)
ANY = pl.BlockSpec(memory_space=pl.ANY)
PARAMS = pltpu.CompilerParams(vmem_limit_bytes=VMEM_LIMIT)


def pack_weights(where, weights, nz):
    rows = weights[0].shape[0]
    widths = [w.shape[1] // nz for w in weights]

    def kernel(where_ref, *refs):
        ins, outs = refs[: len(weights)], refs[len(weights) :]
        for k in range(nz):
            target = where_ref[0] ^ k
            at = 0
            for ref, width in zip(ins, widths):
                start = pl.multiple_of(target * width, width)
                outs[k][:, at : at + width] = ref[:, pl.ds(start, width)]
                at += width

    return pl.pallas_call(
        kernel,
        out_shape=[jax.ShapeDtypeStruct((rows, sum(widths)), bf16)] * nz,
        in_specs=[SMEM] + [WHOLE] * len(weights),
        out_specs=[WHOLE] * nz,
        compiler_params=PARAMS,
        name="pack_weights",
    )(where, *weights)


def unpack_grads(where, own, pieces, widths):
    nz = len(pieces) + 1
    rows = own.shape[0]

    def kernel(where_ref, *refs):
        ins, outs = refs[:nz], refs[nz:]
        for k in range(nz):
            target = where_ref[0] ^ k
            at = 0
            for ref, width in zip(outs, widths):
                start = pl.multiple_of(target * width, width)
                ref[:, pl.ds(start, width)] = ins[k][:, at : at + width].astype(f32)
                at += width

    return pl.pallas_call(
        kernel,
        out_shape=[jax.ShapeDtypeStruct((rows, nz * width), f32) for width in widths],
        in_specs=[SMEM] + [WHOLE] * nz,
        out_specs=[WHOLE] * len(widths),
        compiler_params=PARAMS,
        name="unpack_grads",
    )(where, own, *pieces)


def assemble_weight(where, parts, ny, nb):
    nz, rows, cols = parts[0].shape
    count = nz * ny * nb

    def kernel(where_ref, *refs):
        ins, out, sems = refs[:-2], refs[-2], refs[-1]
        copies = []
        for ky in range(ny):
            for kb in range(nb):
                for kz in range(nz):
                    at = ((where_ref[0] ^ kz) * ny + (where_ref[1] ^ ky)) * nb
                    at = pl.multiple_of((at + (where_ref[2] ^ kb)) * rows, rows)
                    copies.append(
                        pltpu.make_async_copy(
                            ins[ky * nb + kb].at[kz],
                            out.at[pl.ds(at, rows)],
                            sems.at[len(copies)],
                        )
                    )
        for copy in copies:
            copy.start()
        for copy in copies:
            copy.wait()

    return pl.pallas_call(
        kernel,
        out_shape=jax.ShapeDtypeStruct((count * rows, cols), bf16),
        in_specs=[SMEM] + [ANY] * len(parts),
        out_specs=ANY,
        scratch_shapes=[pltpu.SemaphoreType.DMA((count,))],
        compiler_params=PARAMS,
        name="assemble_weight",
    )(where, *parts)


def slot_of(k):
    return ((k & 1) << 1) | (k >> 1)


def natural(ref, lead, slot, flip, columns):
    first = ref[(*lead, flip, slot, slice(None), columns)]
    second = ref[(*lead, 1 - flip, slot, slice(None), columns)]
    return jnp.concatenate([first, second], axis=0)


def dot(left, right, dims):
    return lax.dot_general(left, right, (dims, ((), ())), preferred_element_type=f32)


NN, NT, TN = ((1,), (0,)), ((1,), (1,)), ((0,), (0,))


def decay_matrix(col, row):
    block = row.shape[-1]
    at = lax.broadcasted_iota(jnp.int32, (block, block), 0)
    to = lax.broadcasted_iota(jnp.int32, (block, block), 1)
    return jnp.where(at >= to, jnp.exp(jnp.minimum(col - row, 0.0)), 0.0)


def retention_forward(where, c_row, c_col, keyval, query, gate):
    ny, halves, nz, part, _ = keyval.shape
    block = halves * part

    def kernel(where_ref, row_ref, col_ref, kv_ref, q_ref, g_ref, y_ref, o_ref, s_ref, state):
        j = pl.program_id(0)

        @pl.when(j == 0)
        def _():
            state[...] = jnp.zeros_like(state)

        slot = slot_of((j // ny) ^ where_ref[0])
        ky = (j % ny) ^ where_ref[1]
        flip = where_ref[3]
        row, col = row_ref[j], col_ref[j]
        key = natural(kv_ref, (ky,), slot, flip, slice(0, DK))
        value = natural(kv_ref, (ky,), slot, flip, slice(DK, DK + DV))
        last = row[:, block - 1 :]

        @pl.when(ky == 0)
        def _():
            q = natural(q_ref, (), slot, flip, slice(None))
            state_bf = state[...].astype(bf16)
            s_ref[slot] = state_bf
            weights = (dot(q, key, NT) * decay_matrix(col, row)).astype(bf16)
            out = dot(weights, value, NN) + jnp.exp(col) * dot(q, state_bf, NN)
            normed, _ = normalize(out)
            g = natural(g_ref, (), slot, flip, slice(None))
            mixed = (g * jax.nn.sigmoid(g) * normed).astype(bf16)
            for half in range(2):
                rows = slice(half * part, (half + 1) * part)
                to = (1 - flip) if half else flip
                y_ref[to, slot] = mixed[rows]
                o_ref[to, slot] = out[rows]

        key_tail = (key.astype(f32) * jnp.exp(last - col)).astype(bf16)
        state[...] = jnp.exp(last) * state[...] + dot(key_tail, value, TN)

    return pl.pallas_call(
        kernel,
        grid=(nz * ny,),
        out_shape=[
            jax.ShapeDtypeStruct((halves, nz, part, DV), bf16),
            jax.ShapeDtypeStruct((halves, nz, part, DV), f32),
            jax.ShapeDtypeStruct((nz, DK, DV), bf16),
        ],
        in_specs=[SMEM] + [WHOLE] * 5,
        out_specs=[WHOLE] * 3,
        scratch_shapes=[pltpu.VMEM((DK, DV), f32)],
        compiler_params=PARAMS,
        name="retention_forward",
    )(where, c_row, c_col, keyval, query, gate)


def retention_backward(where, c_row, c_col, keyval, queries, grads, states, cosines, sines):
    ny, halves, nz, part, _ = queries.shape
    block = halves * part
    key_scale = DK ** (-0.5)

    def kernel(
        where_ref, row_ref, col_ref, kv_ref, q_ref, d_ref, s_ref, cos_ref, sin_ref, g_ref, state
    ):
        step = pl.program_id(0)
        j = nz * ny - 1 - step

        @pl.when(step == 0)
        def _():
            state[...] = jnp.zeros_like(state)

        slot = slot_of((j // ny) ^ where_ref[0])
        ky = (j % ny) ^ where_ref[1]
        flip = where_ref[3]
        row, col = row_ref[j], col_ref[j]
        last = row[:, block - 1 :]
        q = natural(q_ref, (ky,), slot, flip, slice(None))
        grad = natural(d_ref, (ky,), slot, flip, slice(None))
        entry = jnp.exp(col)

        @pl.when(ky == 0)
        def _():
            key = natural(kv_ref, (), slot, flip, slice(0, DK))
            value = natural(kv_ref, (), slot, flip, slice(DK, DK + DV))
            cos = natural(cos_ref, (), slot, flip, slice(None))
            sin = natural(sin_ref, (), slot, flip, slice(None))
            decays = decay_matrix(col, row)
            tail = jnp.exp(last - col)
            state_bf = state[...].astype(bf16)
            weights = (dot(q, key, NT) * decays).astype(bf16)
            scores = (dot(grad, value, NT) * decays).astype(bf16)
            grad_q = dot(scores, key, NN) + entry * dot(grad, s_ref[slot], NT)
            grad_k = dot(scores, q, TN) + tail * dot(value, state_bf, NT)
            grad_v = dot(weights, grad, TN) + tail * dot(key, state_bf, NN)
            grad_q = rotate(grad_q, cos, -sin).astype(bf16)
            grad_k = (rotate(grad_k, cos, -sin) * key_scale).astype(bf16)
            grad_v = grad_v.astype(bf16)
            for half in range(2):
                rows = slice(half * part, (half + 1) * part)
                to = (1 - flip) if half else flip
                g_ref[to, slot, :, :DK] = grad_k[rows]
                g_ref[to, slot, :, DK : DK + DV] = grad_v[rows]
                g_ref[to, slot, :, DK + DV :] = grad_q[rows]

        query_entry = (q.astype(f32) * entry).astype(bf16)
        state[...] = jnp.exp(last) * state[...] + dot(query_entry, grad, TN)

    return pl.pallas_call(
        kernel,
        grid=(nz * ny,),
        out_shape=jax.ShapeDtypeStruct((halves, nz, part, 2 * DK + DV), bf16),
        in_specs=[SMEM] + [WHOLE] * 8,
        out_specs=WHOLE,
        scratch_shapes=[pltpu.VMEM((DK, DV), f32)],
        compiler_params=PARAMS,
        name="retention_backward",
    )(where, c_row, c_col, keyval, queries, grads, states, cosines, sines)


def shards(
    hidden_in,
    log_decay,
    out_grad,
    ln1_gain,
    ln1_bias,
    w_query,
    w_key,
    w_value,
    w_gate,
    w_out,
    ln2_gain,
    ln2_bias,
    mlp_gate,
    mlp_up,
    mlp_down,
):
    nz, ny = lax.axis_size("row"), lax.axis_size("col")
    nb, nh = lax.axis_size("batch"), lax.axis_size("head")
    z, y = lax.axis_index("row"), lax.axis_index("col")
    b, x = lax.axis_index("batch"), lax.axis_index("head")
    block, width = hidden_in.shape[1:]
    rows = ln1_gain.shape[0]
    part = block // nh
    tokens = nz * block
    where = jnp.stack([z, y, b, x]).astype(jnp.int32)

    def to_heads(pieces):
        return [pieces[0]] + [swap(pieces[k], "row", k) for k in range(1, nz)]

    def spread(pieces):
        own = jnp.stack(pieces)
        parts = []
        for k in range(ny):
            got = swap(own, "col", k) if k else own
            parts += [got, swap(got, "batch", 1)]
        return assemble_weight(where, parts, ny, nb)

    def halves(values):
        return pick(values.reshape(nh, part, -1), x, 0), pick(values.reshape(nh, part, -1), 1 - x, 0)

    def gather_block(values):
        own, other = halves(values)
        two = swap(own, "row", 2)
        one = swap(jnp.concatenate([own, two]), "row", 1)
        mirror = swap(two, "head", 1)
        mirror_one = swap(one, "head", 1)
        return jnp.concatenate([own, two, one, other, mirror, mirror_one])

    def gather_tokens(own):
        two = swap(own, "row", 2)
        pair = jnp.concatenate([own, two])
        one = swap(pair, "row", 1)
        mirror = swap(pair, "head", 1)
        mirror_one = swap(one, "head", 1)
        return jnp.concatenate([pair, one, mirror, mirror_one])

    def reduce_tokens(values, weight):
        half = tokens // 2
        quarter = half // 2
        far = matmul_t(values[half:], weight).astype(bf16)
        got_one = swap(far[quarter:], "head", 1)
        got_two = swap(far[:quarter], "head", 1)
        near = matmul_t(values[:half], weight)
        send = (near[quarter:] + got_one.astype(f32)).astype(bf16)
        got = swap(send, "row", 1)
        keep = near[:quarter] + got_two.astype(f32) + got.astype(f32)
        last = swap(keep[part:].astype(bf16), "row", 2)
        return keep[:part] + last.astype(f32)

    def sum_rows(grad):
        grad = grad.reshape(nz, ny, nb, rows, -1)
        got = swap(pick(grad, 1 - b, 2).astype(bf16), "batch", 1)
        grad = pick(grad, b, 2) + got.astype(f32)
        total = pick(grad, y, 1)
        for k in range(1, ny):
            total = total + swap(pick(grad, y ^ k, 1).astype(bf16), "col", k).astype(f32)
        return total

    def to_rows(total, widths):
        pieces = [swap(pick(total, z ^ k, 0).astype(bf16), "row", k) for k in range(1, nz)]
        return unpack_grads(where, pick(total, z, 0), pieces, widths)

    params = jnp.stack([ln1_gain, ln1_bias, ln2_gain, ln2_bias]).astype(f32)
    small = jnp.concatenate([params.reshape(-1), log_decay.reshape(-1)])
    small = gather_small(small, ("row", "col", "batch"))
    params = small[:, : 4 * rows].reshape(nz * ny * nb, 4, rows)
    gain_one, bias_one, gain_two, bias_two = params.transpose(1, 0, 2).reshape(4, width)
    decay = pick(pick(small[:, 4 * rows :].reshape(nz * ny, nb, nz, block), b, 1), z, 1)
    running = jnp.cumsum(decay, axis=-1)
    c_row, c_col = running[:, None, :], running[:, :, None]

    qkvg_pieces = to_heads(pack_weights(where, (w_key, w_value, w_query, w_gate), nz))
    hidden_all = gather_block(hidden_in[0])
    qkvg_w = spread(qkvg_pieces)
    out_t = after(w_out, qkvg_pieces, hidden_all).T
    out_pieces = to_heads(pack_weights(where, (out_t,), nz))
    out_w = spread(out_pieces)
    mlp_own = after((mlp_gate, mlp_up, mlp_down), out_pieces, qkvg_w)
    mlp_pieces = to_heads(pack_weights(where, (mlp_own[0], mlp_own[1], mlp_own[2].T), nz))
    mlp_w = spread(mlp_pieces)
    units = mlp_w.shape[1] // 3
    up_w, down_w = mlp_w[:, : 2 * units], mlp_w[:, 2 * units :]
    down_bf = gather_block(after(out_grad[0], mlp_pieces))

    scaled_one, _ = normalize(hidden_all.astype(f32))
    first_bf = (scaled_one * gain_one + bias_one).astype(bf16)
    projected = matmul(first_bf, qkvg_w)
    key_pre = projected[:, :DK]
    value_bf = projected[:, DK : DK + DV].astype(bf16)
    query_pre = projected[:, DK + DV : 2 * DK + DV]
    gate = projected[:, 2 * DK + DV :]

    half_dim = DK // 2
    freqs = 10000.0 ** (-jnp.arange(half_dim, dtype=f32) / half_dim)
    block_at = (jnp.array(ORDER) ^ z) * ny + y
    half_at = jnp.arange(nh) ^ x
    positions = (
        block_at[None, :, None] * block + half_at[:, None, None] * part + jnp.arange(part)
    )
    angles = positions.astype(f32).reshape(-1)[:, None] * freqs[None, :]
    cosines, sines = jnp.cos(angles), jnp.sin(angles)
    key_scale = DK ** (-0.5)
    query_bf = rotate(query_pre, cosines, sines).astype(bf16)
    key_bf = (rotate(key_pre, cosines, sines) * key_scale).astype(bf16)

    def split(values):
        return values.reshape(nh, nz, part, -1)

    def gather_col(values):
        return jnp.stack([values] + [swap(values, "col", k) for k in range(1, ny)])

    keyval = split(jnp.concatenate([key_bf, value_bf], axis=-1))
    keyvals = gather_col(keyval)
    queries = gather_col(after(split(query_bf), keyvals))
    mixed, retained, states = retention_forward(
        where, c_row, c_col, keyvals, split(query_bf), split(gate)
    )
    mixed_bf = mixed.reshape(tokens, DV)

    inputs = halves(hidden_in[0])[0].astype(f32)
    middle = inputs + reduce_tokens(mixed_bf, out_w)
    scaled_two, rstd_two = normalize(middle)
    second_bf = gather_tokens((scaled_two * gain_two + bias_two).astype(bf16))
    up = matmul(second_bf, up_w)
    up_gate, up_lin = up[:, :units], up[:, units:]
    gelu_val, gelu_pull = jax.vjp(lambda v: jax.nn.gelu(v, approximate=False), up_gate)
    hidden_bf = (gelu_val * up_lin).astype(bf16)

    grad_hidden = matmul(down_bf, down_w)
    grad_upgate = gelu_pull(grad_hidden * up_lin)[0].astype(bf16)
    grad_uplin = (grad_hidden * gelu_val).astype(bf16)
    grad_up = jnp.concatenate([grad_upgate, grad_uplin], axis=-1)
    grad_two = reduce_tokens(grad_up, up_w)
    cotangent = halves(out_grad[0])[0].astype(f32)
    grad_middle = cotangent + norm_back(grad_two * gain_two, scaled_two, rstd_two)
    attn_bf = gather_tokens(grad_middle.astype(bf16))
    up_sum = sum_rows(outer_sum(second_bf, grad_up))
    down_sum = sum_rows(outer_sum(down_bf, hidden_bf))

    grp_norm, grp_rstd = normalize(retained.reshape(tokens, DV))
    gate_sig = jax.nn.sigmoid(gate)
    gate_act = gate * gate_sig
    grad_mixed = matmul(attn_bf, out_w)
    grad_gate = (grad_mixed * grp_norm * (gate_sig * (1.0 + gate * (1.0 - gate_sig)))).astype(bf16)
    ret_bf = norm_back(grad_mixed * gate_act, grp_norm, grp_rstd).astype(bf16)
    ret_all = gather_col(split(ret_bf))
    grad_kvq = retention_backward(
        where, c_row, c_col, keyval, queries, ret_all, states, split(cosines), split(sines)
    )
    grad_proj = jnp.concatenate([grad_kvq.reshape(tokens, -1), grad_gate], axis=-1)
    grad_one = reduce_tokens(grad_proj, qkvg_w)

    result = middle + reduce_tokens(after(hidden_bf, attn_bf), down_w)
    result = result.astype(bf16)
    result_other = swap(result, "head", 1)
    up_sum, down_sum = after((up_sum, down_sum), attn_bf)
    grad_gates, grad_ups = to_rows(up_sum, (units, units))
    (grad_downs,) = to_rows(down_sum, (units,))
    out_sum = sum_rows(outer_sum(attn_bf, mixed_bf))
    (grad_outs,) = to_rows(out_sum, (DV,))
    qkvg_sum = sum_rows(outer_sum(first_bf, grad_proj))
    grad_k, grad_v, grad_q, grad_g = to_rows(qkvg_sum, (DK, DV, DK, DV))

    scaled_own, rstd_own = normalize(inputs)
    grad_in = grad_middle + norm_back(grad_one * gain_one, scaled_own, rstd_own)
    grad_in_other = swap(grad_in, "head", 1)

    def join(own, other):
        first = jnp.where(x == 0, own, other)
        second = jnp.where(x == 0, other, own)
        return jnp.concatenate([first, second]).reshape(1, block, width)

    norm_sums = jnp.stack(
        [
            jnp.sum(grad_one * scaled_own, axis=0),
            jnp.sum(grad_one, axis=0),
            jnp.sum(grad_two * scaled_two, axis=0),
            jnp.sum(grad_two, axis=0),
        ]
    )
    norm_sums = norm_sums + swap(norm_sums, "head", 1)
    norm_sums = norm_sums.reshape(4, nz, ny, nb, rows)
    for name, axis in (("batch", 3), ("col", 2), ("row", 1)):
        me = lax.axis_index(name)
        summed = pick(norm_sums, me, axis)
        for k in range(1, lax.axis_size(name)):
            summed = summed + swap(pick(norm_sums, me ^ k, axis), name, k)
        norm_sums = summed

    return (
        join(result, result_other),
        join(grad_in, grad_in_other),
        norm_sums[0],
        norm_sums[1],
        grad_q,
        grad_k,
        grad_v,
        grad_g,
        grad_outs.T,
        norm_sums[2],
        norm_sums[3],
        grad_gates,
        grad_ups,
        grad_downs.T,
    )


def solution(mesh):
    seq = ("row", "col")
    tokens = P("batch", seq, None)
    params = P((*seq, "batch"))
    by_rows = P((*seq, "batch"), "head")
    by_cols = P("head", (*seq, "batch"))

    def run(*arrays):
        rows = arrays[1].shape[1] // mesh.shape["head"]
        sizes = (rows, mesh.shape["seq"] // rows, mesh.shape["batch"], mesh.shape["head"])
        order = [mesh.axis_names.index(n) for n in ("seq", "batch", "head")]
        fine = Mesh(
            mesh.devices.transpose(order).reshape(sizes), ("row", "col", "batch", "head")
        )
        weights = (by_rows, by_rows, by_rows, by_rows, by_cols)
        feeds = (by_rows, by_rows, by_cols)
        return jax.shard_map(
            shards,
            mesh=fine,
            in_specs=(
                tokens,
                P("batch", "head", seq),
                tokens,
                params,
                params,
                *weights,
                params,
                params,
                *feeds,
            ),
            out_specs=(tokens, tokens, params, params, *weights, params, params, *feeds),
            check_vma=False,
        )(*arrays)

    return run
```

```python
import jax
import jax.numpy as jnp
from jax import lax
from jax.experimental import pallas as pl
from jax.experimental.pallas import tpu as pltpu
from jax.sharding import Mesh
from jax.sharding import PartitionSpec as P

DK = 256
DV = 512

epsilon = 1e-05
f32 = jnp.float32
bf16 = jnp.bfloat16
VMEM_LIMIT = 32 * 1024 * 1024

ORDER = (0, 2, 1, 3)


def swap(values, axis, k):
    count = lax.axis_size(axis)
    return lax.ppermute(values, axis, [(i, i ^ k) for i in range(count)])


def pick(values, index, axis):
    return lax.dynamic_index_in_dim(values, index, axis, keepdims=False)


def after(values, *others):
    return lax.optimization_barrier((values, others))[0]


def gather_small(values, names):
    values = values[None]
    for name in reversed(names):
        bit = 1
        while bit < lax.axis_size(name):
            other = swap(values, name, bit)
            low = (lax.axis_index(name) & bit) == 0
            values = jnp.where(
                low, jnp.concatenate([values, other]), jnp.concatenate([other, values])
            )
            bit *= 2
    return values


def matmul(values, weight):
    return jnp.dot(values, weight, preferred_element_type=f32)


def matmul_t(values, weight):
    return lax.dot_general(values, weight, (((1,), (1,)), ((), ())), preferred_element_type=f32)


def outer_sum(values, other):
    return lax.dot_general(values, other, (((0,), (0,)), ((), ())), preferred_element_type=f32)


def normalize(values):
    center = values - jnp.mean(values, axis=-1, keepdims=True)
    rstd = lax.rsqrt(jnp.mean(center * center, axis=-1, keepdims=True) + epsilon)
    return center * rstd, rstd


def norm_back(scaled_grad, scaled, rstd):
    return rstd * (
        scaled_grad
        - jnp.mean(scaled_grad, axis=-1, keepdims=True)
        - scaled * jnp.mean(scaled_grad * scaled, axis=-1, keepdims=True)
    )


def rotate(values, cosines, sines):
    half_dim = values.shape[-1] // 2
    first_half = values[..., :half_dim]
    second_half = values[..., half_dim:]
    return jnp.concatenate(
        [first_half * cosines - second_half * sines, first_half * sines + second_half * cosines],
        axis=-1,
    )


SMEM = pl.BlockSpec(memory_space=pltpu.SMEM)
WHOLE = pl.BlockSpec(memory_space=pltpu.VMEM)
PARAMS = pltpu.CompilerParams(vmem_limit_bytes=VMEM_LIMIT)


def pack_weights(where, weights, nz):
    rows = weights[0].shape[0]
    widths = [w.shape[1] // nz for w in weights]

    def kernel(where_ref, *refs):
        ins, outs = refs[: len(weights)], refs[len(weights) :]
        for k in range(nz):
            target = where_ref[0] ^ k
            at = 0
            for ref, width in zip(ins, widths):
                start = pl.multiple_of(target * width, width)
                outs[k][:, at : at + width] = ref[:, pl.ds(start, width)]
                at += width

    return pl.pallas_call(
        kernel,
        out_shape=[jax.ShapeDtypeStruct((rows, sum(widths)), bf16)] * nz,
        in_specs=[SMEM] + [WHOLE] * len(weights),
        out_specs=[WHOLE] * nz,
        compiler_params=PARAMS,
        name="pack_weights",
    )(where, *weights)


def unpack_grads(where, own, pieces, widths):
    nz = len(pieces) + 1
    rows = own.shape[0]

    def kernel(where_ref, *refs):
        ins, outs = refs[:nz], refs[nz:]
        for k in range(nz):
            target = where_ref[0] ^ k
            at = 0
            for ref, width in zip(outs, widths):
                start = pl.multiple_of(target * width, width)
                ref[:, pl.ds(start, width)] = ins[k][:, at : at + width].astype(f32)
                at += width

    return pl.pallas_call(
        kernel,
        out_shape=[jax.ShapeDtypeStruct((rows, nz * width), f32) for width in widths],
        in_specs=[SMEM] + [WHOLE] * nz,
        out_specs=[WHOLE] * len(widths),
        compiler_params=PARAMS,
        name="unpack_grads",
    )(where, own, *pieces)


def assemble_weight(where, parts, ny, nb):
    nz, rows, cols = parts[0].shape

    def kernel(where_ref, *refs):
        ins, out = refs[:-1], refs[-1]
        for ky in range(ny):
            for kb in range(nb):
                for kz in range(nz):
                    at = ((where_ref[0] ^ kz) * ny + (where_ref[1] ^ ky)) * nb
                    at = pl.multiple_of((at + (where_ref[2] ^ kb)) * rows, rows)
                    out[pl.ds(at, rows), :] = ins[ky * nb + kb][kz]

    return pl.pallas_call(
        kernel,
        out_shape=jax.ShapeDtypeStruct((nz * ny * nb * rows, cols), bf16),
        in_specs=[SMEM] + [WHOLE] * len(parts),
        out_specs=WHOLE,
        compiler_params=PARAMS,
        name="assemble_weight",
    )(where, *parts)


def slot_of(k):
    return ((k & 1) << 1) | (k >> 1)


def natural(ref, lead, slot, flip, columns):
    first = ref[(*lead, flip, slot, slice(None), columns)]
    second = ref[(*lead, 1 - flip, slot, slice(None), columns)]
    return jnp.concatenate([first, second], axis=0)


def dot(left, right, dims):
    return lax.dot_general(left, right, (dims, ((), ())), preferred_element_type=f32)


NN, NT, TN = ((1,), (0,)), ((1,), (1,)), ((0,), (0,))


def decay_matrix(col, row):
    block = row.shape[-1]
    at = lax.broadcasted_iota(jnp.int32, (block, block), 0)
    to = lax.broadcasted_iota(jnp.int32, (block, block), 1)
    return jnp.where(at >= to, jnp.exp(jnp.minimum(col - row, 0.0)), 0.0)


def retention_forward(where, c_row, c_col, keyval, query, gate):
    ny, halves, nz, part, _ = keyval.shape
    block = halves * part

    def kernel(where_ref, row_ref, col_ref, kv_ref, q_ref, g_ref, y_ref, o_ref, s_ref, state):
        j = pl.program_id(0)

        @pl.when(j == 0)
        def _():
            state[...] = jnp.zeros_like(state)

        slot = slot_of((j // ny) ^ where_ref[0])
        ky = (j % ny) ^ where_ref[1]
        flip = where_ref[3]
        row, col = row_ref[j], col_ref[j]
        key = natural(kv_ref, (ky,), slot, flip, slice(0, DK))
        value = natural(kv_ref, (ky,), slot, flip, slice(DK, DK + DV))
        last = row[:, block - 1 :]

        @pl.when(ky == 0)
        def _():
            q = natural(q_ref, (), slot, flip, slice(None))
            state_bf = state[...].astype(bf16)
            s_ref[slot] = state_bf
            weights = (dot(q, key, NT) * decay_matrix(col, row)).astype(bf16)
            out = dot(weights, value, NN) + jnp.exp(col) * dot(q, state_bf, NN)
            normed, _ = normalize(out)
            g = natural(g_ref, (), slot, flip, slice(None))
            mixed = (g * jax.nn.sigmoid(g) * normed).astype(bf16)
            for half in range(2):
                rows = slice(half * part, (half + 1) * part)
                to = (1 - flip) if half else flip
                y_ref[to, slot] = mixed[rows]
                o_ref[to, slot] = out[rows]

        key_tail = (key.astype(f32) * jnp.exp(last - col)).astype(bf16)
        state[...] = jnp.exp(last) * state[...] + dot(key_tail, value, TN)

    return pl.pallas_call(
        kernel,
        grid=(nz * ny,),
        out_shape=[
            jax.ShapeDtypeStruct((halves, nz, part, DV), bf16),
            jax.ShapeDtypeStruct((halves, nz, part, DV), f32),
            jax.ShapeDtypeStruct((nz, DK, DV), bf16),
        ],
        in_specs=[SMEM] + [WHOLE] * 5,
        out_specs=[WHOLE] * 3,
        scratch_shapes=[pltpu.VMEM((DK, DV), f32)],
        compiler_params=PARAMS,
        name="retention_forward",
    )(where, c_row, c_col, keyval, query, gate)


def retention_backward(where, c_row, c_col, keyval, queries, grads, states, cosines, sines):
    ny, halves, nz, part, _ = queries.shape
    block = halves * part
    key_scale = DK ** (-0.5)

    def kernel(
        where_ref, row_ref, col_ref, kv_ref, q_ref, d_ref, s_ref, cos_ref, sin_ref, g_ref, state
    ):
        step = pl.program_id(0)
        j = nz * ny - 1 - step

        @pl.when(step == 0)
        def _():
            state[...] = jnp.zeros_like(state)

        slot = slot_of((j // ny) ^ where_ref[0])
        ky = (j % ny) ^ where_ref[1]
        flip = where_ref[3]
        row, col = row_ref[j], col_ref[j]
        last = row[:, block - 1 :]
        q = natural(q_ref, (ky,), slot, flip, slice(None))
        grad = natural(d_ref, (ky,), slot, flip, slice(None))
        entry = jnp.exp(col)

        @pl.when(ky == 0)
        def _():
            key = natural(kv_ref, (), slot, flip, slice(0, DK))
            value = natural(kv_ref, (), slot, flip, slice(DK, DK + DV))
            cos = natural(cos_ref, (), slot, flip, slice(None))
            sin = natural(sin_ref, (), slot, flip, slice(None))
            decays = decay_matrix(col, row)
            tail = jnp.exp(last - col)
            state_bf = state[...].astype(bf16)
            weights = (dot(q, key, NT) * decays).astype(bf16)
            scores = (dot(grad, value, NT) * decays).astype(bf16)
            grad_q = dot(scores, key, NN) + entry * dot(grad, s_ref[slot], NT)
            grad_k = dot(scores, q, TN) + tail * dot(value, state_bf, NT)
            grad_v = dot(weights, grad, TN) + tail * dot(key, state_bf, NN)
            grad_q = rotate(grad_q, cos, -sin).astype(bf16)
            grad_k = (rotate(grad_k, cos, -sin) * key_scale).astype(bf16)
            grad_v = grad_v.astype(bf16)
            for half in range(2):
                rows = slice(half * part, (half + 1) * part)
                to = (1 - flip) if half else flip
                g_ref[to, slot, :, :DK] = grad_k[rows]
                g_ref[to, slot, :, DK : DK + DV] = grad_v[rows]
                g_ref[to, slot, :, DK + DV :] = grad_q[rows]

        query_entry = (q.astype(f32) * entry).astype(bf16)
        state[...] = jnp.exp(last) * state[...] + dot(query_entry, grad, TN)

    return pl.pallas_call(
        kernel,
        grid=(nz * ny,),
        out_shape=jax.ShapeDtypeStruct((halves, nz, part, 2 * DK + DV), bf16),
        in_specs=[SMEM] + [WHOLE] * 8,
        out_specs=WHOLE,
        scratch_shapes=[pltpu.VMEM((DK, DV), f32)],
        compiler_params=PARAMS,
        name="retention_backward",
    )(where, c_row, c_col, keyval, queries, grads, states, cosines, sines)


def shards(
    hidden_in,
    log_decay,
    out_grad,
    ln1_gain,
    ln1_bias,
    w_query,
    w_key,
    w_value,
    w_gate,
    w_out,
    ln2_gain,
    ln2_bias,
    mlp_gate,
    mlp_up,
    mlp_down,
):
    nz, ny = lax.axis_size("row"), lax.axis_size("col")
    nb, nh = lax.axis_size("batch"), lax.axis_size("head")
    z, y = lax.axis_index("row"), lax.axis_index("col")
    b, x = lax.axis_index("batch"), lax.axis_index("head")
    block, width = hidden_in.shape[1:]
    rows = ln1_gain.shape[0]
    part = block // nh
    tokens = nz * block
    where = jnp.stack([z, y, b, x]).astype(jnp.int32)

    def to_heads(pieces):
        return [pieces[0]] + [swap(pieces[k], "row", k) for k in range(1, nz)]

    def spread(pieces):
        own = jnp.stack(pieces)
        parts = []
        for k in range(ny):
            got = swap(own, "col", k) if k else own
            parts += [got, swap(got, "batch", 1)]
        return assemble_weight(where, parts, ny, nb)

    def halves(values):
        return pick(values.reshape(nh, part, -1), x, 0), pick(values.reshape(nh, part, -1), 1 - x, 0)

    def gather_block(values):
        own, other = halves(values)
        two = swap(own, "row", 2)
        one = swap(jnp.concatenate([own, two]), "row", 1)
        mirror = swap(two, "head", 1)
        mirror_one = swap(one, "head", 1)
        return jnp.concatenate([own, two, one, other, mirror, mirror_one])

    def gather_tokens(own):
        two = swap(own, "row", 2)
        pair = jnp.concatenate([own, two])
        one = swap(pair, "row", 1)
        mirror = swap(pair, "head", 1)
        mirror_one = swap(one, "head", 1)
        return jnp.concatenate([pair, one, mirror, mirror_one])

    def reduce_tokens(values, weight):
        half = tokens // 2
        quarter = half // 2
        far = matmul_t(values[half:], weight).astype(bf16)
        got_one = swap(far[quarter:], "head", 1)
        got_two = swap(far[:quarter], "head", 1)
        near = matmul_t(values[:half], weight)
        send = (near[quarter:] + got_one.astype(f32)).astype(bf16)
        got = swap(send, "row", 1)
        keep = near[:quarter] + got_two.astype(f32) + got.astype(f32)
        last = swap(keep[part:].astype(bf16), "row", 2)
        return keep[:part] + last.astype(f32)

    def sum_rows(grad):
        grad = grad.reshape(nz, ny, nb, rows, -1)
        got = swap(pick(grad, 1 - b, 2).astype(bf16), "batch", 1)
        grad = pick(grad, b, 2) + got.astype(f32)
        total = pick(grad, y, 1)
        for k in range(1, ny):
            total = total + swap(pick(grad, y ^ k, 1).astype(bf16), "col", k).astype(f32)
        return total

    def to_rows(total, widths):
        pieces = [swap(pick(total, z ^ k, 0).astype(bf16), "row", k) for k in range(1, nz)]
        return unpack_grads(where, pick(total, z, 0), pieces, widths)

    params = jnp.stack([ln1_gain, ln1_bias, ln2_gain, ln2_bias]).astype(f32)
    small = jnp.concatenate([params.reshape(-1), log_decay.reshape(-1)])
    small = gather_small(small, ("row", "col", "batch"))
    params = small[:, : 4 * rows].reshape(nz * ny * nb, 4, rows)
    gain_one, bias_one, gain_two, bias_two = params.transpose(1, 0, 2).reshape(4, width)
    decay = pick(pick(small[:, 4 * rows :].reshape(nz * ny, nb, nz, block), b, 1), z, 1)
    running = jnp.cumsum(decay, axis=-1)
    c_row, c_col = running[:, None, :], running[:, :, None]

    qkvg_pieces = to_heads(pack_weights(where, (w_key, w_value, w_query, w_gate), nz))
    hidden_all = gather_block(hidden_in[0])
    qkvg_w = spread(qkvg_pieces)
    out_t = after(w_out, qkvg_pieces, hidden_all).T
    out_pieces = to_heads(pack_weights(where, (out_t,), nz))
    out_w = spread(out_pieces)
    mlp_own = after((mlp_gate, mlp_up, mlp_down), out_pieces, qkvg_w)
    mlp_pieces = to_heads(pack_weights(where, (mlp_own[0], mlp_own[1], mlp_own[2].T), nz))
    mlp_w = spread(mlp_pieces)
    units = mlp_w.shape[1] // 3
    up_w, down_w = mlp_w[:, : 2 * units], mlp_w[:, 2 * units :]
    down_bf = gather_block(after(out_grad[0], mlp_pieces))

    scaled_one, _ = normalize(hidden_all.astype(f32))
    first_bf = (scaled_one * gain_one + bias_one).astype(bf16)
    projected = matmul(first_bf, qkvg_w)
    key_pre = projected[:, :DK]
    value_bf = projected[:, DK : DK + DV].astype(bf16)
    query_pre = projected[:, DK + DV : 2 * DK + DV]
    gate = projected[:, 2 * DK + DV :]

    half_dim = DK // 2
    freqs = 10000.0 ** (-jnp.arange(half_dim, dtype=f32) / half_dim)
    block_at = (jnp.array(ORDER) ^ z) * ny + y
    half_at = jnp.arange(nh) ^ x
    positions = (
        block_at[None, :, None] * block + half_at[:, None, None] * part + jnp.arange(part)
    )
    angles = positions.astype(f32).reshape(-1)[:, None] * freqs[None, :]
    cosines, sines = jnp.cos(angles), jnp.sin(angles)
    key_scale = DK ** (-0.5)
    query_bf = rotate(query_pre, cosines, sines).astype(bf16)
    key_bf = (rotate(key_pre, cosines, sines) * key_scale).astype(bf16)

    def split(values):
        return values.reshape(nh, nz, part, -1)

    def gather_col(values):
        return jnp.stack([values] + [swap(values, "col", k) for k in range(1, ny)])

    keyval = split(jnp.concatenate([key_bf, value_bf], axis=-1))
    keyvals = gather_col(keyval)
    queries = gather_col(after(split(query_bf), keyvals))
    mixed, retained, states = retention_forward(
        where, c_row, c_col, keyvals, split(query_bf), split(gate)
    )
    mixed_bf = mixed.reshape(tokens, DV)

    inputs = halves(hidden_in[0])[0].astype(f32)
    middle = inputs + reduce_tokens(mixed_bf, out_w)
    scaled_two, rstd_two = normalize(middle)
    second_bf = gather_tokens((scaled_two * gain_two + bias_two).astype(bf16))
    up = matmul(second_bf, up_w)
    up_gate, up_lin = up[:, :units], up[:, units:]
    gelu_val, gelu_pull = jax.vjp(lambda v: jax.nn.gelu(v, approximate=False), up_gate)
    hidden_bf = (gelu_val * up_lin).astype(bf16)

    grad_hidden = matmul(down_bf, down_w)
    grad_upgate = gelu_pull(grad_hidden * up_lin)[0].astype(bf16)
    grad_uplin = (grad_hidden * gelu_val).astype(bf16)
    grad_up = jnp.concatenate([grad_upgate, grad_uplin], axis=-1)
    grad_two = reduce_tokens(grad_up, up_w)
    cotangent = halves(out_grad[0])[0].astype(f32)
    grad_middle = cotangent + norm_back(grad_two * gain_two, scaled_two, rstd_two)
    attn_bf = gather_tokens(grad_middle.astype(bf16))
    up_sum = sum_rows(outer_sum(second_bf, grad_up))
    down_sum = sum_rows(outer_sum(down_bf, hidden_bf))

    grp_norm, grp_rstd = normalize(retained.reshape(tokens, DV))
    gate_sig = jax.nn.sigmoid(gate)
    gate_act = gate * gate_sig
    grad_mixed = matmul(attn_bf, out_w)
    grad_gate = (grad_mixed * grp_norm * (gate_sig * (1.0 + gate * (1.0 - gate_sig)))).astype(bf16)
    ret_bf = norm_back(grad_mixed * gate_act, grp_norm, grp_rstd).astype(bf16)
    ret_all = gather_col(split(ret_bf))
    grad_kvq = retention_backward(
        where, c_row, c_col, keyval, queries, ret_all, states, split(cosines), split(sines)
    )
    grad_proj = jnp.concatenate([grad_kvq.reshape(tokens, -1), grad_gate], axis=-1)
    grad_one = reduce_tokens(grad_proj, qkvg_w)

    result = middle + reduce_tokens(after(hidden_bf, attn_bf), down_w)
    result = result.astype(bf16)
    result_other = swap(result, "head", 1)
    up_sum, down_sum = after((up_sum, down_sum), attn_bf)
    grad_gates, grad_ups = to_rows(up_sum, (units, units))
    (grad_downs,) = to_rows(down_sum, (units,))
    out_sum = sum_rows(outer_sum(attn_bf, mixed_bf))
    (grad_outs,) = to_rows(out_sum, (DV,))
    qkvg_sum = sum_rows(outer_sum(first_bf, grad_proj))
    grad_k, grad_v, grad_q, grad_g = to_rows(qkvg_sum, (DK, DV, DK, DV))

    scaled_own, rstd_own = normalize(inputs)
    grad_in = grad_middle + norm_back(grad_one * gain_one, scaled_own, rstd_own)
    grad_in_other = swap(grad_in, "head", 1)

    def join(own, other):
        first = jnp.where(x == 0, own, other)
        second = jnp.where(x == 0, other, own)
        return jnp.concatenate([first, second]).reshape(1, block, width)

    norm_sums = jnp.stack(
        [
            jnp.sum(grad_one * scaled_own, axis=0),
            jnp.sum(grad_one, axis=0),
            jnp.sum(grad_two * scaled_two, axis=0),
            jnp.sum(grad_two, axis=0),
        ]
    )
    norm_sums = norm_sums + swap(norm_sums, "head", 1)
    norm_sums = norm_sums.reshape(4, nz, ny, nb, rows)
    for name, axis in (("batch", 3), ("col", 2), ("row", 1)):
        me = lax.axis_index(name)
        summed = pick(norm_sums, me, axis)
        for k in range(1, lax.axis_size(name)):
            summed = summed + swap(pick(norm_sums, me ^ k, axis), name, k)
        norm_sums = summed

    return (
        join(result, result_other),
        join(grad_in, grad_in_other),
        norm_sums[0],
        norm_sums[1],
        grad_q,
        grad_k,
        grad_v,
        grad_g,
        grad_outs.T,
        norm_sums[2],
        norm_sums[3],
        grad_gates,
        grad_ups,
        grad_downs.T,
    )


def solution(mesh):
    seq = ("row", "col")
    tokens = P("batch", seq, None)
    params = P((*seq, "batch"))
    by_rows = P((*seq, "batch"), "head")
    by_cols = P("head", (*seq, "batch"))

    def run(*arrays):
        rows = arrays[1].shape[1] // mesh.shape["head"]
        sizes = (rows, mesh.shape["seq"] // rows, mesh.shape["batch"], mesh.shape["head"])
        order = [mesh.axis_names.index(n) for n in ("seq", "batch", "head")]
        fine = Mesh(
            mesh.devices.transpose(order).reshape(sizes), ("row", "col", "batch", "head")
        )
        weights = (by_rows, by_rows, by_rows, by_rows, by_cols)
        feeds = (by_rows, by_rows, by_cols)
        return jax.shard_map(
            shards,
            mesh=fine,
            in_specs=(
                tokens,
                P("batch", "head", seq),
                tokens,
                params,
                params,
                *weights,
                params,
                params,
                *feeds,
            ),
            out_specs=(tokens, tokens, params, params, *weights, params, params, *feeds),
            check_vma=False,
        )(*arrays)

    return run
```

```python
import jax
import jax.numpy as jnp
from jax import lax
from jax.experimental import pallas as pl
from jax.experimental.pallas import tpu as pltpu
from jax.sharding import Mesh
from jax.sharding import PartitionSpec as P

DK = 256
DV = 512

epsilon = 1e-05
f32 = jnp.float32
bf16 = jnp.bfloat16
VMEM_LIMIT = 32 * 1024 * 1024

ORDER = (0, 2, 1, 3)


def swap(values, axis, k):
    count = lax.axis_size(axis)
    return lax.ppermute(values, axis, [(i, i ^ k) for i in range(count)])


def pick(values, index, axis):
    return lax.dynamic_index_in_dim(values, index, axis, keepdims=False)


def after(values, *others):
    return lax.optimization_barrier((values, others))[0]


def gather_small(values, names):
    values = values[None]
    for name in reversed(names):
        bit = 1
        while bit < lax.axis_size(name):
            other = swap(values, name, bit)
            low = (lax.axis_index(name) & bit) == 0
            values = jnp.where(
                low, jnp.concatenate([values, other]), jnp.concatenate([other, values])
            )
            bit *= 2
    return values


def matmul(values, weight):
    return jnp.dot(values, weight, preferred_element_type=f32)


def matmul_t(values, weight):
    return lax.dot_general(values, weight, (((1,), (1,)), ((), ())), preferred_element_type=f32)


def outer_sum(values, other):
    return lax.dot_general(values, other, (((0,), (0,)), ((), ())), preferred_element_type=f32)


def normalize(values):
    center = values - jnp.mean(values, axis=-1, keepdims=True)
    rstd = lax.rsqrt(jnp.mean(center * center, axis=-1, keepdims=True) + epsilon)
    return center * rstd, rstd


def norm_back(scaled_grad, scaled, rstd):
    return rstd * (
        scaled_grad
        - jnp.mean(scaled_grad, axis=-1, keepdims=True)
        - scaled * jnp.mean(scaled_grad * scaled, axis=-1, keepdims=True)
    )


def rotate(values, cosines, sines):
    half_dim = values.shape[-1] // 2
    first_half = values[..., :half_dim]
    second_half = values[..., half_dim:]
    return jnp.concatenate(
        [first_half * cosines - second_half * sines, first_half * sines + second_half * cosines],
        axis=-1,
    )


SMEM = pl.BlockSpec(memory_space=pltpu.SMEM)
WHOLE = pl.BlockSpec(memory_space=pltpu.VMEM)
PARAMS = pltpu.CompilerParams(vmem_limit_bytes=VMEM_LIMIT)


def pack_weights(where, weights, nz):
    rows = weights[0].shape[0]
    widths = [w.shape[1] // nz for w in weights]

    def kernel(where_ref, *refs):
        ins, outs = refs[: len(weights)], refs[len(weights) :]
        for k in range(nz):
            target = where_ref[0] ^ k
            at = 0
            for ref, width in zip(ins, widths):
                start = pl.multiple_of(target * width, width)
                outs[k][:, at : at + width] = ref[:, pl.ds(start, width)]
                at += width

    return pl.pallas_call(
        kernel,
        out_shape=[jax.ShapeDtypeStruct((rows, sum(widths)), bf16)] * nz,
        in_specs=[SMEM] + [WHOLE] * len(weights),
        out_specs=[WHOLE] * nz,
        compiler_params=PARAMS,
        name="pack_weights",
    )(where, *weights)


def unpack_grads(where, own, pieces, widths):
    nz = len(pieces) + 1
    rows = own.shape[0]

    def kernel(where_ref, *refs):
        ins, outs = refs[:nz], refs[nz:]
        for k in range(nz):
            target = where_ref[0] ^ k
            at = 0
            for ref, width in zip(outs, widths):
                start = pl.multiple_of(target * width, width)
                ref[:, pl.ds(start, width)] = ins[k][:, at : at + width].astype(f32)
                at += width

    return pl.pallas_call(
        kernel,
        out_shape=[jax.ShapeDtypeStruct((rows, nz * width), f32) for width in widths],
        in_specs=[SMEM] + [WHOLE] * nz,
        out_specs=[WHOLE] * len(widths),
        compiler_params=PARAMS,
        name="unpack_grads",
    )(where, own, *pieces)


def assemble_weight(where, parts, ny, nb):
    nz, rows, cols = parts[0].shape

    def kernel(where_ref, *refs):
        ins, out = refs[:-1], refs[-1]
        for ky in range(ny):
            for kb in range(nb):
                for kz in range(nz):
                    at = ((where_ref[0] ^ kz) * ny + (where_ref[1] ^ ky)) * nb
                    at = pl.multiple_of((at + (where_ref[2] ^ kb)) * rows, rows)
                    out[pl.ds(at, rows), :] = ins[ky * nb + kb][kz]

    return pl.pallas_call(
        kernel,
        out_shape=jax.ShapeDtypeStruct((nz * ny * nb * rows, cols), bf16),
        in_specs=[SMEM] + [WHOLE] * len(parts),
        out_specs=WHOLE,
        compiler_params=PARAMS,
        name="assemble_weight",
    )(where, *parts)


def slot_of(k):
    return ((k & 1) << 1) | (k >> 1)


def natural(ref, lead, slot, flip, columns):
    first = ref[(*lead, flip, slot, slice(None), columns)]
    second = ref[(*lead, 1 - flip, slot, slice(None), columns)]
    return jnp.concatenate([first, second], axis=0)


def dot(left, right, dims):
    return lax.dot_general(left, right, (dims, ((), ())), preferred_element_type=f32)


NN, NT, TN = ((1,), (0,)), ((1,), (1,)), ((0,), (0,))


def decay_matrix(col, row):
    block = row.shape[-1]
    at = lax.broadcasted_iota(jnp.int32, (block, block), 0)
    to = lax.broadcasted_iota(jnp.int32, (block, block), 1)
    return jnp.where(at >= to, jnp.exp(jnp.minimum(col - row, 0.0)), 0.0)


def retention_forward(where, c_row, c_col, keyval, query, gate):
    ny, halves, nz, part, _ = keyval.shape
    block = halves * part

    def kernel(where_ref, row_ref, col_ref, kv_ref, q_ref, g_ref, y_ref, o_ref, s_ref, state):
        j = pl.program_id(0)

        @pl.when(j == 0)
        def _():
            state[...] = jnp.zeros_like(state)

        slot = slot_of((j // ny) ^ where_ref[0])
        ky = (j % ny) ^ where_ref[1]
        flip = where_ref[3]
        row, col = row_ref[j], col_ref[j]
        key = natural(kv_ref, (ky,), slot, flip, slice(0, DK))
        value = natural(kv_ref, (ky,), slot, flip, slice(DK, DK + DV))
        last = row[:, block - 1 :]

        @pl.when(ky == 0)
        def _():
            q = natural(q_ref, (), slot, flip, slice(None))
            state_bf = state[...].astype(bf16)
            s_ref[slot] = state_bf
            weights = (dot(q, key, NT) * decay_matrix(col, row)).astype(bf16)
            out = dot(weights, value, NN) + jnp.exp(col) * dot(q, state_bf, NN)
            normed, _ = normalize(out)
            g = natural(g_ref, (), slot, flip, slice(None))
            mixed = (g * jax.nn.sigmoid(g) * normed).astype(bf16)
            for half in range(2):
                rows = slice(half * part, (half + 1) * part)
                to = (1 - flip) if half else flip
                y_ref[to, slot] = mixed[rows]
                o_ref[to, slot] = out[rows]

        key_tail = (key.astype(f32) * jnp.exp(last - col)).astype(bf16)
        state[...] = jnp.exp(last) * state[...] + dot(key_tail, value, TN)

    return pl.pallas_call(
        kernel,
        grid=(nz * ny,),
        out_shape=[
            jax.ShapeDtypeStruct((halves, nz, part, DV), bf16),
            jax.ShapeDtypeStruct((halves, nz, part, DV), f32),
            jax.ShapeDtypeStruct((nz, DK, DV), bf16),
        ],
        in_specs=[SMEM] + [WHOLE] * 5,
        out_specs=[WHOLE] * 3,
        scratch_shapes=[pltpu.VMEM((DK, DV), f32)],
        compiler_params=PARAMS,
        name="retention_forward",
    )(where, c_row, c_col, keyval, query, gate)


def retention_backward(where, c_row, c_col, keyval, queries, grads, states, cosines, sines):
    ny, halves, nz, part, _ = queries.shape
    block = halves * part
    key_scale = DK ** (-0.5)

    def kernel(
        where_ref, row_ref, col_ref, kv_ref, q_ref, d_ref, s_ref, cos_ref, sin_ref, g_ref, state
    ):
        step = pl.program_id(0)
        j = nz * ny - 1 - step

        @pl.when(step == 0)
        def _():
            state[...] = jnp.zeros_like(state)

        slot = slot_of((j // ny) ^ where_ref[0])
        ky = (j % ny) ^ where_ref[1]
        flip = where_ref[3]
        row, col = row_ref[j], col_ref[j]
        last = row[:, block - 1 :]
        q = natural(q_ref, (ky,), slot, flip, slice(None))
        grad = natural(d_ref, (ky,), slot, flip, slice(None))
        entry = jnp.exp(col)

        @pl.when(ky == 0)
        def _():
            key = natural(kv_ref, (), slot, flip, slice(0, DK))
            value = natural(kv_ref, (), slot, flip, slice(DK, DK + DV))
            cos = natural(cos_ref, (), slot, flip, slice(None))
            sin = natural(sin_ref, (), slot, flip, slice(None))
            decays = decay_matrix(col, row)
            tail = jnp.exp(last - col)
            state_bf = state[...].astype(bf16)
            weights = (dot(q, key, NT) * decays).astype(bf16)
            scores = (dot(grad, value, NT) * decays).astype(bf16)
            grad_q = dot(scores, key, NN) + entry * dot(grad, s_ref[slot], NT)
            grad_k = dot(scores, q, TN) + tail * dot(value, state_bf, NT)
            grad_v = dot(weights, grad, TN) + tail * dot(key, state_bf, NN)
            grad_q = rotate(grad_q, cos, -sin).astype(bf16)
            grad_k = (rotate(grad_k, cos, -sin) * key_scale).astype(bf16)
            grad_v = grad_v.astype(bf16)
            for half in range(2):
                rows = slice(half * part, (half + 1) * part)
                to = (1 - flip) if half else flip
                g_ref[to, slot, :, :DK] = grad_k[rows]
                g_ref[to, slot, :, DK : DK + DV] = grad_v[rows]
                g_ref[to, slot, :, DK + DV :] = grad_q[rows]

        query_entry = (q.astype(f32) * entry).astype(bf16)
        state[...] = jnp.exp(last) * state[...] + dot(query_entry, grad, TN)

    return pl.pallas_call(
        kernel,
        grid=(nz * ny,),
        out_shape=jax.ShapeDtypeStruct((halves, nz, part, 2 * DK + DV), bf16),
        in_specs=[SMEM] + [WHOLE] * 8,
        out_specs=WHOLE,
        scratch_shapes=[pltpu.VMEM((DK, DV), f32)],
        compiler_params=PARAMS,
        name="retention_backward",
    )(where, c_row, c_col, keyval, queries, grads, states, cosines, sines)


def shards(
    hidden_in,
    log_decay,
    out_grad,
    ln1_gain,
    ln1_bias,
    w_query,
    w_key,
    w_value,
    w_gate,
    w_out,
    ln2_gain,
    ln2_bias,
    mlp_gate,
    mlp_up,
    mlp_down,
):
    nz, ny = lax.axis_size("row"), lax.axis_size("col")
    nb, nh = lax.axis_size("batch"), lax.axis_size("head")
    z, y = lax.axis_index("row"), lax.axis_index("col")
    b, x = lax.axis_index("batch"), lax.axis_index("head")
    block, width = hidden_in.shape[1:]
    rows = ln1_gain.shape[0]
    part = block // nh
    tokens = nz * block
    where = jnp.stack([z, y, b, x]).astype(jnp.int32)

    def to_heads(pieces):
        return [pieces[0]] + [swap(pieces[k], "row", k) for k in range(1, nz)]

    def spread(pieces):
        own = jnp.stack(pieces)
        parts = []
        for k in range(ny):
            got = swap(own, "col", k) if k else own
            parts += [got, swap(got, "batch", 1)]
        return assemble_weight(where, parts, ny, nb)

    def halves(values):
        values = values.reshape(nh, part, -1)
        return pick(values, x, 0), pick(values, 1 - x, 0)

    def gather_block(values):
        own, other = halves(values)
        two = swap(own, "row", 2)
        one = swap(jnp.concatenate([own, two]), "row", 1)
        mirror = swap(two, "head", 1)
        mirror_one = swap(one, "head", 1)
        return jnp.concatenate([own, two, one, other, mirror, mirror_one])

    def gather_tokens(own, *others):
        two = swap(own, "row", 2)
        pair = jnp.concatenate([own, two])
        one = swap(pair, "row", 1)
        pair = after(pair, *others)
        mirror = swap(pair, "head", 1)
        mirror_one = swap(one, "head", 1)
        return jnp.concatenate([pair, one, mirror, mirror_one])

    quarter = tokens // 4

    def reduce_far(*terms):
        far = sum(matmul_t(values[tokens // 2 :], weight) for values, weight in terms)
        far = far.astype(bf16)
        return swap(far[quarter:], "head", 1), swap(far[:quarter], "head", 1)

    def reduce_near(got, *terms):
        near = sum(matmul_t(values[: tokens // 2], weight) for values, weight in terms)
        send = (near[quarter:] + got[0].astype(f32)).astype(bf16)
        return send, near[:quarter] + got[1].astype(f32)

    def reduce_rows(send, keep):
        keep = keep + swap(send, "row", 1).astype(f32)
        last = swap(keep[part:].astype(bf16), "row", 2)
        return keep[:part] + last.astype(f32)

    def row_groups(values):
        values = values.reshape(tokens, nz, ny, nb, rows)
        groups = []
        for ky in range(ny):
            at = pick(values, y ^ ky, 2)
            groups.append([pick(at, b ^ kb, 2).reshape(tokens, nz * rows) for kb in range(nb)])
        return groups

    def grad_batch(groups, other):
        far = jnp.concatenate([g[1] for g in groups], axis=1)
        got = swap(outer_sum(far, other).astype(bf16), "batch", 1)
        got = got.reshape(ny, nz * rows, -1)
        return [outer_sum(g[0], other) + got[ky].astype(f32) for ky, g in enumerate(groups)]

    def grad_col(sums):
        total = sums[0]
        for k in range(1, ny):
            total = total + swap(sums[k].astype(bf16), "col", k).astype(f32)
        return total.reshape(nz, rows, -1)

    def grad_row(total, widths):
        pieces = [swap(pick(total, z ^ k, 0).astype(bf16), "row", k) for k in range(1, nz)]
        return unpack_grads(where, pick(total, z, 0), pieces, widths)

    params = jnp.stack([ln1_gain, ln1_bias, ln2_gain, ln2_bias]).astype(f32)
    small = jnp.concatenate([params.reshape(-1), log_decay.reshape(-1)])
    small = gather_small(small, ("row", "col", "batch"))
    params = small[:, : 4 * rows].reshape(nz * ny * nb, 4, rows)
    gain_one, bias_one, gain_two, bias_two = params.transpose(1, 0, 2).reshape(4, width)
    decay = pick(pick(small[:, 4 * rows :].reshape(nz * ny, nb, nz, block), b, 1), z, 1)
    running = jnp.cumsum(decay, axis=-1)
    c_row, c_col = running[:, None, :], running[:, :, None]

    kv_pieces = to_heads(pack_weights(where, (w_key, w_value), nz))
    hidden_all = gather_block(hidden_in[0])
    kv_w = spread(kv_pieces)
    qg_own = after((w_query, w_gate), kv_pieces)
    qg_pieces = to_heads(pack_weights(where, qg_own, nz))
    qg_w = spread(qg_pieces)

    half_dim = DK // 2
    freqs = 10000.0 ** (-jnp.arange(half_dim, dtype=f32) / half_dim)
    block_at = (jnp.array(ORDER) ^ z) * ny + y
    half_at = jnp.arange(nh) ^ x
    positions = (
        block_at[None, :, None] * block + half_at[:, None, None] * part + jnp.arange(part)
    )
    angles = positions.astype(f32).reshape(-1)[:, None] * freqs[None, :]
    cosines, sines = jnp.cos(angles), jnp.sin(angles)
    key_scale = DK ** (-0.5)

    scaled_one, _ = normalize(hidden_all.astype(f32))
    first_bf = (scaled_one * gain_one + bias_one).astype(bf16)
    key_value = matmul(first_bf, kv_w)
    key_bf = (rotate(key_value[:, :DK], cosines, sines) * key_scale).astype(bf16)
    value_bf = key_value[:, DK:].astype(bf16)

    def split(values):
        return values.reshape(nh, nz, part, -1)

    def gather_col(values):
        return jnp.stack([values] + [swap(values, "col", k) for k in range(1, ny)])

    keyval = split(jnp.concatenate([key_bf, value_bf], axis=-1))
    keyvals = gather_col(keyval)

    out_t = after(w_out, keyval, qg_pieces).T
    out_pieces = to_heads(pack_weights(where, (out_t,), nz))
    out_w = spread(out_pieces)
    down_bf = gather_block(after(out_grad[0], out_pieces))
    mlp_own = after((mlp_gate, mlp_up, mlp_down), out_pieces, keyvals)
    mlp_pieces = to_heads(pack_weights(where, (mlp_own[0], mlp_own[1], mlp_own[2].T), nz))
    mlp_w = spread(mlp_pieces)
    units = mlp_w.shape[1] // 3
    up_w, down_w = mlp_w[:, : 2 * units], mlp_w[:, 2 * units :]

    query_gate = matmul(first_bf, qg_w)
    query_bf = rotate(query_gate[:, :DK], cosines, sines).astype(bf16)
    gate = query_gate[:, DK:]

    mixed, retained, states = retention_forward(
        where, c_row, c_col, keyvals, split(query_bf), split(gate)
    )
    mixed_bf = mixed.reshape(tokens, DV)
    queries = gather_col(after(split(query_bf), keyvals))

    inputs = halves(hidden_in[0])[0].astype(f32)
    got = reduce_far((mixed_bf, out_w))
    middle = inputs + reduce_rows(*reduce_near(got, (mixed_bf, out_w)))
    middle, queries = lax.optimization_barrier((middle, queries))
    scaled_two, rstd_two = normalize(middle)
    second_bf = gather_tokens((scaled_two * gain_two + bias_two).astype(bf16))
    up = matmul(second_bf, up_w)
    up_gate, up_lin = up[:, :units], up[:, units:]
    gelu_val, gelu_pull = jax.vjp(lambda v: jax.nn.gelu(v, approximate=False), up_gate)
    hidden_bf = (gelu_val * up_lin).astype(bf16)

    grad_hidden = matmul(down_bf, down_w)
    grad_upgate = gelu_pull(grad_hidden * up_lin)[0].astype(bf16)
    grad_uplin = (grad_hidden * gelu_val).astype(bf16)
    grad_up = jnp.concatenate([grad_upgate, grad_uplin], axis=-1)
    got = reduce_far((grad_up, up_w))
    grad_two = reduce_rows(*reduce_near(got, (grad_up, up_w)))
    cotangent = halves(out_grad[0])[0].astype(f32)
    grad_middle = cotangent + norm_back(grad_two * gain_two, scaled_two, rstd_two)

    grad_up_late, hidden_late = after((grad_up, hidden_bf), got)
    up_sums = grad_batch(row_groups(second_bf), grad_up_late)
    down_sums = grad_batch(row_groups(down_bf), hidden_late)
    up_sum, down_sum = grad_col(up_sums), grad_col(down_sums)
    down_got = reduce_far((hidden_late, down_w))
    down_send, down_keep = reduce_near(down_got, (hidden_late, down_w))

    attn_bf = gather_tokens(grad_middle.astype(bf16), down_got)
    attn_bf, up_sum, down_sum, down_send = lax.optimization_barrier(
        (attn_bf, up_sum, down_sum, down_send)
    )

    grp_norm, grp_rstd = normalize(retained.reshape(tokens, DV))
    gate_sig = jax.nn.sigmoid(gate)
    gate_act = gate * gate_sig
    grad_mixed = matmul(attn_bf, out_w)
    grad_gate = (grad_mixed * grp_norm * (gate_sig * (1.0 + gate * (1.0 - gate_sig)))).astype(bf16)
    ret_bf = norm_back(grad_mixed * gate_act, grp_norm, grp_rstd).astype(bf16)
    ret_all = gather_col(split(ret_bf))

    result = (middle + reduce_rows(down_send, down_keep)).astype(bf16)
    result_other = swap(result, "head", 1)
    grad_gates, grad_ups = grad_row(up_sum, (units, units))
    (grad_downs,) = grad_row(down_sum, (units,))
    first_groups = row_groups(first_bf)
    attn_late, gate_late = after((attn_bf, grad_gate), ret_bf)
    gate_sums = grad_batch(first_groups, gate_late)
    out_sums = grad_batch(row_groups(attn_late), mixed_bf)

    grad_kvq = retention_backward(
        where, c_row, c_col, keyval, queries, ret_all, states, split(cosines), split(sines)
    )
    grad_kvq = grad_kvq.reshape(tokens, -1)
    grad_qg = jnp.concatenate([grad_kvq[:, DK + DV :], grad_gate], axis=-1)
    terms = ((grad_kvq[:, : DK + DV], kv_w), (grad_qg, qg_w))
    got = reduce_far(*terms)
    kvq_sums = grad_batch(first_groups, grad_kvq)
    both_sums = [jnp.concatenate(pair, axis=-1) for pair in zip(gate_sums, out_sums)]
    both_sums = after(both_sums, ret_all)
    both_sum = grad_col(both_sums)
    send, keep = reduce_near(got, *terms)
    send, both_sum, result_other, grad_gates, grad_ups, grad_downs = lax.optimization_barrier(
        (send, both_sum, result_other, grad_gates, grad_ups, grad_downs)
    )
    grad_one = reduce_rows(send, keep)
    grad_g, grad_outs = grad_row(both_sum, (DV, DV))
    kvq_sum = grad_col(kvq_sums)
    grad_one, kvq_sum = lax.optimization_barrier((grad_one, kvq_sum))
    grad_k, grad_v, grad_q = grad_row(kvq_sum, (DK, DV, DK))

    scaled_own, rstd_own = normalize(inputs)
    grad_in = grad_middle + norm_back(grad_one * gain_one, scaled_own, rstd_own)
    grad_in_other = swap(grad_in, "head", 1)

    def join(own, other):
        first = jnp.where(x == 0, own, other)
        second = jnp.where(x == 0, other, own)
        return jnp.concatenate([first, second]).reshape(1, block, width)

    norm_sums = jnp.stack(
        [
            jnp.sum(grad_one * scaled_own, axis=0),
            jnp.sum(grad_one, axis=0),
            jnp.sum(grad_two * scaled_two, axis=0),
            jnp.sum(grad_two, axis=0),
        ]
    )
    norm_sums = norm_sums + swap(norm_sums, "head", 1)
    norm_sums = norm_sums.reshape(4, nz, ny, nb, rows)
    for name, axis in (("batch", 3), ("col", 2), ("row", 1)):
        me = lax.axis_index(name)
        summed = pick(norm_sums, me, axis)
        for k in range(1, lax.axis_size(name)):
            summed = summed + swap(pick(norm_sums, me ^ k, axis), name, k)
        norm_sums = summed

    return (
        join(result, result_other),
        join(grad_in, grad_in_other),
        norm_sums[0],
        norm_sums[1],
        grad_q,
        grad_k,
        grad_v,
        grad_g,
        grad_outs.T,
        norm_sums[2],
        norm_sums[3],
        grad_gates,
        grad_ups,
        grad_downs.T,
    )


def solution(mesh):
    seq = ("row", "col")
    tokens = P("batch", seq, None)
    params = P((*seq, "batch"))
    by_rows = P((*seq, "batch"), "head")
    by_cols = P("head", (*seq, "batch"))

    def run(*arrays):
        rows = arrays[1].shape[1] // mesh.shape["head"]
        sizes = (rows, mesh.shape["seq"] // rows, mesh.shape["batch"], mesh.shape["head"])
        order = [mesh.axis_names.index(n) for n in ("seq", "batch", "head")]
        fine = Mesh(
            mesh.devices.transpose(order).reshape(sizes), ("row", "col", "batch", "head")
        )
        weights = (by_rows, by_rows, by_rows, by_rows, by_cols)
        feeds = (by_rows, by_rows, by_cols)
        return jax.shard_map(
            shards,
            mesh=fine,
            in_specs=(
                tokens,
                P("batch", "head", seq),
                tokens,
                params,
                params,
                *weights,
                params,
                params,
                *feeds,
            ),
            out_specs=(tokens, tokens, params, params, *weights, params, params, *feeds),
            check_vma=False,
        )(*arrays)

    return run
```

```python
import jax
import jax.numpy as jnp
from jax import lax
from jax.experimental import pallas as pl
from jax.experimental.pallas import tpu as pltpu
from jax.sharding import Mesh
from jax.sharding import PartitionSpec as P

DK = 256
DV = 512

epsilon = 1e-05
f32 = jnp.float32
bf16 = jnp.bfloat16
VMEM_LIMIT = 32 * 1024 * 1024

ORDER = (0, 2, 1, 3)


def swap(values, axis, k):
    count = lax.axis_size(axis)
    return lax.ppermute(values, axis, [(i, i ^ k) for i in range(count)])


def pick(values, index, axis):
    return lax.dynamic_index_in_dim(values, index, axis, keepdims=False)


def tie(*values):
    return lax.optimization_barrier(values)


def after(values, *others):
    return tie(values, others)[0]


def gather_small(values, names):
    values = values[None]
    for name in reversed(names):
        bit = 1
        while bit < lax.axis_size(name):
            other = swap(values, name, bit)
            low = (lax.axis_index(name) & bit) == 0
            values = jnp.where(
                low, jnp.concatenate([values, other]), jnp.concatenate([other, values])
            )
            bit *= 2
    return values


def matmul(values, weight):
    return jnp.dot(values, weight, preferred_element_type=f32)


def matmul_t(values, weight):
    return lax.dot_general(values, weight, (((1,), (1,)), ((), ())), preferred_element_type=f32)


def outer_sum(values, other):
    return lax.dot_general(values, other, (((0,), (0,)), ((), ())), preferred_element_type=f32)


def normalize(values):
    center = values - jnp.mean(values, axis=-1, keepdims=True)
    rstd = lax.rsqrt(jnp.mean(center * center, axis=-1, keepdims=True) + epsilon)
    return center * rstd, rstd


def norm_back(scaled_grad, scaled, rstd):
    return rstd * (
        scaled_grad
        - jnp.mean(scaled_grad, axis=-1, keepdims=True)
        - scaled * jnp.mean(scaled_grad * scaled, axis=-1, keepdims=True)
    )


def rotate(values, cosines, sines):
    half_dim = values.shape[-1] // 2
    first_half = values[..., :half_dim]
    second_half = values[..., half_dim:]
    return jnp.concatenate(
        [first_half * cosines - second_half * sines, first_half * sines + second_half * cosines],
        axis=-1,
    )


SMEM = pl.BlockSpec(memory_space=pltpu.SMEM)
WHOLE = pl.BlockSpec(memory_space=pltpu.VMEM)
PARAMS = pltpu.CompilerParams(vmem_limit_bytes=VMEM_LIMIT)


def pack_weights(where, weights, nz):
    rows = weights[0].shape[0]
    widths = [w.shape[1] // nz for w in weights]

    def kernel(where_ref, *refs):
        ins, outs = refs[: len(weights)], refs[len(weights) :]
        for k in range(nz):
            target = where_ref[0] ^ k
            at = 0
            for ref, width in zip(ins, widths):
                start = pl.multiple_of(target * width, width)
                outs[k][:, at : at + width] = ref[:, pl.ds(start, width)]
                at += width

    return pl.pallas_call(
        kernel,
        out_shape=[jax.ShapeDtypeStruct((rows, sum(widths)), bf16)] * nz,
        in_specs=[SMEM] + [WHOLE] * len(weights),
        out_specs=[WHOLE] * nz,
        compiler_params=PARAMS,
        name="pack_weights",
    )(where, *weights)


def unpack_grads(where, own, pieces, widths):
    nz = len(pieces) + 1
    rows = own.shape[0]

    def kernel(where_ref, *refs):
        ins, outs = refs[:nz], refs[nz:]
        for k in range(nz):
            target = where_ref[0] ^ k
            at = 0
            for ref, width in zip(outs, widths):
                start = pl.multiple_of(target * width, width)
                ref[:, pl.ds(start, width)] = ins[k][:, at : at + width].astype(f32)
                at += width

    return pl.pallas_call(
        kernel,
        out_shape=[jax.ShapeDtypeStruct((rows, nz * width), f32) for width in widths],
        in_specs=[SMEM] + [WHOLE] * nz,
        out_specs=[WHOLE] * len(widths),
        compiler_params=PARAMS,
        name="unpack_grads",
    )(where, own, *pieces)


def assemble_weight(where, parts, ny, nb):
    nz, rows, cols = parts[0].shape

    def kernel(where_ref, *refs):
        ins, out = refs[:-1], refs[-1]
        for ky in range(ny):
            for kb in range(nb):
                for kz in range(nz):
                    at = ((where_ref[0] ^ kz) * ny + (where_ref[1] ^ ky)) * nb
                    at = pl.multiple_of((at + (where_ref[2] ^ kb)) * rows, rows)
                    out[pl.ds(at, rows), :] = ins[ky * nb + kb][kz]

    return pl.pallas_call(
        kernel,
        out_shape=jax.ShapeDtypeStruct((nz * ny * nb * rows, cols), bf16),
        in_specs=[SMEM] + [WHOLE] * len(parts),
        out_specs=WHOLE,
        compiler_params=PARAMS,
        name="assemble_weight",
    )(where, *parts)


def place_rows(where, pieces, sizes, norm=None):
    nz, ny, nb = sizes
    width = pieces[0].shape[1]
    tokens = sum(piece.shape[0] for piece in pieces)
    rows = width // (nz * ny * nb)
    aligned = rows % 128 == 0
    norm = list(norm or ())

    def kernel(where_ref, *refs):
        ins, rest = refs[: len(pieces)], refs[len(pieces) :]
        params, outs = rest[: len(norm)], rest[len(norm) :]
        full = outs[0]
        at = 0
        for ref in ins:
            count = ref.shape[0]
            values = ref[...]
            if norm:
                values, _ = normalize(values.astype(f32))
                values = (values * params[0][...] + params[1][...]).astype(bf16)
            full[at : at + count, :] = values
            at += count
        if aligned:
            for kb in range(nb):
                for ky in range(ny):
                    for z in range(nz):
                        source = (z * ny + (where_ref[1] ^ ky)) * nb + (where_ref[2] ^ kb)
                        source = pl.multiple_of(source * rows, rows)
                        to = ((kb * ny + ky) * nz + z) * rows
                        outs[1][:, to : to + rows] = full[:, pl.ds(source, rows)]

    shape = jax.ShapeDtypeStruct((tokens, width), bf16)
    outs = pl.pallas_call(
        kernel,
        out_shape=[shape] * (2 if aligned else 1),
        in_specs=[SMEM] + [WHOLE] * (len(pieces) + len(norm)),
        out_specs=[WHOLE] * (2 if aligned else 1),
        compiler_params=PARAMS,
        name="place_rows",
    )(where, *pieces, *norm)
    if aligned:
        return outs
    groups = outs[0].reshape(tokens, nz, ny, nb, rows)
    groups = jnp.take(groups, jnp.arange(ny) ^ where[1], axis=2)
    groups = jnp.take(groups, jnp.arange(nb) ^ where[2], axis=3)
    return outs[0], groups.transpose(0, 3, 2, 1, 4).reshape(tokens, width)


def slot_of(k):
    return ((k & 1) << 1) | (k >> 1)


def natural(ref, lead, slot, flip, columns):
    first = ref[(*lead, flip, slot, slice(None), columns)]
    second = ref[(*lead, 1 - flip, slot, slice(None), columns)]
    return jnp.concatenate([first, second], axis=0)


def dot(left, right, dims):
    return lax.dot_general(left, right, (dims, ((), ())), preferred_element_type=f32)


NN, NT, TN = ((1,), (0,)), ((1,), (1,)), ((0,), (0,))


def decay_matrix(col, row):
    block = row.shape[-1]
    at = lax.broadcasted_iota(jnp.int32, (block, block), 0)
    to = lax.broadcasted_iota(jnp.int32, (block, block), 1)
    return jnp.where(at >= to, jnp.exp(jnp.minimum(col - row, 0.0)), 0.0)


def retention_forward(where, c_row, c_col, keyval, query, gate):
    ny, halves, nz, part, _ = keyval.shape
    block = halves * part

    def kernel(where_ref, row_ref, col_ref, kv_ref, q_ref, g_ref, y_ref, o_ref, s_ref, state):
        j = pl.program_id(0)

        @pl.when(j == 0)
        def _():
            state[...] = jnp.zeros_like(state)

        slot = slot_of((j // ny) ^ where_ref[0])
        ky = (j % ny) ^ where_ref[1]
        flip = where_ref[3]
        row, col = row_ref[j], col_ref[j]
        key = natural(kv_ref, (ky,), slot, flip, slice(0, DK))
        value = natural(kv_ref, (ky,), slot, flip, slice(DK, DK + DV))
        last = row[:, block - 1 :]

        @pl.when(ky == 0)
        def _():
            q = natural(q_ref, (), slot, flip, slice(None))
            state_bf = state[...].astype(bf16)
            s_ref[slot] = state_bf
            weights = (dot(q, key, NT) * decay_matrix(col, row)).astype(bf16)
            out = dot(weights, value, NN) + jnp.exp(col) * dot(q, state_bf, NN)
            normed, _ = normalize(out)
            g = natural(g_ref, (), slot, flip, slice(None))
            mixed = (g * jax.nn.sigmoid(g) * normed).astype(bf16)
            for half in range(2):
                rows = slice(half * part, (half + 1) * part)
                to = (1 - flip) if half else flip
                y_ref[to, slot] = mixed[rows]
                o_ref[to, slot] = out[rows]

        key_tail = (key.astype(f32) * jnp.exp(last - col)).astype(bf16)
        state[...] = jnp.exp(last) * state[...] + dot(key_tail, value, TN)

    return pl.pallas_call(
        kernel,
        grid=(nz * ny,),
        out_shape=[
            jax.ShapeDtypeStruct((halves, nz, part, DV), bf16),
            jax.ShapeDtypeStruct((halves, nz, part, DV), f32),
            jax.ShapeDtypeStruct((nz, DK, DV), bf16),
        ],
        in_specs=[SMEM] + [WHOLE] * 5,
        out_specs=[WHOLE] * 3,
        scratch_shapes=[pltpu.VMEM((DK, DV), f32)],
        compiler_params=PARAMS,
        name="retention_forward",
    )(where, c_row, c_col, keyval, query, gate)


def retention_backward(where, c_row, c_col, keyval, queries, grads, states, cosines, sines):
    ny, halves, nz, part, _ = queries.shape
    block = halves * part
    key_scale = DK ** (-0.5)

    def kernel(
        where_ref, row_ref, col_ref, kv_ref, q_ref, d_ref, s_ref, cos_ref, sin_ref, g_ref, state
    ):
        step = pl.program_id(0)
        j = nz * ny - 1 - step

        @pl.when(step == 0)
        def _():
            state[...] = jnp.zeros_like(state)

        slot = slot_of((j // ny) ^ where_ref[0])
        ky = (j % ny) ^ where_ref[1]
        flip = where_ref[3]
        row, col = row_ref[j], col_ref[j]
        last = row[:, block - 1 :]
        q = natural(q_ref, (ky,), slot, flip, slice(None))
        grad = natural(d_ref, (ky,), slot, flip, slice(None))
        entry = jnp.exp(col)

        @pl.when(ky == 0)
        def _():
            key = natural(kv_ref, (), slot, flip, slice(0, DK))
            value = natural(kv_ref, (), slot, flip, slice(DK, DK + DV))
            cos = natural(cos_ref, (), slot, flip, slice(None))
            sin = natural(sin_ref, (), slot, flip, slice(None))
            decays = decay_matrix(col, row)
            tail = jnp.exp(last - col)
            state_bf = state[...].astype(bf16)
            weights = (dot(q, key, NT) * decays).astype(bf16)
            scores = (dot(grad, value, NT) * decays).astype(bf16)
            grad_q = dot(scores, key, NN) + entry * dot(grad, s_ref[slot], NT)
            grad_k = dot(scores, q, TN) + tail * dot(value, state_bf, NT)
            grad_v = dot(weights, grad, TN) + tail * dot(key, state_bf, NN)
            grad_q = rotate(grad_q, cos, -sin).astype(bf16)
            grad_k = (rotate(grad_k, cos, -sin) * key_scale).astype(bf16)
            grad_v = grad_v.astype(bf16)
            for half in range(2):
                rows = slice(half * part, (half + 1) * part)
                to = (1 - flip) if half else flip
                g_ref[to, slot, :, :DK] = grad_k[rows]
                g_ref[to, slot, :, DK : DK + DV] = grad_v[rows]
                g_ref[to, slot, :, DK + DV :] = grad_q[rows]

        query_entry = (q.astype(f32) * entry).astype(bf16)
        state[...] = jnp.exp(last) * state[...] + dot(query_entry, grad, TN)

    return pl.pallas_call(
        kernel,
        grid=(nz * ny,),
        out_shape=jax.ShapeDtypeStruct((halves, nz, part, 2 * DK + DV), bf16),
        in_specs=[SMEM] + [WHOLE] * 8,
        out_specs=WHOLE,
        scratch_shapes=[pltpu.VMEM((DK, DV), f32)],
        compiler_params=PARAMS,
        name="retention_backward",
    )(where, c_row, c_col, keyval, queries, grads, states, cosines, sines)


def shards(
    hidden_in,
    log_decay,
    out_grad,
    ln1_gain,
    ln1_bias,
    w_query,
    w_key,
    w_value,
    w_gate,
    w_out,
    ln2_gain,
    ln2_bias,
    mlp_gate,
    mlp_up,
    mlp_down,
):
    nz, ny = lax.axis_size("row"), lax.axis_size("col")
    nb, nh = lax.axis_size("batch"), lax.axis_size("head")
    z, y = lax.axis_index("row"), lax.axis_index("col")
    b, x = lax.axis_index("batch"), lax.axis_index("head")
    block, width = hidden_in.shape[1:]
    rows = ln1_gain.shape[0]
    part = block // nh
    tokens = nz * block
    where = jnp.stack([z, y, b, x]).astype(jnp.int32)

    sizes = (nz, ny, nb)

    def to_heads(pieces):
        return jnp.stack([pieces[0]] + [swap(pieces[k], "row", k) for k in range(1, nz)])

    def spread(own):
        parts = []
        for k in range(ny):
            got = swap(own, "col", k) if k else own
            parts += [got, swap(got, "batch", 1)]
        return assemble_weight(where, parts, ny, nb)

    def halves(values):
        values = values.reshape(nh, part, -1)
        return pick(values, x, 0), pick(values, 1 - x, 0)

    def gather_block(own):
        two = swap(own, "row", 2)
        one = swap(jnp.concatenate([own, two]), "row", 1)
        return two, one

    def gather_tokens(own):
        two = swap(own, "row", 2)
        pair = jnp.concatenate([own, two])
        return pair, swap(pair, "row", 1)

    def mirror(values):
        return swap(values, "head", 1)

    quarter = tokens // 4

    def reduce_far(*terms):
        far = sum(matmul_t(values[tokens // 2 :], weight) for values, weight in terms)
        far = far.astype(bf16)
        return mirror(far[quarter:]), mirror(far[:quarter])

    def reduce_near(got, *terms):
        near = sum(matmul_t(values[: tokens // 2], weight) for values, weight in terms)
        send = (near[quarter:] + got[0].astype(f32)).astype(bf16)
        return send, near[:quarter] + got[1].astype(f32)

    def reduce_one(send, keep):
        keep = keep + swap(send, "row", 1).astype(f32)
        return keep[part:].astype(bf16), keep[:part]

    def reduce_two(send, keep):
        return keep + swap(send, "row", 2).astype(f32)

    group = nz * rows

    def grad_far(grouped, other):
        return outer_sum(grouped[:, ny * group :], other).astype(bf16)

    def grad_near(grouped, other, got):
        near = outer_sum(grouped[:, : ny * group], other) + got.astype(f32)
        return near[:group], near[group:].astype(bf16)

    def grad_col(keep, send):
        for k in range(1, ny):
            piece = send[(k - 1) * group : k * group]
            keep = keep + swap(piece, "col", k).astype(f32)
        return keep.reshape(nz, rows, -1)

    def grad_row(total):
        own = pick(total, z, 0)
        return [own] + [swap(pick(total, z ^ k, 0).astype(bf16), "row", k) for k in range(1, nz)]

    def unpack(pieces, widths):
        return unpack_grads(where, pieces[0], pieces[1:], widths)

    params = jnp.stack([ln1_gain, ln1_bias, ln2_gain, ln2_bias]).astype(f32)
    small = jnp.concatenate([params.reshape(-1), log_decay.reshape(-1)])
    small = gather_small(small, ("row", "col", "batch"))
    params = small[:, : 4 * rows].reshape(nz * ny * nb, 4, rows)
    gain_one, bias_one, gain_two, bias_two = params.transpose(1, 0, 2).reshape(4, width)
    decay = pick(pick(small[:, 4 * rows :].reshape(nz * ny, nb, nz, block), b, 1), z, 1)
    running = jnp.cumsum(decay, axis=-1)
    c_row, c_col = running[:, None, :], running[:, :, None]

    kv_own = to_heads(pack_weights(where, (w_key, w_value), nz))
    own_in, other_in = halves(hidden_in[0])
    two_in, one_in = gather_block(own_in)
    kv_w = spread(kv_own)
    qg_packed = pack_weights(where, after((w_query, w_gate), kv_own), nz)
    qg_own = to_heads(qg_packed)
    qg_w = spread(qg_own)
    out_own = to_heads(pack_weights(where, (after(w_out, qg_own).T,), nz))
    out_w = spread(out_own)
    feed = after((mlp_gate, mlp_up, mlp_down), out_own)
    mlp_own = to_heads(pack_weights(where, (feed[0], feed[1], feed[2].T), nz))
    own_grad, other_grad = halves(out_grad[0])
    two_grad, one_grad = gather_block(after(own_grad, mlp_own))

    half_dim = DK // 2
    freqs = 10000.0 ** (-jnp.arange(half_dim, dtype=f32) / half_dim)
    block_at = (jnp.array(ORDER) ^ z) * ny + y
    half_at = jnp.arange(nh) ^ x
    positions = (
        block_at[None, :, None] * block + half_at[:, None, None] * part + jnp.arange(part)
    )
    angles = positions.astype(f32).reshape(-1)[:, None] * freqs[None, :]
    cosines, sines = jnp.cos(angles), jnp.sin(angles)
    key_scale = DK ** (-0.5)

    first_bf, first_groups = place_rows(
        where,
        (own_in, two_in, one_in, other_in, mirror(two_in), mirror(one_in)),
        sizes,
        (gain_one[None], bias_one[None]),
    )
    first_kv, kv_w, out_own = tie(first_bf, kv_w, out_own)
    key_value = matmul(first_kv, kv_w)
    key_bf = (rotate(key_value[:, :DK], cosines, sines) * key_scale).astype(bf16)
    value_bf = key_value[:, DK:].astype(bf16)

    def split(values):
        return values.reshape(nh, nz, part, -1)

    def gather_col(values):
        return jnp.stack([values] + [swap(values, "col", k) for k in range(1, ny)])

    keyval = split(jnp.concatenate([key_bf, value_bf], axis=-1))
    query_gate = matmul(after(first_bf, keyval), qg_w)
    query_bf = rotate(query_gate[:, :DK], cosines, sines).astype(bf16)
    gate = query_gate[:, DK:]

    keyvals, mlp_own, query_bf = tie(gather_col(keyval), mlp_own, query_bf)
    mlp_w = spread(mlp_own)
    units = mlp_w.shape[1] // 3
    up_w, down_w = mlp_w[:, : 2 * units], mlp_w[:, 2 * units :]
    mixed, retained, states = retention_forward(
        where, c_row, c_col, keyvals, split(query_bf), split(gate)
    )
    mixed_bf = mixed.reshape(tokens, DV)
    queries = gather_col(split(after(query_bf, mixed)))

    inputs = own_in.astype(f32)
    got = reduce_far((mixed_bf, out_w))
    send, keep = reduce_near(got, (mixed_bf, out_w))
    send, two_grad, one_grad = tie(send, two_grad, one_grad)
    mirror_grads = mirror(two_grad), mirror(one_grad)
    send, keep = reduce_one(send, keep)
    middle, queries = tie(inputs + reduce_two(send, keep), queries)
    scaled_two, rstd_two = normalize(middle)
    pair, one = gather_tokens((scaled_two * gain_two + bias_two).astype(bf16))
    pair, mirror_grads = tie(pair, mirror_grads)
    second_bf, second_groups = place_rows(where, (pair, one, mirror(pair), mirror(one)), sizes)
    down_bf, down_groups = place_rows(
        where, (own_grad, two_grad, one_grad, other_grad, *mirror_grads), sizes
    )
    up = matmul(second_bf, up_w)
    up_gate, up_lin = up[:, :units], up[:, units:]
    gelu_val, gelu_pull = jax.vjp(lambda v: jax.nn.gelu(v, approximate=False), up_gate)
    hidden_bf = (gelu_val * up_lin).astype(bf16)

    grad_hidden = matmul(down_bf, down_w)
    grad_upgate = gelu_pull(grad_hidden * up_lin)[0].astype(bf16)
    grad_uplin = (grad_hidden * gelu_val).astype(bf16)
    grad_up = jnp.concatenate([grad_upgate, grad_uplin], axis=-1)
    got = reduce_far((grad_up, up_w))
    up_far = grad_far(second_groups, grad_up)
    down_far = grad_far(down_groups, hidden_bf)
    send, keep = reduce_near(got, (grad_up, up_w))
    send, hidden_late, up_far, down_far = tie(send, hidden_bf, up_far, down_far)
    up_keep, up_send = grad_near(second_groups, grad_up, swap(up_far, "batch", 1))
    down_keep, down_send = grad_near(down_groups, hidden_late, swap(down_far, "batch", 1))
    result_got = reduce_far((hidden_late, down_w))
    send, keep = reduce_one(send, keep)
    send, up_send, down_send = tie(send, up_send, down_send)
    grad_two = reduce_two(send, keep)
    grad_middle = own_grad.astype(f32) + norm_back(grad_two * gain_two, scaled_two, rstd_two)
    pair, one = gather_tokens(grad_middle.astype(bf16))
    result_send, result_keep = reduce_near(result_got, (hidden_late, down_w))
    pair, result_send = tie(pair, result_send)
    attn_bf, attn_groups = place_rows(where, (pair, one, mirror(pair), mirror(one)), sizes)
    up_sum, down_sum = grad_col(up_keep, up_send), grad_col(down_keep, down_send)
    attn_bf, up_sum, down_sum, result_send = tie(attn_bf, up_sum, down_sum, result_send)

    grp_norm, grp_rstd = normalize(retained.reshape(tokens, DV))
    gate_sig = jax.nn.sigmoid(gate)
    gate_act = gate * gate_sig
    grad_mixed = matmul(attn_bf, out_w)
    grad_gate = (grad_mixed * grp_norm * (gate_sig * (1.0 + gate * (1.0 - gate_sig)))).astype(bf16)
    ret_bf = norm_back(grad_mixed * gate_act, grp_norm, grp_rstd).astype(bf16)
    ret_all = gather_col(split(ret_bf))

    up_sum, down_sum, late_gate = after((up_sum, down_sum, grad_gate), ret_bf)
    up_pieces, down_pieces = grad_row(up_sum), grad_row(down_sum)
    gate_far = grad_far(first_groups, late_gate)
    outs_far = grad_far(attn_groups, after(mixed_bf, ret_bf))
    gate_keep, gate_send = grad_near(first_groups, late_gate, swap(gate_far, "batch", 1))
    outs_keep, outs_send = grad_near(attn_groups, mixed_bf, swap(outs_far, "batch", 1))
    both_keep = jnp.concatenate([gate_keep, outs_keep], axis=-1)
    both_send = jnp.concatenate([gate_send, outs_send], axis=-1)
    result_send, result_keep = reduce_one(result_send, result_keep)
    ret_all, both_send, result_send = tie(ret_all, both_send, result_send)

    grad_kvq = retention_backward(
        where, c_row, c_col, keyval, queries, ret_all, states, split(cosines), split(sines)
    )
    grad_kvq = grad_kvq.reshape(tokens, -1)
    grad_qg = jnp.concatenate([grad_kvq[:, DK + DV :], grad_gate], axis=-1)
    terms = ((grad_kvq[:, : DK + DV], kv_w), (grad_qg, qg_w))
    got = reduce_far(*terms)
    kvq_far = grad_far(first_groups, grad_kvq)
    result = (middle + reduce_two(result_send, result_keep)).astype(bf16)
    send, keep = reduce_near(got, *terms)
    send, kvq_far, result, up_pieces, down_pieces = tie(
        send, kvq_far, result, up_pieces, down_pieces
    )
    kvq_keep, kvq_send = grad_near(first_groups, grad_kvq, swap(kvq_far, "batch", 1))
    both_sum = grad_col(both_keep, both_send)
    send, keep = reduce_one(send, keep)
    send, kvq_send, both_sum = tie(send, kvq_send, both_sum)
    grad_one = reduce_two(send, keep)
    both_pieces = grad_row(both_sum)
    kvq_sum = grad_col(kvq_keep, kvq_send)
    grad_one, both_pieces, kvq_sum = tie(grad_one, both_pieces, kvq_sum)
    kvq_pieces = grad_row(kvq_sum)

    scaled_own, rstd_own = normalize(inputs)
    grad_in = grad_middle + norm_back(grad_one * gain_one, scaled_own, rstd_own)
    grad_in_other = mirror(grad_in)
    result_other = mirror(result)
    grad_gates, grad_ups = unpack(up_pieces, (units, units))
    (grad_downs,) = unpack(down_pieces, (units,))
    grad_g, grad_outs = unpack(both_pieces, (DV, DV))
    grad_k, grad_v, grad_q = unpack(kvq_pieces, (DK, DV, DK))

    def join(own, other):
        first = jnp.where(x == 0, own, other)
        second = jnp.where(x == 0, other, own)
        return jnp.concatenate([first, second]).reshape(1, block, width)

    norm_sums = jnp.stack(
        [
            jnp.sum(grad_one * scaled_own, axis=0),
            jnp.sum(grad_one, axis=0),
            jnp.sum(grad_two * scaled_two, axis=0),
            jnp.sum(grad_two, axis=0),
        ]
    )
    norm_sums = norm_sums + swap(norm_sums, "head", 1)
    norm_sums = norm_sums.reshape(4, nz, ny, nb, rows)
    for name, axis in (("batch", 3), ("col", 2), ("row", 1)):
        me = lax.axis_index(name)
        summed = pick(norm_sums, me, axis)
        for k in range(1, lax.axis_size(name)):
            summed = summed + swap(pick(norm_sums, me ^ k, axis), name, k)
        norm_sums = summed

    return (
        join(result, result_other),
        join(grad_in, grad_in_other),
        norm_sums[0],
        norm_sums[1],
        grad_q,
        grad_k,
        grad_v,
        grad_g,
        grad_outs.T,
        norm_sums[2],
        norm_sums[3],
        grad_gates,
        grad_ups,
        grad_downs.T,
    )


def solution(mesh):
    seq = ("row", "col")
    tokens = P("batch", seq, None)
    params = P((*seq, "batch"))
    by_rows = P((*seq, "batch"), "head")
    by_cols = P("head", (*seq, "batch"))

    def run(*arrays):
        rows = arrays[1].shape[1] // mesh.shape["head"]
        sizes = (rows, mesh.shape["seq"] // rows, mesh.shape["batch"], mesh.shape["head"])
        order = [mesh.axis_names.index(n) for n in ("seq", "batch", "head")]
        fine = Mesh(
            mesh.devices.transpose(order).reshape(sizes), ("row", "col", "batch", "head")
        )
        weights = (by_rows, by_rows, by_rows, by_rows, by_cols)
        feeds = (by_rows, by_rows, by_cols)
        return jax.shard_map(
            shards,
            mesh=fine,
            in_specs=(
                tokens,
                P("batch", "head", seq),
                tokens,
                params,
                params,
                *weights,
                params,
                params,
                *feeds,
            ),
            out_specs=(tokens, tokens, params, params, *weights, params, params, *feeds),
            check_vma=False,
        )(*arrays)

    return run
```

```python
import jax
import jax.numpy as jnp
from jax import lax
from jax.experimental import pallas as pl
from jax.experimental.pallas import tpu as pltpu
from jax.sharding import Mesh
from jax.sharding import PartitionSpec as P

DK = 256
DV = 512

epsilon = 1e-05
f32 = jnp.float32
bf16 = jnp.bfloat16
VMEM_LIMIT = 32 * 1024 * 1024

ORDER = (0, 2, 1, 3)


def swap(values, axis, k):
    count = lax.axis_size(axis)
    return lax.ppermute(values, axis, [(i, i ^ k) for i in range(count)])


def pick(values, index, axis):
    return lax.dynamic_index_in_dim(values, index, axis, keepdims=False)


def tie(*values):
    return lax.optimization_barrier(values)


def after(values, *others):
    return tie(values, others)[0]


def gather_small(values, names):
    values = values[None]
    for name in reversed(names):
        bit = 1
        while bit < lax.axis_size(name):
            other = swap(values, name, bit)
            low = (lax.axis_index(name) & bit) == 0
            values = jnp.where(
                low, jnp.concatenate([values, other]), jnp.concatenate([other, values])
            )
            bit *= 2
    return values


def matmul(values, weight):
    return jnp.dot(values, weight, preferred_element_type=f32)


def matmul_t(values, weight):
    return lax.dot_general(values, weight, (((1,), (1,)), ((), ())), preferred_element_type=f32)


def outer_sum(values, other):
    return lax.dot_general(values, other, (((0,), (0,)), ((), ())), preferred_element_type=f32)


def normalize(values):
    center = values - jnp.mean(values, axis=-1, keepdims=True)
    rstd = lax.rsqrt(jnp.mean(center * center, axis=-1, keepdims=True) + epsilon)
    return center * rstd, rstd


def norm_back(scaled_grad, scaled, rstd):
    return rstd * (
        scaled_grad
        - jnp.mean(scaled_grad, axis=-1, keepdims=True)
        - scaled * jnp.mean(scaled_grad * scaled, axis=-1, keepdims=True)
    )


def rotate(values, cosines, sines):
    half_dim = values.shape[-1] // 2
    first_half = values[..., :half_dim]
    second_half = values[..., half_dim:]
    return jnp.concatenate(
        [first_half * cosines - second_half * sines, first_half * sines + second_half * cosines],
        axis=-1,
    )


SMEM = pl.BlockSpec(memory_space=pltpu.SMEM)
WHOLE = pl.BlockSpec(memory_space=pltpu.VMEM)
PARAMS = pltpu.CompilerParams(vmem_limit_bytes=VMEM_LIMIT)


def pack_weights(where, weights, nz):
    rows = weights[0].shape[0]
    widths = [w.shape[1] // nz for w in weights]

    def kernel(where_ref, *refs):
        ins, outs = refs[: len(weights)], refs[len(weights) :]
        for k in range(nz):
            target = where_ref[0] ^ k
            at = 0
            for ref, width in zip(ins, widths):
                start = pl.multiple_of(target * width, width)
                outs[k][:, at : at + width] = ref[:, pl.ds(start, width)]
                at += width

    return pl.pallas_call(
        kernel,
        out_shape=[jax.ShapeDtypeStruct((rows, sum(widths)), bf16)] * nz,
        in_specs=[SMEM] + [WHOLE] * len(weights),
        out_specs=[WHOLE] * nz,
        compiler_params=PARAMS,
        name="pack_weights",
    )(where, *weights)


def unpack_grads(where, own, pieces, widths):
    nz = len(pieces) + 1
    rows = own.shape[0]

    def kernel(where_ref, *refs):
        ins, outs = refs[:nz], refs[nz:]
        for k in range(nz):
            target = where_ref[0] ^ k
            at = 0
            for ref, width in zip(outs, widths):
                start = pl.multiple_of(target * width, width)
                ref[:, pl.ds(start, width)] = ins[k][:, at : at + width].astype(f32)
                at += width

    return pl.pallas_call(
        kernel,
        out_shape=[jax.ShapeDtypeStruct((rows, nz * width), f32) for width in widths],
        in_specs=[SMEM] + [WHOLE] * nz,
        out_specs=[WHOLE] * len(widths),
        compiler_params=PARAMS,
        name="unpack_grads",
    )(where, own, *pieces)


def assemble_weight(where, parts):
    ny, nb, nz, rows, cols = parts.shape

    def kernel(where_ref, ref, out):
        for y in range(ny):
            for b in range(nb):
                for kz in range(nz):
                    at = ((where_ref[0] ^ kz) * ny + y) * nb + b
                    out[pl.ds(pl.multiple_of(at * rows, rows), rows), :] = ref[y, b, kz]

    return pl.pallas_call(
        kernel,
        out_shape=jax.ShapeDtypeStruct((nz * ny * nb * rows, cols), bf16),
        in_specs=[SMEM, WHOLE],
        out_specs=WHOLE,
        compiler_params=PARAMS,
        name="assemble_weight",
    )(where, parts)


def assemble_pieces(where, parts, ny, nb):
    nz, rows, cols = parts[0].shape

    def kernel(where_ref, *refs):
        ins, out = refs[:-1], refs[-1]
        for ky in range(ny):
            for kb in range(nb):
                for kz in range(nz):
                    at = ((where_ref[0] ^ kz) * ny + (where_ref[1] ^ ky)) * nb
                    at = pl.multiple_of((at + (where_ref[2] ^ kb)) * rows, rows)
                    out[pl.ds(at, rows), :] = ins[ky * nb + kb][kz]

    return pl.pallas_call(
        kernel,
        out_shape=jax.ShapeDtypeStruct((nz * ny * nb * rows, cols), bf16),
        in_specs=[SMEM] + [WHOLE] * len(parts),
        out_specs=WHOLE,
        compiler_params=PARAMS,
        name="assemble_pieces",
    )(where, *parts)


def place_rows(where, pieces, sizes, norm=None, near=False):
    nz, ny, nb = sizes
    width = pieces[0].shape[1]
    tokens = sum(piece.shape[0] for piece in pieces)
    rows = width // (nz * ny * nb)
    aligned = rows % 128 == 0
    norm = list(norm or ())
    count = 1 + (1 + near) * aligned

    def kernel(where_ref, *refs):
        ins, rest = refs[: len(pieces)], refs[len(pieces) :]
        params, outs = rest[: len(norm)], rest[len(norm) :]
        full = outs[0]
        at = 0
        for ref in ins:
            values = ref[...]
            if norm:
                values, _ = normalize(values.astype(f32))
                values = (values * params[0][...] + params[1][...]).astype(bf16)
            full[at : at + ref.shape[0], :] = values
            at += ref.shape[0]
        for z in range(nz):
            for y in range(ny):
                for b in range(nb):
                    if count > 1:
                        source = ((z * ny + y) * nb + b) * rows
                        to = ((y * nb + b) * nz + z) * rows
                        outs[1][:, to : to + rows] = full[:, source : source + rows]
                    if count > 2:
                        source = (z * ny + (where_ref[1] ^ y)) * nb + (where_ref[2] ^ b)
                        source = pl.multiple_of(source * rows, rows)
                        to = ((b * ny + y) * nz + z) * rows
                        outs[2][:, to : to + rows] = full[:, pl.ds(source, rows)]

    outs = pl.pallas_call(
        kernel,
        out_shape=[jax.ShapeDtypeStruct((tokens, width), bf16)] * count,
        in_specs=[SMEM] + [WHOLE] * (len(pieces) + len(norm)),
        out_specs=[WHOLE] * count,
        compiler_params=PARAMS,
        name="place_rows",
    )(where, *pieces, *norm)
    if aligned:
        return outs
    groups = outs[0].reshape(tokens, nz, ny, nb, rows)
    outs = [outs[0], groups.transpose(0, 2, 3, 1, 4).reshape(tokens, width)]
    if near:
        groups = jnp.take(groups, jnp.arange(ny) ^ where[1], axis=2)
        groups = jnp.take(groups, jnp.arange(nb) ^ where[2], axis=3)
        outs.append(groups.transpose(0, 3, 2, 1, 4).reshape(tokens, width))
    return outs


def slot_of(k):
    return ((k & 1) << 1) | (k >> 1)


def natural(ref, lead, slot, flip, columns):
    first = ref[(*lead, flip, slot, slice(None), columns)]
    second = ref[(*lead, 1 - flip, slot, slice(None), columns)]
    return jnp.concatenate([first, second], axis=0)


def dot(left, right, dims):
    return lax.dot_general(left, right, (dims, ((), ())), preferred_element_type=f32)


NN, NT, TN = ((1,), (0,)), ((1,), (1,)), ((0,), (0,))


def decay_matrix(col, row):
    block = row.shape[-1]
    at = lax.broadcasted_iota(jnp.int32, (block, block), 0)
    to = lax.broadcasted_iota(jnp.int32, (block, block), 1)
    return jnp.where(at >= to, jnp.exp(jnp.minimum(col - row, 0.0)), 0.0)


def retention_forward(where, c_row, c_col, keyval, query, gate):
    ny, halves, nz, part, _ = keyval.shape
    block = halves * part

    def kernel(where_ref, row_ref, col_ref, kv_ref, q_ref, g_ref, y_ref, o_ref, s_ref, state):
        j = pl.program_id(0)

        @pl.when(j == 0)
        def _():
            state[...] = jnp.zeros_like(state)

        slot = slot_of((j // ny) ^ where_ref[0])
        ky = (j % ny) ^ where_ref[1]
        flip = where_ref[3]
        row, col = row_ref[j], col_ref[j]
        key = natural(kv_ref, (ky,), slot, flip, slice(0, DK))
        value = natural(kv_ref, (ky,), slot, flip, slice(DK, DK + DV))
        last = row[:, block - 1 :]

        @pl.when(ky == 0)
        def _():
            q = natural(q_ref, (), slot, flip, slice(None))
            state_bf = state[...].astype(bf16)
            s_ref[slot] = state_bf
            weights = (dot(q, key, NT) * decay_matrix(col, row)).astype(bf16)
            out = dot(weights, value, NN) + jnp.exp(col) * dot(q, state_bf, NN)
            normed, _ = normalize(out)
            g = natural(g_ref, (), slot, flip, slice(None))
            mixed = (g * jax.nn.sigmoid(g) * normed).astype(bf16)
            for half in range(2):
                rows = slice(half * part, (half + 1) * part)
                to = (1 - flip) if half else flip
                y_ref[to, slot] = mixed[rows]
                o_ref[to, slot] = out[rows]

        key_tail = (key.astype(f32) * jnp.exp(last - col)).astype(bf16)
        state[...] = jnp.exp(last) * state[...] + dot(key_tail, value, TN)

    return pl.pallas_call(
        kernel,
        grid=(nz * ny,),
        out_shape=[
            jax.ShapeDtypeStruct((halves, nz, part, DV), bf16),
            jax.ShapeDtypeStruct((halves, nz, part, DV), f32),
            jax.ShapeDtypeStruct((nz, DK, DV), bf16),
        ],
        in_specs=[SMEM] + [WHOLE] * 5,
        out_specs=[WHOLE] * 3,
        scratch_shapes=[pltpu.VMEM((DK, DV), f32)],
        compiler_params=PARAMS,
        name="retention_forward",
    )(where, c_row, c_col, keyval, query, gate)


def retention_backward(where, c_row, c_col, keyval, queries, grads, states, cosines, sines):
    ny, halves, nz, part, _ = queries.shape
    block = halves * part
    key_scale = DK ** (-0.5)

    def kernel(
        where_ref, row_ref, col_ref, kv_ref, q_ref, d_ref, s_ref, cos_ref, sin_ref, g_ref, state
    ):
        step = pl.program_id(0)
        j = nz * ny - 1 - step

        @pl.when(step == 0)
        def _():
            state[...] = jnp.zeros_like(state)

        slot = slot_of((j // ny) ^ where_ref[0])
        ky = (j % ny) ^ where_ref[1]
        flip = where_ref[3]
        row, col = row_ref[j], col_ref[j]
        last = row[:, block - 1 :]
        q = natural(q_ref, (ky,), slot, flip, slice(None))
        grad = natural(d_ref, (ky,), slot, flip, slice(None))
        entry = jnp.exp(col)

        @pl.when(ky == 0)
        def _():
            key = natural(kv_ref, (), slot, flip, slice(0, DK))
            value = natural(kv_ref, (), slot, flip, slice(DK, DK + DV))
            cos = natural(cos_ref, (), slot, flip, slice(None))
            sin = natural(sin_ref, (), slot, flip, slice(None))
            decays = decay_matrix(col, row)
            tail = jnp.exp(last - col)
            state_bf = state[...].astype(bf16)
            weights = (dot(q, key, NT) * decays).astype(bf16)
            scores = (dot(grad, value, NT) * decays).astype(bf16)
            grad_q = dot(scores, key, NN) + entry * dot(grad, s_ref[slot], NT)
            grad_k = dot(scores, q, TN) + tail * dot(value, state_bf, NT)
            grad_v = dot(weights, grad, TN) + tail * dot(key, state_bf, NN)
            grad_q = rotate(grad_q, cos, -sin).astype(bf16)
            grad_k = (rotate(grad_k, cos, -sin) * key_scale).astype(bf16)
            grad_v = grad_v.astype(bf16)
            for half in range(2):
                rows = slice(half * part, (half + 1) * part)
                to = (1 - flip) if half else flip
                g_ref[to, slot, :, :DK] = grad_k[rows]
                g_ref[to, slot, :, DK : DK + DV] = grad_v[rows]
                g_ref[to, slot, :, DK + DV :] = grad_q[rows]

        query_entry = (q.astype(f32) * entry).astype(bf16)
        state[...] = jnp.exp(last) * state[...] + dot(query_entry, grad, TN)

    return pl.pallas_call(
        kernel,
        grid=(nz * ny,),
        out_shape=jax.ShapeDtypeStruct((halves, nz, part, 2 * DK + DV), bf16),
        in_specs=[SMEM] + [WHOLE] * 8,
        out_specs=WHOLE,
        scratch_shapes=[pltpu.VMEM((DK, DV), f32)],
        compiler_params=PARAMS,
        name="retention_backward",
    )(where, c_row, c_col, keyval, queries, grads, states, cosines, sines)


def shards(
    hidden_in,
    log_decay,
    out_grad,
    ln1_gain,
    ln1_bias,
    w_query,
    w_key,
    w_value,
    w_gate,
    w_out,
    ln2_gain,
    ln2_bias,
    mlp_gate,
    mlp_up,
    mlp_down,
):
    nz, ny = lax.axis_size("row"), lax.axis_size("col")
    nb, nh = lax.axis_size("batch"), lax.axis_size("head")
    z, y = lax.axis_index("row"), lax.axis_index("col")
    b, x = lax.axis_index("batch"), lax.axis_index("head")
    block, width = hidden_in.shape[1:]
    rows = ln1_gain.shape[0]
    part = block // nh
    tokens = nz * block
    where = jnp.stack([z, y, b, x]).astype(jnp.int32)

    sizes = (nz, ny, nb)

    def to_heads(pieces):
        return jnp.stack([pieces[0]] + [swap(pieces[k], "row", k) for k in range(1, nz)])

    def spread(own):
        parts = []
        for k in range(ny):
            got = swap(own, "col", k) if k else own
            parts += [got, swap(got, "batch", 1)]
        return assemble_pieces(where, parts, ny, nb)

    def spread_all(own):
        parts = lax.all_gather(own, ("col", "batch"))
        return assemble_weight(where, parts.reshape(ny, nb, *own.shape))

    def sum_grad(groups, other):
        grad = outer_sum(groups, other).astype(bf16)
        grad = lax.psum_scatter(grad, ("col", "batch"), scatter_dimension=0, tiled=True)
        return grad.reshape(nz, rows, -1)

    def halves(values):
        values = values.reshape(nh, part, -1)
        return pick(values, x, 0), pick(values, 1 - x, 0)

    def gather_block(own):
        two = swap(own, "row", 2)
        one = swap(jnp.concatenate([own, two]), "row", 1)
        return two, one

    def gather_tokens(own):
        two = swap(own, "row", 2)
        pair = jnp.concatenate([own, two])
        return pair, swap(pair, "row", 1)

    def mirror(values):
        return swap(values, "head", 1)

    quarter = tokens // 4

    def reduce_far(*terms):
        far = sum(matmul_t(values[tokens // 2 :], weight) for values, weight in terms)
        far = far.astype(bf16)
        return mirror(far[quarter:]), mirror(far[:quarter])

    def reduce_near(got, *terms):
        near = sum(matmul_t(values[: tokens // 2], weight) for values, weight in terms)
        send = (near[quarter:] + got[0].astype(f32)).astype(bf16)
        return send, near[:quarter] + got[1].astype(f32)

    def reduce_one(send, keep):
        keep = keep + swap(send, "row", 1).astype(f32)
        return keep[part:].astype(bf16), keep[:part]

    def reduce_two(send, keep):
        return keep + swap(send, "row", 2).astype(f32)

    group = nz * rows

    def grad_far(grouped, other):
        return outer_sum(grouped[:, ny * group :], other).astype(bf16)

    def grad_near(grouped, other, got):
        near = outer_sum(grouped[:, : ny * group], other) + got.astype(f32)
        return near[:group], near[group:].astype(bf16)

    def grad_col(keep, send):
        for k in range(1, ny):
            piece = send[(k - 1) * group : k * group]
            keep = keep + swap(piece, "col", k).astype(f32)
        return keep.reshape(nz, rows, -1)

    def grad_row(*totals):
        pieces = []
        for k in range(nz):
            piece = [pick(total, z ^ k, 0).astype(bf16) for total in totals]
            piece = jnp.concatenate(piece, axis=-1)
            pieces.append(swap(piece, "row", k) if k else piece)
        return pieces

    def unpack(pieces, widths):
        return unpack_grads(where, pieces[0], pieces[1:], widths)

    params = jnp.stack([ln1_gain, ln1_bias, ln2_gain, ln2_bias]).astype(f32)
    small = jnp.concatenate([params.reshape(-1), log_decay.reshape(-1)])
    small = gather_small(small, ("row", "col", "batch"))
    params = small[:, : 4 * rows].reshape(nz * ny * nb, 4, rows)
    gain_one, bias_one, gain_two, bias_two = params.transpose(1, 0, 2).reshape(4, width)
    decay = pick(pick(small[:, 4 * rows :].reshape(nz * ny, nb, nz, block), b, 1), z, 1)
    running = jnp.cumsum(decay, axis=-1)
    c_row, c_col = running[:, None, :], running[:, :, None]

    kv_own = to_heads(pack_weights(where, (w_key, w_value), nz))
    own_in, other_in = halves(hidden_in[0])
    two_in, one_in = gather_block(own_in)
    kv_w = spread(kv_own)
    qg_packed = pack_weights(where, after((w_query, w_gate), kv_own), nz)
    qg_own = to_heads(qg_packed)
    qg_w = spread_all(qg_own)
    out_own = to_heads(pack_weights(where, (after(w_out, qg_own).T,), nz))
    out_w = spread_all(out_own)
    feed = after((mlp_gate, mlp_up, mlp_down), out_own)
    mlp_own = to_heads(pack_weights(where, (feed[0], feed[1], feed[2].T), nz))
    own_grad, other_grad = halves(out_grad[0])
    two_grad, one_grad = gather_block(after(own_grad, mlp_own))

    half_dim = DK // 2
    freqs = 10000.0 ** (-jnp.arange(half_dim, dtype=f32) / half_dim)
    block_at = (jnp.array(ORDER) ^ z) * ny + y
    half_at = jnp.arange(nh) ^ x
    positions = (
        block_at[None, :, None] * block + half_at[:, None, None] * part + jnp.arange(part)
    )
    angles = positions.astype(f32).reshape(-1)[:, None] * freqs[None, :]
    cosines, sines = jnp.cos(angles), jnp.sin(angles)
    key_scale = DK ** (-0.5)

    first_bf, first_groups, first_near = place_rows(
        where,
        (own_in, two_in, one_in, other_in, mirror(two_in), mirror(one_in)),
        sizes,
        (gain_one[None], bias_one[None]),
        near=True,
    )
    first_kv, kv_w, out_own = tie(first_bf, kv_w, out_own)
    key_value = matmul(first_kv, kv_w)
    key_bf = (rotate(key_value[:, :DK], cosines, sines) * key_scale).astype(bf16)
    value_bf = key_value[:, DK:].astype(bf16)

    def split(values):
        return values.reshape(nh, nz, part, -1)

    def gather_col(values):
        return jnp.stack([values] + [swap(values, "col", k) for k in range(1, ny)])

    keyval = split(jnp.concatenate([key_bf, value_bf], axis=-1))
    query_gate = matmul(after(first_bf, keyval), qg_w)
    query_bf = rotate(query_gate[:, :DK], cosines, sines).astype(bf16)
    gate = query_gate[:, DK:]

    keyvals, mlp_own, query_bf = tie(gather_col(keyval), mlp_own, query_bf)
    mlp_w = spread_all(mlp_own)
    units = mlp_w.shape[1] // 3
    up_w, down_w = mlp_w[:, : 2 * units], mlp_w[:, 2 * units :]
    mixed, retained, states = retention_forward(
        where, c_row, c_col, keyvals, split(query_bf), split(gate)
    )
    mixed_bf = mixed.reshape(tokens, DV)
    queries = gather_col(split(after(query_bf, mixed)))

    inputs = own_in.astype(f32)
    got = reduce_far((mixed_bf, out_w))
    send, keep = reduce_near(got, (mixed_bf, out_w))
    send, two_grad, one_grad = tie(send, two_grad, one_grad)
    mirror_grads = mirror(two_grad), mirror(one_grad)
    send, keep = reduce_one(send, keep)
    middle, queries = tie(inputs + reduce_two(send, keep), queries)
    scaled_two, rstd_two = normalize(middle)
    pair, one = gather_tokens((scaled_two * gain_two + bias_two).astype(bf16))
    pair, mirror_grads = tie(pair, mirror_grads)
    second_bf, second_groups = place_rows(where, (pair, one, mirror(pair), mirror(one)), sizes)
    down_bf, down_groups = place_rows(
        where, (own_grad, two_grad, one_grad, other_grad, *mirror_grads), sizes
    )
    up = matmul(second_bf, up_w)
    up_gate, up_lin = up[:, :units], up[:, units:]
    gelu_cdf = 0.5 * (1.0 + lax.erf(up_gate * (0.5**0.5)))
    gelu_val = up_gate * gelu_cdf
    gelu_slope = gelu_cdf + up_gate * jnp.exp(-0.5 * up_gate * up_gate) * (2.0 * jnp.pi) ** -0.5
    hidden_bf = (gelu_val * up_lin).astype(bf16)

    grad_hidden = matmul(down_bf, down_w)
    grad_upgate = (grad_hidden * up_lin * gelu_slope).astype(bf16)
    grad_uplin = (grad_hidden * gelu_val).astype(bf16)
    grad_up = jnp.concatenate([grad_upgate, grad_uplin], axis=-1)
    got = reduce_far((grad_up, up_w))
    up_sum = sum_grad(second_groups, grad_up)
    down_sum = sum_grad(down_groups, hidden_bf)
    send, keep = reduce_near(got, (grad_up, up_w))
    hidden_late = after(hidden_bf, send)
    result_got = reduce_far((hidden_late, down_w))
    send, keep = reduce_one(send, keep)
    grad_two = reduce_two(send, keep)
    grad_middle = own_grad.astype(f32) + norm_back(grad_two * gain_two, scaled_two, rstd_two)
    pair, one = gather_tokens(grad_middle.astype(bf16))
    result_send, result_keep = reduce_near(result_got, (hidden_late, down_w))
    pair, result_send = tie(pair, result_send)
    attn_bf, attn_groups = place_rows(where, (pair, one, mirror(pair), mirror(one)), sizes)

    grp_norm, grp_rstd = normalize(retained.reshape(tokens, DV))
    gate_sig = jax.nn.sigmoid(gate)
    gate_act = gate * gate_sig
    grad_mixed = matmul(attn_bf, out_w)
    grad_gate = (grad_mixed * grp_norm * (gate_sig * (1.0 + gate * (1.0 - gate_sig)))).astype(bf16)
    ret_bf = norm_back(grad_mixed * gate_act, grp_norm, grp_rstd).astype(bf16)
    ret_all = gather_col(split(ret_bf))

    late_gate, late_mixed, result_send = after((grad_gate, mixed_bf, result_send), ret_bf)
    gate_sum = sum_grad(first_groups, late_gate)
    outs_sum = sum_grad(attn_groups, late_mixed)
    result_send, result_keep = reduce_one(result_send, result_keep)
    feed_pieces = grad_row(*after((up_sum, down_sum), ret_bf))

    grad_kvq = retention_backward(
        where, c_row, c_col, keyval, queries, ret_all, states, split(cosines), split(sines)
    )
    grad_kvq = grad_kvq.reshape(tokens, -1)
    grad_qg = jnp.concatenate([grad_kvq[:, DK + DV :], grad_gate], axis=-1)
    terms = ((grad_kvq[:, : DK + DV], kv_w), (grad_qg, qg_w))
    got = reduce_far(*terms)
    kvq_far = grad_far(first_near, grad_kvq)
    send, keep = reduce_near(got, *terms)
    kvq_keep, kvq_send = grad_near(first_near, grad_kvq, swap(kvq_far, "batch", 1))
    send, kvq_send, result_send = tie(send, kvq_send, result_send)
    result = (middle + reduce_two(result_send, result_keep)).astype(bf16)
    send, keep = reduce_one(send, keep)
    send, result, feed_pieces = tie(send, result, feed_pieces)
    grad_gates, grad_ups, grad_downs = unpack(feed_pieces, (units, units, units))
    both_pieces = grad_row(gate_sum, outs_sum)
    grad_one = reduce_two(send, keep)
    kvq_sum = grad_col(kvq_keep, kvq_send)
    grad_one, kvq_sum, grad_gates, grad_ups, grad_downs = tie(
        grad_one, kvq_sum, grad_gates, grad_ups, grad_downs
    )
    kvq_pieces = grad_row(kvq_sum)

    scaled_own, rstd_own = normalize(inputs)
    grad_in = grad_middle + norm_back(grad_one * gain_one, scaled_own, rstd_own)
    grad_in_other = mirror(grad_in)
    result_other = mirror(result)
    grad_g, grad_outs = unpack(both_pieces, (DV, DV))
    grad_k, grad_v, grad_q = unpack(kvq_pieces, (DK, DV, DK))

    def join(own, other):
        first = jnp.where(x == 0, own, other)
        second = jnp.where(x == 0, other, own)
        return jnp.concatenate([first, second]).reshape(1, block, width)

    norm_sums = jnp.stack(
        [
            jnp.sum(grad_one * scaled_own, axis=0),
            jnp.sum(grad_one, axis=0),
            jnp.sum(grad_two * scaled_two, axis=0),
            jnp.sum(grad_two, axis=0),
        ]
    )
    norm_sums = norm_sums + swap(norm_sums, "head", 1)
    norm_sums = norm_sums.reshape(4, nz, ny, nb, rows)
    for name, axis in (("batch", 3), ("col", 2), ("row", 1)):
        me = lax.axis_index(name)
        summed = pick(norm_sums, me, axis)
        for k in range(1, lax.axis_size(name)):
            summed = summed + swap(pick(norm_sums, me ^ k, axis), name, k)
        norm_sums = summed

    return (
        join(result, result_other),
        join(grad_in, grad_in_other),
        norm_sums[0],
        norm_sums[1],
        grad_q,
        grad_k,
        grad_v,
        grad_g,
        grad_outs.T,
        norm_sums[2],
        norm_sums[3],
        grad_gates,
        grad_ups,
        grad_downs.T,
    )


def solution(mesh):
    seq = ("row", "col")
    tokens = P("batch", seq, None)
    params = P((*seq, "batch"))
    by_rows = P((*seq, "batch"), "head")
    by_cols = P("head", (*seq, "batch"))

    def run(*arrays):
        rows = arrays[1].shape[1] // mesh.shape["head"]
        sizes = (rows, mesh.shape["seq"] // rows, mesh.shape["batch"], mesh.shape["head"])
        order = [mesh.axis_names.index(n) for n in ("seq", "batch", "head")]
        fine = Mesh(
            mesh.devices.transpose(order).reshape(sizes), ("row", "col", "batch", "head")
        )
        weights = (by_rows, by_rows, by_rows, by_rows, by_cols)
        feeds = (by_rows, by_rows, by_cols)
        return jax.shard_map(
            shards,
            mesh=fine,
            in_specs=(
                tokens,
                P("batch", "head", seq),
                tokens,
                params,
                params,
                *weights,
                params,
                params,
                *feeds,
            ),
            out_specs=(tokens, tokens, params, params, *weights, params, params, *feeds),
            check_vma=False,
        )(*arrays)

    return run
```

```python
import jax
import jax.numpy as jnp
from jax import lax
from jax.experimental import pallas as pl
from jax.experimental.pallas import tpu as pltpu
from jax.sharding import Mesh
from jax.sharding import PartitionSpec as P

DK = 256
DV = 512

epsilon = 1e-05
f32 = jnp.float32
bf16 = jnp.bfloat16
VMEM_LIMIT = 32 * 1024 * 1024

ORDER = (0, 2, 1, 3)


def swap(values, axis, k):
    count = lax.axis_size(axis)
    return lax.ppermute(values, axis, [(i, i ^ k) for i in range(count)])


def pick(values, index, axis):
    return lax.dynamic_index_in_dim(values, index, axis, keepdims=False)


def tie(*values):
    return lax.optimization_barrier(values)


def after(values, *others):
    return tie(values, others)[0]


def gather_small(values, name, only=None):
    bit = only or 1
    while bit < (2 * only if only else lax.axis_size(name)):
        other = swap(values, name, bit)
        low = (lax.axis_index(name) & bit) == 0
        values = jnp.where(low, jnp.concatenate([values, other]), jnp.concatenate([other, values]))
        bit *= 2
    return values


def matmul(values, weight):
    return jnp.dot(values, weight, preferred_element_type=f32)


def matmul_t(values, weight):
    return lax.dot_general(values, weight, (((1,), (1,)), ((), ())), preferred_element_type=f32)


def outer_sum(values, other):
    return lax.dot_general(values, other, (((0,), (0,)), ((), ())), preferred_element_type=f32)


def normalize(values):
    center = values - jnp.mean(values, axis=-1, keepdims=True)
    rstd = lax.rsqrt(jnp.mean(center * center, axis=-1, keepdims=True) + epsilon)
    return center * rstd, rstd


def norm_back(scaled_grad, scaled, rstd):
    return rstd * (
        scaled_grad
        - jnp.mean(scaled_grad, axis=-1, keepdims=True)
        - scaled * jnp.mean(scaled_grad * scaled, axis=-1, keepdims=True)
    )


def rotate(values, cosines, sines):
    half_dim = values.shape[-1] // 2
    first_half = values[..., :half_dim]
    second_half = values[..., half_dim:]
    return jnp.concatenate(
        [first_half * cosines - second_half * sines, first_half * sines + second_half * cosines],
        axis=-1,
    )


SMEM = pl.BlockSpec(memory_space=pltpu.SMEM)
WHOLE = pl.BlockSpec(memory_space=pltpu.VMEM)
PARAMS = pltpu.CompilerParams(vmem_limit_bytes=VMEM_LIMIT)


def pack_weights(where, weights, nz):
    rows = weights[0].shape[0]
    widths = [w.shape[1] // nz for w in weights]

    def kernel(where_ref, *refs):
        ins, outs = refs[: len(weights)], refs[len(weights) :]
        for k in range(nz):
            target = where_ref[0] ^ k
            at = 0
            for ref, width in zip(ins, widths):
                start = pl.multiple_of(target * width, width)
                outs[k][:, at : at + width] = ref[:, pl.ds(start, width)]
                at += width

    return pl.pallas_call(
        kernel,
        out_shape=[jax.ShapeDtypeStruct((rows, sum(widths)), bf16)] * nz,
        in_specs=[SMEM] + [WHOLE] * len(weights),
        out_specs=[WHOLE] * nz,
        compiler_params=PARAMS,
        name="pack_weights",
    )(where, *weights)


def unpack_grads(where, own, pieces, widths):
    nz = len(pieces) + 1
    rows = own.shape[0]

    def kernel(where_ref, *refs):
        ins, outs = refs[:nz], refs[nz:]
        for k in range(nz):
            target = where_ref[0] ^ k
            at = 0
            for ref, width in zip(outs, widths):
                start = pl.multiple_of(target * width, width)
                ref[:, pl.ds(start, width)] = ins[k][:, at : at + width].astype(f32)
                at += width

    return pl.pallas_call(
        kernel,
        out_shape=[jax.ShapeDtypeStruct((rows, nz * width), f32) for width in widths],
        in_specs=[SMEM] + [WHOLE] * nz,
        out_specs=[WHOLE] * len(widths),
        compiler_params=PARAMS,
        name="unpack_grads",
    )(where, own, *pieces)


def assemble_weight(where, parts):
    ny, nb, nz, rows, cols = parts.shape

    def kernel(where_ref, ref, out):
        for y in range(ny):
            for b in range(nb):
                for kz in range(nz):
                    at = ((where_ref[0] ^ kz) * ny + y) * nb + b
                    out[pl.ds(pl.multiple_of(at * rows, rows), rows), :] = ref[y, b, kz]

    return pl.pallas_call(
        kernel,
        out_shape=jax.ShapeDtypeStruct((nz * ny * nb * rows, cols), bf16),
        in_specs=[SMEM, WHOLE],
        out_specs=WHOLE,
        compiler_params=PARAMS,
        name="assemble_weight",
    )(where, parts)


def assemble_pieces(where, parts, ny, nb):
    nz, rows, cols = parts[0].shape

    def kernel(where_ref, *refs):
        ins, out = refs[:-1], refs[-1]
        for ky in range(ny):
            for kb in range(nb):
                for kz in range(nz):
                    at = ((where_ref[0] ^ kz) * ny + (where_ref[1] ^ ky)) * nb
                    at = pl.multiple_of((at + (where_ref[2] ^ kb)) * rows, rows)
                    out[pl.ds(at, rows), :] = ins[ky * nb + kb][kz]

    return pl.pallas_call(
        kernel,
        out_shape=jax.ShapeDtypeStruct((nz * ny * nb * rows, cols), bf16),
        in_specs=[SMEM] + [WHOLE] * len(parts),
        out_specs=WHOLE,
        compiler_params=PARAMS,
        name="assemble_pieces",
    )(where, *parts)


def place_rows(where, pieces, sizes, norm=None, near=False):
    nz, ny, nb = sizes
    width = pieces[0].shape[1]
    tokens = sum(piece.shape[0] for piece in pieces)
    rows = width // (nz * ny * nb)
    aligned = rows % 128 == 0
    norm = list(norm or ())
    count = 1 + (1 + near) * aligned

    def kernel(where_ref, *refs):
        ins, rest = refs[: len(pieces)], refs[len(pieces) :]
        params, outs = rest[: len(norm)], rest[len(norm) :]
        full = outs[0]
        at = 0
        for ref in ins:
            values = ref[...]
            if norm:
                values, _ = normalize(values.astype(f32))
                values = (values * params[0][...] + params[1][...]).astype(bf16)
            full[at : at + ref.shape[0], :] = values
            at += ref.shape[0]
        for z in range(nz):
            for y in range(ny):
                for b in range(nb):
                    if count > 1:
                        source = ((z * ny + y) * nb + b) * rows
                        to = ((y * nb + b) * nz + z) * rows
                        outs[1][:, to : to + rows] = full[:, source : source + rows]
                    if count > 2:
                        source = (z * ny + (where_ref[1] ^ y)) * nb + (where_ref[2] ^ b)
                        source = pl.multiple_of(source * rows, rows)
                        to = ((b * ny + y) * nz + z) * rows
                        outs[2][:, to : to + rows] = full[:, pl.ds(source, rows)]

    outs = pl.pallas_call(
        kernel,
        out_shape=[jax.ShapeDtypeStruct((tokens, width), bf16)] * count,
        in_specs=[SMEM] + [WHOLE] * (len(pieces) + len(norm)),
        out_specs=[WHOLE] * count,
        compiler_params=PARAMS,
        name="place_rows",
    )(where, *pieces, *norm)
    if aligned:
        return outs
    groups = outs[0].reshape(tokens, nz, ny, nb, rows)
    outs = [outs[0], groups.transpose(0, 2, 3, 1, 4).reshape(tokens, width)]
    if near:
        groups = jnp.take(groups, jnp.arange(ny) ^ where[1], axis=2)
        groups = jnp.take(groups, jnp.arange(nb) ^ where[2], axis=3)
        outs.append(groups.transpose(0, 3, 2, 1, 4).reshape(tokens, width))
    return outs


def slot_of(k):
    return ((k & 1) << 1) | (k >> 1)


def natural(ref, lead, slot, flip, columns):
    first = ref[(*lead, flip, slot, slice(None), columns)]
    second = ref[(*lead, 1 - flip, slot, slice(None), columns)]
    return jnp.concatenate([first, second], axis=0)


def dot(left, right, dims):
    return lax.dot_general(left, right, (dims, ((), ())), preferred_element_type=f32)


NN, NT, TN = ((1,), (0,)), ((1,), (1,)), ((0,), (0,))


def decay_matrix(col, row):
    block = row.shape[-1]
    at = lax.broadcasted_iota(jnp.int32, (block, block), 0)
    to = lax.broadcasted_iota(jnp.int32, (block, block), 1)
    return jnp.where(at >= to, jnp.exp(jnp.minimum(col - row, 0.0)), 0.0)


def retention_forward(where, c_row, c_col, keyval, query, gate):
    ny, halves, nz, part, _ = keyval.shape
    block = halves * part

    def kernel(where_ref, row_ref, col_ref, kv_ref, q_ref, g_ref, y_ref, o_ref, s_ref, state):
        j = pl.program_id(0)

        @pl.when(j == 0)
        def _():
            state[...] = jnp.zeros_like(state)

        slot = slot_of((j // ny) ^ where_ref[0])
        ky = (j % ny) ^ where_ref[1]
        flip = where_ref[3]
        row, col = row_ref[j], col_ref[j]
        key = natural(kv_ref, (ky,), slot, flip, slice(0, DK))
        value = natural(kv_ref, (ky,), slot, flip, slice(DK, DK + DV))
        last = row[:, block - 1 :]

        @pl.when(ky == 0)
        def _():
            q = natural(q_ref, (), slot, flip, slice(None))
            state_bf = state[...].astype(bf16)
            s_ref[slot] = state_bf
            weights = (dot(q, key, NT) * decay_matrix(col, row)).astype(bf16)
            out = dot(weights, value, NN) + jnp.exp(col) * dot(q, state_bf, NN)
            normed, _ = normalize(out)
            g = natural(g_ref, (), slot, flip, slice(None))
            mixed = (g * jax.nn.sigmoid(g) * normed).astype(bf16)
            for half in range(2):
                rows = slice(half * part, (half + 1) * part)
                to = (1 - flip) if half else flip
                y_ref[to, slot] = mixed[rows]
                o_ref[to, slot] = out[rows]

        key_tail = (key.astype(f32) * jnp.exp(last - col)).astype(bf16)
        state[...] = jnp.exp(last) * state[...] + dot(key_tail, value, TN)

    return pl.pallas_call(
        kernel,
        grid=(nz * ny,),
        out_shape=[
            jax.ShapeDtypeStruct((halves, nz, part, DV), bf16),
            jax.ShapeDtypeStruct((halves, nz, part, DV), f32),
            jax.ShapeDtypeStruct((nz, DK, DV), bf16),
        ],
        in_specs=[SMEM] + [WHOLE] * 5,
        out_specs=[WHOLE] * 3,
        scratch_shapes=[pltpu.VMEM((DK, DV), f32)],
        compiler_params=PARAMS,
        name="retention_forward",
    )(where, c_row, c_col, keyval, query, gate)


def retention_backward(where, c_row, c_col, keyval, queries, grads, states, cosines, sines):
    ny, halves, nz, part, _ = queries.shape
    block = halves * part
    key_scale = DK ** (-0.5)

    def kernel(
        where_ref, row_ref, col_ref, kv_ref, q_ref, d_ref, s_ref, cos_ref, sin_ref, g_ref, state
    ):
        step = pl.program_id(0)
        j = nz * ny - 1 - step

        @pl.when(step == 0)
        def _():
            state[...] = jnp.zeros_like(state)

        slot = slot_of((j // ny) ^ where_ref[0])
        ky = (j % ny) ^ where_ref[1]
        flip = where_ref[3]
        row, col = row_ref[j], col_ref[j]
        last = row[:, block - 1 :]
        q = natural(q_ref, (ky,), slot, flip, slice(None))
        grad = natural(d_ref, (ky,), slot, flip, slice(None))
        entry = jnp.exp(col)

        @pl.when(ky == 0)
        def _():
            key = natural(kv_ref, (), slot, flip, slice(0, DK))
            value = natural(kv_ref, (), slot, flip, slice(DK, DK + DV))
            cos = natural(cos_ref, (), slot, flip, slice(None))
            sin = natural(sin_ref, (), slot, flip, slice(None))
            decays = decay_matrix(col, row)
            tail = jnp.exp(last - col)
            state_bf = state[...].astype(bf16)
            weights = (dot(q, key, NT) * decays).astype(bf16)
            scores = (dot(grad, value, NT) * decays).astype(bf16)
            grad_q = dot(scores, key, NN) + entry * dot(grad, s_ref[slot], NT)
            grad_k = dot(scores, q, TN) + tail * dot(value, state_bf, NT)
            grad_v = dot(weights, grad, TN) + tail * dot(key, state_bf, NN)
            grad_q = rotate(grad_q, cos, -sin).astype(bf16)
            grad_k = (rotate(grad_k, cos, -sin) * key_scale).astype(bf16)
            grad_v = grad_v.astype(bf16)
            for half in range(2):
                rows = slice(half * part, (half + 1) * part)
                to = (1 - flip) if half else flip
                g_ref[to, slot, :, :DK] = grad_k[rows]
                g_ref[to, slot, :, DK : DK + DV] = grad_v[rows]
                g_ref[to, slot, :, DK + DV :] = grad_q[rows]

        query_entry = (q.astype(f32) * entry).astype(bf16)
        state[...] = jnp.exp(last) * state[...] + dot(query_entry, grad, TN)

    return pl.pallas_call(
        kernel,
        grid=(nz * ny,),
        out_shape=jax.ShapeDtypeStruct((halves, nz, part, 2 * DK + DV), bf16),
        in_specs=[SMEM] + [WHOLE] * 8,
        out_specs=WHOLE,
        scratch_shapes=[pltpu.VMEM((DK, DV), f32)],
        compiler_params=PARAMS,
        name="retention_backward",
    )(where, c_row, c_col, keyval, queries, grads, states, cosines, sines)


def shards(
    hidden_in,
    log_decay,
    out_grad,
    ln1_gain,
    ln1_bias,
    w_query,
    w_key,
    w_value,
    w_gate,
    w_out,
    ln2_gain,
    ln2_bias,
    mlp_gate,
    mlp_up,
    mlp_down,
):
    nz, ny = lax.axis_size("row"), lax.axis_size("col")
    nb, nh = lax.axis_size("batch"), lax.axis_size("head")
    z, y = lax.axis_index("row"), lax.axis_index("col")
    b, x = lax.axis_index("batch"), lax.axis_index("head")
    block, width = hidden_in.shape[1:]
    rows = ln1_gain.shape[0]
    part = block // nh
    tokens = nz * block
    where = jnp.stack([z, y, b, x]).astype(jnp.int32)

    sizes = (nz, ny, nb)

    def to_heads(pieces):
        return jnp.stack([pieces[0]] + [swap(pieces[k], "row", k) for k in range(1, nz)])

    def spread(own):
        parts = []
        for got in own:
            parts += [got, swap(got, "batch", 1)]
        return assemble_pieces(where, parts, ny, nb)

    def spread_all(own):
        parts = lax.all_gather(own, ("col", "batch"))
        return assemble_weight(where, parts.reshape(ny, nb, *own.shape))

    def sum_grad(grad):
        grad = lax.psum_scatter(grad, ("col", "batch"), scatter_dimension=0, tiled=True)
        return grad.reshape(nz, rows, -1)

    def halves(values):
        values = values.reshape(nh, part, -1)
        return pick(values, x, 0), pick(values, 1 - x, 0)

    def gather_tokens(own):
        two = swap(own, "row", 2)
        pair = jnp.concatenate([own, two])
        return pair, swap(pair, "row", 1)

    def mirror(values):
        return swap(values, "head", 1)

    quarter = tokens // 4

    def reduce_far(*terms):
        far = sum(matmul_t(values[tokens // 2 :], weight) for values, weight in terms)
        far = far.astype(bf16)
        return mirror(far[quarter:]), mirror(far[:quarter])

    def reduce_near(got, *terms):
        near = sum(matmul_t(values[: tokens // 2], weight) for values, weight in terms)
        send = (near[quarter:] + got[0].astype(f32)).astype(bf16)
        return send, near[:quarter] + got[1].astype(f32)

    def reduce_one(send, keep):
        keep = keep + swap(send, "row", 1).astype(f32)
        return keep[part:].astype(bf16), keep[:part]

    def reduce_two(send, keep):
        return keep + swap(send, "row", 2).astype(f32)

    group = nz * rows

    def grad_far(grouped, other):
        return outer_sum(grouped[:, ny * group :], other).astype(bf16)

    def grad_near(grouped, other, got):
        near = outer_sum(grouped[:, : ny * group], other) + got.astype(f32)
        return near[:group], near[group:].astype(bf16)

    def grad_col(keep, send):
        for k in range(1, ny):
            piece = send[(k - 1) * group : k * group]
            keep = keep + swap(piece, "col", k).astype(f32)
        return keep.reshape(nz, rows, -1)

    def grad_row(*totals):
        pieces = []
        for k in range(nz):
            piece = [pick(total, z ^ k, 0).astype(bf16) for total in totals]
            piece = jnp.concatenate(piece, axis=-1)
            pieces.append(swap(piece, "row", k) if k else piece)
        return pieces

    def unpack(pieces, widths):
        return unpack_grads(where, pieces[0], pieces[1:], widths)

    params = jnp.stack([ln1_gain, ln1_bias, ln2_gain, ln2_bias]).astype(f32)
    small = jnp.concatenate([params.reshape(-1), log_decay.reshape(-1)])[None]
    small = gather_small(gather_small(small, "batch"), "col")
    kv_own = to_heads(pack_weights(where, (w_key, w_value), nz))
    own_in, other_in = halves(hidden_in[0])
    two_in = swap(own_in, "row", 2)
    kv_own, two_in, small, qg_own, out_own = tie(
        kv_own, two_in, small, (w_query, w_gate), w_out
    )
    kv_own = [kv_own] + [swap(kv_own, "col", k) for k in range(1, ny)]
    one_in = swap(jnp.concatenate([own_in, two_in]), "row", 1)
    mirror_two = mirror(two_in)
    small = gather_small(small, "row", 1)
    qg_own = to_heads(pack_weights(where, qg_own, nz))
    kv_own, one_in, mirror_two, small, qg_own, out_own, feed = tie(
        kv_own, one_in, mirror_two, small, qg_own, out_own, (mlp_gate, mlp_up, mlp_down)
    )
    kv_w = spread(kv_own)
    mirror_one = mirror(one_in)
    small = gather_small(small, "row", 2)
    qg_own = [qg_own] + [swap(qg_own, "col", k) for k in range(1, ny)]
    out_own = to_heads(pack_weights(where, (out_own.T,), nz))
    kv_w, mirror_one, small, qg_own, out_own, feed, own_grad = tie(
        kv_w, mirror_one, small, qg_own, out_own, feed, halves(out_grad[0])[0]
    )
    qg_w = spread(qg_own)
    out_w = spread_all(out_own)
    mlp_own = to_heads(pack_weights(where, (feed[0], feed[1], feed[2].T), nz))
    other_grad = halves(out_grad[0])[1]

    params = small[:, : 4 * rows].reshape(nz * ny * nb, 4, rows)
    gain_one, bias_one, gain_two, bias_two = params.transpose(1, 0, 2).reshape(4, width)
    decay = pick(pick(small[:, 4 * rows :].reshape(nz * ny, nb, nz, block), b, 1), z, 1)
    running = jnp.cumsum(decay, axis=-1)
    c_row, c_col = running[:, None, :], running[:, :, None]

    half_dim = DK // 2
    freqs = 10000.0 ** (-jnp.arange(half_dim, dtype=f32) / half_dim)
    block_at = (jnp.array(ORDER) ^ z) * ny + y
    half_at = jnp.arange(nh) ^ x
    positions = (
        block_at[None, :, None] * block + half_at[:, None, None] * part + jnp.arange(part)
    )
    angles = positions.astype(f32).reshape(-1)[:, None] * freqs[None, :]
    cosines, sines = jnp.cos(angles), jnp.sin(angles)
    key_scale = DK ** (-0.5)

    first_bf, first_groups, first_near = place_rows(
        where,
        (own_in, two_in, one_in, other_in, mirror_two, mirror_one),
        sizes,
        (gain_one[None], bias_one[None]),
        near=True,
    )
    key_value = matmul(first_bf, kv_w)
    key_bf = (rotate(key_value[:, :DK], cosines, sines) * key_scale).astype(bf16)
    value_bf = key_value[:, DK:].astype(bf16)

    def split(values):
        return values.reshape(nh, nz, part, -1)

    def gather_col(values):
        return jnp.stack([values] + [swap(values, "col", k) for k in range(1, ny)])

    keyval = split(jnp.concatenate([key_bf, value_bf], axis=-1))
    query_gate = matmul(after(first_bf, keyval), qg_w)
    query_bf = rotate(query_gate[:, :DK], cosines, sines).astype(bf16)
    gate = query_gate[:, DK:]

    keyvals, query_bf = tie(gather_col(keyval), query_bf)
    mixed, retained, states = retention_forward(
        where, c_row, c_col, keyvals, split(query_bf), split(gate)
    )
    mixed, mlp_own = tie(mixed, mlp_own)
    mlp_w = spread_all(mlp_own)
    units = mlp_w.shape[1] // 3
    up_w, down_w = mlp_w[:, : 2 * units], mlp_w[:, 2 * units :]
    two_grad = swap(after(own_grad, mlp_own), "row", 2)
    mixed_bf = mixed.reshape(tokens, DV)
    queries = gather_col(split(after(query_bf, mixed)))

    inputs = own_in.astype(f32)
    got = reduce_far((mixed_bf, out_w))
    send, keep = reduce_near(got, (mixed_bf, out_w))
    send, two_grad = tie(send, two_grad)
    one_grad = swap(jnp.concatenate([own_grad, two_grad]), "row", 1)
    mirror_two = mirror(two_grad)
    send, keep = reduce_one(send, keep)
    send, one_grad = tie(send, one_grad)
    mirror_one = mirror(one_grad)
    middle = inputs + reduce_two(send, keep)
    middle, queries, mirror_two, mirror_one = tie(middle, queries, mirror_two, mirror_one)
    scaled_two, rstd_two = normalize(middle)
    pair, one = gather_tokens((scaled_two * gain_two + bias_two).astype(bf16))
    second_bf, second_groups = place_rows(where, (pair, one, mirror(pair), mirror(one)), sizes)
    down_bf, down_groups = place_rows(
        where, (own_grad, two_grad, one_grad, other_grad, mirror_two, mirror_one), sizes
    )
    up = matmul(second_bf, up_w)
    up_gate, up_lin = up[:, :units], up[:, units:]
    gelu_cdf = 0.5 * (1.0 + lax.erf(up_gate * (0.5**0.5)))
    gelu_val = up_gate * gelu_cdf
    gelu_slope = gelu_cdf + up_gate * jnp.exp(-0.5 * up_gate * up_gate) * (2.0 * jnp.pi) ** -0.5
    hidden_bf = (gelu_val * up_lin).astype(bf16)

    grad_hidden = matmul(down_bf, down_w)
    grad_upgate = (grad_hidden * up_lin * gelu_slope).astype(bf16)
    grad_uplin = (grad_hidden * gelu_val).astype(bf16)
    grad_up = jnp.concatenate([grad_upgate, grad_uplin], axis=-1)
    got = reduce_far((grad_up, up_w))
    feed_grad = (outer_sum(second_groups, grad_up), outer_sum(down_groups, hidden_bf))
    feed_grad = jnp.concatenate([grad.astype(bf16) for grad in feed_grad], axis=-1)
    send, keep = reduce_near(got, (grad_up, up_w))
    send, feed_grad, hidden_late = tie(send, feed_grad, hidden_bf)
    feed_sum = sum_grad(feed_grad)
    result_got = reduce_far((hidden_late, down_w))
    send, keep = reduce_one(send, keep)
    grad_two = reduce_two(send, keep)
    result_send, result_keep = reduce_near(result_got, (hidden_late, down_w))
    grad_two, result_send = tie(grad_two, result_send)
    grad_middle = own_grad.astype(f32) + norm_back(grad_two * gain_two, scaled_two, rstd_two)
    pair, one = gather_tokens(grad_middle.astype(bf16))
    attn_bf, attn_groups = place_rows(where, (pair, one, mirror(pair), mirror(one)), sizes)
    attn_bf, attn_groups, result_send, feed_sum = tie(
        attn_bf, attn_groups, result_send, feed_sum
    )

    grp_norm, grp_rstd = normalize(retained.reshape(tokens, DV))
    gate_sig = jax.nn.sigmoid(gate)
    gate_act = gate * gate_sig
    grad_mixed = matmul(attn_bf, out_w)
    grad_gate = (grad_mixed * grp_norm * (gate_sig * (1.0 + gate * (1.0 - gate_sig)))).astype(bf16)
    ret_bf = norm_back(grad_mixed * gate_act, grp_norm, grp_rstd).astype(bf16)
    ret_all = gather_col(split(ret_bf))

    outs_sum = sum_grad(outer_sum(attn_groups, after(mixed_bf, ret_bf)).astype(bf16))
    result_send, result_keep = reduce_one(result_send, result_keep)
    feed_pieces = grad_row(feed_sum)
    ret_all, result_send = tie(ret_all, result_send)
    result = (middle + reduce_two(result_send, result_keep)).astype(bf16)

    grad_kvq = retention_backward(
        where, c_row, c_col, keyval, queries, ret_all, states, split(cosines), split(sines)
    )
    grad_kvq = grad_kvq.reshape(tokens, -1)
    grad_qg = jnp.concatenate([grad_kvq[:, DK + DV :], grad_gate], axis=-1)
    terms = ((grad_kvq[:, : DK + DV], kv_w), (grad_qg, qg_w))
    got = reduce_far(*terms)
    kvq_far = grad_far(first_near, grad_kvq)
    send, keep = reduce_near(got, *terms)
    kvq_keep, kvq_send = grad_near(first_near, grad_kvq, swap(kvq_far, "batch", 1))
    gate_grad = outer_sum(first_groups, after(grad_gate, grad_kvq)).astype(bf16)
    send, kvq_send, result, gate_grad, feed_pieces = tie(
        send, kvq_send, result, gate_grad, feed_pieces
    )
    gate_sum = sum_grad(gate_grad)
    grad_gates, grad_ups, grad_downs = unpack(feed_pieces, (units, units, units))
    send, keep = reduce_one(send, keep)
    grad_one = reduce_two(send, keep)
    kvq_sum = grad_col(kvq_keep, kvq_send)
    grad_one, kvq_sum, outs_sum, grad_gates, grad_ups, grad_downs = tie(
        grad_one, kvq_sum, outs_sum, grad_gates, grad_ups, grad_downs
    )
    kvq_pieces = grad_row(kvq_sum)
    both_pieces = grad_row(gate_sum, outs_sum)
    result_other = mirror(result)

    scaled_own, rstd_own = normalize(inputs)
    grad_in = grad_middle + norm_back(grad_one * gain_one, scaled_own, rstd_own)
    grad_in_other = mirror(grad_in)
    grad_g, grad_outs = unpack(both_pieces, (DV, DV))
    grad_k, grad_v, grad_q = unpack(kvq_pieces, (DK, DV, DK))

    def join(own, other):
        first = jnp.where(x == 0, own, other)
        second = jnp.where(x == 0, other, own)
        return jnp.concatenate([first, second]).reshape(1, block, width)

    norm_sums = jnp.stack(
        [
            jnp.sum(grad_one * scaled_own, axis=0),
            jnp.sum(grad_one, axis=0),
            jnp.sum(grad_two * scaled_two, axis=0),
            jnp.sum(grad_two, axis=0),
        ]
    )
    norm_sums = norm_sums + swap(norm_sums, "head", 1)
    norm_sums = norm_sums.reshape(4, nz, ny, nb, rows)
    for name, axis in (("batch", 3), ("col", 2), ("row", 1)):
        me = lax.axis_index(name)
        summed = pick(norm_sums, me, axis)
        for k in range(1, lax.axis_size(name)):
            summed = summed + swap(pick(norm_sums, me ^ k, axis), name, k)
        norm_sums = summed

    return (
        join(result, result_other),
        join(grad_in, grad_in_other),
        norm_sums[0],
        norm_sums[1],
        grad_q,
        grad_k,
        grad_v,
        grad_g,
        grad_outs.T,
        norm_sums[2],
        norm_sums[3],
        grad_gates,
        grad_ups,
        grad_downs.T,
    )


def solution(mesh):
    seq = ("row", "col")
    tokens = P("batch", seq, None)
    params = P((*seq, "batch"))
    by_rows = P((*seq, "batch"), "head")
    by_cols = P("head", (*seq, "batch"))

    def run(*arrays):
        rows = arrays[1].shape[1] // mesh.shape["head"]
        sizes = (rows, mesh.shape["seq"] // rows, mesh.shape["batch"], mesh.shape["head"])
        order = [mesh.axis_names.index(n) for n in ("seq", "batch", "head")]
        fine = Mesh(
            mesh.devices.transpose(order).reshape(sizes), ("row", "col", "batch", "head")
        )
        weights = (by_rows, by_rows, by_rows, by_rows, by_cols)
        feeds = (by_rows, by_rows, by_cols)
        return jax.shard_map(
            shards,
            mesh=fine,
            in_specs=(
                tokens,
                P("batch", "head", seq),
                tokens,
                params,
                params,
                *weights,
                params,
                params,
                *feeds,
            ),
            out_specs=(tokens, tokens, params, params, *weights, params, params, *feeds),
            check_vma=False,
        )(*arrays)

    return run
```

```python
import jax
import jax.numpy as jnp
from jax import lax
from jax.experimental import pallas as pl
from jax.experimental.pallas import tpu as pltpu
from jax.sharding import Mesh
from jax.sharding import PartitionSpec as P

DK = 256
DV = 512

epsilon = 1e-05
f32 = jnp.float32
bf16 = jnp.bfloat16
VMEM_LIMIT = 12 * 1024 * 1024

ORDER = (0, 2, 1, 3)


def swap(values, axis, k):
    count = lax.axis_size(axis)
    return lax.ppermute(values, axis, [(i, i ^ k) for i in range(count)])


def pick(values, index, axis):
    return lax.dynamic_index_in_dim(values, index, axis, keepdims=False)


def tie(*values):
    return lax.optimization_barrier(values)


def after(values, *others):
    return tie(values, others)[0]


def matmul(values, weight):
    return jnp.dot(values, weight, preferred_element_type=f32)


def matmul_t(values, weight):
    return lax.dot_general(values, weight, (((1,), (1,)), ((), ())), preferred_element_type=f32)


def outer_sum(values, other):
    return lax.dot_general(values, other, (((0,), (0,)), ((), ())), preferred_element_type=f32)


def normalize(values):
    center = values - jnp.mean(values, axis=-1, keepdims=True)
    rstd = lax.rsqrt(jnp.mean(center * center, axis=-1, keepdims=True) + epsilon)
    return center * rstd, rstd


def norm_back(scaled_grad, scaled, rstd):
    return rstd * (
        scaled_grad
        - jnp.mean(scaled_grad, axis=-1, keepdims=True)
        - scaled * jnp.mean(scaled_grad * scaled, axis=-1, keepdims=True)
    )


def rotate(values, cosines, sines):
    half_dim = values.shape[-1] // 2
    first_half = values[..., :half_dim]
    second_half = values[..., half_dim:]
    return jnp.concatenate(
        [first_half * cosines - second_half * sines, first_half * sines + second_half * cosines],
        axis=-1,
    )


SMEM = pl.BlockSpec(memory_space=pltpu.SMEM)
WHOLE = pl.BlockSpec(memory_space=pltpu.VMEM)
PARAMS = pltpu.CompilerParams(vmem_limit_bytes=VMEM_LIMIT)


def pack_weights(where, weights, nz):
    rows = weights[0].shape[0]
    widths = [w.shape[1] // nz for w in weights]

    def kernel(where_ref, *refs):
        ins, outs = refs[: len(weights)], refs[len(weights) :]
        for k in range(nz):
            target = where_ref[0] ^ k
            at = 0
            for ref, width in zip(ins, widths):
                start = pl.multiple_of(target * width, width)
                outs[k][:, at : at + width] = ref[:, pl.ds(start, width)]
                at += width

    return pl.pallas_call(
        kernel,
        out_shape=[jax.ShapeDtypeStruct((rows, sum(widths)), bf16)] * nz,
        in_specs=[SMEM] + [WHOLE] * len(weights),
        out_specs=[WHOLE] * nz,
        compiler_params=PARAMS,
        name="pack_weights",
    )(where, *weights)


EXTRA = 16


def pack_first(where, weights, gains, decays, nz):
    rows = weights[0].shape[0]
    widths = [w.shape[1] // nz for w in weights]
    block = decays.shape[1]
    gains = jnp.pad(gains, ((0, 0), (0, sum(widths) - gains.shape[1])))

    def kernel(where_ref, gain_ref, decay_ref, *refs):
        ins, outs = refs[: len(weights)], refs[len(weights) :]
        at = lax.broadcasted_iota(jnp.int32, (EXTRA, 1), 0)
        gain_rows = jnp.where(at == 0, gain_ref[...].astype(f32), 0.0)
        for k in range(nz):
            target = where_ref[0] ^ k
            to = 0
            for ref, width in zip(ins, widths):
                start = pl.multiple_of(target * width, width)
                outs[k][:rows, to : to + width] = ref[:, pl.ds(start, width)]
                to += width
            rest = decay_ref[pl.ds(target, 1), :]
            parts = gain_rows[:, :block]
            for row in range(1, 4):
                part = rest.astype(bf16).astype(f32)
                parts = jnp.where(at == row, part, parts)
                rest = rest - part
            outs[k][rows:, :] = gain_rows.astype(bf16)
            outs[k][rows:, :block] = parts.astype(bf16)

    return pl.pallas_call(
        kernel,
        out_shape=[jax.ShapeDtypeStruct((rows + EXTRA, sum(widths)), bf16)] * nz,
        in_specs=[SMEM] + [WHOLE] * (2 + len(weights)),
        out_specs=[WHOLE] * nz,
        compiler_params=PARAMS,
        name="pack_first",
    )(where, gains, decays, *weights)


def unpack_grads(where, own, pieces, widths):
    nz = len(pieces) + 1
    rows = own.shape[0]

    def kernel(where_ref, *refs):
        ins, outs = refs[:nz], refs[nz:]
        for k in range(nz):
            target = where_ref[0] ^ k
            at = 0
            for ref, width in zip(outs, widths):
                start = pl.multiple_of(target * width, width)
                ref[:, pl.ds(start, width)] = ins[k][:, at : at + width].astype(f32)
                at += width

    return pl.pallas_call(
        kernel,
        out_shape=[jax.ShapeDtypeStruct((rows, nz * width), f32) for width in widths],
        in_specs=[SMEM] + [WHOLE] * nz,
        out_specs=[WHOLE] * len(widths),
        compiler_params=PARAMS,
        name="unpack_grads",
    )(where, own, *pieces)


def assemble_weight(where, parts):
    ny, nb, nz, rows, cols = parts.shape

    def kernel(where_ref, ref, out):
        for y in range(ny):
            for b in range(nb):
                for kz in range(nz):
                    at = ((where_ref[0] ^ kz) * ny + y) * nb + b
                    out[pl.ds(pl.multiple_of(at * rows, rows), rows), :] = ref[y, b, kz]

    return pl.pallas_call(
        kernel,
        out_shape=jax.ShapeDtypeStruct((nz * ny * nb * rows, cols), bf16),
        in_specs=[SMEM, WHOLE],
        out_specs=WHOLE,
        compiler_params=PARAMS,
        name="assemble_weight",
    )(where, parts)


def assemble_pieces(where, parts, ny, nb, extra=0):
    nz, rows, cols = parts[0].shape
    rows -= extra
    count = nz * ny * nb

    def kernel(where_ref, *refs):
        ins, outs = refs[: len(parts)], refs[len(parts) :]
        for ky in range(ny):
            for kb in range(nb):
                for kz in range(nz):
                    block = (where_ref[0] ^ kz) * ny + (where_ref[1] ^ ky)
                    device = block * nb + (where_ref[2] ^ kb)
                    piece = ins[ky * nb + kb]
                    at = pl.multiple_of(device * rows, rows)
                    outs[0][pl.ds(at, rows), :] = piece[kz, :rows, :]
                    if extra:
                        tail = piece[kz, rows:, :].astype(f32)
                        outs[1][pl.ds(device, 1), :] = tail[:1]
                        if kb == 0:
                            outs[2][pl.ds(block, 1), :] = (tail[1:2] + tail[2:3]) + tail[3:4]

    shapes = [jax.ShapeDtypeStruct((count * rows, cols), bf16)]
    if extra:
        shapes.append(jax.ShapeDtypeStruct((count, cols), f32))
        shapes.append(jax.ShapeDtypeStruct((nz * ny, cols), f32))
    outs = pl.pallas_call(
        kernel,
        out_shape=shapes,
        in_specs=[SMEM] + [WHOLE] * len(parts),
        out_specs=[WHOLE] * len(shapes),
        compiler_params=PARAMS,
        name="assemble_pieces",
    )(where, *parts)
    return outs if extra else outs[0]


def weight_grads(lefts, rights, first=0):
    tokens, width = lefts[0].shape
    widths = [right.shape[1] for right in rights]
    step = min(512, width - first)

    def kernel(*refs):
        ins, out = refs[:-1], refs[-1]
        at = 0
        for left, right, cols in zip(ins[: len(lefts)], ins[len(lefts) :], widths):
            out[:, at : at + cols] = dot(left[...], right[...], TN).astype(bf16)
            at += cols

    return pl.pallas_call(
        kernel,
        grid=((width - first) // step,),
        out_shape=jax.ShapeDtypeStruct((width - first, sum(widths)), bf16),
        in_specs=[pl.BlockSpec((tokens, step), lambda i: (0, i + first // step))] * len(lefts)
        + [pl.BlockSpec((tokens, cols), lambda i: (0, 0)) for cols in widths],
        out_specs=pl.BlockSpec((step, sum(widths)), lambda i: (i, 0)),
        compiler_params=PARAMS,
        name="weight_grads",
    )(*lefts, *rights)


def place_rows(where, pieces, sizes, norm=None, near=False, halves=0):
    nz, ny, nb = sizes
    width = pieces[0].shape[-1]
    tokens = sum(piece.size // width for piece in pieces)
    rows = width // (nz * ny * nb)
    aligned = rows % 128 == 0
    norm = list(norm or ())
    count = 1 + (1 + near) * aligned

    def kernel(where_ref, *refs):
        ins, rest = refs[: len(pieces)], refs[len(pieces) :]
        params, outs = rest[: len(norm)], rest[len(norm) :]
        full = outs[0]
        at = 0
        if halves:
            part = ins[0].shape[1] // halves
            for half in range(halves):
                for k in ORDER:
                    start = pl.multiple_of((where_ref[3] ^ half) * part, part)
                    full[at : at + part, :] = ins[0][where_ref[0] ^ k, pl.ds(start, part), :]
                    at += part
        for ref in () if halves else ins:
            values = ref[...]
            if norm:
                values, _ = normalize(values.astype(f32))
                values = (values * params[0][...] + params[1][...]).astype(bf16)
            full[at : at + ref.shape[0], :] = values
            at += ref.shape[0]
        for z in range(nz):
            for y in range(ny):
                for b in range(nb):
                    if count > 1:
                        source = ((z * ny + y) * nb + b) * rows
                        to = ((y * nb + b) * nz + z) * rows
                        outs[1][:, to : to + rows] = full[:, source : source + rows]
                    if count > 2:
                        source = (z * ny + (where_ref[1] ^ y)) * nb + (where_ref[2] ^ b)
                        source = pl.multiple_of(source * rows, rows)
                        to = ((b * ny + y) * nz + z) * rows
                        outs[2][:, to : to + rows] = full[:, pl.ds(source, rows)]

    outs = pl.pallas_call(
        kernel,
        out_shape=[jax.ShapeDtypeStruct((tokens, width), bf16)] * count,
        in_specs=[SMEM] + [WHOLE] * (len(pieces) + len(norm)),
        out_specs=[WHOLE] * count,
        compiler_params=PARAMS,
        name="place_rows",
    )(where, *pieces, *norm)
    if aligned:
        return outs
    groups = outs[0].reshape(tokens, nz, ny, nb, rows)
    outs = [outs[0], groups.transpose(0, 2, 3, 1, 4).reshape(tokens, width)]
    if near:
        groups = jnp.take(groups, jnp.arange(ny) ^ where[1], axis=2)
        groups = jnp.take(groups, jnp.arange(nb) ^ where[2], axis=3)
        outs.append(groups.transpose(0, 3, 2, 1, 4).reshape(tokens, width))
    return outs


def slot_of(k):
    return ((k & 1) << 1) | (k >> 1)


def natural(ref, lead, slot, flip, columns):
    first = ref[(*lead, flip, slot, slice(None), columns)]
    second = ref[(*lead, 1 - flip, slot, slice(None), columns)]
    return jnp.concatenate([first, second], axis=0)


def dot(left, right, dims):
    return lax.dot_general(left, right, (dims, ((), ())), preferred_element_type=f32)


NN, NT, TN = ((1,), (0,)), ((1,), (1,)), ((0,), (0,))


def decay_matrix(col, row):
    block = row.shape[-1]
    at = lax.broadcasted_iota(jnp.int32, (block, block), 0)
    to = lax.broadcasted_iota(jnp.int32, (block, block), 1)
    return jnp.where(at >= to, jnp.exp(jnp.minimum(col - row, 0.0)), 0.0)


def retention_forward(where, c_row, c_col, keyval, query, gate):
    ny, halves, nz, part, _ = keyval.shape
    block = halves * part

    def kernel(where_ref, row_ref, col_ref, kv_ref, q_ref, g_ref, y_ref, o_ref, s_ref, state):
        j = pl.program_id(0)

        @pl.when(j == 0)
        def _():
            state[...] = jnp.zeros_like(state)

        slot = slot_of((j // ny) ^ where_ref[0])
        ky = (j % ny) ^ where_ref[1]
        flip = where_ref[3]
        row, col = row_ref[j], col_ref[j]
        key = natural(kv_ref, (ky,), slot, flip, slice(0, DK))
        value = natural(kv_ref, (ky,), slot, flip, slice(DK, DK + DV))
        last = row[:, block - 1 :]

        @pl.when(ky == 0)
        def _():
            q = natural(q_ref, (), slot, flip, slice(None))
            state_bf = state[...].astype(bf16)
            s_ref[slot] = state_bf
            weights = (dot(q, key, NT) * decay_matrix(col, row)).astype(bf16)
            out = dot(weights, value, NN) + jnp.exp(col) * dot(q, state_bf, NN)
            normed, _ = normalize(out)
            g = natural(g_ref, (), slot, flip, slice(None))
            mixed = (g * jax.nn.sigmoid(g) * normed).astype(bf16)
            for half in range(2):
                rows = slice(half * part, (half + 1) * part)
                to = (1 - flip) if half else flip
                y_ref[to, slot] = mixed[rows]
                o_ref[to, slot] = out[rows]

        key_tail = (key.astype(f32) * jnp.exp(last - col)).astype(bf16)
        state[...] = jnp.exp(last) * state[...] + dot(key_tail, value, TN)

    return pl.pallas_call(
        kernel,
        grid=(nz * ny,),
        out_shape=[
            jax.ShapeDtypeStruct((halves, nz, part, DV), bf16),
            jax.ShapeDtypeStruct((halves, nz, part, DV), f32),
            jax.ShapeDtypeStruct((nz, DK, DV), bf16),
        ],
        in_specs=[SMEM] + [WHOLE] * 5,
        out_specs=[WHOLE] * 3,
        scratch_shapes=[pltpu.VMEM((DK, DV), f32)],
        compiler_params=PARAMS,
        name="retention_forward",
    )(where, c_row, c_col, keyval, query, gate)


def retention_backward(where, c_row, c_col, keyval, queries, grads, states, cosines, sines):
    ny, halves, nz, part, _ = queries.shape
    block = halves * part
    key_scale = DK ** (-0.5)

    def kernel(
        where_ref, row_ref, col_ref, kv_ref, q_ref, d_ref, s_ref, cos_ref, sin_ref, g_ref, state
    ):
        step = pl.program_id(0)
        j = nz * ny - 1 - step

        @pl.when(step == 0)
        def _():
            state[...] = jnp.zeros_like(state)

        slot = slot_of((j // ny) ^ where_ref[0])
        ky = (j % ny) ^ where_ref[1]
        flip = where_ref[3]
        row, col = row_ref[j], col_ref[j]
        last = row[:, block - 1 :]
        q = natural(q_ref, (ky,), slot, flip, slice(None))
        grad = natural(d_ref, (ky,), slot, flip, slice(None))
        entry = jnp.exp(col)

        @pl.when(ky == 0)
        def _():
            key = natural(kv_ref, (), slot, flip, slice(0, DK))
            value = natural(kv_ref, (), slot, flip, slice(DK, DK + DV))
            cos = natural(cos_ref, (), slot, flip, slice(None))
            sin = natural(sin_ref, (), slot, flip, slice(None))
            decays = decay_matrix(col, row)
            tail = jnp.exp(last - col)
            state_bf = state[...].astype(bf16)
            weights = (dot(q, key, NT) * decays).astype(bf16)
            scores = (dot(grad, value, NT) * decays).astype(bf16)
            grad_q = dot(scores, key, NN) + entry * dot(grad, s_ref[slot], NT)
            grad_k = dot(scores, q, TN) + tail * dot(value, state_bf, NT)
            grad_v = dot(weights, grad, TN) + tail * dot(key, state_bf, NN)
            grad_q = rotate(grad_q, cos, -sin).astype(bf16)
            grad_k = (rotate(grad_k, cos, -sin) * key_scale).astype(bf16)
            grad_v = grad_v.astype(bf16)
            for half in range(2):
                rows = slice(half * part, (half + 1) * part)
                to = (1 - flip) if half else flip
                g_ref[to, slot, :, :DK] = grad_k[rows]
                g_ref[to, slot, :, DK : DK + DV] = grad_v[rows]
                g_ref[to, slot, :, DK + DV :] = grad_q[rows]

        query_entry = (q.astype(f32) * entry).astype(bf16)
        state[...] = jnp.exp(last) * state[...] + dot(query_entry, grad, TN)

    return pl.pallas_call(
        kernel,
        grid=(nz * ny,),
        out_shape=jax.ShapeDtypeStruct((halves, nz, part, 2 * DK + DV), bf16),
        in_specs=[SMEM] + [WHOLE] * 8,
        out_specs=WHOLE,
        scratch_shapes=[pltpu.VMEM((DK, DV), f32)],
        compiler_params=PARAMS,
        name="retention_backward",
    )(where, c_row, c_col, keyval, queries, grads, states, cosines, sines)


def shards(
    hidden_in,
    log_decay,
    out_grad,
    ln1_gain,
    ln1_bias,
    w_query,
    w_key,
    w_value,
    w_gate,
    w_out,
    ln2_gain,
    ln2_bias,
    mlp_gate,
    mlp_up,
    mlp_down,
):
    nz, ny = lax.axis_size("row"), lax.axis_size("col")
    nb, nh = lax.axis_size("batch"), lax.axis_size("head")
    z, y = lax.axis_index("row"), lax.axis_index("col")
    b, x = lax.axis_index("batch"), lax.axis_index("head")
    block, width = hidden_in.shape[1:]
    rows = ln1_gain.shape[0]
    part = block // nh
    tokens = nz * block
    where = jnp.stack([z, y, b, x]).astype(jnp.int32)

    sizes = (nz, ny, nb)

    def to_heads(pieces):
        return jnp.stack([pieces[0]] + [swap(pieces[k], "row", k) for k in range(1, nz)])

    def spread(own, extra=0):
        parts = []
        for got in own:
            parts += [got, swap(got, "batch", 1)]
        return assemble_pieces(where, parts, ny, nb, extra)

    def spread_all(own):
        parts = lax.all_gather(own, ("col", "batch"))
        return assemble_weight(where, parts.reshape(ny, nb, *own.shape))

    def sum_grad(grad):
        grad = grad.reshape(ny * nb, nz, rows, -1)
        return lax.psum_scatter(grad, ("col", "batch"), scatter_dimension=0)

    def halves(values):
        values = values.reshape(nh, part, -1)
        return pick(values, x, 0), pick(values, 1 - x, 0)

    def gather_tokens(own):
        two = swap(own, "row", 2)
        pair = jnp.concatenate([own, two])
        return pair, swap(pair, "row", 1)

    def mirror(values):
        return swap(values, "head", 1)

    quarter = tokens // 4

    def reduce_far(*terms):
        far = sum(matmul_t(values[tokens // 2 :], weight) for values, weight in terms)
        far = far.astype(bf16)
        return mirror(far[quarter:]), mirror(far[:quarter])

    def reduce_near(got, *terms):
        near = sum(matmul_t(values[: tokens // 2], weight) for values, weight in terms)
        send = (near[quarter:] + got[0].astype(f32)).astype(bf16)
        return send, near[:quarter] + got[1].astype(f32)

    def reduce_one(send, keep):
        keep = keep + swap(send, "row", 1).astype(f32)
        return keep[part:].astype(bf16), keep[:part]

    def reduce_two(send, keep):
        return keep + swap(send, "row", 2).astype(f32)

    group = nz * rows

    def grad_near(grouped, other, got):
        near = outer_sum(grouped[:, : ny * group], other) + got.astype(f32)
        return near[:group], near[group:].astype(bf16)

    def grad_col(keep, send):
        for k in range(1, ny):
            piece = send[(k - 1) * group : k * group]
            keep = keep + swap(piece, "col", k).astype(f32)
        return keep.reshape(nz, rows, -1)

    def grad_row(*totals):
        pieces = []
        for k in range(nz):
            piece = [pick(total, z ^ k, 0).astype(bf16) for total in totals]
            piece = jnp.concatenate(piece, axis=-1)
            pieces.append(swap(piece, "row", k) if k else piece)
        return pieces

    def unpack(pieces, widths):
        return unpack_grads(where, pieces[0], pieces[1:], widths)

    def over_col(own):
        return [own] + [swap(own, "col", k) for k in range(1, ny)]

    gains = jnp.concatenate([ln1_gain, ln1_bias, ln2_gain, ln2_bias])[None]
    kv_own = to_heads(pack_first(where, (w_key, w_value), gains, log_decay[0], nz))
    own_in, other_in = halves(hidden_in[0])
    two_in = swap(own_in, "row", 2)
    kv_own, two_in, qg_own = tie(kv_own, two_in, (w_query, w_gate))
    kv_own = over_col(kv_own)
    one_in = swap(jnp.concatenate([own_in, two_in]), "row", 1)
    mirror_two = mirror(two_in)
    qg_own = to_heads(pack_weights(where, qg_own, nz))
    kv_own, one_in, mirror_two, qg_own, own_grad = tie(
        kv_own, one_in, mirror_two, qg_own, out_grad[0]
    )
    kv_w, small, decay = spread(kv_own, EXTRA)
    mirror_one = mirror(one_in)
    qg_w = spread(over_col(qg_own))
    grad_blocks = lax.all_gather(own_grad, "row")

    params = small[:, : 4 * rows].reshape(nz * ny * nb, 4, rows)
    gain_one, bias_one, gain_two, bias_two = params.transpose(1, 0, 2).reshape(4, width)
    running = jnp.cumsum(decay[:, :block], axis=-1)
    c_row, c_col = running[:, None, :], running[:, :, None]

    half_dim = DK // 2
    freqs = 10000.0 ** (-jnp.arange(half_dim, dtype=f32) / half_dim)
    block_at = (jnp.array(ORDER) ^ z) * ny + y
    half_at = jnp.arange(nh) ^ x
    positions = (
        block_at[None, :, None] * block + half_at[:, None, None] * part + jnp.arange(part)
    )
    angles = positions.astype(f32).reshape(-1)[:, None] * freqs[None, :]
    cosines, sines = jnp.cos(angles), jnp.sin(angles)
    key_scale = DK ** (-0.5)

    first_bf, first_groups, first_near = place_rows(
        where,
        (own_in, two_in, one_in, other_in, mirror_two, mirror_one),
        sizes,
        (gain_one[None], bias_one[None]),
        near=True,
    )
    key_value = matmul(first_bf, kv_w)
    key_bf = (rotate(key_value[:, :DK], cosines, sines) * key_scale).astype(bf16)
    value_bf = key_value[:, DK:].astype(bf16)

    def split(values):
        return values.reshape(nh, nz, part, -1)

    def gather_col(values):
        return jnp.stack([values] + [swap(values, "col", k) for k in range(1, ny)])

    keyval = split(jnp.concatenate([key_bf, value_bf], axis=-1))
    query_gate = matmul(after(first_bf, keyval), qg_w)
    query_bf = rotate(query_gate[:, :DK], cosines, sines).astype(bf16)
    gate = query_gate[:, DK:]

    out_own = to_heads(pack_weights(where, (after(w_out, keyval).T,), nz))
    keyvals, query_bf, out_own = tie(gather_col(keyval), query_bf, out_own)
    out_w = spread(over_col(out_own))
    feed = after((mlp_gate, mlp_up, mlp_down), out_own)
    mlp_own = to_heads(pack_weights(where, (feed[0], feed[1], feed[2].T), nz))
    mixed, retained, states = retention_forward(
        where, c_row, c_col, keyvals, split(query_bf), split(gate)
    )
    mixed, mlp_own = tie(mixed, mlp_own)
    mlp_w = spread_all(mlp_own)
    units = mlp_w.shape[1] // 3
    up_w, down_w = mlp_w[:, : 2 * units], mlp_w[:, 2 * units :]
    mixed_bf = mixed.reshape(tokens, DV)
    queries = gather_col(split(after(query_bf, mixed)))

    inputs = own_in.astype(f32)
    got = reduce_far((mixed_bf, out_w))
    send, keep = reduce_near(got, (mixed_bf, out_w))
    down_bf, down_groups = place_rows(where, (grad_blocks,), sizes, halves=nh)
    send, keep = reduce_one(send, keep)
    middle = inputs + reduce_two(send, keep)
    middle, queries, down_bf = tie(middle, queries, down_bf)
    scaled_two, rstd_two = normalize(middle)
    pair, one = gather_tokens((scaled_two * gain_two + bias_two).astype(bf16))
    second_bf, second_groups = place_rows(where, (pair, one, mirror(pair), mirror(one)), sizes)
    up = matmul(second_bf, up_w)
    up_gate, up_lin = up[:, :units], up[:, units:]
    gelu_cdf = 0.5 * (1.0 + lax.erf(up_gate * (0.5**0.5)))
    gelu_val = up_gate * gelu_cdf
    gelu_slope = gelu_cdf + up_gate * jnp.exp(-0.5 * up_gate * up_gate) * (2.0 * jnp.pi) ** -0.5
    hidden_bf = (gelu_val * up_lin).astype(bf16)

    grad_hidden = matmul(down_bf, down_w)
    grad_upgate = (grad_hidden * up_lin * gelu_slope).astype(bf16)
    grad_uplin = (grad_hidden * gelu_val).astype(bf16)
    grad_up = jnp.concatenate([grad_upgate, grad_uplin], axis=-1)
    got = reduce_far((grad_up, up_w))
    feed_grad = weight_grads((second_groups, down_groups), (grad_up, hidden_bf))
    send, keep = reduce_near(got, (grad_up, up_w))
    send, feed_grad, hidden_late = tie(send, feed_grad, hidden_bf)
    feed_sum = sum_grad(feed_grad)
    result_got = reduce_far((hidden_late, down_w))
    send, keep = reduce_one(send, keep)
    grad_two = reduce_two(send, keep)
    result_send, result_keep = reduce_near(result_got, (hidden_late, down_w))
    grad_two, result_send = tie(grad_two, result_send)
    grad_middle = halves(out_grad[0])[0].astype(f32) + norm_back(grad_two * gain_two, scaled_two, rstd_two)
    pair, one = gather_tokens(grad_middle.astype(bf16))
    attn_bf, attn_groups = place_rows(where, (pair, one, mirror(pair), mirror(one)), sizes)
    attn_bf, attn_groups, result_send, feed_sum = tie(
        attn_bf, attn_groups, result_send, feed_sum
    )

    grp_norm, grp_rstd = normalize(retained.reshape(tokens, DV))
    gate_sig = jax.nn.sigmoid(gate)
    gate_act = gate * gate_sig
    grad_mixed = matmul(attn_bf, out_w)
    grad_gate = (grad_mixed * grp_norm * (gate_sig * (1.0 + gate * (1.0 - gate_sig)))).astype(bf16)
    ret_bf = norm_back(grad_mixed * gate_act, grp_norm, grp_rstd).astype(bf16)
    ret_all = gather_col(split(ret_bf))

    late_gate, late_mixed = after((grad_gate, mixed_bf), ret_bf)
    both_sum = sum_grad(weight_grads((first_groups, attn_groups), (late_gate, late_mixed)))
    result_send, result_keep = reduce_one(result_send, result_keep)
    feed_pieces = grad_row(feed_sum)
    ret_all, result_send = tie(ret_all, result_send)
    result = (middle + reduce_two(result_send, result_keep)).astype(bf16)

    grad_kvq = retention_backward(
        where, c_row, c_col, keyval, queries, ret_all, states, split(cosines), split(sines)
    )
    grad_kvq = grad_kvq.reshape(tokens, -1)
    grad_qg = jnp.concatenate([grad_kvq[:, DK + DV :], grad_gate], axis=-1)
    terms = ((grad_kvq[:, : DK + DV], kv_w), (grad_qg, qg_w))
    got = reduce_far(*terms)
    kvq_far = weight_grads((first_near,), (grad_kvq,), ny * group)
    send, keep = reduce_near(got, *terms)
    kvq_keep, kvq_send = grad_near(first_near, grad_kvq, swap(kvq_far, "batch", 1))
    send, kvq_send, result, feed_pieces = tie(send, kvq_send, result, feed_pieces)
    grad_gates, grad_ups, grad_downs = unpack(feed_pieces, (units, units, units))
    send, keep = reduce_one(send, keep)
    grad_one = reduce_two(send, keep)
    kvq_sum = grad_col(kvq_keep, kvq_send)
    both_pieces = grad_row(both_sum)
    grad_one, kvq_sum, both_pieces, grad_gates, grad_ups, grad_downs = tie(
        grad_one, kvq_sum, both_pieces, grad_gates, grad_ups, grad_downs
    )
    kvq_pieces = grad_row(kvq_sum)
    result_other = mirror(result)

    scaled_own, rstd_own = normalize(inputs)
    grad_in = grad_middle + norm_back(grad_one * gain_one, scaled_own, rstd_own)
    grad_in_other = mirror(grad_in)
    grad_g, grad_outs = unpack(both_pieces, (DV, DV))
    grad_k, grad_v, grad_q = unpack(kvq_pieces, (DK, DV, DK))

    def join(own, other):
        first = jnp.where(x == 0, own, other)
        second = jnp.where(x == 0, other, own)
        return jnp.concatenate([first, second]).reshape(1, block, width)

    norm_sums = jnp.stack(
        [
            jnp.sum(grad_one * scaled_own, axis=0),
            jnp.sum(grad_one, axis=0),
            jnp.sum(grad_two * scaled_two, axis=0),
            jnp.sum(grad_two, axis=0),
        ]
    )
    norm_sums = norm_sums + swap(norm_sums, "head", 1)
    norm_sums = norm_sums.reshape(4, nz, ny, nb, rows)
    for name, axis in (("batch", 3), ("col", 2), ("row", 1)):
        me = lax.axis_index(name)
        summed = pick(norm_sums, me, axis)
        for k in range(1, lax.axis_size(name)):
            summed = summed + swap(pick(norm_sums, me ^ k, axis), name, k)
        norm_sums = summed

    return (
        join(result, result_other),
        join(grad_in, grad_in_other),
        norm_sums[0],
        norm_sums[1],
        grad_q,
        grad_k,
        grad_v,
        grad_g,
        grad_outs.T,
        norm_sums[2],
        norm_sums[3],
        grad_gates,
        grad_ups,
        grad_downs.T,
    )


def solution(mesh):
    seq = ("row", "col")
    tokens = P("batch", seq, None)
    params = P((*seq, "batch"))
    by_rows = P((*seq, "batch"), "head")
    by_cols = P("head", (*seq, "batch"))

    def run(*arrays):
        rows = arrays[1].shape[1] // mesh.shape["head"]
        sizes = (rows, mesh.shape["seq"] // rows, mesh.shape["batch"], mesh.shape["head"])
        order = [mesh.axis_names.index(n) for n in ("seq", "batch", "head")]
        fine = Mesh(
            mesh.devices.transpose(order).reshape(sizes), ("row", "col", "batch", "head")
        )
        weights = (by_rows, by_rows, by_rows, by_rows, by_cols)
        feeds = (by_rows, by_rows, by_cols)
        return jax.shard_map(
            shards,
            mesh=fine,
            in_specs=(
                tokens,
                P("batch", "head", seq),
                tokens,
                params,
                params,
                *weights,
                params,
                params,
                *feeds,
            ),
            out_specs=(tokens, tokens, params, params, *weights, params, params, *feeds),
            check_vma=False,
        )(*arrays)

    return run
```

```python
import jax
import jax.numpy as jnp
from jax import lax
from jax.experimental import pallas as pl
from jax.experimental.pallas import tpu as pltpu
from jax.sharding import Mesh
from jax.sharding import PartitionSpec as P

DK = 256
DV = 512

epsilon = 1e-05
f32 = jnp.float32
bf16 = jnp.bfloat16
VMEM_LIMIT = 12 * 1024 * 1024

ORDER = (0, 2, 1, 3)


def swap(values, axis, k):
    count = lax.axis_size(axis)
    return lax.ppermute(values, axis, [(i, i ^ k) for i in range(count)])


def pick(values, index, axis):
    return lax.dynamic_index_in_dim(values, index, axis, keepdims=False)


def tie(*values):
    return lax.optimization_barrier(values)


def after(values, *others):
    return tie(values, others)[0]


def matmul(values, weight):
    return jnp.dot(values, weight, preferred_element_type=f32)


def matmul_t(values, weight):
    return lax.dot_general(values, weight, (((1,), (1,)), ((), ())), preferred_element_type=f32)


def outer_sum(values, other):
    return lax.dot_general(values, other, (((0,), (0,)), ((), ())), preferred_element_type=f32)


def normalize(values):
    center = values - jnp.mean(values, axis=-1, keepdims=True)
    rstd = lax.rsqrt(jnp.mean(center * center, axis=-1, keepdims=True) + epsilon)
    return center * rstd, rstd


def norm_back(scaled_grad, scaled, rstd):
    return rstd * (
        scaled_grad
        - jnp.mean(scaled_grad, axis=-1, keepdims=True)
        - scaled * jnp.mean(scaled_grad * scaled, axis=-1, keepdims=True)
    )


def rotate(values, cosines, sines):
    half_dim = values.shape[-1] // 2
    first_half = values[..., :half_dim]
    second_half = values[..., half_dim:]
    return jnp.concatenate(
        [first_half * cosines - second_half * sines, first_half * sines + second_half * cosines],
        axis=-1,
    )


SMEM = pl.BlockSpec(memory_space=pltpu.SMEM)
WHOLE = pl.BlockSpec(memory_space=pltpu.VMEM)
PARAMS = pltpu.CompilerParams(vmem_limit_bytes=VMEM_LIMIT)


def pack_weights(where, weights, nz):
    rows = weights[0].shape[0]
    widths = [w.shape[1] // nz for w in weights]

    def kernel(where_ref, *refs):
        ins, outs = refs[: len(weights)], refs[len(weights) :]
        for k in range(nz):
            target = where_ref[0] ^ k
            at = 0
            for ref, width in zip(ins, widths):
                start = pl.multiple_of(target * width, width)
                outs[k][:, at : at + width] = ref[:, pl.ds(start, width)]
                at += width

    return pl.pallas_call(
        kernel,
        out_shape=[jax.ShapeDtypeStruct((rows, sum(widths)), bf16)] * nz,
        in_specs=[SMEM] + [WHOLE] * len(weights),
        out_specs=[WHOLE] * nz,
        compiler_params=PARAMS,
        name="pack_weights",
    )(where, *weights)


EXTRA = 16


def pack_first(where, weights, gains, decays, nz):
    rows = weights[0].shape[0]
    widths = [w.shape[1] // nz for w in weights]
    block = decays.shape[1]
    gains = jnp.pad(gains, ((0, 0), (0, sum(widths) - gains.shape[1])))

    def kernel(where_ref, gain_ref, decay_ref, *refs):
        ins, outs = refs[: len(weights)], refs[len(weights) :]
        at = lax.broadcasted_iota(jnp.int32, (EXTRA, 1), 0)
        gain_rows = jnp.where(at == 0, gain_ref[...].astype(f32), 0.0)
        for k in range(nz):
            target = where_ref[0] ^ k
            to = 0
            for ref, width in zip(ins, widths):
                start = pl.multiple_of(target * width, width)
                outs[k][:rows, to : to + width] = ref[:, pl.ds(start, width)]
                to += width
            rest = decay_ref[pl.ds(target, 1), :]
            parts = gain_rows[:, :block]
            for row in range(1, 4):
                part = rest.astype(bf16).astype(f32)
                parts = jnp.where(at == row, part, parts)
                rest = rest - part
            outs[k][rows:, :] = gain_rows.astype(bf16)
            outs[k][rows:, :block] = parts.astype(bf16)

    return pl.pallas_call(
        kernel,
        out_shape=[jax.ShapeDtypeStruct((rows + EXTRA, sum(widths)), bf16)] * nz,
        in_specs=[SMEM] + [WHOLE] * (2 + len(weights)),
        out_specs=[WHOLE] * nz,
        compiler_params=PARAMS,
        name="pack_first",
    )(where, gains, decays, *weights)


def unpack_grads(where, own, pieces, widths):
    nz = len(pieces) + 1
    rows = own.shape[0]

    def kernel(where_ref, *refs):
        ins, outs = refs[:nz], refs[nz:]
        for k in range(nz):
            target = where_ref[0] ^ k
            at = 0
            for ref, width in zip(outs, widths):
                start = pl.multiple_of(target * width, width)
                ref[:, pl.ds(start, width)] = ins[k][:, at : at + width].astype(f32)
                at += width

    return pl.pallas_call(
        kernel,
        out_shape=[jax.ShapeDtypeStruct((rows, nz * width), f32) for width in widths],
        in_specs=[SMEM] + [WHOLE] * nz,
        out_specs=[WHOLE] * len(widths),
        compiler_params=PARAMS,
        name="unpack_grads",
    )(where, own, *pieces)


def assemble_weight(where, parts):
    ny, nb, nz, rows, cols = parts.shape

    def kernel(where_ref, ref, out):
        for y in range(ny):
            for b in range(nb):
                for kz in range(nz):
                    at = ((where_ref[0] ^ kz) * ny + y) * nb + b
                    out[pl.ds(pl.multiple_of(at * rows, rows), rows), :] = ref[y, b, kz]

    return pl.pallas_call(
        kernel,
        out_shape=jax.ShapeDtypeStruct((nz * ny * nb * rows, cols), bf16),
        in_specs=[SMEM, WHOLE],
        out_specs=WHOLE,
        compiler_params=PARAMS,
        name="assemble_weight",
    )(where, parts)


def assemble_pieces(where, parts, ny, nb, extra=0):
    nz, rows, cols = parts[0].shape
    rows -= extra
    count = nz * ny * nb

    def kernel(where_ref, *refs):
        ins, outs = refs[: len(parts)], refs[len(parts) :]
        for ky in range(ny):
            for kb in range(nb):
                for kz in range(nz):
                    block = (where_ref[0] ^ kz) * ny + (where_ref[1] ^ ky)
                    device = block * nb + (where_ref[2] ^ kb)
                    piece = ins[ky * nb + kb]
                    at = pl.multiple_of(device * rows, rows)
                    outs[0][pl.ds(at, rows), :] = piece[kz, :rows, :]
                    if extra:
                        tail = piece[kz, rows:, :].astype(f32)
                        outs[1][pl.ds(device, 1), :] = tail[:1]
                        if kb == 0:
                            outs[2][pl.ds(block, 1), :] = (tail[1:2] + tail[2:3]) + tail[3:4]

    shapes = [jax.ShapeDtypeStruct((count * rows, cols), bf16)]
    if extra:
        shapes.append(jax.ShapeDtypeStruct((count, cols), f32))
        shapes.append(jax.ShapeDtypeStruct((nz * ny, cols), f32))
    outs = pl.pallas_call(
        kernel,
        out_shape=shapes,
        in_specs=[SMEM] + [WHOLE] * len(parts),
        out_specs=[WHOLE] * len(shapes),
        compiler_params=PARAMS,
        name="assemble_pieces",
    )(where, *parts)
    return outs if extra else outs[0]


def row_groups(where, left, sizes, near):
    nz, ny, nb = sizes
    groups = left.reshape(left.shape[0], nz, ny, nb, -1)
    if near:
        groups = jnp.take(groups, jnp.arange(ny) ^ where[1], axis=2)
        groups = jnp.take(groups, jnp.arange(nb) ^ where[2], axis=3)
        return groups.transpose(0, 3, 2, 1, 4).reshape(left.shape)
    return groups.transpose(0, 2, 3, 1, 4).reshape(left.shape)


def weight_grads(where, lefts, rights, sizes, near=None, got=None):
    nz, ny, nb = sizes
    width = lefts[0].shape[1]
    rows = width // (nz * ny * nb)
    group = nz * rows
    steps = ny * nb if near is None else ny
    widths = [right.shape[1] for right in rights]
    total = sum(widths)
    aligned = rows % 128 == 0
    if not aligned:
        lefts = [row_groups(where, left, sizes, near is not None) for left in lefts]

    def columns(where_ref, left, step):
        if not aligned:
            start = (step if near is None else near * ny + step) * group
            return left[:, pl.ds(pl.multiple_of(start, group), group)]
        if near is None:
            y, b = step // nb, step % nb
        else:
            y, b = where_ref[1] ^ step, where_ref[2] ^ near
        tiles = []
        for z in range(nz):
            start = pl.multiple_of(((z * ny + y) * nb + b) * rows, rows)
            tiles.append(left[:, pl.ds(start, rows)])
        return jnp.concatenate(tiles, axis=1)

    def kernel(where_ref, *refs):
        ins, rest = refs[: len(lefts)], refs[len(lefts) :]
        others, rest = rest[: len(rights)], rest[len(rights) :]
        step = pl.program_id(0)
        at = 0
        for left, right, cols in zip(ins, others, widths):
            value = dot(columns(where_ref, left, step), right[...], TN)
            to = slice(at, at + cols)
            if got is None:
                rest[0][:, to] = value.astype(bf16)
            else:
                value = value + rest[0][:, to].astype(f32)

                @pl.when(step == 0)
                def _():
                    rest[1][:, to] = value

                rest[2][:, to] = value.astype(bf16)
            at += cols

    blocks = pl.BlockSpec((group, total), lambda i: (i, 0))
    shape = jax.ShapeDtypeStruct((steps * group, total), bf16)
    if got is not None:
        blocks = [pl.BlockSpec((group, total), lambda i: (0, 0)), blocks]
        shape = [jax.ShapeDtypeStruct((group, total), f32), shape]
    return pl.pallas_call(
        kernel,
        grid=(steps,),
        out_shape=shape,
        in_specs=[SMEM]
        + [WHOLE] * (len(lefts) + len(rights))
        + ([] if got is None else [pl.BlockSpec((group, total), lambda i: (i, 0))]),
        out_specs=blocks,
        compiler_params=PARAMS,
        name="weight_grads",
    )(where, *lefts, *rights, *(() if got is None else (got,)))


def order_rows(where, values):
    halves, nz, part, cols = values.shape

    def kernel(where_ref, ref, out):
        for z in range(nz):
            for x in range(halves):
                out[z, x] = ref[where_ref[3] ^ x, slot_of(where_ref[0] ^ z)]

    return pl.pallas_call(
        kernel,
        out_shape=jax.ShapeDtypeStruct((nz, halves, part, cols), values.dtype),
        in_specs=[SMEM, WHOLE],
        out_specs=WHOLE,
        compiler_params=PARAMS,
        name="order_rows",
    )(where, values)


def place_rows(where, pieces, norm=None, halves=0):
    width = pieces[0].shape[-1]
    tokens = sum(piece.size // width for piece in pieces)
    norm = list(norm or ())

    def kernel(where_ref, *refs):
        ins, params, full = refs[: len(pieces)], refs[len(pieces) : -1], refs[-1]
        at = 0
        if halves:
            part = ins[0].shape[1] // halves
            for half in range(halves):
                for k in ORDER:
                    start = pl.multiple_of((where_ref[3] ^ half) * part, part)
                    full[at : at + part, :] = ins[0][where_ref[0] ^ k, pl.ds(start, part), :]
                    at += part
        for ref in () if halves else ins:
            values = ref[...]
            if norm:
                values, _ = normalize(values.astype(f32))
                values = (values * params[0][...] + params[1][...]).astype(bf16)
            full[at : at + ref.shape[0], :] = values
            at += ref.shape[0]

    return pl.pallas_call(
        kernel,
        out_shape=jax.ShapeDtypeStruct((tokens, width), bf16),
        in_specs=[SMEM] + [WHOLE] * (len(pieces) + len(norm)),
        out_specs=WHOLE,
        compiler_params=PARAMS,
        name="place_rows",
    )(where, *pieces, *norm)


def slot_of(k):
    return ((k & 1) << 1) | (k >> 1)


def natural(ref, slot, flip, columns=slice(None)):
    first = ref[flip, slot, :, columns]
    second = ref[1 - flip, slot, :, columns]
    return jnp.concatenate([first, second], axis=0)


def choose(refs, ky, slot, flip, columns=slice(None)):
    values = natural(refs[0], slot, flip, columns)
    for k in range(1, len(refs)):
        values = jnp.where(ky == k, natural(refs[k], slot, flip, columns), values)
    return values


def dot(left, right, dims):
    return lax.dot_general(left, right, (dims, ((), ())), preferred_element_type=f32)


NN, NT, TN = ((1,), (0,)), ((1,), (1,)), ((0,), (0,))


def decay_matrix(col, row):
    block = row.shape[-1]
    at = lax.broadcasted_iota(jnp.int32, (block, block), 0)
    to = lax.broadcasted_iota(jnp.int32, (block, block), 1)
    return jnp.where(at >= to, jnp.exp(jnp.minimum(col - row, 0.0)), 0.0)


def retention_forward(where, c_row, c_col, keyvals, query, gate):
    ny = len(keyvals)
    halves, nz, part, _ = query.shape
    block = halves * part

    def kernel(where_ref, row_ref, col_ref, *refs):
        kv_refs, (q_ref, g_ref, y_ref, o_ref, s_ref, state) = refs[:ny], refs[ny:]
        j = pl.program_id(0)

        @pl.when(j == 0)
        def _():
            state[...] = jnp.zeros_like(state)

        slot = slot_of((j // ny) ^ where_ref[0])
        ky = (j % ny) ^ where_ref[1]
        flip = where_ref[3]
        row, col = row_ref[j], col_ref[j]
        key = choose(kv_refs, ky, slot, flip, slice(0, DK))
        value = choose(kv_refs, ky, slot, flip, slice(DK, DK + DV))
        last = row[:, block - 1 :]

        @pl.when(ky == 0)
        def _():
            q = natural(q_ref, slot, flip)
            state_bf = state[...].astype(bf16)
            s_ref[slot] = state_bf
            weights = (dot(q, key, NT) * decay_matrix(col, row)).astype(bf16)
            out = dot(weights, value, NN) + jnp.exp(col) * dot(q, state_bf, NN)
            normed, _ = normalize(out)
            g = natural(g_ref, slot, flip)
            mixed = (g * jax.nn.sigmoid(g) * normed).astype(bf16)
            for half in range(2):
                rows = slice(half * part, (half + 1) * part)
                to = (1 - flip) if half else flip
                y_ref[to, slot] = mixed[rows]
                o_ref[to, slot] = out[rows]

        key_tail = (key.astype(f32) * jnp.exp(last - col)).astype(bf16)
        state[...] = jnp.exp(last) * state[...] + dot(key_tail, value, TN)

    return pl.pallas_call(
        kernel,
        grid=(nz * ny,),
        out_shape=[
            jax.ShapeDtypeStruct((halves, nz, part, DV), bf16),
            jax.ShapeDtypeStruct((halves, nz, part, DV), f32),
            jax.ShapeDtypeStruct((nz, DK, DV), bf16),
        ],
        in_specs=[SMEM] + [WHOLE] * (4 + ny),
        out_specs=[WHOLE] * 3,
        scratch_shapes=[pltpu.VMEM((DK, DV), f32)],
        compiler_params=PARAMS,
        name="retention_forward",
    )(where, c_row, c_col, *keyvals, query, gate)


def retention_backward(where, c_row, c_col, keyval, queries, grads, states, cosines, sines):
    ny = len(queries)
    halves, nz, part, _ = keyval.shape
    block = halves * part
    key_scale = DK ** (-0.5)

    def kernel(where_ref, row_ref, col_ref, *refs):
        q_refs, d_refs, rest = refs[:ny], refs[ny : 2 * ny], refs[2 * ny :]
        kv_ref, s_ref, cos_ref, sin_ref, g_ref, state = rest
        step = pl.program_id(0)
        j = nz * ny - 1 - step

        @pl.when(step == 0)
        def _():
            state[...] = jnp.zeros_like(state)

        slot = slot_of((j // ny) ^ where_ref[0])
        ky = (j % ny) ^ where_ref[1]
        flip = where_ref[3]
        row, col = row_ref[j], col_ref[j]
        last = row[:, block - 1 :]
        q = choose(q_refs, ky, slot, flip)
        grad = choose(d_refs, ky, slot, flip)
        entry = jnp.exp(col)

        @pl.when(ky == 0)
        def _():
            key = natural(kv_ref, slot, flip, slice(0, DK))
            value = natural(kv_ref, slot, flip, slice(DK, DK + DV))
            cos = natural(cos_ref, slot, flip)
            sin = natural(sin_ref, slot, flip)
            decays = decay_matrix(col, row)
            tail = jnp.exp(last - col)
            state_bf = state[...].astype(bf16)
            weights = (dot(q, key, NT) * decays).astype(bf16)
            scores = (dot(grad, value, NT) * decays).astype(bf16)
            grad_q = dot(scores, key, NN) + entry * dot(grad, s_ref[slot], NT)
            grad_k = dot(scores, q, TN) + tail * dot(value, state_bf, NT)
            grad_v = dot(weights, grad, TN) + tail * dot(key, state_bf, NN)
            grad_q = rotate(grad_q, cos, -sin).astype(bf16)
            grad_k = (rotate(grad_k, cos, -sin) * key_scale).astype(bf16)
            grad_v = grad_v.astype(bf16)
            for half in range(2):
                rows = slice(half * part, (half + 1) * part)
                to = (1 - flip) if half else flip
                g_ref[to, slot, :, :DK] = grad_k[rows]
                g_ref[to, slot, :, DK : DK + DV] = grad_v[rows]
                g_ref[to, slot, :, DK + DV :] = grad_q[rows]

        query_entry = (q.astype(f32) * entry).astype(bf16)
        state[...] = jnp.exp(last) * state[...] + dot(query_entry, grad, TN)

    return pl.pallas_call(
        kernel,
        grid=(nz * ny,),
        out_shape=jax.ShapeDtypeStruct((halves, nz, part, 2 * DK + DV), bf16),
        in_specs=[SMEM] + [WHOLE] * (6 + 2 * ny),
        out_specs=WHOLE,
        scratch_shapes=[pltpu.VMEM((DK, DV), f32)],
        compiler_params=PARAMS,
        name="retention_backward",
    )(where, c_row, c_col, *queries, *grads, keyval, states, cosines, sines)


def shards(
    hidden_in,
    log_decay,
    out_grad,
    ln1_gain,
    ln1_bias,
    w_query,
    w_key,
    w_value,
    w_gate,
    w_out,
    ln2_gain,
    ln2_bias,
    mlp_gate,
    mlp_up,
    mlp_down,
):
    nz, ny = lax.axis_size("row"), lax.axis_size("col")
    nb, nh = lax.axis_size("batch"), lax.axis_size("head")
    z, y = lax.axis_index("row"), lax.axis_index("col")
    b, x = lax.axis_index("batch"), lax.axis_index("head")
    block, width = hidden_in.shape[1:]
    rows = ln1_gain.shape[0]
    part = block // nh
    tokens = nz * block
    where = jnp.stack([z, y, b, x]).astype(jnp.int32)

    sizes = (nz, ny, nb)

    def to_heads(pieces):
        return jnp.stack([pieces[0]] + [swap(pieces[k], "row", k) for k in range(1, nz)])

    def spread(own, extra=0):
        parts = []
        for got in own:
            parts += [got, swap(got, "batch", 1)]
        return assemble_pieces(where, parts, ny, nb, extra)

    def spread_all(own):
        parts = lax.all_gather(own, ("col", "batch"))
        return assemble_weight(where, parts.reshape(ny, nb, *own.shape))

    def sum_grad(grad):
        grad = grad.reshape(ny * nb, nz, rows, -1)
        return lax.psum_scatter(grad, ("col", "batch"), scatter_dimension=0)

    def halves(values):
        values = values.reshape(nh, part, -1)
        return pick(values, x, 0), pick(values, 1 - x, 0)

    def gather_tokens(own):
        two = swap(own, "row", 2)
        pair = jnp.concatenate([own, two])
        return pair, swap(pair, "row", 1)

    def mirror(values):
        return swap(values, "head", 1)

    quarter = tokens // 4

    def reduce_far(*terms):
        far = sum(matmul_t(values[tokens // 2 :], weight) for values, weight in terms)
        far = far.astype(bf16)
        return mirror(far[quarter:]), mirror(far[:quarter])

    def reduce_near(got, *terms):
        near = sum(matmul_t(values[: tokens // 2], weight) for values, weight in terms)
        send = (near[quarter:] + got[0].astype(f32)).astype(bf16)
        return send, near[:quarter] + got[1].astype(f32)

    def reduce_one(send, keep):
        keep = keep + swap(send, "row", 1).astype(f32)
        return keep[part:].astype(bf16), keep[:part]

    def reduce_two(send, keep):
        return keep + swap(send, "row", 2).astype(f32)

    group = nz * rows

    def grad_col(keep, send):
        for k in range(1, ny):
            keep = keep + swap(send[k * group : (k + 1) * group], "col", k).astype(f32)
        return keep.reshape(nz, rows, -1)

    def grad_row(*totals):
        pieces = []
        for k in range(nz):
            piece = [pick(total, z ^ k, 0).astype(bf16) for total in totals]
            piece = jnp.concatenate(piece, axis=-1)
            pieces.append(swap(piece, "row", k) if k else piece)
        return pieces

    def unpack(pieces, widths):
        return unpack_grads(where, pieces[0], pieces[1:], widths)

    def over_col(own):
        return [own] + [swap(own, "col", k) for k in range(1, ny)]

    gains = jnp.concatenate([ln1_gain, ln1_bias, ln2_gain, ln2_bias])[None]
    kvq_own = to_heads(pack_first(where, (w_key, w_value, w_query), gains, log_decay[0], nz))
    own_in, other_in = halves(hidden_in[0])
    two_in = swap(own_in, "row", 2)
    kvq_own, two_in, gate_own = tie(kvq_own, two_in, w_gate)
    kvq_own = over_col(kvq_own)
    one_in = swap(jnp.concatenate([own_in, two_in]), "row", 1)
    mirror_two = mirror(two_in)
    gate_own = to_heads(pack_weights(where, (gate_own,), nz))
    kvq_own, one_in, mirror_two, gate_own, out_own = tie(
        kvq_own, one_in, mirror_two, gate_own, w_out
    )
    kvq_w, small, decay = spread(kvq_own, EXTRA)
    mirror_one = mirror(one_in)
    gate_own = over_col(gate_own)
    out_own = to_heads(pack_weights(where, (out_own.T,), nz))
    kvq_w, mirror_one, gate_own, out_own, feed = tie(
        kvq_w, mirror_one, gate_own, out_own, (mlp_gate, mlp_up, mlp_down)
    )
    out_w = spread_all(out_own)
    gate_w = spread(gate_own)
    mlp_own = to_heads(pack_weights(where, (feed[0], feed[1], feed[2].T), nz))

    params = small[:, : 4 * rows].reshape(nz * ny * nb, 4, rows)
    gain_one, bias_one, gain_two, bias_two = params.transpose(1, 0, 2).reshape(4, width)
    running = jnp.cumsum(decay[:, :block], axis=-1)
    c_row, c_col = running[:, None, :], running[:, :, None]

    half_dim = DK // 2
    freqs = 10000.0 ** (-jnp.arange(half_dim, dtype=f32) / half_dim)
    block_at = (jnp.array(ORDER) ^ z) * ny + y
    half_at = jnp.arange(nh) ^ x
    positions = (
        block_at[None, :, None] * block + half_at[:, None, None] * part + jnp.arange(part)
    )
    angles = positions.astype(f32).reshape(-1)[:, None] * freqs[None, :]
    cosines, sines = jnp.cos(angles), jnp.sin(angles)
    key_scale = DK ** (-0.5)

    first_bf = place_rows(
        where,
        (own_in, two_in, one_in, other_in, mirror_two, mirror_one),
        (gain_one[None], bias_one[None]),
    )
    projected = matmul(first_bf, kvq_w)
    key_bf = (rotate(projected[:, :DK], cosines, sines) * key_scale).astype(bf16)
    value_bf = projected[:, DK : DK + DV].astype(bf16)
    query_bf = rotate(projected[:, DK + DV :], cosines, sines).astype(bf16)

    def split(values):
        return values.reshape(nh, nz, part, -1)

    keyval = split(jnp.concatenate([key_bf, value_bf], axis=-1))
    gate = matmul(after(first_bf, keyval), gate_w)

    keyvals, mlp_own, gate = tie(over_col(keyval), mlp_own, gate)
    mixed, retained, states = retention_forward(
        where, c_row, c_col, keyvals, split(query_bf), split(gate)
    )
    grad_blocks = lax.all_gather(after(out_grad[0], out_w), "row")
    mlp_w = spread_all(after(mlp_own, grad_blocks))
    units = mlp_w.shape[1] // 3
    up_w, down_w = mlp_w[:, : 2 * units], mlp_w[:, 2 * units :]
    mixed_bf = mixed.reshape(tokens, DV)
    queries = over_col(split(after(query_bf, mixed)))

    inputs = own_in.astype(f32)
    got = reduce_far((mixed_bf, out_w))
    send, keep = reduce_near(got, (mixed_bf, out_w))
    send, keep = reduce_one(send, keep)
    middle = inputs + reduce_two(send, keep)
    down_bf = place_rows(where, (grad_blocks,), halves=nh)
    middle, queries, down_bf = tie(middle, queries, down_bf)
    scaled_two, rstd_two = normalize(middle)
    pair, one = gather_tokens((scaled_two * gain_two + bias_two).astype(bf16))
    one, up_w, down_w = tie(one, up_w, down_w)
    second_bf = place_rows(where, (pair, one, mirror(pair), mirror(one)))
    up = matmul(second_bf, up_w)
    up_gate, up_lin = up[:, :units], up[:, units:]
    gelu_cdf = 0.5 * (1.0 + lax.erf(up_gate * (0.5**0.5)))
    gelu_val = up_gate * gelu_cdf
    gelu_slope = gelu_cdf + up_gate * jnp.exp(-0.5 * up_gate * up_gate) * (2.0 * jnp.pi) ** -0.5
    hidden_bf = (gelu_val * up_lin).astype(bf16)

    grad_hidden = matmul(down_bf, down_w)
    grad_upgate = (grad_hidden * up_lin * gelu_slope).astype(bf16)
    grad_uplin = (grad_hidden * gelu_val).astype(bf16)
    grad_up = jnp.concatenate([grad_upgate, grad_uplin], axis=-1)
    got = reduce_far((grad_up, up_w))
    feed_grad = weight_grads(where, (second_bf, down_bf), (grad_up, hidden_bf), sizes)
    send, keep = reduce_near(got, (grad_up, up_w))
    send, feed_grad, hidden_late = tie(send, feed_grad, hidden_bf)
    feed_sum = sum_grad(feed_grad)
    result = matmul_t(order_rows(where, split(hidden_late)).reshape(tokens, -1), down_w)
    result = result.astype(bf16).reshape(nz * nh, part, width)
    result = lax.psum_scatter(result, ("row", "head"), scatter_dimension=0).astype(f32)
    result = (middle + result).astype(bf16)
    send, keep = reduce_one(send, keep)
    grad_two = reduce_two(send, keep)
    grad_middle = halves(out_grad[0])[0].astype(f32) + norm_back(
        grad_two * gain_two, scaled_two, rstd_two
    )
    pair, one = gather_tokens(grad_middle.astype(bf16))
    attn_bf = place_rows(where, (pair, one, mirror(pair), mirror(one)))
    attn_bf, feed_sum = tie(attn_bf, feed_sum)

    grp_norm, grp_rstd = normalize(retained.reshape(tokens, DV))
    gate_sig = jax.nn.sigmoid(gate)
    gate_act = gate * gate_sig
    grad_mixed = matmul(attn_bf, out_w)
    grad_gate = (grad_mixed * grp_norm * (gate_sig * (1.0 + gate * (1.0 - gate_sig)))).astype(bf16)
    ret_bf = norm_back(grad_mixed * gate_act, grp_norm, grp_rstd).astype(bf16)
    ret_all = over_col(split(ret_bf))

    feed_pieces = grad_row(after(feed_sum, ret_bf))
    late_gate, late_mixed, result = after((grad_gate, mixed_bf, result), ret_all)
    both_grad = weight_grads(where, (first_bf, attn_bf), (late_gate, late_mixed), sizes)
    both_sum = sum_grad(both_grad)

    grad_kvq = retention_backward(
        where, c_row, c_col, keyval, queries, ret_all, states, split(cosines), split(sines)
    )
    grad_kvq = grad_kvq.reshape(tokens, -1)
    terms = ((grad_kvq, kvq_w), (grad_gate, gate_w))
    got = reduce_far(*terms)
    kvq_far = weight_grads(where, (first_bf,), (grad_kvq,), sizes, 1)
    send, keep = reduce_near(got, *terms)
    kvq_got = swap(kvq_far, "batch", 1)
    kvq_keep, kvq_send = weight_grads(where, (first_bf,), (grad_kvq,), sizes, 0, kvq_got)
    send, kvq_send, feed_pieces = tie(send, kvq_send, feed_pieces)
    grad_gates, grad_ups, grad_downs = unpack(feed_pieces, (units, units, units))
    send, keep = reduce_one(send, keep)
    grad_one = reduce_two(send, keep)
    kvq_sum = grad_col(kvq_keep, kvq_send)
    grad_one, kvq_sum, grad_gates, grad_ups, grad_downs = tie(
        grad_one, kvq_sum, grad_gates, grad_ups, grad_downs
    )
    last_pieces = grad_row(kvq_sum, both_sum)
    result_other = mirror(result)

    scaled_own, rstd_own = normalize(inputs)
    grad_in = grad_middle + norm_back(grad_one * gain_one, scaled_own, rstd_own)
    grad_in_other = mirror(grad_in)
    grad_k, grad_v, grad_q, grad_g, grad_outs = unpack(last_pieces, (DK, DV, DK, DV, DV))

    def join(own, other):
        first = jnp.where(x == 0, own, other)
        second = jnp.where(x == 0, other, own)
        return jnp.concatenate([first, second]).reshape(1, block, width)

    norm_sums = jnp.stack(
        [
            jnp.sum(grad_one * scaled_own, axis=0),
            jnp.sum(grad_one, axis=0),
            jnp.sum(grad_two * scaled_two, axis=0),
            jnp.sum(grad_two, axis=0),
        ]
    )
    norm_sums = norm_sums + swap(norm_sums, "head", 1)
    norm_sums = norm_sums.reshape(4, nz, ny, nb, rows)
    for name, axis in (("batch", 3), ("col", 2), ("row", 1)):
        me = lax.axis_index(name)
        summed = pick(norm_sums, me, axis)
        for k in range(1, lax.axis_size(name)):
            summed = summed + swap(pick(norm_sums, me ^ k, axis), name, k)
        norm_sums = summed

    return (
        join(result, result_other),
        join(grad_in, grad_in_other),
        norm_sums[0],
        norm_sums[1],
        grad_q,
        grad_k,
        grad_v,
        grad_g,
        grad_outs.T,
        norm_sums[2],
        norm_sums[3],
        grad_gates,
        grad_ups,
        grad_downs.T,
    )


def solution(mesh):
    seq = ("row", "col")
    tokens = P("batch", seq, None)
    params = P((*seq, "batch"))
    by_rows = P((*seq, "batch"), "head")
    by_cols = P("head", (*seq, "batch"))

    def run(*arrays):
        rows = arrays[1].shape[1] // mesh.shape["head"]
        sizes = (rows, mesh.shape["seq"] // rows, mesh.shape["batch"], mesh.shape["head"])
        order = [mesh.axis_names.index(n) for n in ("seq", "batch", "head")]
        fine = Mesh(
            mesh.devices.transpose(order).reshape(sizes), ("row", "col", "batch", "head")
        )
        weights = (by_rows, by_rows, by_rows, by_rows, by_cols)
        feeds = (by_rows, by_rows, by_cols)
        return jax.shard_map(
            shards,
            mesh=fine,
            in_specs=(
                tokens,
                P("batch", "head", seq),
                tokens,
                params,
                params,
                *weights,
                params,
                params,
                *feeds,
            ),
            out_specs=(tokens, tokens, params, params, *weights, params, params, *feeds),
            check_vma=False,
        )(*arrays)

    return run
```

```python
import jax
import jax.numpy as jnp
from jax import lax
from jax.experimental import pallas as pl
from jax.experimental.pallas import tpu as pltpu
from jax.sharding import Mesh
from jax.sharding import PartitionSpec as P

DK = 256
DV = 512

epsilon = 1e-05
f32 = jnp.float32
bf16 = jnp.bfloat16
VMEM_LIMIT = 12 * 1024 * 1024

ORDER = (0, 2, 1, 3)


def swap(values, axis, k):
    count = lax.axis_size(axis)
    return lax.ppermute(values, axis, [(i, i ^ k) for i in range(count)])


def pick(values, index, axis):
    return lax.dynamic_index_in_dim(values, index, axis, keepdims=False)


def tie(*values):
    return lax.optimization_barrier(values)


def after(values, *others):
    return tie(values, others)[0]


def matmul(values, weight):
    return jnp.dot(values, weight, preferred_element_type=f32)


def matmul_t(values, weight):
    return lax.dot_general(values, weight, (((1,), (1,)), ((), ())), preferred_element_type=f32)


def outer_sum(values, other):
    return lax.dot_general(values, other, (((0,), (0,)), ((), ())), preferred_element_type=f32)


def normalize(values):
    center = values - jnp.mean(values, axis=-1, keepdims=True)
    rstd = lax.rsqrt(jnp.mean(center * center, axis=-1, keepdims=True) + epsilon)
    return center * rstd, rstd


def norm_back(scaled_grad, scaled, rstd):
    return rstd * (
        scaled_grad
        - jnp.mean(scaled_grad, axis=-1, keepdims=True)
        - scaled * jnp.mean(scaled_grad * scaled, axis=-1, keepdims=True)
    )


def rotate(values, cosines, sines):
    half_dim = values.shape[-1] // 2
    first_half = values[..., :half_dim]
    second_half = values[..., half_dim:]
    return jnp.concatenate(
        [first_half * cosines - second_half * sines, first_half * sines + second_half * cosines],
        axis=-1,
    )


SMEM = pl.BlockSpec(memory_space=pltpu.SMEM)
WHOLE = pl.BlockSpec(memory_space=pltpu.VMEM)
PARAMS = pltpu.CompilerParams(vmem_limit_bytes=VMEM_LIMIT)


def pack_weights(where, weights, nz):
    rows = weights[0].shape[0]
    widths = [w.shape[1] // nz for w in weights]

    def kernel(where_ref, *refs):
        ins, outs = refs[: len(weights)], refs[len(weights) :]
        for k in range(nz):
            target = where_ref[0] ^ k
            at = 0
            for ref, width in zip(ins, widths):
                start = pl.multiple_of(target * width, width)
                outs[k][:, at : at + width] = ref[:, pl.ds(start, width)]
                at += width

    return pl.pallas_call(
        kernel,
        out_shape=[jax.ShapeDtypeStruct((rows, sum(widths)), bf16)] * nz,
        in_specs=[SMEM] + [WHOLE] * len(weights),
        out_specs=[WHOLE] * nz,
        compiler_params=PARAMS,
        name="pack_weights",
    )(where, *weights)


EXTRA = 16


def pack_first(where, weights, gains, decays, nz):
    rows = weights[0].shape[0]
    widths = [w.shape[1] // nz for w in weights]
    block = decays.shape[1]
    gains = jnp.pad(gains, ((0, 0), (0, sum(widths) - gains.shape[1])))

    def kernel(where_ref, gain_ref, decay_ref, *refs):
        ins, outs = refs[: len(weights)], refs[len(weights) :]
        at = lax.broadcasted_iota(jnp.int32, (EXTRA, 1), 0)
        gain_rows = jnp.where(at == 0, gain_ref[...].astype(f32), 0.0)
        for k in range(nz):
            target = where_ref[0] ^ k
            to = 0
            for ref, width in zip(ins, widths):
                start = pl.multiple_of(target * width, width)
                outs[k][:rows, to : to + width] = ref[:, pl.ds(start, width)]
                to += width
            rest = decay_ref[pl.ds(target, 1), :]
            parts = gain_rows[:, :block]
            for row in range(1, 4):
                part = rest.astype(bf16).astype(f32)
                parts = jnp.where(at == row, part, parts)
                rest = rest - part
            outs[k][rows:, :] = gain_rows.astype(bf16)
            outs[k][rows:, :block] = parts.astype(bf16)

    return pl.pallas_call(
        kernel,
        out_shape=[jax.ShapeDtypeStruct((rows + EXTRA, sum(widths)), bf16)] * nz,
        in_specs=[SMEM] + [WHOLE] * (2 + len(weights)),
        out_specs=[WHOLE] * nz,
        compiler_params=PARAMS,
        name="pack_first",
    )(where, gains, decays, *weights)


def unpack_grads(where, own, pieces, widths):
    nz = len(pieces) + 1
    rows = own.shape[0]

    def kernel(where_ref, *refs):
        ins, outs = refs[:nz], refs[nz:]
        for k in range(nz):
            target = where_ref[0] ^ k
            at = 0
            for ref, width in zip(outs, widths):
                start = pl.multiple_of(target * width, width)
                ref[:, pl.ds(start, width)] = ins[k][:, at : at + width].astype(f32)
                at += width

    return pl.pallas_call(
        kernel,
        out_shape=[jax.ShapeDtypeStruct((rows, nz * width), f32) for width in widths],
        in_specs=[SMEM] + [WHOLE] * nz,
        out_specs=[WHOLE] * len(widths),
        compiler_params=PARAMS,
        name="unpack_grads",
    )(where, own, *pieces)


def assemble(where, parts, ny, nb, widths, extra=0):
    nz, rows, _ = parts[0][0].shape
    rows -= extra
    count = nz * ny * nb
    total = sum(widths)
    sizes = [len(part) for part in parts]

    def kernel(where_ref, *refs):
        ins, outs = refs[: sum(sizes)], refs[sum(sizes) :]
        for ky in range(ny):
            for kb in range(nb):
                pieces, ins = ins[: sizes[ky * nb + kb]], ins[sizes[ky * nb + kb] :]
                for kz in range(nz):
                    block = (where_ref[0] ^ kz) * ny + (where_ref[1] ^ ky)
                    device = block * nb + (where_ref[2] ^ kb)
                    at = pl.multiple_of(device * rows, rows)
                    column = 0
                    for piece in pieces:
                        cols = piece.shape[-1]
                        start = 0
                        for out, width in zip(outs, widths):
                            low, high = max(start, column), min(start + width, column + cols)
                            if low < high:
                                out[pl.ds(at, rows), low - start : high - start] = piece[
                                    kz, :rows, low - column : high - column
                                ]
                            start += width
                        column += cols
                    if extra:
                        tail = pieces[0][kz, rows:, :].astype(f32)
                        outs[-2][pl.ds(device, 1), :] = tail[:1]
                        if kb == 0:
                            outs[-1][pl.ds(block, 1), :] = (tail[1:2] + tail[2:3]) + tail[3:4]

    shapes = [jax.ShapeDtypeStruct((count * rows, width), bf16) for width in widths]
    if extra:
        shapes.append(jax.ShapeDtypeStruct((count, total), f32))
        shapes.append(jax.ShapeDtypeStruct((nz * ny, total), f32))
    return pl.pallas_call(
        kernel,
        out_shape=shapes,
        in_specs=[SMEM] + [WHOLE] * sum(sizes),
        out_specs=[WHOLE] * len(shapes),
        compiler_params=PARAMS,
        name="assemble",
    )(where, *[piece for part in parts for piece in part])


def row_groups(where, left, sizes, near):
    nz, ny, nb = sizes
    groups = left.reshape(left.shape[0], nz, ny, nb, -1)
    if near:
        groups = jnp.take(groups, jnp.arange(ny) ^ where[1], axis=2)
        groups = jnp.take(groups, jnp.arange(nb) ^ where[2], axis=3)
        return groups.transpose(0, 3, 2, 1, 4).reshape(left.shape)
    return groups.transpose(0, 2, 3, 1, 4).reshape(left.shape)


def weight_grads(where, lefts, rights, sizes, near=None, got=None):
    nz, ny, nb = sizes
    width = lefts[0].shape[1]
    rows = width // (nz * ny * nb)
    group = nz * rows
    steps = ny * nb if near is None else ny
    widths = [right.shape[1] for right in rights]
    total = sum(widths)
    aligned = rows % 128 == 0
    if not aligned:
        lefts = [row_groups(where, left, sizes, near is not None) for left in lefts]

    def columns(where_ref, left, step):
        if not aligned:
            start = (step if near is None else near * ny + step) * group
            return left[:, pl.ds(pl.multiple_of(start, group), group)]
        if near is None:
            y, b = step // nb, step % nb
        else:
            y, b = where_ref[1] ^ step, where_ref[2] ^ near
        tiles = []
        for z in range(nz):
            start = pl.multiple_of(((z * ny + y) * nb + b) * rows, rows)
            tiles.append(left[:, pl.ds(start, rows)])
        return jnp.concatenate(tiles, axis=1)

    def kernel(where_ref, *refs):
        ins, rest = refs[: len(lefts)], refs[len(lefts) :]
        others, rest = rest[: len(rights)], rest[len(rights) :]
        step = pl.program_id(0)
        at = 0
        for left, right, cols in zip(ins, others, widths):
            value = dot(columns(where_ref, left, step), right[...], TN)
            to = slice(at, at + cols)
            if got is None:
                rest[0][:, to] = value.astype(bf16)
            else:
                value = value + rest[0][:, to].astype(f32)

                @pl.when(step == 0)
                def _():
                    rest[1][:, to] = value

                rest[2][:, to] = value.astype(bf16)
            at += cols

    blocks = pl.BlockSpec((group, total), lambda i: (i, 0))
    shape = jax.ShapeDtypeStruct((steps * group, total), bf16)
    if got is not None:
        blocks = [pl.BlockSpec((group, total), lambda i: (0, 0)), blocks]
        shape = [jax.ShapeDtypeStruct((group, total), f32), shape]
    return pl.pallas_call(
        kernel,
        grid=(steps,),
        out_shape=shape,
        in_specs=[SMEM]
        + [WHOLE] * (len(lefts) + len(rights))
        + ([] if got is None else [pl.BlockSpec((group, total), lambda i: (i, 0))]),
        out_specs=blocks,
        compiler_params=PARAMS,
        name="weight_grads",
    )(where, *lefts, *rights, *(() if got is None else (got,)))


def place_rows(where, pieces, norm=None, halves=0):
    width = pieces[0].shape[-1]
    tokens = sum(piece.size // width for piece in pieces)
    norm = list(norm or ())

    def kernel(where_ref, *refs):
        ins, params, full = refs[: len(pieces)], refs[len(pieces) : -1], refs[-1]
        at = 0
        if halves:
            part = ins[0].shape[1] // halves
            for half in range(halves):
                for k in ORDER:
                    start = pl.multiple_of((where_ref[3] ^ half) * part, part)
                    full[at : at + part, :] = ins[0][where_ref[0] ^ k, pl.ds(start, part), :]
                    at += part
        for ref in () if halves else ins:
            values = ref[...]
            if norm:
                values, _ = normalize(values.astype(f32))
                values = (values * params[0][...] + params[1][...]).astype(bf16)
            full[at : at + ref.shape[0], :] = values
            at += ref.shape[0]

    return pl.pallas_call(
        kernel,
        out_shape=jax.ShapeDtypeStruct((tokens, width), bf16),
        in_specs=[SMEM] + [WHOLE] * (len(pieces) + len(norm)),
        out_specs=WHOLE,
        compiler_params=PARAMS,
        name="place_rows",
    )(where, *pieces, *norm)


def slot_of(k):
    return ((k & 1) << 1) | (k >> 1)


def natural(ref, slot, flip, columns=slice(None)):
    first = ref[flip, slot, :, columns]
    second = ref[1 - flip, slot, :, columns]
    return jnp.concatenate([first, second], axis=0)


def choose(refs, ky, slot, flip, columns=slice(None)):
    values = natural(refs[0], slot, flip, columns)
    for k in range(1, len(refs)):
        values = jnp.where(ky == k, natural(refs[k], slot, flip, columns), values)
    return values


def dot(left, right, dims):
    return lax.dot_general(left, right, (dims, ((), ())), preferred_element_type=f32)


NN, NT, TN = ((1,), (0,)), ((1,), (1,)), ((0,), (0,))


def decay_matrix(col, row):
    block = row.shape[-1]
    at = lax.broadcasted_iota(jnp.int32, (block, block), 0)
    to = lax.broadcasted_iota(jnp.int32, (block, block), 1)
    return jnp.where(at >= to, jnp.exp(jnp.minimum(col - row, 0.0)), 0.0)


def retention_forward(where, c_row, c_col, keyvals, query, gate):
    ny = len(keyvals)
    halves, nz, part, _ = query.shape
    block = halves * part

    def kernel(where_ref, row_ref, col_ref, *refs):
        kv_refs, (q_ref, g_ref, y_ref, o_ref, s_ref, state) = refs[:ny], refs[ny:]
        j = pl.program_id(0)

        @pl.when(j == 0)
        def _():
            state[...] = jnp.zeros_like(state)

        slot = slot_of((j // ny) ^ where_ref[0])
        ky = (j % ny) ^ where_ref[1]
        flip = where_ref[3]
        row, col = row_ref[j], col_ref[j]
        key = choose(kv_refs, ky, slot, flip, slice(0, DK))
        value = choose(kv_refs, ky, slot, flip, slice(DK, DK + DV))
        last = row[:, block - 1 :]

        @pl.when(ky == 0)
        def _():
            q = natural(q_ref, slot, flip)
            state_bf = state[...].astype(bf16)
            s_ref[slot] = state_bf
            weights = (dot(q, key, NT) * decay_matrix(col, row)).astype(bf16)
            out = dot(weights, value, NN) + jnp.exp(col) * dot(q, state_bf, NN)
            normed, _ = normalize(out)
            g = natural(g_ref, slot, flip)
            mixed = (g * jax.nn.sigmoid(g) * normed).astype(bf16)
            for half in range(2):
                rows = slice(half * part, (half + 1) * part)
                to = (1 - flip) if half else flip
                y_ref[to, slot] = mixed[rows]
                o_ref[to, slot] = out[rows]

        key_tail = (key.astype(f32) * jnp.exp(last - col)).astype(bf16)
        state[...] = jnp.exp(last) * state[...] + dot(key_tail, value, TN)

    return pl.pallas_call(
        kernel,
        grid=(nz * ny,),
        out_shape=[
            jax.ShapeDtypeStruct((halves, nz, part, DV), bf16),
            jax.ShapeDtypeStruct((halves, nz, part, DV), f32),
            jax.ShapeDtypeStruct((nz, DK, DV), bf16),
        ],
        in_specs=[SMEM] + [WHOLE] * (4 + ny),
        out_specs=[WHOLE] * 3,
        scratch_shapes=[pltpu.VMEM((DK, DV), f32)],
        compiler_params=PARAMS,
        name="retention_forward",
    )(where, c_row, c_col, *keyvals, query, gate)


def retention_backward(where, c_row, c_col, keyval, queries, grads, states, cosines, sines):
    ny = len(queries)
    halves, nz, part, _ = keyval.shape
    block = halves * part
    key_scale = DK ** (-0.5)

    def kernel(where_ref, row_ref, col_ref, *refs):
        q_refs, d_refs, rest = refs[:ny], refs[ny : 2 * ny], refs[2 * ny :]
        kv_ref, s_ref, cos_ref, sin_ref, g_ref, state = rest
        step = pl.program_id(0)
        j = nz * ny - 1 - step

        @pl.when(step == 0)
        def _():
            state[...] = jnp.zeros_like(state)

        slot = slot_of((j // ny) ^ where_ref[0])
        ky = (j % ny) ^ where_ref[1]
        flip = where_ref[3]
        row, col = row_ref[j], col_ref[j]
        last = row[:, block - 1 :]
        q = choose(q_refs, ky, slot, flip)
        grad = choose(d_refs, ky, slot, flip)
        entry = jnp.exp(col)

        @pl.when(ky == 0)
        def _():
            key = natural(kv_ref, slot, flip, slice(0, DK))
            value = natural(kv_ref, slot, flip, slice(DK, DK + DV))
            cos = natural(cos_ref, slot, flip)
            sin = natural(sin_ref, slot, flip)
            decays = decay_matrix(col, row)
            tail = jnp.exp(last - col)
            state_bf = state[...].astype(bf16)
            weights = (dot(q, key, NT) * decays).astype(bf16)
            scores = (dot(grad, value, NT) * decays).astype(bf16)
            grad_q = dot(scores, key, NN) + entry * dot(grad, s_ref[slot], NT)
            grad_k = dot(scores, q, TN) + tail * dot(value, state_bf, NT)
            grad_v = dot(weights, grad, TN) + tail * dot(key, state_bf, NN)
            grad_q = rotate(grad_q, cos, -sin).astype(bf16)
            grad_k = (rotate(grad_k, cos, -sin) * key_scale).astype(bf16)
            grad_v = grad_v.astype(bf16)
            for half in range(2):
                rows = slice(half * part, (half + 1) * part)
                to = (1 - flip) if half else flip
                g_ref[to, slot, :, :DK] = grad_k[rows]
                g_ref[to, slot, :, DK : DK + DV] = grad_v[rows]
                g_ref[to, slot, :, DK + DV :] = grad_q[rows]

        query_entry = (q.astype(f32) * entry).astype(bf16)
        state[...] = jnp.exp(last) * state[...] + dot(query_entry, grad, TN)

    return pl.pallas_call(
        kernel,
        grid=(nz * ny,),
        out_shape=jax.ShapeDtypeStruct((halves, nz, part, 2 * DK + DV), bf16),
        in_specs=[SMEM] + [WHOLE] * (6 + 2 * ny),
        out_specs=WHOLE,
        scratch_shapes=[pltpu.VMEM((DK, DV), f32)],
        compiler_params=PARAMS,
        name="retention_backward",
    )(where, c_row, c_col, *queries, *grads, keyval, states, cosines, sines)


def shards(
    hidden_in,
    log_decay,
    out_grad,
    ln1_gain,
    ln1_bias,
    w_query,
    w_key,
    w_value,
    w_gate,
    w_out,
    ln2_gain,
    ln2_bias,
    mlp_gate,
    mlp_up,
    mlp_down,
):
    nz, ny = lax.axis_size("row"), lax.axis_size("col")
    nb, nh = lax.axis_size("batch"), lax.axis_size("head")
    z, y = lax.axis_index("row"), lax.axis_index("col")
    b, x = lax.axis_index("batch"), lax.axis_index("head")
    block, width = hidden_in.shape[1:]
    rows = ln1_gain.shape[0]
    part = block // nh
    tokens = nz * block
    where = jnp.stack([z, y, b, x]).astype(jnp.int32)

    sizes = (nz, ny, nb)
    half, quarter = tokens // 2, tokens // 4
    group = nz * rows

    def trade(pieces, k):
        return swap(pieces[k], "row", k) if k else pieces[k]

    def over_col(own):
        return [own] + [swap(own, "col", k) for k in range(1, ny)]

    def over_batch(values):
        return [swap(value, "batch", 1) for value in values]

    def mirror(values):
        return swap(values, "head", 1)

    def pairs(own, other):
        return [(part,) for both in zip(own, other) for part in both]

    def halves(values):
        values = values.reshape(nh, part, -1)
        return pick(values, x, 0), pick(values, 1 - x, 0)

    def split(values):
        return values.reshape(nh, nz, part, -1)

    def sum_grad(grad):
        grad = grad.reshape(ny * nb, nz, rows, -1)
        return lax.psum_scatter(grad, ("col", "batch"), scatter_dimension=0)

    def head_pieces(*totals):
        pieces = []
        for k in range(nz):
            piece = [pick(total, z ^ k, 0).astype(bf16) for total in totals]
            pieces.append(jnp.concatenate(piece, axis=-1))
        return pieces

    def reduce_far(*terms):
        far = sum(matmul_t(values[half:], weight) for values, weight in terms).astype(bf16)
        return far[quarter:], far[:quarter]

    def reduce_near(*terms):
        near = sum(matmul_t(values[:half], weight) for values, weight in terms)
        return near[quarter:], near[:quarter]

    def add(values, got):
        return values + got.astype(f32)

    gains = jnp.concatenate([ln1_gain, ln1_bias, ln2_gain, ln2_bias])[None]
    kvq = pack_first(where, (w_key, w_value, w_query), gains, log_decay[0], nz)
    kvq = [trade(kvq, k) for k in range(nz)]
    own_in, other_in = halves(hidden_in[0])
    two_in = swap(own_in, "row", 2)
    kvq, two_in, late = tie(kvq, two_in, (w_gate, w_out))
    kvq = jnp.stack(kvq)
    kvq_cols, kvq_mate = over_col(kvq), swap(kvq, "batch", 1)
    one_in = swap(jnp.concatenate([own_in, two_in]), "row", 1)
    wide = pack_weights(where, (late[0], late[1].T), nz)
    wide = [trade(wide, k) for k in range(nz)]
    kvq_cols, kvq_mate, one_in, wide, feed = tie(
        kvq_cols, kvq_mate, one_in, wide, (mlp_gate, mlp_up, mlp_down)
    )
    kvq_mates = [kvq_mate] + over_batch(kvq_cols[1:])
    mirror_in = mirror(jnp.concatenate([two_in, one_in]))
    gate_cols = over_col(jnp.stack([piece[:, :DV] for piece in wide]))
    feed = pack_weights(where, (feed[0], feed[1], feed[2].T), nz)
    feed_two = trade(feed, 2)
    kvq_mates, mirror_in, gate_cols, feed_two = tie(kvq_mates, mirror_in, gate_cols, feed_two)
    kvq_w, small, decay = assemble(
        where, pairs(kvq_cols, kvq_mates), ny, nb, (2 * DK + DV,), EXTRA
    )

    params = small[:, : 4 * rows].reshape(nz * ny * nb, 4, rows)
    gain_one, bias_one, gain_two, bias_two = params.transpose(1, 0, 2).reshape(4, width)
    running = jnp.cumsum(decay[:, :block], axis=-1)
    c_row, c_col = running[:, None, :], running[:, :, None]

    half_dim = DK // 2
    freqs = 10000.0 ** (-jnp.arange(half_dim, dtype=f32) / half_dim)
    block_at = (jnp.array(ORDER) ^ z) * ny + y
    half_at = jnp.arange(nh) ^ x
    positions = (
        block_at[None, :, None] * block + half_at[:, None, None] * part + jnp.arange(part)
    )
    angles = positions.astype(f32).reshape(-1)[:, None] * freqs[None, :]
    cosines, sines = jnp.cos(angles), jnp.sin(angles)
    key_scale = DK ** (-0.5)

    first_bf = place_rows(
        where, (own_in, two_in, one_in, other_in, mirror_in), (gain_one[None], bias_one[None])
    )
    projected = matmul(first_bf, kvq_w)
    key_bf = (rotate(projected[:, :DK], cosines, sines) * key_scale).astype(bf16)
    value_bf = projected[:, DK : DK + DV].astype(bf16)
    query_bf = rotate(projected[:, DK + DV :], cosines, sines).astype(bf16)
    keyval = split(jnp.concatenate([key_bf, value_bf], axis=-1))

    keyval, gate_cols, feed = tie(keyval, gate_cols, feed)
    keyvals = over_col(keyval)
    (gate_w,) = assemble(where, pairs(gate_cols, over_batch(gate_cols)), ny, nb, (DV,))
    gate = matmul(first_bf, gate_w)
    feed_three = trade(feed, 3)
    keyvals, gate, feed_three = tie(keyvals, gate, feed_three)
    out_cols = over_col(jnp.stack([piece[:, DV:] for piece in after(wide, keyvals)]))
    feed_one = trade(after(feed, keyvals), 1)
    mixed, retained, states = retention_forward(
        where, c_row, c_col, keyvals, split(query_bf), split(gate)
    )
    mixed, out_cols, feed_one = tie(mixed, out_cols, feed_one)
    (out_w,) = assemble(where, pairs(out_cols, over_batch(out_cols)), ny, nb, (DV,))
    mixed_bf = mixed.reshape(tokens, DV)
    feed = jnp.stack([feed[0], feed_one, feed_two, feed_three])
    units = feed.shape[-1] // 3

    far = reduce_far((mixed_bf, out_w))
    got = mirror(far[0])
    near = reduce_near((mixed_bf, out_w))
    feed_gates = over_col(feed[..., :units])[1:]
    got, near, feed_gates = tie(got, near, feed_gates)
    got, got_far = swap(add(near[0], got).astype(bf16), "row", 1), mirror(far[1])
    feed, own_grad, other_grad = after((feed, *halves(out_grad[0])), near)
    feed_ups = over_col(feed[..., units : 2 * units])[1:]
    two_grad = swap(own_grad, "row", 2)
    got, got_far, feed_ups, two_grad = tie(got, got_far, feed_ups, two_grad)
    keep = add(add(near[1], got_far), got)
    got = swap(keep[part:].astype(bf16), "row", 2)
    feed = after(feed, keep)
    feed_downs = over_col(feed[..., 2 * units :])[1:]
    feed_mate = swap(feed, "batch", 1)
    one_grad = swap(jnp.concatenate([own_grad, two_grad]), "row", 1)
    mirror_two = mirror(two_grad)
    got, feed_downs, feed_mate, one_grad, mirror_two = tie(
        got, feed_downs, feed_mate, one_grad, mirror_two
    )
    inputs = own_in.astype(f32)
    middle = inputs + add(keep[:part], got)
    scaled_two, rstd_two = normalize(middle)
    own = (scaled_two * gain_two + bias_two).astype(bf16)
    two = swap(own, "row", 2)
    feed_cols = list(zip(feed_gates, feed_ups, feed_downs))
    feed_cols = after(feed_cols, own)
    feed_mates = [over_batch(cols) for cols in feed_cols]
    mirror_one = mirror(after(one_grad, own))
    two, feed_mates, mirror_one = tie(two, feed_mates, mirror_one)
    pair = jnp.concatenate([own, two])
    one, mirror_pair = swap(pair, "row", 1), mirror(pair)
    queries = over_col(split(after(query_bf, pair)))
    one, mirror_pair, queries = tie(one, mirror_pair, queries)
    mirror_last = mirror(one)
    parts = [(feed,), (feed_mate,)]
    for cols, mates in zip(feed_cols, feed_mates):
        parts += [tuple(cols), tuple(mates)]
    up_w, down_w = assemble(where, after(parts, one), ny, nb, (2 * units, units))
    down_bf = place_rows(
        where, after((own_grad, two_grad, one_grad, other_grad, mirror_two, mirror_one), one)
    )
    mirror_last, up_w, down_w, down_bf = tie(mirror_last, up_w, down_w, down_bf)
    second_bf = place_rows(where, (pair, one, mirror_pair, mirror_last))

    up = matmul(second_bf, up_w)
    up_gate, up_lin = up[:, :units], up[:, units:]
    gelu_cdf = 0.5 * (1.0 + lax.erf(up_gate * (0.5**0.5)))
    gelu_val = up_gate * gelu_cdf
    gelu_slope = gelu_cdf + up_gate * jnp.exp(-0.5 * up_gate * up_gate) * (2.0 * jnp.pi) ** -0.5
    hidden_bf = (gelu_val * up_lin).astype(bf16)
    grad_hidden = matmul(down_bf, down_w)
    grad_upgate = (grad_hidden * up_lin * gelu_slope).astype(bf16)
    grad_uplin = (grad_hidden * gelu_val).astype(bf16)
    grad_up = jnp.concatenate([grad_upgate, grad_uplin], axis=-1)
    far = reduce_far((grad_up, up_w))
    got = mirror(far[0])
    near = reduce_near((grad_up, up_w))
    feed_grad = weight_grads(where, (second_bf, down_bf), (grad_up, hidden_bf), sizes)
    got, near, feed_grad, hidden_bf = tie(got, near, feed_grad, hidden_bf)
    got, got_far = swap(add(near[0], got).astype(bf16), "row", 1), mirror(far[1])
    feed_sum = sum_grad(feed_grad)
    result_far = reduce_far((hidden_bf, down_w))
    got, got_far, result_far, hidden_bf = tie(got, got_far, result_far, hidden_bf)
    keep = add(add(near[1], got_far), got)
    got = swap(keep[part:].astype(bf16), "row", 2)
    result_got = mirror(result_far[0])
    result_near = reduce_near((hidden_bf, down_w))
    got, result_got, result_near = tie(got, result_got, result_near)
    grad_two = add(keep[:part], got)
    grad_middle = own_grad.astype(f32) + norm_back(grad_two * gain_two, scaled_two, rstd_two)
    own = grad_middle.astype(bf16)
    two = swap(own, "row", 2)
    result_got_far = mirror(after(result_far[1], own))
    two, result_got_far = tie(two, result_got_far)
    pair = jnp.concatenate([own, two])
    one, mirror_pair = swap(pair, "row", 1), mirror(pair)
    result_send = add(result_near[0], result_got).astype(bf16)
    one, mirror_pair, result_send = tie(one, mirror_pair, result_send)
    mirror_last = mirror(one)
    result_got = swap(result_send, "row", 1)
    mirror_last, result_got, feed_sum = tie(mirror_last, result_got, feed_sum)
    attn_bf = place_rows(where, (pair, one, mirror_pair, mirror_last))

    grp_norm, grp_rstd = normalize(retained.reshape(tokens, DV))
    gate_sig = jax.nn.sigmoid(gate)
    gate_act = gate * gate_sig
    grad_mixed = matmul(attn_bf, out_w)
    grad_gate = (grad_mixed * grp_norm * (gate_sig * (1.0 + gate * (1.0 - gate_sig)))).astype(bf16)
    ret_bf = norm_back(grad_mixed * gate_act, grp_norm, grp_rstd).astype(bf16)
    ret_bf, feed_sum = tie(split(ret_bf), feed_sum)
    ret_all = over_col(ret_bf)
    feed_grads = head_pieces(feed_sum)
    feed_two = trade(feed_grads, 2)
    ret_all, feed_two = tie(ret_all, feed_two)
    grad_kvq = retention_backward(
        where, c_row, c_col, keyval, queries, ret_all, states, split(cosines), split(sines)
    )
    grad_kvq = grad_kvq.reshape(tokens, -1)
    terms = ((grad_kvq, kvq_w), (grad_gate, gate_w))
    far = reduce_far(*terms)
    got = mirror(far[0])
    feed_grads, result_got, late = after(
        (feed_grads, result_got, (grad_gate, attn_bf, mixed_bf)), grad_kvq
    )
    feed_three, feed_one = trade(feed_grads, 3), trade(feed_grads, 1)
    kvq_got = swap(weight_grads(where, (first_bf,), (grad_kvq,), sizes, 1), "batch", 1)
    near = reduce_near(*terms)
    both_grad = weight_grads(where, (first_bf, late[1]), (late[0], late[2]), sizes)
    got, near, feed_three, feed_one, kvq_got, both_grad = tie(
        got, near, feed_three, feed_one, kvq_got, both_grad
    )
    got, got_far = swap(add(near[0], got).astype(bf16), "row", 1), mirror(far[1])
    both_sum = sum_grad(both_grad)
    result_keep = add(add(result_near[1], result_got_far), result_got)
    result_got = swap(after(result_keep[part:].astype(bf16), near), "row", 2)
    kvq_keep, kvq_send = weight_grads(where, (first_bf,), (grad_kvq,), sizes, 0, kvq_got)
    got, got_far, result_got, kvq_send = tie(got, got_far, result_got, kvq_send)
    keep = add(add(near[1], got_far), got)
    got = swap(keep[part:].astype(bf16), "row", 2)
    result = (middle + add(result_keep[:part], result_got)).astype(bf16)
    result_other = mirror(result)
    grad_gates, grad_ups, grad_downs = unpack_grads(
        where, feed_grads[0], (feed_one, feed_two, feed_three), (units, units, units)
    )
    for k in range(1, ny):
        kvq_keep = add(kvq_keep, swap(kvq_send[k * group : (k + 1) * group], "col", k))
    got, result_other, grad_gates, grad_ups, grad_downs = tie(
        got, result_other, grad_gates, grad_ups, grad_downs
    )
    grad_one = add(keep[:part], got)
    last = head_pieces(kvq_keep.reshape(nz, rows, -1), both_sum)
    last = [trade(last, k) for k in range(nz)]

    scaled_own, rstd_own = normalize(inputs)
    grad_in = grad_middle + norm_back(grad_one * gain_one, scaled_own, rstd_own)
    grad_in_other = mirror(grad_in)
    grad_k, grad_v, grad_q, grad_g, grad_outs = unpack_grads(
        where, last[0], last[1:], (DK, DV, DK, DV, DV)
    )

    def join(own, other):
        first = jnp.where(x == 0, own, other)
        second = jnp.where(x == 0, other, own)
        return jnp.concatenate([first, second]).reshape(1, block, width)

    norm_sums = jnp.stack(
        [
            jnp.sum(grad_one * scaled_own, axis=0),
            jnp.sum(grad_one, axis=0),
            jnp.sum(grad_two * scaled_two, axis=0),
            jnp.sum(grad_two, axis=0),
        ]
    )
    norm_sums = norm_sums + swap(norm_sums, "head", 1)
    norm_sums = norm_sums.reshape(4, nz, ny, nb, rows)
    for name, axis in (("batch", 3), ("col", 2), ("row", 1)):
        me = lax.axis_index(name)
        summed = pick(norm_sums, me, axis)
        for k in range(1, lax.axis_size(name)):
            summed = summed + swap(pick(norm_sums, me ^ k, axis), name, k)
        norm_sums = summed

    return (
        join(result, result_other),
        join(grad_in, grad_in_other),
        norm_sums[0],
        norm_sums[1],
        grad_q,
        grad_k,
        grad_v,
        grad_g,
        grad_outs.T,
        norm_sums[2],
        norm_sums[3],
        grad_gates,
        grad_ups,
        grad_downs.T,
    )


def solution(mesh):
    seq = ("row", "col")
    tokens = P("batch", seq, None)
    params = P((*seq, "batch"))
    by_rows = P((*seq, "batch"), "head")
    by_cols = P("head", (*seq, "batch"))

    def run(*arrays):
        rows = arrays[1].shape[1] // mesh.shape["head"]
        sizes = (rows, mesh.shape["seq"] // rows, mesh.shape["batch"], mesh.shape["head"])
        order = [mesh.axis_names.index(n) for n in ("seq", "batch", "head")]
        fine = Mesh(
            mesh.devices.transpose(order).reshape(sizes), ("row", "col", "batch", "head")
        )
        weights = (by_rows, by_rows, by_rows, by_rows, by_cols)
        feeds = (by_rows, by_rows, by_cols)
        return jax.shard_map(
            shards,
            mesh=fine,
            in_specs=(
                tokens,
                P("batch", "head", seq),
                tokens,
                params,
                params,
                *weights,
                params,
                params,
                *feeds,
            ),
            out_specs=(tokens, tokens, params, params, *weights, params, params, *feeds),
            check_vma=False,
        )(*arrays)

    return run
```

```python
import jax
import jax.numpy as jnp
from jax import lax
from jax.experimental import pallas as pl
from jax.experimental.pallas import tpu as pltpu
from jax.sharding import Mesh
from jax.sharding import PartitionSpec as P

DK = 256
DV = 512

epsilon = 1e-05
f32 = jnp.float32
bf16 = jnp.bfloat16
VMEM_LIMIT = 12 * 1024 * 1024

ORDER = (0, 2, 1, 3)


def swap(values, axis, k):
    count = lax.axis_size(axis)
    return lax.ppermute(values, axis, [(i, i ^ k) for i in range(count)])


def pick(values, index, axis):
    return lax.dynamic_index_in_dim(values, index, axis, keepdims=False)


def tie(*values):
    return lax.optimization_barrier(values)


def after(values, *others):
    return tie(values, others)[0]


def matmul(values, weight):
    return jnp.dot(values, weight, preferred_element_type=f32)


def matmul_t(values, weight):
    return lax.dot_general(values, weight, (((1,), (1,)), ((), ())), preferred_element_type=f32)


def outer_sum(values, other):
    return lax.dot_general(values, other, (((0,), (0,)), ((), ())), preferred_element_type=f32)


def normalize(values):
    center = values - jnp.mean(values, axis=-1, keepdims=True)
    rstd = lax.rsqrt(jnp.mean(center * center, axis=-1, keepdims=True) + epsilon)
    return center * rstd, rstd


def norm_back(scaled_grad, scaled, rstd):
    return rstd * (
        scaled_grad
        - jnp.mean(scaled_grad, axis=-1, keepdims=True)
        - scaled * jnp.mean(scaled_grad * scaled, axis=-1, keepdims=True)
    )


def rotate(values, cosines, sines):
    half_dim = values.shape[-1] // 2
    first_half = values[..., :half_dim]
    second_half = values[..., half_dim:]
    return jnp.concatenate(
        [first_half * cosines - second_half * sines, first_half * sines + second_half * cosines],
        axis=-1,
    )


SMEM = pl.BlockSpec(memory_space=pltpu.SMEM)
WHOLE = pl.BlockSpec(memory_space=pltpu.VMEM)
PARAMS = pltpu.CompilerParams(vmem_limit_bytes=VMEM_LIMIT)


def pack_weights(where, weights, nz):
    rows = weights[0].shape[0]
    widths = [w.shape[1] // nz for w in weights]

    def kernel(where_ref, *refs):
        ins, outs = refs[: len(weights)], refs[len(weights) :]
        for k in range(nz):
            target = where_ref[0] ^ k
            at = 0
            for ref, width in zip(ins, widths):
                start = pl.multiple_of(target * width, width)
                outs[k][:, at : at + width] = ref[:, pl.ds(start, width)]
                at += width

    return pl.pallas_call(
        kernel,
        out_shape=[jax.ShapeDtypeStruct((rows, sum(widths)), bf16)] * nz,
        in_specs=[SMEM] + [WHOLE] * len(weights),
        out_specs=[WHOLE] * nz,
        compiler_params=PARAMS,
        name="pack_weights",
    )(where, *weights)


EXTRA = 16


def pack_first(where, weights, gains, decays, nz):
    rows = weights[0].shape[0]
    widths = [w.shape[1] // nz for w in weights]
    block = decays.shape[1]
    gains = jnp.pad(gains, ((0, 0), (0, sum(widths) - gains.shape[1])))

    def kernel(where_ref, gain_ref, decay_ref, *refs):
        ins, outs = refs[: len(weights)], refs[len(weights) :]
        at = lax.broadcasted_iota(jnp.int32, (EXTRA, 1), 0)
        gain_rows = jnp.where(at == 0, gain_ref[...].astype(f32), 0.0)
        for k in range(nz):
            target = where_ref[0] ^ k
            to = 0
            for ref, width in zip(ins, widths):
                start = pl.multiple_of(target * width, width)
                outs[k][:rows, to : to + width] = ref[:, pl.ds(start, width)]
                to += width
            rest = decay_ref[pl.ds(target, 1), :]
            parts = gain_rows[:, :block]
            for row in range(1, 4):
                part = rest.astype(bf16).astype(f32)
                parts = jnp.where(at == row, part, parts)
                rest = rest - part
            outs[k][rows:, :] = gain_rows.astype(bf16)
            outs[k][rows:, :block] = parts.astype(bf16)

    return pl.pallas_call(
        kernel,
        out_shape=[jax.ShapeDtypeStruct((rows + EXTRA, sum(widths)), bf16)] * nz,
        in_specs=[SMEM] + [WHOLE] * (2 + len(weights)),
        out_specs=[WHOLE] * nz,
        compiler_params=PARAMS,
        name="pack_first",
    )(where, gains, decays, *weights)


def unpack_grads(where, own, pieces, widths):
    nz = len(pieces) + 1
    rows = own.shape[0]

    def kernel(where_ref, *refs):
        ins, outs = refs[:nz], refs[nz:]
        for k in range(nz):
            target = where_ref[0] ^ k
            at = 0
            for ref, width in zip(outs, widths):
                start = pl.multiple_of(target * width, width)
                ref[:, pl.ds(start, width)] = ins[k][:, at : at + width].astype(f32)
                at += width

    return pl.pallas_call(
        kernel,
        out_shape=[jax.ShapeDtypeStruct((rows, nz * width), f32) for width in widths],
        in_specs=[SMEM] + [WHOLE] * nz,
        out_specs=[WHOLE] * len(widths),
        compiler_params=PARAMS,
        name="unpack_grads",
    )(where, own, *pieces)


def assemble(where, parts, ny, nb, widths, extra=0):
    nz, rows, _ = parts[0][0].shape
    rows -= extra
    count = nz * ny * nb
    total = sum(widths)
    sizes = [len(part) for part in parts]

    def kernel(where_ref, *refs):
        ins, outs = refs[: sum(sizes)], refs[sum(sizes) :]
        for ky in range(ny):
            for kb in range(nb):
                pieces, ins = ins[: sizes[ky * nb + kb]], ins[sizes[ky * nb + kb] :]
                for kz in range(nz):
                    block = (where_ref[0] ^ kz) * ny + (where_ref[1] ^ ky)
                    device = block * nb + (where_ref[2] ^ kb)
                    at = pl.multiple_of(device * rows, rows)
                    column = 0
                    for piece in pieces:
                        cols = piece.shape[-1]
                        start = 0
                        for out, width in zip(outs, widths):
                            low, high = max(start, column), min(start + width, column + cols)
                            if low < high:
                                out[pl.ds(at, rows), low - start : high - start] = piece[
                                    kz, :rows, low - column : high - column
                                ]
                            start += width
                        column += cols
                    if extra:
                        tail = pieces[0][kz, rows:, :].astype(f32)
                        outs[-2][pl.ds(device, 1), :] = tail[:1]
                        if kb == 0:
                            outs[-1][pl.ds(block, 1), :] = (tail[1:2] + tail[2:3]) + tail[3:4]

    shapes = [jax.ShapeDtypeStruct((count * rows, width), bf16) for width in widths]
    if extra:
        shapes.append(jax.ShapeDtypeStruct((count, total), f32))
        shapes.append(jax.ShapeDtypeStruct((nz * ny, total), f32))
    return pl.pallas_call(
        kernel,
        out_shape=shapes,
        in_specs=[SMEM] + [WHOLE] * sum(sizes),
        out_specs=[WHOLE] * len(shapes),
        compiler_params=PARAMS,
        name="assemble",
    )(where, *[piece for part in parts for piece in part])


def row_groups(where, left, sizes):
    nz, ny, nb = sizes
    groups = left.reshape(left.shape[0], nz, ny, nb, -1)
    groups = jnp.take(groups, jnp.arange(ny) ^ where[1], axis=2)
    groups = jnp.take(groups, jnp.arange(nb) ^ where[2], axis=3)
    return groups.transpose(0, 3, 2, 1, 4).reshape(left.shape)


def weight_grads(where, lefts, rights, sizes, widths=None, got=None):
    nz, ny, nb = sizes
    width = lefts[0].shape[1]
    rows = width // (nz * ny * nb)
    group = nz * rows
    total = sum(right.shape[1] for right in rights)
    kb = 1 if got is None else 0
    aligned = rows % 128 == 0
    if not aligned:
        lefts = [row_groups(where, left, sizes) for left in lefts]

    def columns(where_ref, left, step):
        if not aligned:
            return left[:, pl.ds(pl.multiple_of((kb * ny + step) * group, group), group)]
        tiles = []
        for z in range(nz):
            start = ((z * ny + (where_ref[1] ^ step)) * nb + (where_ref[2] ^ kb)) * rows
            tiles.append(left[:, pl.ds(pl.multiple_of(start, rows), rows)])
        return jnp.concatenate(tiles, axis=1)

    def kernel(where_ref, *refs):
        ins, rest = refs[: len(lefts)], refs[len(lefts) :]
        others, rest = rest[: len(rights)], rest[len(rights) :]
        step = pl.program_id(0)
        values = []
        for left, right in zip(ins, others):
            values.append(dot(columns(where_ref, left, step), right[...], TN))
        if got is None:
            at = 0
            for value in values:
                rest[0][:, at : at + value.shape[1]] = value.astype(bf16)
                at += value.shape[1]
            return
        value = jnp.concatenate(values, axis=1) + rest[0][...].astype(f32)
        keeps, sends = rest[1 : 1 + len(widths)], rest[1 + len(widths) :]
        at = 0
        for keep, send, cols in zip(keeps, sends, widths):
            part = value[:, at : at + cols]
            send[...] = part.astype(bf16)

            @pl.when(step == 0)
            def _():
                keep[...] = part

            at += cols

    moving = lambda cols: pl.BlockSpec((group, cols), lambda i: (i, 0))
    if got is None:
        specs = moving(total)
        shapes = jax.ShapeDtypeStruct((ny * group, total), bf16)
    else:
        specs = [pl.BlockSpec((group, cols), lambda i: (0, 0)) for cols in widths]
        specs += [moving(cols) for cols in widths]
        shapes = [jax.ShapeDtypeStruct((group, cols), f32) for cols in widths]
        shapes += [jax.ShapeDtypeStruct((ny * group, cols), bf16) for cols in widths]
    outs = pl.pallas_call(
        kernel,
        grid=(ny,),
        out_shape=shapes,
        in_specs=[SMEM]
        + [WHOLE] * (len(lefts) + len(rights))
        + ([] if got is None else [moving(total)]),
        out_specs=specs,
        compiler_params=PARAMS,
        name="weight_grads",
    )(where, *lefts, *rights, *(() if got is None else (got,)))
    return outs if got is None else (outs[: len(widths)], outs[len(widths) :])


def place_rows(where, pieces, norm=None, halves=0):
    width = pieces[0].shape[-1]
    tokens = sum(piece.size // width for piece in pieces)
    norm = list(norm or ())

    def kernel(where_ref, *refs):
        ins, params, full = refs[: len(pieces)], refs[len(pieces) : -1], refs[-1]
        at = 0
        if halves:
            part = ins[0].shape[1] // halves
            for half in range(halves):
                for k in ORDER:
                    start = pl.multiple_of((where_ref[3] ^ half) * part, part)
                    full[at : at + part, :] = ins[0][where_ref[0] ^ k, pl.ds(start, part), :]
                    at += part
        for ref in () if halves else ins:
            values = ref[...]
            if norm:
                values, _ = normalize(values.astype(f32))
                values = (values * params[0][...] + params[1][...]).astype(bf16)
            full[at : at + ref.shape[0], :] = values
            at += ref.shape[0]

    return pl.pallas_call(
        kernel,
        out_shape=jax.ShapeDtypeStruct((tokens, width), bf16),
        in_specs=[SMEM] + [WHOLE] * (len(pieces) + len(norm)),
        out_specs=WHOLE,
        compiler_params=PARAMS,
        name="place_rows",
    )(where, *pieces, *norm)


def slot_of(k):
    return ((k & 1) << 1) | (k >> 1)


def natural(ref, slot, flip, columns=slice(None)):
    first = ref[flip, slot, :, columns]
    second = ref[1 - flip, slot, :, columns]
    return jnp.concatenate([first, second], axis=0)


def choose(refs, ky, slot, flip, columns=slice(None)):
    values = natural(refs[0], slot, flip, columns)
    for k in range(1, len(refs)):
        values = jnp.where(ky == k, natural(refs[k], slot, flip, columns), values)
    return values


def dot(left, right, dims):
    return lax.dot_general(left, right, (dims, ((), ())), preferred_element_type=f32)


NN, NT, TN = ((1,), (0,)), ((1,), (1,)), ((0,), (0,))


def decay_matrix(col, row):
    block = row.shape[-1]
    at = lax.broadcasted_iota(jnp.int32, (block, block), 0)
    to = lax.broadcasted_iota(jnp.int32, (block, block), 1)
    return jnp.where(at >= to, jnp.exp(jnp.minimum(col - row, 0.0)), 0.0)


def retention_forward(where, c_row, c_col, keyvals, query, gate):
    ny = len(keyvals)
    halves, nz, part, _ = query.shape
    block = halves * part

    def kernel(where_ref, row_ref, col_ref, *refs):
        kv_refs, (q_ref, g_ref, y_ref, o_ref, s_ref, state) = refs[:ny], refs[ny:]
        j = pl.program_id(0)

        @pl.when(j == 0)
        def _():
            state[...] = jnp.zeros_like(state)

        slot = slot_of((j // ny) ^ where_ref[0])
        ky = (j % ny) ^ where_ref[1]
        flip = where_ref[3]
        row, col = row_ref[j], col_ref[j]
        key = choose(kv_refs, ky, slot, flip, slice(0, DK))
        value = choose(kv_refs, ky, slot, flip, slice(DK, DK + DV))
        last = row[:, block - 1 :]

        @pl.when(ky == 0)
        def _():
            q = natural(q_ref, slot, flip)
            state_bf = state[...].astype(bf16)
            s_ref[slot] = state_bf
            weights = (dot(q, key, NT) * decay_matrix(col, row)).astype(bf16)
            out = dot(weights, value, NN) + jnp.exp(col) * dot(q, state_bf, NN)
            normed, _ = normalize(out)
            g = natural(g_ref, slot, flip)
            mixed = (g * jax.nn.sigmoid(g) * normed).astype(bf16)
            for half in range(2):
                rows = slice(half * part, (half + 1) * part)
                to = (1 - flip) if half else flip
                y_ref[to, slot] = mixed[rows]
                o_ref[to, slot] = out[rows]

        key_tail = (key.astype(f32) * jnp.exp(last - col)).astype(bf16)
        state[...] = jnp.exp(last) * state[...] + dot(key_tail, value, TN)

    return pl.pallas_call(
        kernel,
        grid=(nz * ny,),
        out_shape=[
            jax.ShapeDtypeStruct((halves, nz, part, DV), bf16),
            jax.ShapeDtypeStruct((halves, nz, part, DV), f32),
            jax.ShapeDtypeStruct((nz, DK, DV), bf16),
        ],
        in_specs=[SMEM] + [WHOLE] * (4 + ny),
        out_specs=[WHOLE] * 3,
        scratch_shapes=[pltpu.VMEM((DK, DV), f32)],
        compiler_params=PARAMS,
        name="retention_forward",
    )(where, c_row, c_col, *keyvals, query, gate)


def retention_backward(where, c_row, c_col, keyval, queries, grads, states, cosines, sines):
    ny = len(queries)
    halves, nz, part, _ = keyval.shape
    block = halves * part
    key_scale = DK ** (-0.5)

    def kernel(where_ref, row_ref, col_ref, *refs):
        q_refs, d_refs, rest = refs[:ny], refs[ny : 2 * ny], refs[2 * ny :]
        kv_ref, s_ref, cos_ref, sin_ref, g_ref, state = rest
        step = pl.program_id(0)
        j = nz * ny - 1 - step

        @pl.when(step == 0)
        def _():
            state[...] = jnp.zeros_like(state)

        slot = slot_of((j // ny) ^ where_ref[0])
        ky = (j % ny) ^ where_ref[1]
        flip = where_ref[3]
        row, col = row_ref[j], col_ref[j]
        last = row[:, block - 1 :]
        q = choose(q_refs, ky, slot, flip)
        grad = choose(d_refs, ky, slot, flip)
        entry = jnp.exp(col)

        @pl.when(ky == 0)
        def _():
            key = natural(kv_ref, slot, flip, slice(0, DK))
            value = natural(kv_ref, slot, flip, slice(DK, DK + DV))
            cos = natural(cos_ref, slot, flip)
            sin = natural(sin_ref, slot, flip)
            decays = decay_matrix(col, row)
            tail = jnp.exp(last - col)
            state_bf = state[...].astype(bf16)
            weights = (dot(q, key, NT) * decays).astype(bf16)
            scores = (dot(grad, value, NT) * decays).astype(bf16)
            grad_q = dot(scores, key, NN) + entry * dot(grad, s_ref[slot], NT)
            grad_k = dot(scores, q, TN) + tail * dot(value, state_bf, NT)
            grad_v = dot(weights, grad, TN) + tail * dot(key, state_bf, NN)
            grad_q = rotate(grad_q, cos, -sin).astype(bf16)
            grad_k = (rotate(grad_k, cos, -sin) * key_scale).astype(bf16)
            grad_v = grad_v.astype(bf16)
            for half in range(2):
                rows = slice(half * part, (half + 1) * part)
                to = (1 - flip) if half else flip
                g_ref[to, slot, :, :DK] = grad_k[rows]
                g_ref[to, slot, :, DK : DK + DV] = grad_v[rows]
                g_ref[to, slot, :, DK + DV :] = grad_q[rows]

        query_entry = (q.astype(f32) * entry).astype(bf16)
        state[...] = jnp.exp(last) * state[...] + dot(query_entry, grad, TN)

    return pl.pallas_call(
        kernel,
        grid=(nz * ny,),
        out_shape=jax.ShapeDtypeStruct((halves, nz, part, 2 * DK + DV), bf16),
        in_specs=[SMEM] + [WHOLE] * (6 + 2 * ny),
        out_specs=WHOLE,
        scratch_shapes=[pltpu.VMEM((DK, DV), f32)],
        compiler_params=PARAMS,
        name="retention_backward",
    )(where, c_row, c_col, *queries, *grads, keyval, states, cosines, sines)


def shards(
    hidden_in,
    log_decay,
    out_grad,
    ln1_gain,
    ln1_bias,
    w_query,
    w_key,
    w_value,
    w_gate,
    w_out,
    ln2_gain,
    ln2_bias,
    mlp_gate,
    mlp_up,
    mlp_down,
):
    nz, ny = lax.axis_size("row"), lax.axis_size("col")
    nb, nh = lax.axis_size("batch"), lax.axis_size("head")
    z, y = lax.axis_index("row"), lax.axis_index("col")
    b, x = lax.axis_index("batch"), lax.axis_index("head")
    block, width = hidden_in.shape[1:]
    rows = ln1_gain.shape[0]
    part = block // nh
    tokens = nz * block
    where = jnp.stack([z, y, b, x]).astype(jnp.int32)

    sizes = (nz, ny, nb)
    half, quarter = tokens // 2, tokens // 4
    group = nz * rows

    def trade(pieces, k):
        return swap(pieces[k], "row", k) if k else pieces[k]

    def over_col(own):
        return [own] + [swap(own, "col", k) for k in range(1, ny)]

    def over_batch(values):
        return [swap(value, "batch", 1) for value in values]

    def mirror(values):
        return swap(values, "head", 1)

    def pairs(own, other):
        return [(part,) for both in zip(own, other) for part in both]

    def halves(values):
        values = values.reshape(nh, part, -1)
        return pick(values, x, 0), pick(values, 1 - x, 0)

    def split(values):
        return values.reshape(nh, nz, part, -1)

    def sum_col(keep, send):
        for k in range(1, ny):
            keep = add(keep, swap(send[k * group : (k + 1) * group], "col", k))
        return keep.reshape(nz, rows, -1)

    def head_pieces(*totals):
        pieces = []
        for k in range(nz):
            piece = [pick(total, z ^ k, 0).astype(bf16) for total in totals]
            pieces.append(jnp.concatenate(piece, axis=-1))
        return pieces

    def reduce_far(*terms):
        far = sum(matmul_t(values[half:], weight) for values, weight in terms).astype(bf16)
        return far[quarter:], far[:quarter]

    def reduce_near(*terms):
        near = sum(matmul_t(values[:half], weight) for values, weight in terms)
        return near[quarter:], near[:quarter]

    def add(values, got):
        return values + got.astype(f32)

    gains = jnp.concatenate([ln1_gain, ln1_bias, ln2_gain, ln2_bias])[None]
    kvq = pack_first(where, (w_key, w_value, w_query), gains, log_decay[0], nz)
    kvq = [trade(kvq, k) for k in range(nz)]
    own_in, other_in = halves(hidden_in[0])
    two_in = swap(own_in, "row", 2)
    kvq, two_in, late = tie(kvq, two_in, (w_gate, w_out))
    kvq = jnp.stack(kvq)
    kvq_cols = over_col(kvq)
    one_in = swap(jnp.concatenate([own_in, two_in]), "row", 1)
    wide = pack_weights(where, (late[0], late[1].T), nz)
    wide = [trade(wide, k) for k in range(nz)]
    feed = pack_weights(where, (mlp_gate, mlp_up, mlp_down.T), nz)
    kvq_cols, one_in, wide, feed = tie(kvq_cols, one_in, wide, feed)
    kvq_mates = over_batch(kvq_cols)
    mirror_in = mirror(jnp.concatenate([two_in, one_in]))
    wide_cols = over_col(jnp.stack(wide))
    feed_two = trade(feed, 2)
    kvq_mates, mirror_in, wide_cols, feed_two = tie(kvq_mates, mirror_in, wide_cols, feed_two)
    kvq_w, small, decay = assemble(
        where, pairs(kvq_cols, kvq_mates), ny, nb, (2 * DK + DV,), EXTRA
    )

    params = small[:, : 4 * rows].reshape(nz * ny * nb, 4, rows)
    gain_one, bias_one, gain_two, bias_two = params.transpose(1, 0, 2).reshape(4, width)
    running = jnp.cumsum(decay[:, :block], axis=-1)
    c_row, c_col = running[:, None, :], running[:, :, None]

    half_dim = DK // 2
    freqs = 10000.0 ** (-jnp.arange(half_dim, dtype=f32) / half_dim)
    block_at = (jnp.array(ORDER) ^ z) * ny + y
    half_at = jnp.arange(nh) ^ x
    positions = (
        block_at[None, :, None] * block + half_at[:, None, None] * part + jnp.arange(part)
    )
    angles = positions.astype(f32).reshape(-1)[:, None] * freqs[None, :]
    cosines, sines = jnp.cos(angles), jnp.sin(angles)
    key_scale = DK ** (-0.5)

    first_bf = place_rows(
        where, (own_in, two_in, one_in, other_in, mirror_in), (gain_one[None], bias_one[None])
    )
    projected = matmul(first_bf, kvq_w)
    key_bf = (rotate(projected[:, :DK], cosines, sines) * key_scale).astype(bf16)
    value_bf = projected[:, DK : DK + DV].astype(bf16)
    query_bf = rotate(projected[:, DK + DV :], cosines, sines).astype(bf16)
    keyval = split(jnp.concatenate([key_bf, value_bf], axis=-1))

    keyval, wide_cols, feed = tie(keyval, wide_cols, feed)
    keyvals = over_col(keyval)
    gate_w, out_w = assemble(where, pairs(wide_cols, over_batch(wide_cols)), ny, nb, (DV, DV))
    gate = matmul(first_bf, gate_w)
    feed_three, feed_one = trade(feed, 3), trade(feed, 1)
    keyvals, gate, feed_three, feed_one = tie(keyvals, gate, feed_three, feed_one)
    feed = jnp.stack([feed[0], feed_one, feed_two, feed_three])
    units = feed.shape[-1] // 3
    own_grad, other_grad = halves(after(out_grad[0], keyvals))
    feed_gates = over_col(feed[..., :units])[1:]
    two_grad = swap(own_grad, "row", 2)
    mixed, retained, states = retention_forward(
        where, c_row, c_col, keyvals, split(query_bf), split(gate)
    )
    mixed, feed_gates, two_grad, feed = tie(mixed, feed_gates, two_grad, feed)
    mixed_bf = mixed.reshape(tokens, DV)

    far = reduce_far((mixed_bf, out_w))
    got = mirror(far[0])
    near = reduce_near((mixed_bf, out_w))
    feed_ups = over_col(feed[..., units : 2 * units])[1:]
    one_grad = swap(jnp.concatenate([own_grad, two_grad]), "row", 1)
    got, near, feed_ups, one_grad, feed = tie(got, near, feed_ups, one_grad, feed)
    got, got_far = swap(add(near[0], got).astype(bf16), "row", 1), mirror(far[1])
    feed_downs = over_col(feed[..., 2 * units :])[1:]
    feed_mate = swap(feed, "batch", 1)
    got, got_far, feed_downs, feed_mate = tie(got, got_far, feed_downs, feed_mate)
    keep = add(add(near[1], got_far), got)
    got = swap(keep[part:].astype(bf16), "row", 2)
    feed_cols = list(zip(feed_gates, feed_ups, feed_downs))
    feed_mates = [over_batch(cols) for cols in feed_cols]
    mirror_two = mirror(after(two_grad, keep))
    got, feed_mates, mirror_two = tie(got, feed_mates, mirror_two)
    inputs = own_in.astype(f32)
    middle = inputs + add(keep[:part], got)
    scaled_two, rstd_two = normalize(middle)
    own = (scaled_two * gain_two + bias_two).astype(bf16)
    two = swap(own, "row", 2)
    mirror_one = mirror(after(one_grad, own))
    two, mirror_one = tie(two, mirror_one)
    pair = jnp.concatenate([own, two])
    one, mirror_pair = swap(pair, "row", 1), mirror(pair)
    queries = over_col(split(after(query_bf, pair)))
    one, mirror_pair, queries = tie(one, mirror_pair, queries)
    mirror_last = mirror(one)
    parts = [(feed,), (feed_mate,)]
    for cols, mates in zip(feed_cols, feed_mates):
        parts += [tuple(cols), tuple(mates)]
    up_w, down_w = assemble(where, after(parts, one), ny, nb, (2 * units, units))
    down_bf = place_rows(
        where, after((own_grad, two_grad, one_grad, other_grad, mirror_two, mirror_one), one)
    )
    mirror_last, up_w, down_w, down_bf = tie(mirror_last, up_w, down_w, down_bf)
    second_bf = place_rows(where, (pair, one, mirror_pair, mirror_last))

    up = matmul(second_bf, up_w)
    up_gate, up_lin = up[:, :units], up[:, units:]
    gelu_cdf = 0.5 * (1.0 + lax.erf(up_gate * (0.5**0.5)))
    gelu_val = up_gate * gelu_cdf
    gelu_slope = gelu_cdf + up_gate * jnp.exp(-0.5 * up_gate * up_gate) * (2.0 * jnp.pi) ** -0.5
    hidden_bf = (gelu_val * up_lin).astype(bf16)
    grad_hidden = matmul(down_bf, down_w)
    grad_upgate = (grad_hidden * up_lin * gelu_slope).astype(bf16)
    grad_uplin = (grad_hidden * gelu_val).astype(bf16)
    grad_up = jnp.concatenate([grad_upgate, grad_uplin], axis=-1)
    far = reduce_far((grad_up, up_w))
    got = mirror(far[0])
    near = reduce_near((grad_up, up_w))
    feed_far = weight_grads(where, (second_bf, down_bf), (grad_up, hidden_bf), sizes)
    got, near, feed_far, hidden_bf = tie(got, near, feed_far, hidden_bf)
    got, got_far = swap(add(near[0], got).astype(bf16), "row", 1), mirror(far[1])
    result_far = reduce_far((hidden_bf, down_w))
    feed_keeps, feed_sends = weight_grads(
        where,
        (second_bf, down_bf),
        (grad_up, hidden_bf),
        sizes,
        (units, units, units),
        swap(feed_far, "batch", 1),
    )
    got, got_far, result_far, hidden_bf, feed_sends = tie(
        got, got_far, result_far, hidden_bf, feed_sends
    )
    keep = add(add(near[1], got_far), got)
    got = swap(keep[part:].astype(bf16), "row", 2)
    result_got = mirror(result_far[0])
    result_near = reduce_near((hidden_bf, down_w))
    gate_sum = sum_col(feed_keeps[0], feed_sends[0])
    got, result_got, result_near, gate_sum = tie(got, result_got, result_near, gate_sum)
    grad_two = add(keep[:part], got)
    grad_middle = own_grad.astype(f32) + norm_back(grad_two * gain_two, scaled_two, rstd_two)
    result_send = add(result_near[0], result_got).astype(bf16)
    own, up_send, result_send = tie(grad_middle.astype(bf16), feed_sends[1], result_send)
    two = swap(own, "row", 2)
    result_got_far = mirror(after(result_far[1], own))
    result_got = swap(result_send, "row", 1)
    up_sum = sum_col(feed_keeps[1], up_send)
    two, result_got_far, result_got, up_sum = tie(two, result_got_far, result_got, up_sum)
    pair = jnp.concatenate([own, two])
    one, mirror_pair = swap(pair, "row", 1), mirror(pair)
    down_sum = sum_col(feed_keeps[2], after(feed_sends[2], pair))
    feed_grads = head_pieces(gate_sum, up_sum, down_sum)
    result_keep = add(add(result_near[1], result_got_far), result_got)
    result_send = result_keep[part:].astype(bf16)
    one, mirror_pair, feed_grads, result_send = tie(one, mirror_pair, feed_grads, result_send)
    mirror_last = mirror(one)
    feed_two = trade(feed_grads, 2)
    mirror_last, feed_two, feed_grads = tie(mirror_last, feed_two, feed_grads)
    attn_bf = place_rows(where, (pair, one, mirror_pair, mirror_last))

    grp_norm, grp_rstd = normalize(retained.reshape(tokens, DV))
    gate_sig = jax.nn.sigmoid(gate)
    gate_act = gate * gate_sig
    grad_mixed = matmul(attn_bf, out_w)
    grad_gate = (grad_mixed * grp_norm * (gate_sig * (1.0 + gate * (1.0 - gate_sig)))).astype(bf16)
    ret_bf = norm_back(grad_mixed * gate_act, grp_norm, grp_rstd).astype(bf16)
    ret_bf, feed_grads = tie(split(ret_bf), feed_grads)
    ret_all = over_col(ret_bf)
    feed_three = trade(feed_grads, 3)
    lefts, rights = (first_bf, attn_bf), (grad_gate, mixed_bf)
    both_far = weight_grads(where, lefts, rights, sizes)
    ret_all, feed_three, both_far, feed_grads = tie(ret_all, feed_three, both_far, feed_grads)
    grad_kvq = retention_backward(
        where, c_row, c_col, keyval, queries, ret_all, states, split(cosines), split(sines)
    )
    grad_kvq = grad_kvq.reshape(tokens, -1)
    terms = ((grad_kvq, kvq_w), (grad_gate, gate_w))
    far = reduce_far(*terms)
    got = mirror(far[0])
    kvq_far = weight_grads(where, (first_bf,), (grad_kvq,), sizes)
    feed_grads, result_send, both_far = after((feed_grads, result_send, both_far), grad_kvq)
    feed_one = trade(feed_grads, 1)
    result_got = swap(result_send, "row", 2)
    near = reduce_near(*terms)
    kvq_got, both_got = over_batch((kvq_far, both_far))
    kvq_keeps, kvq_sends = weight_grads(
        where, (first_bf,), (grad_kvq,), sizes, (DV, 2 * DK), kvq_got
    )
    got, near, feed_one, result_got, kvq_sends, both_got = tie(
        got, near, feed_one, result_got, kvq_sends, both_got
    )
    got, got_far = swap(add(near[0], got).astype(bf16), "row", 1), mirror(far[1])
    kvq_first = sum_col(kvq_keeps[0], kvq_sends[0])
    both_keeps, both_sends = weight_grads(where, lefts, rights, sizes, (2 * DV,), both_got)
    got, got_far, kvq_first, both_sends, kvq_sends = tie(
        got, got_far, kvq_first, both_sends, kvq_sends
    )
    keep = add(add(near[1], got_far), got)
    got = swap(keep[part:].astype(bf16), "row", 2)
    result = (middle + add(result_keep[:part], result_got)).astype(bf16)
    result_other = mirror(result)
    grad_gates, grad_ups, grad_downs = unpack_grads(
        where, feed_grads[0], (feed_one, feed_two, feed_three), (units, units, units)
    )
    kvq_second = sum_col(kvq_keeps[1], kvq_sends[1])
    last = head_pieces(kvq_first, kvq_second)
    got, result_other, grad_gates, grad_ups, grad_downs, last, both_sends = tie(
        got, result_other, grad_gates, grad_ups, grad_downs, last, both_sends
    )
    grad_one = add(keep[:part], got)
    kvq_pieces = [trade(last, k) for k in range(nz)]
    both_pieces = head_pieces(sum_col(both_keeps[0], both_sends[0]))
    kvq_pieces, both_pieces = tie(kvq_pieces, both_pieces)
    both_pieces = [trade(both_pieces, k) for k in range(nz)]

    scaled_own, rstd_own = normalize(inputs)
    grad_in = grad_middle + norm_back(grad_one * gain_one, scaled_own, rstd_own)
    grad_in_other = mirror(grad_in)
    grad_k, grad_v, grad_q = unpack_grads(where, kvq_pieces[0], kvq_pieces[1:], (DK, DV, DK))
    grad_g, grad_outs = unpack_grads(where, both_pieces[0], both_pieces[1:], (DV, DV))

    def join(own, other):
        first = jnp.where(x == 0, own, other)
        second = jnp.where(x == 0, other, own)
        return jnp.concatenate([first, second]).reshape(1, block, width)

    norm_sums = jnp.stack(
        [
            jnp.sum(grad_one * scaled_own, axis=0),
            jnp.sum(grad_one, axis=0),
            jnp.sum(grad_two * scaled_two, axis=0),
            jnp.sum(grad_two, axis=0),
        ]
    )
    norm_sums = norm_sums + swap(norm_sums, "head", 1)
    norm_sums = norm_sums.reshape(4, nz, ny, nb, rows)
    for name, axis in (("batch", 3), ("col", 2), ("row", 1)):
        me = lax.axis_index(name)
        summed = pick(norm_sums, me, axis)
        for k in range(1, lax.axis_size(name)):
            summed = summed + swap(pick(norm_sums, me ^ k, axis), name, k)
        norm_sums = summed

    return (
        join(result, result_other),
        join(grad_in, grad_in_other),
        norm_sums[0],
        norm_sums[1],
        grad_q,
        grad_k,
        grad_v,
        grad_g,
        grad_outs.T,
        norm_sums[2],
        norm_sums[3],
        grad_gates,
        grad_ups,
        grad_downs.T,
    )


def solution(mesh):
    seq = ("row", "col")
    tokens = P("batch", seq, None)
    params = P((*seq, "batch"))
    by_rows = P((*seq, "batch"), "head")
    by_cols = P("head", (*seq, "batch"))

    def run(*arrays):
        rows = arrays[1].shape[1] // mesh.shape["head"]
        sizes = (rows, mesh.shape["seq"] // rows, mesh.shape["batch"], mesh.shape["head"])
        order = [mesh.axis_names.index(n) for n in ("seq", "batch", "head")]
        fine = Mesh(
            mesh.devices.transpose(order).reshape(sizes), ("row", "col", "batch", "head")
        )
        weights = (by_rows, by_rows, by_rows, by_rows, by_cols)
        feeds = (by_rows, by_rows, by_cols)
        return jax.shard_map(
            shards,
            mesh=fine,
            in_specs=(
                tokens,
                P("batch", "head", seq),
                tokens,
                params,
                params,
                *weights,
                params,
                params,
                *feeds,
            ),
            out_specs=(tokens, tokens, params, params, *weights, params, params, *feeds),
            check_vma=False,
        )(*arrays)

    return run
```

```python
import jax
import jax.numpy as jnp
from jax import lax
from jax.experimental import pallas as pl
from jax.experimental.pallas import tpu as pltpu
from jax.sharding import Mesh
from jax.sharding import PartitionSpec as P

DK = 256
DV = 512

epsilon = 1e-05
f32 = jnp.float32
bf16 = jnp.bfloat16
VMEM_LIMIT = 12 * 1024 * 1024

ORDER = (0, 2, 1, 3)


def swap(values, axis, k):
    count = lax.axis_size(axis)
    return lax.ppermute(values, axis, [(i, i ^ k) for i in range(count)])


def pick(values, index, axis):
    return lax.dynamic_index_in_dim(values, index, axis, keepdims=False)


def tie(*values):
    return lax.optimization_barrier(values)


def after(values, *others):
    return tie(values, others)[0]


def matmul(values, weight):
    return jnp.dot(values, weight, preferred_element_type=f32)


def matmul_t(values, weight):
    return lax.dot_general(values, weight, (((1,), (1,)), ((), ())), preferred_element_type=f32)


def outer_sum(values, other):
    return lax.dot_general(values, other, (((0,), (0,)), ((), ())), preferred_element_type=f32)


def normalize(values):
    center = values - jnp.mean(values, axis=-1, keepdims=True)
    rstd = lax.rsqrt(jnp.mean(center * center, axis=-1, keepdims=True) + epsilon)
    return center * rstd, rstd


def norm_back(scaled_grad, scaled, rstd):
    return rstd * (
        scaled_grad
        - jnp.mean(scaled_grad, axis=-1, keepdims=True)
        - scaled * jnp.mean(scaled_grad * scaled, axis=-1, keepdims=True)
    )


def rotate(values, cosines, sines):
    half_dim = values.shape[-1] // 2
    first_half = values[..., :half_dim]
    second_half = values[..., half_dim:]
    return jnp.concatenate(
        [first_half * cosines - second_half * sines, first_half * sines + second_half * cosines],
        axis=-1,
    )


SMEM = pl.BlockSpec(memory_space=pltpu.SMEM)
WHOLE = pl.BlockSpec(memory_space=pltpu.VMEM)
PARAMS = pltpu.CompilerParams(vmem_limit_bytes=VMEM_LIMIT)


def call(kernel, name, shapes, *operands, grid=None, scratch=()):
    many = isinstance(shapes, list)
    return pl.pallas_call(
        kernel,
        grid=() if grid is None else grid,
        out_shape=shapes,
        in_specs=[SMEM] + [WHOLE] * (len(operands) - 1),
        out_specs=[WHOLE] * len(shapes) if many else WHOLE,
        scratch_shapes=list(scratch),
        compiler_params=PARAMS,
        name=name,
    )(*operands)


def shape(dims, dtype):
    return jax.ShapeDtypeStruct(tuple(dims), dtype)


def cut_halves(where, values, heads):
    block, width = values.shape
    part = block // heads

    def kernel(where_ref, ref, own, other):
        for out, half in ((own, where_ref[3]), (other, 1 - where_ref[3])):
            out[...] = ref[pl.ds(pl.multiple_of(half * part, part), part), :]

    return call(kernel, "cut_halves", [shape((part, width), values.dtype)] * 2, where, values)


def join_halves(where, own, other):
    part, width = own.shape

    def kernel(where_ref, own_ref, other_ref, out):
        for ref, half in ((own_ref, where_ref[3]), (other_ref, 1 - where_ref[3])):
            out[pl.ds(pl.multiple_of(half * part, part), part), :] = ref[...]

    return call(kernel, "join_halves", shape((2 * part, width), own.dtype), where, own, other)


def cut_heads(where, totals):
    nz, rows, _ = totals[0].shape
    width = sum(total.shape[2] for total in totals)

    def kernel(where_ref, *refs):
        ins, outs = refs[: len(totals)], refs[len(totals) :]
        for k in range(nz):
            at = 0
            for ref in ins:
                cols = ref.shape[2]
                outs[k][:, at : at + cols] = ref[where_ref[0] ^ k].astype(bf16)
                at += cols

    return call(kernel, "cut_heads", [shape((rows, width), bf16)] * nz, where, *totals)


def pack_weights(where, weights, nz, rows, extras=None):
    widths = [w.size // rows // nz for w in weights]
    total = sum(widths)
    count = 0
    if extras:
        gains, decays = extras
        block = decays.shape[1]
        extras = (jnp.pad(gains, ((0, 0), (0, total - gains.shape[1]))), decays)
        count = EXTRA

    def kernel(where_ref, *refs):
        ins, rest = refs[: len(weights)], refs[len(weights) :]
        outs = rest[-nz:]
        for k in range(nz):
            target = where_ref[0] ^ k
            at = 0
            for ref, width in zip(ins, widths):
                start = pl.multiple_of(target * width, width)
                if ref.shape[0] == rows:
                    piece = ref[:, pl.ds(start, width)]
                else:
                    piece = ref[pl.ds(start, width), :].astype(f32).T.astype(bf16)
                outs[k][:rows, at : at + width] = piece
                at += width
            if extras:
                line = lax.broadcasted_iota(jnp.int32, (EXTRA, 1), 0)
                gain_rows = jnp.where(line == 0, rest[0][...].astype(f32), 0.0)
                parts = gain_rows[:, :block]
                left = rest[1][pl.ds(target, 1), :]
                for number in range(1, 4):
                    part = left.astype(bf16).astype(f32)
                    parts = jnp.where(line == number, part, parts)
                    left = left - part
                outs[k][rows:, :] = gain_rows.astype(bf16)
                outs[k][rows:, :block] = parts.astype(bf16)

    shapes = [shape((rows + count, total), bf16)] * nz
    return call(kernel, "pack_weights", shapes, where, *weights, *(extras or ()))


def unpack_grads(where, pieces, outs):
    nz = len(pieces)
    rows = pieces[0].shape[0]

    def kernel(where_ref, *refs):
        ins, results = refs[:nz], refs[nz:]
        for k in range(nz):
            target = where_ref[0] ^ k
            at = 0
            for ref, (width, turned) in zip(results, outs):
                to = pl.ds(pl.multiple_of(target * width, width), width)
                piece = ins[k][:, at : at + width].astype(f32)
                if turned:
                    ref[to, :] = piece.T
                else:
                    ref[:, to] = piece
                at += width

    shapes = [shape((nz * w, rows) if turned else (rows, nz * w), f32) for w, turned in outs]
    return call(kernel, "unpack_grads", shapes, where, *pieces)


EXTRA = 16


def assemble(where, parts, ny, nb, widths, extra=0, block=0):
    nz, rows, _ = parts[0][0].shape
    rows -= extra
    count = nz * ny * nb
    total = sum(widths)
    sizes = [len(part) for part in parts]
    aligned = rows % 128 == 0

    def kernel(where_ref, *refs):
        ins, outs = refs[: sum(sizes)], refs[sum(sizes) :]
        for ky in range(ny):
            for kb in range(nb):
                pieces, ins = ins[: sizes[ky * nb + kb]], ins[sizes[ky * nb + kb] :]
                for kz in range(nz):
                    place = (where_ref[0] ^ kz) * ny + (where_ref[1] ^ ky)
                    device = place * nb + (where_ref[2] ^ kb)
                    at = pl.multiple_of(device * rows, rows)
                    column = 0
                    for piece in pieces:
                        cols = piece.shape[-1]
                        start = 0
                        for out, width in zip(outs, widths):
                            low, high = max(start, column), min(start + width, column + cols)
                            if low < high:
                                out[pl.ds(at, rows), low - start : high - start] = piece[
                                    kz, :rows, low - column : high - column
                                ]
                            start += width
                        column += cols
                    if extra:
                        tail = pieces[0][kz, rows:, :].astype(f32)
                        if aligned:
                            for number in range(4):
                                gain = tail[:1, number * rows : (number + 1) * rows]
                                outs[-2][number : number + 1, pl.ds(at, rows)] = gain
                        else:
                            outs[-2][pl.ds(device, 1), :] = tail[:1]
                        if kb == 0:
                            decay = (tail[1:2] + tail[2:3]) + tail[3:4]
                            outs[-1][pl.ds(place, 1), :] = decay[:, :block]

    shapes = [shape((count * rows, width), bf16) for width in widths]
    if extra:
        shapes.append(shape((4, count * rows) if aligned else (count, total), f32))
        shapes.append(shape((nz * ny, block), f32))
    outs = list(call(kernel, "assemble", shapes, where, *[p for part in parts for p in part]))
    if extra and not aligned:
        gains = outs[-2][:, : 4 * rows].reshape(count, 4, rows)
        outs[-2] = gains.transpose(1, 0, 2).reshape(4, count * rows)
    return outs


def row_groups(where, left, sizes):
    nz, ny, nb = sizes
    groups = left.reshape(left.shape[0], nz, ny, nb, -1)
    groups = jnp.take(groups, jnp.arange(ny) ^ where[1], axis=2)
    groups = jnp.take(groups, jnp.arange(nb) ^ where[2], axis=3)
    return groups.transpose(0, 3, 2, 1, 4).reshape(left.shape)


def weight_grads(where, lefts, rights, sizes, widths=None, got=None):
    nz, ny, nb = sizes
    width = lefts[0].shape[1]
    rows = width // (nz * ny * nb)
    group = nz * rows
    rights = [right if isinstance(right, tuple) else (right, 0, right.shape[1]) for right in rights]
    ranges = [right[1:] for right in rights]
    rights = [right[0] for right in rights]
    total = sum(high - low for low, high in ranges)
    kb = 1 if got is None else 0
    aligned = rows % 128 == 0
    if not aligned:
        lefts = [row_groups(where, left, sizes) for left in lefts]

    def columns(where_ref, left, step):
        if not aligned:
            return left[:, pl.ds(pl.multiple_of((kb * ny + step) * group, group), group)]
        tiles = []
        for z in range(nz):
            start = ((z * ny + (where_ref[1] ^ step)) * nb + (where_ref[2] ^ kb)) * rows
            tiles.append(left[:, pl.ds(pl.multiple_of(start, rows), rows)])
        return jnp.concatenate(tiles, axis=1)

    def kernel(where_ref, *refs):
        ins, rest = refs[: len(lefts)], refs[len(lefts) :]
        others, rest = rest[: len(rights)], rest[len(rights) :]
        step = pl.program_id(0)
        values = []
        for left, right, (low, high) in zip(ins, others, ranges):
            values.append(dot(columns(where_ref, left, step), right[:, low:high], TN))
        if got is None:
            at = 0
            for value in values:
                rest[0][:, at : at + value.shape[1]] = value.astype(bf16)
                at += value.shape[1]
            return
        value = jnp.concatenate(values, axis=1) + rest[0][...].astype(f32)
        keeps, sends = rest[1 : 1 + len(widths)], rest[1 + len(widths) :]
        at = 0
        for keep, send, cols in zip(keeps, sends, widths):
            part = value[:, at : at + cols]
            send[...] = part.astype(bf16)

            @pl.when(step == 0)
            def _():
                keep[...] = part

            at += cols

    moving = lambda cols: pl.BlockSpec((group, cols), lambda i: (i, 0))
    if got is None:
        specs = moving(total)
        shapes = shape((ny * group, total), bf16)
    else:
        specs = [pl.BlockSpec((group, cols), lambda i: (0, 0)) for cols in widths]
        specs += [moving(cols) for cols in widths]
        shapes = [shape((group, cols), f32) for cols in widths]
        shapes += [shape((ny * group, cols), bf16) for cols in widths]
    outs = pl.pallas_call(
        kernel,
        grid=(ny,),
        out_shape=shapes,
        in_specs=[SMEM]
        + [WHOLE] * (len(lefts) + len(rights))
        + ([] if got is None else [moving(total)]),
        out_specs=specs,
        compiler_params=PARAMS,
        name="weight_grads",
    )(where, *lefts, *rights, *(() if got is None else (got,)))
    return outs if got is None else (outs[: len(widths)], outs[len(widths) :])


def place_rows(where, pieces, gains=None):
    width = pieces[0].shape[-1]
    tokens = sum(piece.shape[0] for piece in pieces)

    def kernel(where_ref, *refs):
        ins, full = refs[: len(pieces)], refs[-1]
        at = 0
        for ref in ins:
            values = ref[...]
            if gains is not None:
                values, _ = normalize(values.astype(f32))
                params = refs[-2]
                values = (values * params[0:1, :] + params[1:2, :]).astype(bf16)
            full[at : at + ref.shape[0], :] = values
            at += ref.shape[0]

    more = () if gains is None else (gains,)
    return call(kernel, "place_rows", shape((tokens, width), bf16), where, *pieces, *more)


def slot_of(k):
    return ((k & 1) << 1) | (k >> 1)


def natural(ref, slot, flip, columns=slice(None)):
    first = ref[flip, slot, :, columns]
    second = ref[1 - flip, slot, :, columns]
    return jnp.concatenate([first, second], axis=0)


def choose(refs, ky, slot, flip, columns=slice(None)):
    values = natural(refs[0], slot, flip, columns)
    for k in range(1, len(refs)):
        values = jnp.where(ky == k, natural(refs[k], slot, flip, columns), values)
    return values


def dot(left, right, dims):
    return lax.dot_general(left, right, (dims, ((), ())), preferred_element_type=f32)


NN, NT, TN = ((1,), (0,)), ((1,), (1,)), ((0,), (0,))


def decays_of(row):
    block = row.shape[-1]
    at = lax.broadcasted_iota(jnp.int32, (block, block), 0)
    to = lax.broadcasted_iota(jnp.int32, (block, block), 1)
    turned = jnp.sum(jnp.where(at == to, row, 0.0), axis=1, keepdims=True)
    running = jnp.sum(jnp.where(at <= to, turned, 0.0), axis=0, keepdims=True)
    col = jnp.sum(jnp.where(at == to, running, 0.0), axis=1, keepdims=True)
    matrix = jnp.where(at >= to, jnp.exp(jnp.minimum(col - running, 0.0)), 0.0)
    return col, running[:, block - 1 :], matrix


def retention_forward(where, decays, keyvals, query_gate):
    ny = len(keyvals)
    halves, nz, part, _ = query_gate.shape

    def kernel(where_ref, decay_ref, *refs):
        kv_refs, (qg_ref, y_ref, n_ref, r_ref, s_ref, q_ref, state) = refs[:ny], refs[ny:]
        j = pl.program_id(0)

        @pl.when(j == 0)
        def _():
            state[...] = jnp.zeros_like(state)

        slot = slot_of((j // ny) ^ where_ref[0])
        ky = (j % ny) ^ where_ref[1]
        flip = where_ref[3]
        col, last, matrix = decays_of(decay_ref[pl.ds(j, 1), :])
        key = choose(kv_refs, ky, slot, flip, slice(0, DK))
        value = choose(kv_refs, ky, slot, flip, slice(DK, DK + DV))

        @pl.when(ky == 0)
        def _():
            q = natural(qg_ref, slot, flip, slice(0, DK)).astype(bf16)
            state_bf = state[...].astype(bf16)
            s_ref[slot] = state_bf
            weights = (dot(q, key, NT) * matrix).astype(bf16)
            out = dot(weights, value, NN) + jnp.exp(col) * dot(q, state_bf, NN)
            normed, rstd = normalize(out)
            g = natural(qg_ref, slot, flip, slice(DK, DK + DV))
            mixed = (g * jax.nn.sigmoid(g) * normed).astype(bf16)
            for half in range(2):
                rows = slice(half * part, (half + 1) * part)
                to = (1 - flip) if half else flip
                y_ref[to, slot] = mixed[rows]
                n_ref[to, slot] = normed[rows]
                r_ref[to, slot] = rstd[rows]
                q_ref[to, slot] = q[rows]

        key_tail = (key.astype(f32) * jnp.exp(last - col)).astype(bf16)
        state[...] = jnp.exp(last) * state[...] + dot(key_tail, value, TN)

    return call(
        kernel,
        "retention_forward",
        [
            shape((halves, nz, part, DV), bf16),
            shape((halves, nz, part, DV), f32),
            shape((halves, nz, part, 1), f32),
            shape((nz, DK, DV), bf16),
            shape((halves, nz, part, DK), bf16),
        ],
        where,
        decays,
        *keyvals,
        query_gate,
        grid=(nz * ny,),
        scratch=[pltpu.VMEM((DK, DV), f32)],
    )


def retention_backward(where, decays, keyval, queries, grads, states, cosines, sines, gate):
    ny = len(queries)
    halves, nz, part, _ = keyval.shape
    key_scale = DK ** (-0.5)

    def kernel(where_ref, decay_ref, *refs):
        q_refs, d_refs, rest = refs[:ny], refs[ny : 2 * ny], refs[2 * ny :]
        kv_ref, s_ref, cos_ref, sin_ref, gate_ref, kv_out, qg_out, state = rest
        step = pl.program_id(0)
        j = nz * ny - 1 - step

        @pl.when(step == 0)
        def _():
            state[...] = jnp.zeros_like(state)
            qg_out[:, :, :, DK:] = gate_ref[...]

        slot = slot_of((j // ny) ^ where_ref[0])
        ky = (j % ny) ^ where_ref[1]
        flip = where_ref[3]
        col, last, matrix = decays_of(decay_ref[pl.ds(j, 1), :])
        q = choose(q_refs, ky, slot, flip)
        grad = choose(d_refs, ky, slot, flip)
        entry = jnp.exp(col)

        @pl.when(ky == 0)
        def _():
            key = natural(kv_ref, slot, flip, slice(0, DK))
            value = natural(kv_ref, slot, flip, slice(DK, DK + DV))
            cos = natural(cos_ref, slot, flip)
            sin = natural(sin_ref, slot, flip)
            tail = jnp.exp(last - col)
            state_bf = state[...].astype(bf16)
            weights = (dot(q, key, NT) * matrix).astype(bf16)
            scores = (dot(grad, value, NT) * matrix).astype(bf16)
            grad_q = dot(scores, key, NN) + entry * dot(grad, s_ref[slot], NT)
            grad_k = dot(scores, q, TN) + tail * dot(value, state_bf, NT)
            grad_v = dot(weights, grad, TN) + tail * dot(key, state_bf, NN)
            grad_q = rotate(grad_q, cos, -sin).astype(bf16)
            grad_k = (rotate(grad_k, cos, -sin) * key_scale).astype(bf16)
            grad_v = grad_v.astype(bf16)
            for half in range(2):
                rows = slice(half * part, (half + 1) * part)
                to = (1 - flip) if half else flip
                kv_out[to, slot, :, :DK] = grad_k[rows]
                kv_out[to, slot, :, DK:] = grad_v[rows]
                qg_out[to, slot, :, :DK] = grad_q[rows]

        query_entry = (q.astype(f32) * entry).astype(bf16)
        state[...] = jnp.exp(last) * state[...] + dot(query_entry, grad, TN)

    return call(
        kernel,
        "retention_backward",
        [shape((halves, nz, part, DK + DV), bf16)] * 2,
        where,
        decays,
        *queries,
        *grads,
        keyval,
        states,
        cosines,
        sines,
        gate,
        grid=(nz * ny,),
        scratch=[pltpu.VMEM((DK, DV), f32)],
    )


def shards(
    hidden_in,
    log_decay,
    out_grad,
    ln1_gain,
    ln1_bias,
    w_query,
    w_key,
    w_value,
    w_gate,
    w_out,
    ln2_gain,
    ln2_bias,
    mlp_gate,
    mlp_up,
    mlp_down,
):
    nz, ny = lax.axis_size("row"), lax.axis_size("col")
    nb, nh = lax.axis_size("batch"), lax.axis_size("head")
    block, width = hidden_in.shape[1:]
    rows = ln1_gain.shape[0]
    part = block // nh
    tokens = nz * block
    half, quarter = tokens // 2, tokens // 4
    group = nz * rows
    sizes = (nz, ny, nb)
    where = jnp.stack([lax.axis_index(name) for name in ("row", "col", "batch", "head")])
    (where,) = tie(where.astype(jnp.int32))

    def trade(pieces, k):
        return swap(pieces[k], "row", k) if k else pieces[k]

    def over_col(own):
        return [own] + [swap(own, "col", k) for k in range(1, ny)]

    def over_batch(values):
        return [swap(value, "batch", 1) for value in values]

    def mirror(values):
        return swap(values, "head", 1)

    def pairs(own, other):
        return [(part,) for both in zip(own, other) for part in both]

    def split(values):
        return values.reshape(nh, nz, part, -1)

    def add(values, got):
        return values + got.astype(f32)

    def sum_col(keep, send):
        for k in range(1, ny):
            keep = add(keep, swap(send[k * group : (k + 1) * group], "col", k))
        return keep.reshape(nz, rows, -1)

    def reduce_far(*terms):
        far = sum(matmul_t(values[half:], weight) for values, weight in terms).astype(bf16)
        return far[quarter:], far[:quarter]

    def reduce_near(*terms):
        near = sum(matmul_t(values[:half], weight) for values, weight in terms)
        return near[quarter:], near[:quarter]

    gains = jnp.concatenate([ln1_gain, ln1_bias, ln2_gain, ln2_bias])[None]
    own_in, other_in = cut_halves(where, hidden_in[0], nh)
    two_in = swap(own_in, "row", 2)
    kv = pack_weights(where, (w_key, w_value), nz, rows, (gains, log_decay[0]))
    kv = [trade(kv, k) for k in range(nz)]
    kv, two_in, late = tie(kv, two_in, (w_query, w_gate))
    kv_cols = over_col(jnp.stack(kv))
    one_in = swap(jnp.concatenate([own_in, two_in]), "row", 1)
    query_gate = pack_weights(where, late, nz, rows)
    query_gate = [trade(query_gate, k) for k in range(nz)]
    out = pack_weights(where, (w_out,), nz, rows)
    out_near, out_far = jnp.stack(out[:2]), jnp.stack(out[2:])
    half_dim = DK // 2
    freqs = 10000.0 ** (-jnp.arange(half_dim, dtype=f32) / half_dim)
    block_at = (jnp.array(ORDER, jnp.int32) ^ where[0:1]) * ny + where[1:2]
    half_at = jnp.arange(nh, dtype=jnp.int32) ^ where[3:4]
    positions = (
        block_at[None, :, None] * block + half_at[:, None, None] * part + jnp.arange(part)
    )
    angles = positions.astype(f32)[..., None] * freqs
    cosines, sines = jnp.cos(angles), jnp.sin(angles)
    kv_cols, one_in, query_gate, out_near, out_far, cosines, sines = tie(
        kv_cols, one_in, query_gate, out_near, out_far, cosines, sines
    )
    kv_mates = over_batch(kv_cols)
    mirror_in = mirror(jnp.concatenate([two_in, one_in]))
    qg_cols = over_col(jnp.stack(query_gate))
    out_far = swap(out_far, "row", 2)
    feed = pack_weights(where, (mlp_gate, mlp_up, mlp_down), nz, rows)
    kv_mates, mirror_in, qg_cols, out_far, feed = tie(kv_mates, mirror_in, qg_cols, out_far, feed)
    kv_w, gains, decays = assemble(
        where, pairs(kv_cols, kv_mates), ny, nb, (DK + DV,), EXTRA, block
    )

    first_bf = place_rows(where, (own_in, two_in, one_in, other_in, mirror_in), gains)
    key_scale = DK ** (-0.5)
    projected = split(matmul(first_bf, kv_w))
    key_bf = (rotate(projected[..., :DK], cosines, sines) * key_scale).astype(bf16)
    keyval = jnp.concatenate([key_bf, projected[..., DK:].astype(bf16)], axis=-1)

    keyval, qg_cols, out_far, feed = tie(keyval, qg_cols, out_far, feed)
    keyvals = over_col(keyval)
    out_last = swap(jnp.stack([out_near[1], out_far[1]]), "row", 1)
    feed_two = trade(feed, 2)
    (qg_w,) = assemble(where, pairs(qg_cols, over_batch(qg_cols)), ny, nb, (DK + DV,))
    projected = split(matmul(first_bf, qg_w))
    query_gate = jnp.concatenate(
        [rotate(projected[..., :DK], cosines, sines), projected[..., DK:]], axis=-1
    )
    keyvals, query_gate, out_last, feed_two = tie(keyvals, query_gate, out_last, feed_two)
    out_cols = over_col(jnp.stack([out_near[0], out_last[0], out_far[0], out_last[1]]))
    feed_three = trade(after(feed, keyvals), 3)
    mixed, normed, rstd, states, query = retention_forward(where, decays, keyvals, query_gate)
    mixed, out_cols, feed_three = tie(mixed, out_cols, feed_three)
    (out_w,) = assemble(where, pairs(out_cols, over_batch(out_cols)), ny, nb, (DV,))
    mixed_bf = mixed.reshape(tokens, DV)

    far = reduce_far((mixed_bf, out_w))
    got = mirror(far[0])
    near = reduce_near((mixed_bf, out_w))
    late_feed, late_grad, query = after((feed, out_grad[0], query), mixed)
    own_grad, other_grad = cut_halves(where, late_grad, nh)
    feed_one = trade(late_feed, 1)
    two_grad = swap(own_grad, "row", 2)
    queries = over_col(query)
    got, near, feed_one, two_grad, queries = tie(got, near, feed_one, two_grad, queries)
    got, got_far = swap(add(near[0], got).astype(bf16), "row", 1), mirror(far[1])
    feed = jnp.stack([feed[0], feed_one, feed_two, feed_three])
    units = feed.shape[-1] // 3
    feed_gates = over_col(feed[..., :units])[1:]
    feed_mate = swap(feed, "batch", 1)
    got, got_far, feed_gates, feed_mate, feed = tie(got, got_far, feed_gates, feed_mate, feed)
    keep = add(add(near[1], got_far), got)
    got = swap(keep[part:].astype(bf16), "row", 2)
    late_feed, late_two = after((feed, two_grad), keep)
    feed_ups = over_col(late_feed[..., units : 2 * units])[1:]
    one_grad = swap(jnp.concatenate([own_grad, late_two]), "row", 1)
    mirror_two = mirror(late_two)
    got, feed_ups, one_grad, mirror_two = tie(got, feed_ups, one_grad, mirror_two)
    inputs = own_in.astype(f32)
    middle = inputs + add(keep[:part], got)
    scaled_two, rstd_two = normalize(middle)
    own = (scaled_two * gains[2:3] + gains[3:4]).astype(bf16)
    two = swap(own, "row", 2)
    late_feed, late_one, feed_gates, feed_ups = after((feed, one_grad, feed_gates, feed_ups), own)
    feed_downs = over_col(late_feed[..., 2 * units :])[1:]
    mirror_one = mirror(late_one)
    gate_mates, up_mates = over_batch(feed_gates), over_batch(feed_ups)
    two, feed_downs, mirror_one, gate_mates, up_mates = tie(
        two, feed_downs, mirror_one, gate_mates, up_mates
    )
    pair = jnp.concatenate([own, two])
    one, mirror_pair = swap(pair, "row", 1), mirror(pair)
    down_mates = over_batch(after(feed_downs, pair))
    one, mirror_pair, down_mates = tie(one, mirror_pair, down_mates)
    mirror_last = mirror(one)
    parts = [(feed,), (feed_mate,)]
    for three in zip(feed_gates, feed_ups, feed_downs, gate_mates, up_mates, down_mates):
        parts += [three[:3], three[3:]]
    up_w, down_w = assemble(where, after(parts, one), ny, nb, (2 * units, units))
    down_bf = place_rows(
        where, after((own_grad, two_grad, one_grad, other_grad, mirror_two, mirror_one), one)
    )
    mirror_last, up_w, down_w, down_bf = tie(mirror_last, up_w, down_w, down_bf)
    second_bf = place_rows(where, (pair, one, mirror_pair, mirror_last))

    up = matmul(second_bf, up_w)
    up_gate, up_lin = up[:, :units], up[:, units:]
    gelu_cdf = 0.5 * (1.0 + lax.erf(up_gate * (0.5**0.5)))
    gelu_val = up_gate * gelu_cdf
    gelu_slope = gelu_cdf + up_gate * jnp.exp(-0.5 * up_gate * up_gate) * (2.0 * jnp.pi) ** -0.5
    hidden_bf = (gelu_val * up_lin).astype(bf16)
    grad_hidden = matmul(down_bf, down_w)
    grad_upgate = (grad_hidden * up_lin * gelu_slope).astype(bf16)
    grad_uplin = (grad_hidden * gelu_val).astype(bf16)
    grad_up = jnp.concatenate([grad_upgate, grad_uplin], axis=-1)
    far = reduce_far((grad_up, up_w))
    got = mirror(far[0])
    near = reduce_near((grad_up, up_w))
    lefts, rights = (second_bf, down_bf), (grad_up, hidden_bf)
    feed_far = weight_grads(where, lefts, rights, sizes)
    got, near, feed_far, hidden_bf = tie(got, near, feed_far, hidden_bf)
    got, got_far = swap(add(near[0], got).astype(bf16), "row", 1), mirror(far[1])
    result_far = reduce_far((hidden_bf, down_w))
    feed_got = swap(feed_far, "batch", 1)
    feed_keeps, feed_sends = weight_grads(where, lefts, rights, sizes, (units,) * 3, feed_got)
    got, got_far, result_far, hidden_bf, feed_sends = tie(
        got, got_far, result_far, hidden_bf, feed_sends
    )
    keep = add(add(near[1], got_far), got)
    got = swap(keep[part:].astype(bf16), "row", 2)
    result_got = mirror(result_far[0])
    result_near = reduce_near((hidden_bf, down_w))
    gate_sum = sum_col(feed_keeps[0], feed_sends[0])
    got, result_got, result_near, gate_sum = tie(got, result_got, result_near, gate_sum)
    grad_two = add(keep[:part], got)
    grad_middle = own_grad.astype(f32) + norm_back(grad_two * gains[2:3], scaled_two, rstd_two)
    own, up_send, result_got = tie(grad_middle.astype(bf16), feed_sends[1], result_got)
    two = swap(own, "row", 2)
    result_got_far = mirror(after(result_far[1], own))
    result_got = swap(add(result_near[0], result_got).astype(bf16), "row", 1)
    up_sum = sum_col(feed_keeps[1], up_send)
    two, result_got_far, result_got, up_sum = tie(two, result_got_far, result_got, up_sum)
    pair = jnp.concatenate([own, two])
    one, mirror_pair = swap(pair, "row", 1), mirror(pair)
    down_sum = sum_col(feed_keeps[2], after(feed_sends[2], pair))
    feed_grads = cut_heads(where, (gate_sum, up_sum, down_sum))
    result_keep = add(add(result_near[1], result_got_far), result_got)
    result_send = result_keep[part:].astype(bf16)
    one, mirror_pair, feed_grads, result_send = tie(one, mirror_pair, feed_grads, result_send)
    mirror_last = mirror(one)
    feed_two, feed_one = trade(feed_grads, 2), trade(feed_grads, 1)
    mirror_last, feed_two, feed_one = tie(mirror_last, feed_two, feed_one)
    attn_bf = place_rows(where, (pair, one, mirror_pair, mirror_last))

    grp_norm, grp_rstd = normed.reshape(tokens, DV), rstd.reshape(tokens, 1)
    gate = query_gate.reshape(tokens, -1)[:, DK:]
    gate_sig = jax.nn.sigmoid(gate)
    gate_act = gate * gate_sig
    grad_mixed = matmul(attn_bf, out_w)
    grad_gate = (grad_mixed * grp_norm * (gate_sig * (1.0 + gate * (1.0 - gate_sig)))).astype(bf16)
    ret_bf = norm_back(grad_mixed * gate_act, grp_norm, grp_rstd).astype(bf16)
    ret_bf, feed_grads = tie(split(ret_bf), feed_grads)
    ret_all = over_col(ret_bf)
    feed_three = trade(feed_grads, 3)
    lefts, rights = (first_bf, attn_bf), (grad_gate, mixed_bf)
    both_far = weight_grads(where, lefts, rights, sizes)
    ret_all, feed_three, both_far = tie(ret_all, feed_three, both_far)
    grad_kv, grad_qg = retention_backward(
        where, decays, keyval, queries, ret_all, states, cosines, sines, split(grad_gate)
    )
    grad_kv, grad_qg = grad_kv.reshape(tokens, -1), grad_qg.reshape(tokens, -1)
    terms = ((grad_kv, kv_w), (grad_qg, qg_w))
    far = reduce_far(*terms)
    got = mirror(far[0])
    kvq = ((first_bf, first_bf), (grad_kv, (grad_qg, 0, DK)))
    kvq_far = weight_grads(where, *kvq, sizes)
    result_send, both_far = after((result_send, both_far), grad_kv)
    result_got = swap(result_send, "row", 2)
    near = reduce_near(*terms)
    kvq_got, both_got = over_batch((kvq_far, both_far))
    kvq_keeps, kvq_sends = weight_grads(where, *kvq, sizes, (DV, 2 * DK), kvq_got)
    got, near, result_got, kvq_sends, both_got = tie(got, near, result_got, kvq_sends, both_got)
    got, got_far = swap(add(near[0], got).astype(bf16), "row", 1), mirror(far[1])
    kvq_first = sum_col(kvq_keeps[0], kvq_sends[0])
    both_keeps, both_sends = weight_grads(where, lefts, rights, sizes, (2 * DV,), both_got)
    got, got_far, kvq_first, both_sends, kvq_sends = tie(
        got, got_far, kvq_first, both_sends, kvq_sends
    )
    keep = add(add(near[1], got_far), got)
    got = swap(keep[part:].astype(bf16), "row", 2)
    result = (middle + add(result_keep[:part], result_got)).astype(bf16)
    result_other = mirror(result)
    grad_gates, grad_ups, grad_downs = unpack_grads(
        where,
        (feed_grads[0], feed_one, feed_two, feed_three),
        ((units, False), (units, False), (units, True)),
    )
    kvq_second = sum_col(kvq_keeps[1], kvq_sends[1])
    got, result_other, grad_gates, grad_ups, grad_downs, kvq_second, both_sends = tie(
        got, result_other, grad_gates, grad_ups, grad_downs, kvq_second, both_sends
    )
    kvq_pieces = cut_heads(where, (kvq_first, kvq_second))
    kvq_pieces = [trade(kvq_pieces, k) for k in range(nz)]
    both_sum = sum_col(both_keeps[0], both_sends[0])
    grad_one = add(keep[:part], got)
    scaled_own, rstd_own = normalize(inputs)
    grad_in = grad_middle + norm_back(grad_one * gains[0:1], scaled_own, rstd_own)
    grad_in_other = mirror(grad_in)
    kvq_pieces, both_sum, grad_in_other, grad_one = tie(
        kvq_pieces, both_sum, grad_in_other, grad_one
    )
    both_pieces = cut_heads(where, (both_sum,))
    both_pieces = [trade(both_pieces, k) for k in range(nz)]
    grad_k, grad_v, grad_q = unpack_grads(
        where, kvq_pieces, ((DK, False), (DV, False), (DK, False))
    )
    grad_g, grad_outs = unpack_grads(where, both_pieces, ((DV, False), (DV, True)))

    def join(own, other):
        return join_halves(where, own, other).reshape(1, block, width)

    norm_sums = jnp.stack(
        [
            jnp.sum(grad_one * scaled_own, axis=0),
            jnp.sum(grad_one, axis=0),
            jnp.sum(grad_two * scaled_two, axis=0),
            jnp.sum(grad_two, axis=0),
        ]
    )
    norm_sums = norm_sums + swap(norm_sums, "head", 1)
    norm_sums = norm_sums.reshape(4, nz, ny, nb, rows)
    for name, axis in (("batch", 3), ("col", 2), ("row", 1)):
        me = lax.axis_index(name)
        summed = pick(norm_sums, me, axis)
        for k in range(1, lax.axis_size(name)):
            summed = summed + swap(pick(norm_sums, me ^ k, axis), name, k)
        norm_sums = summed

    return (
        join(result, result_other),
        join(grad_in, grad_in_other),
        norm_sums[0],
        norm_sums[1],
        grad_q,
        grad_k,
        grad_v,
        grad_g,
        grad_outs,
        norm_sums[2],
        norm_sums[3],
        grad_gates,
        grad_ups,
        grad_downs,
    )


def solution(mesh):
    seq = ("row", "col")
    tokens = P("batch", seq, None)
    params = P((*seq, "batch"))
    by_rows = P((*seq, "batch"), "head")
    by_cols = P("head", (*seq, "batch"))

    def run(*arrays):
        rows = arrays[1].shape[1] // mesh.shape["head"]
        sizes = (rows, mesh.shape["seq"] // rows, mesh.shape["batch"], mesh.shape["head"])
        order = [mesh.axis_names.index(n) for n in ("seq", "batch", "head")]
        fine = Mesh(
            mesh.devices.transpose(order).reshape(sizes), ("row", "col", "batch", "head")
        )
        weights = (by_rows, by_rows, by_rows, by_rows, by_cols)
        feeds = (by_rows, by_rows, by_cols)
        return jax.shard_map(
            shards,
            mesh=fine,
            in_specs=(
                tokens,
                P("batch", "head", seq),
                tokens,
                params,
                params,
                *weights,
                params,
                params,
                *feeds,
            ),
            out_specs=(tokens, tokens, params, params, *weights, params, params, *feeds),
            check_vma=False,
        )(*arrays)

    return run
```

```python
import jax
import jax.numpy as jnp
from jax import lax
from jax.experimental import pallas as pl
from jax.experimental.pallas import tpu as pltpu
from jax.sharding import Mesh
from jax.sharding import PartitionSpec as P

DK = 256
DV = 512

epsilon = 1e-05
f32 = jnp.float32
bf16 = jnp.bfloat16
VMEM_LIMIT = 12 * 1024 * 1024

ORDER = (0, 3, 1, 2)


def swap(values, axis, k):
    count = lax.axis_size(axis)
    return lax.ppermute(values, axis, [(i, i ^ k) for i in range(count)])


def pick(values, index, axis):
    return lax.dynamic_index_in_dim(values, index, axis, keepdims=False)


def tie(*values):
    return lax.optimization_barrier(values)


def after(values, *others):
    return tie(values, others)[0]


def matmul(values, weight):
    return jnp.dot(values, weight, preferred_element_type=f32)


def matmul_t(values, weight):
    return lax.dot_general(values, weight, (((1,), (1,)), ((), ())), preferred_element_type=f32)


def outer_sum(values, other):
    return lax.dot_general(values, other, (((0,), (0,)), ((), ())), preferred_element_type=f32)


def normalize(values):
    center = values - jnp.mean(values, axis=-1, keepdims=True)
    rstd = lax.rsqrt(jnp.mean(center * center, axis=-1, keepdims=True) + epsilon)
    return center * rstd, rstd


def norm_back(scaled_grad, scaled, rstd):
    return rstd * (
        scaled_grad
        - jnp.mean(scaled_grad, axis=-1, keepdims=True)
        - scaled * jnp.mean(scaled_grad * scaled, axis=-1, keepdims=True)
    )


def rotate(values, cosines, sines):
    half_dim = values.shape[-1] // 2
    first_half = values[..., :half_dim]
    second_half = values[..., half_dim:]
    return jnp.concatenate(
        [first_half * cosines - second_half * sines, first_half * sines + second_half * cosines],
        axis=-1,
    )


SMEM = pl.BlockSpec(memory_space=pltpu.SMEM)
WHOLE = pl.BlockSpec(memory_space=pltpu.VMEM)
PARAMS = pltpu.CompilerParams(vmem_limit_bytes=VMEM_LIMIT)


def call(kernel, name, shapes, *operands, grid=None, scratch=()):
    many = isinstance(shapes, list)
    return pl.pallas_call(
        kernel,
        grid=() if grid is None else grid,
        out_shape=shapes,
        in_specs=[SMEM] + [WHOLE] * (len(operands) - 1),
        out_specs=[WHOLE] * len(shapes) if many else WHOLE,
        scratch_shapes=list(scratch),
        compiler_params=PARAMS,
        name=name,
    )(*operands)


def shape(dims, dtype):
    return jax.ShapeDtypeStruct(tuple(dims), dtype)


def cut_halves(where, values, heads):
    block, width = values.shape
    part = block // heads

    def kernel(where_ref, ref, own, other):
        for out, half in ((own, where_ref[3]), (other, 1 - where_ref[3])):
            out[...] = ref[pl.ds(pl.multiple_of(half * part, part), part), :]

    return call(kernel, "cut_halves", [shape((part, width), values.dtype)] * 2, where, values)


def join_halves(where, own, other):
    part, width = own.shape

    def kernel(where_ref, own_ref, other_ref, out):
        for ref, half in ((own_ref, where_ref[3]), (other_ref, 1 - where_ref[3])):
            out[pl.ds(pl.multiple_of(half * part, part), part), :] = ref[...]

    return call(kernel, "join_halves", shape((2 * part, width), own.dtype), where, own, other)


def cut_heads(where, totals, first=0):
    nz, rows, _ = totals[0].shape
    width = sum(total.shape[2] for total in totals)

    def kernel(where_ref, *refs):
        ins, outs = refs[: len(totals)], refs[len(totals) :]
        targets = [outs[k] for k in range(nz)] if not first else steps(outs, first)
        for k in range(nz):
            at = 0
            for ref in ins:
                cols = ref.shape[2]
                targets[k][:, at : at + cols] = ref[where_ref[0] ^ k].astype(bf16)
                at += cols

    shapes = [shape((rows, width), bf16)] * nz
    if first:
        shapes = shapes[:2] + [shape((2, rows, width), bf16)]
    return call(kernel, "cut_heads", shapes, where, *totals)


def steps(refs, first):
    stay, second, firsts = refs
    return {0: stay, 4 - first: second, first: firsts.at[0], 2: firsts.at[1]}


def pack_weights(where, weights, nz, rows, extras=None, first=0):
    widths = [w.size // rows // nz for w in weights]
    total = sum(widths)
    count = 0
    if extras:
        gains, decays = extras
        block = decays.shape[1]
        extras = (jnp.pad(gains, ((0, 0), (0, total - gains.shape[1]))), decays)
        count = EXTRA

    def kernel(where_ref, *refs):
        ins, rest = refs[: len(weights)], refs[len(weights) :]
        outs = steps(rest, first) if first else rest[-nz:]
        for k in range(nz):
            target = where_ref[0] ^ k
            at = 0
            for ref, width in zip(ins, widths):
                start = pl.multiple_of(target * width, width)
                if ref.shape[0] == rows:
                    piece = ref[:, pl.ds(start, width)]
                else:
                    piece = ref[pl.ds(start, width), :].astype(f32).T.astype(bf16)
                outs[k][:rows, at : at + width] = piece
                at += width
            if extras:
                line = lax.broadcasted_iota(jnp.int32, (EXTRA, 1), 0)
                gain_rows = jnp.where(line == 0, rest[0][...].astype(f32), 0.0)
                parts = gain_rows[:, :block]
                left = rest[1][pl.ds(target, 1), :]
                for number in range(1, 4):
                    part = left.astype(bf16).astype(f32)
                    parts = jnp.where(line == number, part, parts)
                    left = left - part
                outs[k][rows:, :] = gain_rows.astype(bf16)
                outs[k][rows:, :block] = parts.astype(bf16)

    shapes = [shape((rows + count, total), bf16)] * nz
    if first:
        shapes = shapes[:2] + [shape((2, rows, total), bf16)]
    return call(kernel, "pack_weights", shapes, where, *weights, *(extras or ()))


def unpack_grads(where, pieces, outs):
    nz = len(pieces)
    rows = pieces[0].shape[0]

    def kernel(where_ref, *refs):
        ins, results = refs[:nz], refs[nz:]
        for k in range(nz):
            target = where_ref[0] ^ k
            at = 0
            for ref, (width, turned) in zip(results, outs):
                to = pl.ds(pl.multiple_of(target * width, width), width)
                piece = ins[k][:, at : at + width].astype(f32)
                if turned:
                    ref[to, :] = piece.T
                else:
                    ref[:, to] = piece
                at += width

    shapes = [shape((nz * w, rows) if turned else (rows, nz * w), f32) for w, turned in outs]
    return call(kernel, "unpack_grads", shapes, where, *pieces)


EXTRA = 16


def assemble(where, parts, ny, nb, widths, extra=0, block=0):
    nz, rows, _ = parts[0][0].shape
    rows -= extra
    count = nz * ny * nb
    total = sum(widths)
    sizes = [len(part) for part in parts]
    aligned = rows % 128 == 0

    def kernel(where_ref, *refs):
        ins, outs = refs[: sum(sizes)], refs[sum(sizes) :]
        for ky in range(ny):
            for kb in range(nb):
                pieces, ins = ins[: sizes[ky * nb + kb]], ins[sizes[ky * nb + kb] :]
                for kz in range(nz):
                    place = (where_ref[0] ^ kz) * ny + (where_ref[1] ^ ky)
                    device = place * nb + (where_ref[2] ^ kb)
                    at = pl.multiple_of(device * rows, rows)
                    column = 0
                    for piece in pieces:
                        cols = piece.shape[-1]
                        start = 0
                        for out, width in zip(outs, widths):
                            low, high = max(start, column), min(start + width, column + cols)
                            if low < high:
                                out[pl.ds(at, rows), low - start : high - start] = piece[
                                    kz, :rows, low - column : high - column
                                ]
                            start += width
                        column += cols
                    if extra:
                        tail = pieces[0][kz, rows:, :].astype(f32)
                        if aligned:
                            for number in range(4):
                                gain = tail[:1, number * rows : (number + 1) * rows]
                                outs[-2][number : number + 1, pl.ds(at, rows)] = gain
                        else:
                            outs[-2][pl.ds(device, 1), :] = tail[:1]
                        if kb == 0:
                            decay = (tail[1:2] + tail[2:3]) + tail[3:4]
                            outs[-1][pl.ds(place, 1), :] = decay[:, :block]

    shapes = [shape((count * rows, width), bf16) for width in widths]
    if extra:
        shapes.append(shape((4, count * rows) if aligned else (count, total), f32))
        shapes.append(shape((nz * ny, block), f32))
    outs = list(call(kernel, "assemble", shapes, where, *[p for part in parts for p in part]))
    if extra and not aligned:
        gains = outs[-2][:, : 4 * rows].reshape(count, 4, rows)
        outs[-2] = gains.transpose(1, 0, 2).reshape(4, count * rows)
    return outs


def row_groups(where, left, sizes):
    nz, ny, nb = sizes
    groups = left.reshape(left.shape[0], nz, ny, nb, -1)
    groups = jnp.take(groups, jnp.arange(ny) ^ where[1], axis=2)
    groups = jnp.take(groups, jnp.arange(nb) ^ where[2], axis=3)
    return groups.transpose(0, 3, 2, 1, 4).reshape(left.shape)


def weight_grads(where, lefts, rights, sizes, widths=None, got=None):
    nz, ny, nb = sizes
    width = lefts[0].shape[1]
    rows = width // (nz * ny * nb)
    group = nz * rows
    rights = [right if isinstance(right, tuple) else (right, 0, right.shape[1]) for right in rights]
    ranges = [right[1:] for right in rights]
    rights = [right[0] for right in rights]
    total = sum(high - low for low, high in ranges)
    kb = 1 if got is None else 0
    aligned = rows % 128 == 0
    if not aligned:
        lefts = [row_groups(where, left, sizes) for left in lefts]

    def columns(where_ref, left, step):
        if not aligned:
            return left[:, pl.ds(pl.multiple_of((kb * ny + step) * group, group), group)]
        tiles = []
        for z in range(nz):
            start = ((z * ny + (where_ref[1] ^ step)) * nb + (where_ref[2] ^ kb)) * rows
            tiles.append(left[:, pl.ds(pl.multiple_of(start, rows), rows)])
        return jnp.concatenate(tiles, axis=1)

    def kernel(where_ref, *refs):
        ins, rest = refs[: len(lefts)], refs[len(lefts) :]
        others, rest = rest[: len(rights)], rest[len(rights) :]
        step = pl.program_id(0)
        values = []
        for left, right, (low, high) in zip(ins, others, ranges):
            values.append(dot(columns(where_ref, left, step), right[:, low:high], TN))
        if got is None:
            at = 0
            for value in values:
                rest[0][:, at : at + value.shape[1]] = value.astype(bf16)
                at += value.shape[1]
            return
        value = jnp.concatenate(values, axis=1) + rest[0][...].astype(f32)
        keeps, sends = rest[1 : 1 + len(widths)], rest[1 + len(widths) :]
        at = 0
        for keep, send, cols in zip(keeps, sends, widths):
            part = value[:, at : at + cols]
            send[...] = part.astype(bf16)

            @pl.when(step == 0)
            def _():
                keep[...] = part

            at += cols

    moving = lambda cols: pl.BlockSpec((group, cols), lambda i: (i, 0))
    if got is None:
        specs = moving(total)
        shapes = shape((ny * group, total), bf16)
    else:
        specs = [pl.BlockSpec((group, cols), lambda i: (0, 0)) for cols in widths]
        specs += [moving(cols) for cols in widths]
        shapes = [shape((group, cols), f32) for cols in widths]
        shapes += [shape((ny * group, cols), bf16) for cols in widths]
    outs = pl.pallas_call(
        kernel,
        grid=(ny,),
        out_shape=shapes,
        in_specs=[SMEM]
        + [WHOLE] * (len(lefts) + len(rights))
        + ([] if got is None else [moving(total)]),
        out_specs=specs,
        compiler_params=PARAMS,
        name="weight_grads",
    )(where, *lefts, *rights, *(() if got is None else (got,)))
    return outs if got is None else (outs[: len(widths)], outs[len(widths) :])


def place_rows(where, pieces, gains=None):
    width = pieces[0].shape[-1]
    tokens = sum(piece.shape[0] for piece in pieces)

    def kernel(where_ref, *refs):
        ins, full = refs[: len(pieces)], refs[-1]
        at = 0
        for ref in ins:
            values = ref[...]
            if gains is not None:
                values, _ = normalize(values.astype(f32))
                params = refs[-2]
                values = (values * params[0:1, :] + params[1:2, :]).astype(bf16)
            full[at : at + ref.shape[0], :] = values
            at += ref.shape[0]

    more = () if gains is None else (gains,)
    return call(kernel, "place_rows", shape((tokens, width), bf16), where, *pieces, *more)


LOW = 16


def write_message(ref, values, part, columns=slice(None)):
    count = values.shape[0]
    high = values.astype(bf16)
    ref[:count, columns] = high
    low = values - high.astype(f32)
    line = lax.broadcasted_iota(jnp.int32, (LOW, 1), 0)
    rows = jnp.zeros((LOW, values.shape[1]), f32)
    for number in range(count // part):
        rows = jnp.where(line == number, low[number * part : number * part + 1], rows)
    ref[count:, columns] = rows.astype(bf16)


def read_message(ref, part):
    count = ref.shape[0] - LOW
    values = ref[:count, :].astype(f32)
    low = ref[count:, :].astype(f32)
    line = lax.broadcasted_iota(jnp.int32, (count, 1), 0)
    for number in range(count // part):
        values = values + jnp.where(line == number * part, low[number : number + 1], 0.0)
    return values


def far_messages(where, values, weight, part):
    half = values.shape[0] // 2
    quarter = half // 2
    width, depth = weight.shape
    step = width // 4

    def kernel(where_ref, value_ref, weight_ref, second, first):
        out = dot(value_ref[half:, :], weight_ref[...], NT)
        write_message(second, out[quarter:], part)
        write_message(first, out[:quarter], part)

    return pl.pallas_call(
        kernel,
        grid=(4,),
        out_shape=[shape((quarter + LOW, width), bf16)] * 2,
        in_specs=[SMEM, WHOLE, pl.BlockSpec((step, depth), lambda i: (i, 0))],
        out_specs=[pl.BlockSpec((quarter + LOW, step), lambda i: (0, i))] * 2,
        compiler_params=PARAMS,
        name="far_messages",
    )(where, values, weight)


def pass_message(where, near, got, part):
    def kernel(where_ref, near_ref, got_ref, out):
        write_message(out, near_ref[...] + read_message(got_ref, part), part)

    return call(kernel, "pass_message", shape(got.shape, bf16), where, near, got)


def keep_message(where, near, got_far, got, part):
    width = near.shape[1]

    def kernel(where_ref, near_ref, far_ref, got_ref, keep, out):
        total = near_ref[...] + read_message(far_ref, part) + read_message(got_ref, part)
        keep[...] = total[:part]
        write_message(out, total[part:], part)

    shapes = [shape((part, width), f32), shape((part + LOW, width), bf16)]
    return call(kernel, "keep_message", shapes, where, near, got_far, got)


def second_norm(where, inputs, keep, got, gains, part):
    width = keep.shape[1]

    def kernel(where_ref, in_ref, keep_ref, got_ref, gain_ref, middle, scaled, rstd, out):
        total = in_ref[...].astype(f32) + (keep_ref[...] + read_message(got_ref, part))
        middle[...] = total
        normed, factor = normalize(total)
        scaled[...] = normed
        rstd[...] = factor
        out[...] = (normed * gain_ref[2:3, :] + gain_ref[3:4, :]).astype(bf16)

    full = shape((part, width), f32)
    shapes = [full, full, shape((part, 1), f32), shape((part, width), bf16)]
    return call(kernel, "second_norm", shapes, where, inputs, keep, got, gains)


def second_norm_back(where, grad, keep, got, gains, scaled, rstd, part):
    width = keep.shape[1]

    def kernel(where_ref, g_ref, keep_ref, got_ref, gain_ref, scaled_ref, rstd_ref, two, mid, out):
        total = keep_ref[...] + read_message(got_ref, part)
        two[...] = total
        back = norm_back(total * gain_ref[2:3, :], scaled_ref[...], rstd_ref[...])
        back = g_ref[...].astype(f32) + back
        mid[...] = back
        out[...] = back.astype(bf16)

    full = shape((part, width), f32)
    shapes = [full, full, shape((part, width), bf16)]
    operands = (where, grad, keep, got, gains, scaled, rstd)
    return call(kernel, "second_norm_back", shapes, *operands)


def slot_of(k):
    return (((k & 1) ^ (k >> 1)) << 1) | (k >> 1)


def natural(ref, slot, flip, columns=slice(None)):
    first = ref[flip, slot, :, columns]
    second = ref[1 - flip, slot, :, columns]
    return jnp.concatenate([first, second], axis=0)


def choose(refs, ky, slot, flip, columns=slice(None)):
    values = natural(refs[0], slot, flip, columns)
    for k in range(1, len(refs)):
        values = jnp.where(ky == k, natural(refs[k], slot, flip, columns), values)
    return values


def dot(left, right, dims):
    return lax.dot_general(left, right, (dims, ((), ())), preferred_element_type=f32)


NN, NT, TN = ((1,), (0,)), ((1,), (1,)), ((0,), (0,))


def decays_of(row):
    block = row.shape[-1]
    at = lax.broadcasted_iota(jnp.int32, (block, block), 0)
    to = lax.broadcasted_iota(jnp.int32, (block, block), 1)
    turned = jnp.sum(jnp.where(at == to, row, 0.0), axis=1, keepdims=True)
    running = jnp.sum(jnp.where(at <= to, turned, 0.0), axis=0, keepdims=True)
    col = jnp.sum(jnp.where(at == to, running, 0.0), axis=1, keepdims=True)
    matrix = jnp.where(at >= to, jnp.exp(jnp.minimum(col - running, 0.0)), 0.0)
    return col, running[:, block - 1 :], matrix


def retention_forward(where, decays, keyvals, query_gate):
    ny = len(keyvals)
    halves, nz, part, _ = query_gate.shape

    def kernel(where_ref, decay_ref, *refs):
        kv_refs, (qg_ref, y_ref, n_ref, r_ref, s_ref, q_ref, state) = refs[:ny], refs[ny:]
        j = pl.program_id(0)

        @pl.when(j == 0)
        def _():
            state[...] = jnp.zeros_like(state)

        slot = slot_of((j // ny) ^ where_ref[0])
        ky = (j % ny) ^ where_ref[1]
        flip = where_ref[3]
        col, last, matrix = decays_of(decay_ref[pl.ds(j, 1), :])
        key = choose(kv_refs, ky, slot, flip, slice(0, DK))
        value = choose(kv_refs, ky, slot, flip, slice(DK, DK + DV))

        @pl.when(ky == 0)
        def _():
            q = natural(qg_ref, slot, flip, slice(0, DK)).astype(bf16)
            state_bf = state[...].astype(bf16)
            s_ref[slot] = state_bf
            weights = (dot(q, key, NT) * matrix).astype(bf16)
            out = dot(weights, value, NN) + jnp.exp(col) * dot(q, state_bf, NN)
            normed, rstd = normalize(out)
            g = natural(qg_ref, slot, flip, slice(DK, DK + DV))
            mixed = (g * jax.nn.sigmoid(g) * normed).astype(bf16)
            for half in range(2):
                rows = slice(half * part, (half + 1) * part)
                to = (1 - flip) if half else flip
                y_ref[to, slot] = mixed[rows]
                n_ref[to, slot] = normed[rows]
                r_ref[to, slot] = rstd[rows]
                q_ref[to, slot] = q[rows]

        key_tail = (key.astype(f32) * jnp.exp(last - col)).astype(bf16)
        state[...] = jnp.exp(last) * state[...] + dot(key_tail, value, TN)

    return call(
        kernel,
        "retention_forward",
        [
            shape((halves, nz, part, DV), bf16),
            shape((halves, nz, part, DV), f32),
            shape((halves, nz, part, 1), f32),
            shape((nz, DK, DV), bf16),
            shape((halves, nz, part, DK), bf16),
        ],
        where,
        decays,
        *keyvals,
        query_gate,
        grid=(nz * ny,),
        scratch=[pltpu.VMEM((DK, DV), f32)],
    )


def retention_backward(where, decays, keyval, queries, grads, states, cosines, sines, gate):
    ny = len(queries)
    halves, nz, part, _ = keyval.shape
    key_scale = DK ** (-0.5)

    def kernel(where_ref, decay_ref, *refs):
        q_refs, d_refs, rest = refs[:ny], refs[ny : 2 * ny], refs[2 * ny :]
        kv_ref, s_ref, cos_ref, sin_ref, gate_ref, kv_out, qg_out, state = rest
        step = pl.program_id(0)
        j = nz * ny - 1 - step

        @pl.when(step == 0)
        def _():
            state[...] = jnp.zeros_like(state)
            qg_out[:, :, :, DK:] = gate_ref[...]

        slot = slot_of((j // ny) ^ where_ref[0])
        ky = (j % ny) ^ where_ref[1]
        flip = where_ref[3]
        col, last, matrix = decays_of(decay_ref[pl.ds(j, 1), :])
        q = choose(q_refs, ky, slot, flip)
        grad = choose(d_refs, ky, slot, flip)
        entry = jnp.exp(col)

        @pl.when(ky == 0)
        def _():
            key = natural(kv_ref, slot, flip, slice(0, DK))
            value = natural(kv_ref, slot, flip, slice(DK, DK + DV))
            cos = natural(cos_ref, slot, flip)
            sin = natural(sin_ref, slot, flip)
            tail = jnp.exp(last - col)
            state_bf = state[...].astype(bf16)
            weights = (dot(q, key, NT) * matrix).astype(bf16)
            scores = (dot(grad, value, NT) * matrix).astype(bf16)
            grad_q = dot(scores, key, NN) + entry * dot(grad, s_ref[slot], NT)
            grad_k = dot(scores, q, TN) + tail * dot(value, state_bf, NT)
            grad_v = dot(weights, grad, TN) + tail * dot(key, state_bf, NN)
            grad_q = rotate(grad_q, cos, -sin).astype(bf16)
            grad_k = (rotate(grad_k, cos, -sin) * key_scale).astype(bf16)
            grad_v = grad_v.astype(bf16)
            for half in range(2):
                rows = slice(half * part, (half + 1) * part)
                to = (1 - flip) if half else flip
                kv_out[to, slot, :, :DK] = grad_k[rows]
                kv_out[to, slot, :, DK:] = grad_v[rows]
                qg_out[to, slot, :, :DK] = grad_q[rows]

        query_entry = (q.astype(f32) * entry).astype(bf16)
        state[...] = jnp.exp(last) * state[...] + dot(query_entry, grad, TN)

    return call(
        kernel,
        "retention_backward",
        [shape((halves, nz, part, DK + DV), bf16)] * 2,
        where,
        decays,
        *queries,
        *grads,
        keyval,
        states,
        cosines,
        sines,
        gate,
        grid=(nz * ny,),
        scratch=[pltpu.VMEM((DK, DV), f32)],
    )


def shards(
    hidden_in,
    log_decay,
    out_grad,
    ln1_gain,
    ln1_bias,
    w_query,
    w_key,
    w_value,
    w_gate,
    w_out,
    ln2_gain,
    ln2_bias,
    mlp_gate,
    mlp_up,
    mlp_down,
):
    nz, ny = lax.axis_size("row"), lax.axis_size("col")
    nb, nh = lax.axis_size("batch"), lax.axis_size("head")
    block, width = hidden_in.shape[1:]
    rows = ln1_gain.shape[0]
    part = block // nh
    tokens = nz * block
    half, quarter = tokens // 2, tokens // 4
    group = nz * rows
    sizes = (nz, ny, nb)
    where = jnp.stack([lax.axis_index(name) for name in ("row", "col", "batch", "head")])
    (where,) = tie(where.astype(jnp.int32))

    def trade(pieces, k):
        return swap(pieces[k], "row", k) if k else pieces[k]

    def over_col(own):
        return [own] + [swap(own, "col", k) for k in range(1, ny)]

    def over_batch(values):
        return [swap(value, "batch", 1) for value in values]

    def mirror(values):
        return swap(values, "head", 1)

    def pairs(own, other):
        return [(part,) for both in zip(own, other) for part in both]

    def split(values):
        return values.reshape(nh, nz, part, -1)

    def add(values, got):
        return values + got.astype(f32)

    def sum_col(keep, send):
        for k in range(1, ny):
            keep = add(keep, swap(send[k * group : (k + 1) * group], "col", k))
        return keep.reshape(nz, rows, -1)

    def reduce_far(*terms):
        far = sum(matmul_t(values[half:], weight) for values, weight in terms).astype(bf16)
        return far[quarter:], far[:quarter]

    def reduce_near(*terms):
        near = sum(matmul_t(values[:half], weight) for values, weight in terms)
        return near[quarter:], near[:quarter]

    def step_one(packed, first):
        return swap(packed[2], "row", first)

    def step_two(packed, got, first):
        return swap(jnp.stack([packed[1], got[1]]), "row", 4 - first)

    def in_order(packed, got, last, first):
        pieces = {0: packed[0], first: got[0], 4 - first: last[0], 2: last[1]}
        return [pieces[k] for k in range(4)]

    gains = jnp.concatenate([ln1_gain, ln1_bias, ln2_gain, ln2_bias])[None]
    own_in, other_in = cut_halves(where, hidden_in[0], nh)
    two_in = swap(own_in, "row", 3)
    kv = pack_weights(where, (w_key, w_value), nz, rows, (gains, log_decay[0]))
    kv = [trade(kv, k) for k in range(nz)]
    qg = pack_weights(where, (w_query, w_gate), nz, rows, first=1)
    qg_got = step_one(qg, 1)
    kv, two_in, qg_got, late_grad = tie(kv, two_in, qg_got, out_grad[0])
    kv = jnp.stack(kv)
    kv_cols, kv_mate = over_col(kv), swap(kv, "batch", 1)
    one_in = swap(jnp.concatenate([own_in, two_in]), "row", 1)
    qg_last = step_two(qg, qg_got, 1)
    own_grad, other_grad = cut_halves(where, late_grad, nh)
    two_grad = swap(own_grad, "row", 3)
    half_dim = DK // 2
    freqs = 10000.0 ** (-jnp.arange(half_dim, dtype=f32) / half_dim)
    block_at = (jnp.array(ORDER, jnp.int32) ^ where[0:1]) * ny + where[1:2]
    half_at = jnp.arange(nh, dtype=jnp.int32) ^ where[3:4]
    positions = (
        block_at[None, :, None] * block + half_at[:, None, None] * part + jnp.arange(part)
    )
    angles = positions.astype(f32)[..., None] * freqs
    cosines, sines = jnp.cos(angles), jnp.sin(angles)
    out = pack_weights(where, (w_out,), nz, rows, first=3)
    kv_cols, kv_mate, one_in, qg_last, two_grad, out, cosines, sines = tie(
        kv_cols, kv_mate, one_in, qg_last, two_grad, out, cosines, sines
    )
    kv_mates = [kv_mate] + over_batch(kv_cols[1:])
    mirror_in = mirror(jnp.concatenate([two_in, one_in]))
    qg_cols = over_col(jnp.stack(in_order(qg, qg_got, qg_last, 1)))
    one_grad = swap(jnp.concatenate([own_grad, two_grad]), "row", 1)
    out_got = step_one(out, 3)
    feed = pack_weights(where, (mlp_gate, mlp_up, mlp_down), nz, rows, first=3)
    kv_mates, mirror_in, qg_cols, one_grad, out_got, feed = tie(
        kv_mates, mirror_in, qg_cols, one_grad, out_got, feed
    )
    kv_w, gains, decays = assemble(
        where, pairs(kv_cols, kv_mates), ny, nb, (DK + DV,), EXTRA, block
    )

    first_bf = place_rows(where, (own_in, two_in, one_in, other_in, mirror_in), gains)
    key_scale = DK ** (-0.5)
    projected = split(matmul(first_bf, kv_w))
    key_bf = (rotate(projected[..., :DK], cosines, sines) * key_scale).astype(bf16)
    keyval = jnp.concatenate([key_bf, projected[..., DK:].astype(bf16)], axis=-1)

    keyval, qg_cols, out_got, feed = tie(keyval, qg_cols, out_got, feed)
    keyvals = over_col(keyval)
    out_last = step_two(out, out_got, 3)
    feed_got = step_one(feed, 3)
    (qg_w,) = assemble(where, pairs(qg_cols, over_batch(qg_cols)), ny, nb, (DK + DV,))
    projected = split(matmul(first_bf, qg_w))
    query_gate = jnp.concatenate(
        [rotate(projected[..., :DK], cosines, sines), projected[..., DK:]], axis=-1
    )
    keyvals, query_gate, out_last, feed_got = tie(keyvals, query_gate, out_last, feed_got)
    out_cols = over_col(jnp.stack(in_order(out, out_got, out_last, 3)))
    feed_last = step_two(feed, feed_got, 3)
    mirror_grad = mirror(jnp.concatenate(after([two_grad, one_grad], keyvals)))
    mixed, normed, rstd, states, query = retention_forward(where, decays, keyvals, query_gate)
    mixed, out_cols, feed_last, mirror_grad = tie(mixed, out_cols, feed_last, mirror_grad)
    (out_w,) = assemble(where, pairs(out_cols, over_batch(out_cols)), ny, nb, (DV,))
    mixed_bf = mixed.reshape(tokens, DV)

    far = far_messages(where, mixed_bf, out_w, part)
    got = mirror(far[0])
    near = reduce_near((mixed_bf, out_w))
    feed = jnp.stack(after(in_order(feed, feed_got, feed_last, 3), far))
    units = feed.shape[-1] // 3
    feed_gates = over_col(feed[..., :units])[1:]
    got, near, feed_gates, feed = tie(got, near, feed_gates, feed)
    got, got_far = swap(pass_message(where, near[0], got, part), "row", 1), mirror(far[1])
    feed_ups = over_col(feed[..., units : 2 * units])[1:]
    feed_mate = swap(feed, "batch", 1)
    got, got_far, feed_ups, feed_mate, feed = tie(got, got_far, feed_ups, feed_mate, feed)
    keep, send = keep_message(where, near[1], got_far, got, part)
    got = swap(send, "row", 3)
    gate_mates = over_batch(after(feed_gates, keep))
    got, gate_mates = tie(got, gate_mates)
    middle, scaled_two, rstd_two, own = second_norm(where, own_in, keep, got, gains, part)
    two = swap(own, "row", 3)
    up_mates = over_batch(after(feed_ups, own))
    two, up_mates, query, feed = tie(two, up_mates, query, feed)
    pair = jnp.concatenate([own, two])
    one, mirror_pair = swap(pair, "row", 1), mirror(pair)
    feed_downs = over_col(feed[..., 2 * units :])[1:]
    one, mirror_pair, feed_downs, query = tie(one, mirror_pair, feed_downs, query)
    mirror_last = mirror(one)
    down_mates = over_batch(feed_downs)
    queries = over_col(query)
    parts = [(feed,), (feed_mate,)]
    for three in zip(feed_gates, feed_ups, feed_downs, gate_mates, up_mates, down_mates):
        parts += [three[:3], three[3:]]
    up_w, down_w = assemble(where, parts, ny, nb, (2 * units, units))
    down_bf = place_rows(where, after((own_grad, two_grad, one_grad, other_grad, mirror_grad), one))
    mirror_last, up_w, down_w, down_bf, queries = tie(mirror_last, up_w, down_w, down_bf, queries)
    second_bf = place_rows(where, (pair, one, mirror_pair, mirror_last))

    up = matmul(second_bf, up_w)
    up_gate, up_lin = up[:, :units], up[:, units:]
    gelu_cdf = 0.5 * (1.0 + lax.erf(up_gate * (0.5**0.5)))
    gelu_val = up_gate * gelu_cdf
    gelu_slope = gelu_cdf + up_gate * jnp.exp(-0.5 * up_gate * up_gate) * (2.0 * jnp.pi) ** -0.5
    hidden_bf = (gelu_val * up_lin).astype(bf16)
    grad_hidden = matmul(down_bf, down_w)
    grad_upgate = (grad_hidden * up_lin * gelu_slope).astype(bf16)
    grad_uplin = (grad_hidden * gelu_val).astype(bf16)
    grad_up = jnp.concatenate([grad_upgate, grad_uplin], axis=-1)
    far = far_messages(where, grad_up, up_w, part)
    got = mirror(far[0])
    near = reduce_near((grad_up, up_w))
    lefts, rights = (second_bf, down_bf), (grad_up, hidden_bf)
    feed_far = weight_grads(where, lefts, rights, sizes)
    got, near, feed_far, hidden_bf = tie(got, near, feed_far, hidden_bf)
    got, got_far = swap(pass_message(where, near[0], got, part), "row", 1), mirror(far[1])
    feed_got = swap(feed_far, "batch", 1)
    cuts = (units // 2, units // 2, units, units)
    feed_keeps, feed_sends = weight_grads(where, lefts, rights, sizes, cuts, feed_got)
    got, got_far, feed_sends = tie(got, got_far, feed_sends)
    keep, send = keep_message(where, near[1], got_far, got, part)
    got = swap(send, "row", 3)
    sums = [sum_col(feed_keeps[0], feed_sends[0])]
    got, sums[0], feed_sends, hidden_bf = tie(got, sums[0], feed_sends, hidden_bf)
    grad_two, grad_middle, own = second_norm_back(
        where, own_grad, keep, got, gains, scaled_two, rstd_two, part
    )
    own, feed_sends = tie(own, feed_sends)
    two = swap(own, "row", 3)
    sums.append(sum_col(feed_keeps[1], feed_sends[1]))
    two, sums[1], feed_sends = tie(two, sums[1], feed_sends)
    pair = jnp.concatenate([own, two])
    one, mirror_pair = swap(pair, "row", 1), mirror(pair)
    sums.append(sum_col(feed_keeps[2], feed_sends[2]))
    result_far = reduce_far((hidden_bf, down_w))
    result_near = reduce_near((hidden_bf, down_w))
    one, mirror_pair, sums, feed_sends, result_far, result_near = tie(
        one, mirror_pair, sums, feed_sends, result_far, result_near
    )
    mirror_last = mirror(one)
    sums.append(sum_col(feed_keeps[3], feed_sends[3]))
    wide_grads = cut_heads(where, sums[:3], 3)
    wide_got = step_one(wide_grads, 3)
    mirror_last, sums, wide_got = tie(mirror_last, sums, wide_got)
    attn_bf = place_rows(where, (pair, one, mirror_pair, mirror_last))

    grp_norm, grp_rstd = normed.reshape(tokens, DV), rstd.reshape(tokens, 1)
    gate = query_gate.reshape(tokens, -1)[:, DK:]
    gate_sig = jax.nn.sigmoid(gate)
    gate_act = gate * gate_sig
    grad_mixed = matmul(attn_bf, out_w)
    grad_gate = (grad_mixed * grp_norm * (gate_sig * (1.0 + gate * (1.0 - gate_sig)))).astype(bf16)
    ret_bf = norm_back(grad_mixed * gate_act, grp_norm, grp_rstd).astype(bf16)
    ret_bf, wide_got, last_sum, result_far = tie(split(ret_bf), wide_got, sums[3], result_far)
    ret_all = over_col(ret_bf)
    wide_last = step_two(wide_grads, wide_got, 3)
    down_grads = cut_heads(where, (last_sum,), 3)
    down_got = step_one(down_grads, 3)
    result_got = mirror(result_far[0])
    lefts, rights = (first_bf, attn_bf), (grad_gate, mixed_bf)
    both_got = swap(weight_grads(where, lefts, rights, sizes), "batch", 1)
    both_keeps, both_sends = weight_grads(where, lefts, rights, sizes, (DV, DV), both_got)
    ret_all, wide_last, down_got, result_got, both_sends = tie(
        ret_all, wide_last, down_got, result_got, both_sends
    )
    result_got_far = mirror(after(result_far[1], ret_all))
    grad_kv, grad_qg = retention_backward(
        where, decays, keyval, queries, ret_all, states, cosines, sines, split(grad_gate)
    )
    grad_kv, grad_qg, result_got_far = tie(
        grad_kv.reshape(tokens, -1), grad_qg.reshape(tokens, -1), result_got_far
    )
    terms = ((grad_kv, kv_w), (grad_qg, qg_w))
    far = reduce_far(*terms)
    got = mirror(far[0])
    late_kv, late_qg, late_send, late_result = after((grad_kv, grad_qg, both_sends, result_got), far)
    kvq = ((first_bf, first_bf), (late_kv, (late_qg, 0, DK)))
    kvq_got = swap(weight_grads(where, *kvq, sizes), "batch", 1)
    result_got = swap(add(result_near[0], late_result).astype(bf16), "row", 1)
    out_sum = sum_col(both_keeps[1], late_send[1])
    near = reduce_near(*terms)
    kvq_keeps, kvq_sends = weight_grads(where, *kvq, sizes, (DV, 2 * DK), kvq_got)
    got, near, result_got, kvq_sends, out_sum, both_sends = tie(
        got, near, result_got, kvq_sends, out_sum, both_sends
    )
    got, got_far = swap(add(near[0], got).astype(bf16), "row", 1), mirror(far[1])
    gate_sum = sum_col(both_keeps[0], both_sends[0])
    result_keep = add(add(result_near[1], result_got_far), result_got)
    result_got = swap(result_keep[part:].astype(bf16), "row", 3)
    got, got_far, gate_sum, result_got, kvq_sends, down_got = tie(
        got, got_far, gate_sum, result_got, kvq_sends, down_got
    )
    keep = add(add(near[1], got_far), got)
    got = swap(keep[part:].astype(bf16), "row", 3)
    result = (middle + add(result_keep[:part], result_got)).astype(bf16)
    result_other = mirror(result)
    down_last = step_two(down_grads, down_got, 3)
    kvq_first = sum_col(kvq_keeps[0], kvq_sends[0])
    both_pieces = cut_heads(where, (gate_sum, out_sum))
    got, result_other, down_last, kvq_first, kvq_sends, both_pieces = tie(
        got, result_other, down_last, kvq_first, kvq_sends, both_pieces
    )
    both_pieces = [trade(both_pieces, k) for k in range(nz)]
    kvq_second = sum_col(kvq_keeps[1], kvq_sends[1])
    grad_one = add(keep[:part], got)
    scaled_own, rstd_own = normalize(own_in.astype(f32))
    grad_in = grad_middle + norm_back(grad_one * gains[0:1], scaled_own, rstd_own)
    grad_in_other = mirror(grad_in)
    wide_pieces = in_order(wide_grads, wide_got, wide_last, 3)
    grad_gates, grad_ups = unpack_grads(where, wide_pieces, ((units, False), (units, False)))
    down_pieces = in_order(down_grads, down_got, down_last, 3)
    (grad_downs,) = unpack_grads(where, down_pieces, ((units, True),))
    kvq_pieces = cut_heads(where, (kvq_first, kvq_second))
    both_pieces, kvq_pieces, grad_in_other, grad_one, grad_gates, grad_ups, grad_downs = tie(
        both_pieces, kvq_pieces, grad_in_other, grad_one, grad_gates, grad_ups, grad_downs
    )
    kvq_pieces = [trade(kvq_pieces, k) for k in range(nz)]
    grad_g, grad_outs = unpack_grads(where, both_pieces, ((DV, False), (DV, True)))
    grad_k, grad_v, grad_q = unpack_grads(
        where, kvq_pieces, ((DK, False), (DV, False), (DK, False))
    )

    def join(own, other):
        return join_halves(where, own, other).reshape(1, block, width)

    norm_sums = jnp.stack(
        [
            jnp.sum(grad_one * scaled_own, axis=0),
            jnp.sum(grad_one, axis=0),
            jnp.sum(grad_two * scaled_two, axis=0),
            jnp.sum(grad_two, axis=0),
        ]
    )
    norm_sums = norm_sums + swap(norm_sums, "head", 1)
    norm_sums = norm_sums.reshape(4, nz, ny, nb, rows)
    for name, axis in (("batch", 3), ("col", 2), ("row", 1)):
        me = lax.axis_index(name)
        summed = pick(norm_sums, me, axis)
        for k in range(1, lax.axis_size(name)):
            summed = summed + swap(pick(norm_sums, me ^ k, axis), name, k)
        norm_sums = summed

    return (
        join(result, result_other),
        join(grad_in, grad_in_other),
        norm_sums[0],
        norm_sums[1],
        grad_q,
        grad_k,
        grad_v,
        grad_g,
        grad_outs,
        norm_sums[2],
        norm_sums[3],
        grad_gates,
        grad_ups,
        grad_downs,
    )


def solution(mesh):
    seq = ("row", "col")
    tokens = P("batch", seq, None)
    params = P((*seq, "batch"))
    by_rows = P((*seq, "batch"), "head")
    by_cols = P("head", (*seq, "batch"))

    def run(*arrays):
        rows = arrays[1].shape[1] // mesh.shape["head"]
        sizes = (rows, mesh.shape["seq"] // rows, mesh.shape["batch"], mesh.shape["head"])
        order = [mesh.axis_names.index(n) for n in ("seq", "batch", "head")]
        fine = Mesh(
            mesh.devices.transpose(order).reshape(sizes), ("row", "col", "batch", "head")
        )
        weights = (by_rows, by_rows, by_rows, by_rows, by_cols)
        feeds = (by_rows, by_rows, by_cols)
        return jax.shard_map(
            shards,
            mesh=fine,
            in_specs=(
                tokens,
                P("batch", "head", seq),
                tokens,
                params,
                params,
                *weights,
                params,
                params,
                *feeds,
            ),
            out_specs=(tokens, tokens, params, params, *weights, params, params, *feeds),
            check_vma=False,
        )(*arrays)

    return run
```

```python
import jax
import jax.numpy as jnp
from jax import lax
from jax.experimental import pallas as pl
from jax.experimental.pallas import tpu as pltpu
from jax.sharding import Mesh
from jax.sharding import PartitionSpec as P

DK = 256
DV = 512

epsilon = 1e-05
f32 = jnp.float32
bf16 = jnp.bfloat16
VMEM_LIMIT = 12 * 1024 * 1024

ORDER = (0, 3, 1, 2)


def swap(values, axis, k):
    count = lax.axis_size(axis)
    return lax.ppermute(values, axis, [(i, i ^ k) for i in range(count)])


def pick(values, index, axis):
    return lax.dynamic_index_in_dim(values, index, axis, keepdims=False)


def tie(*values):
    return lax.optimization_barrier(values)


def after(values, *others):
    return tie(values, others)[0]


def matmul(values, weight):
    return jnp.dot(values, weight, preferred_element_type=f32)


def matmul_t(values, weight):
    return lax.dot_general(values, weight, (((1,), (1,)), ((), ())), preferred_element_type=f32)


def outer_sum(values, other):
    return lax.dot_general(values, other, (((0,), (0,)), ((), ())), preferred_element_type=f32)


def normalize(values):
    center = values - jnp.mean(values, axis=-1, keepdims=True)
    rstd = lax.rsqrt(jnp.mean(center * center, axis=-1, keepdims=True) + epsilon)
    return center * rstd, rstd


def norm_back(scaled_grad, scaled, rstd):
    return rstd * (
        scaled_grad
        - jnp.mean(scaled_grad, axis=-1, keepdims=True)
        - scaled * jnp.mean(scaled_grad * scaled, axis=-1, keepdims=True)
    )


def rotate(values, cosines, sines):
    half_dim = values.shape[-1] // 2
    first_half = values[..., :half_dim]
    second_half = values[..., half_dim:]
    return jnp.concatenate(
        [first_half * cosines - second_half * sines, first_half * sines + second_half * cosines],
        axis=-1,
    )


SMEM = pl.BlockSpec(memory_space=pltpu.SMEM)
WHOLE = pl.BlockSpec(memory_space=pltpu.VMEM)
PARAMS = pltpu.CompilerParams(vmem_limit_bytes=VMEM_LIMIT)


def call(kernel, name, shapes, *operands, grid=None, scratch=()):
    many = isinstance(shapes, list)
    return pl.pallas_call(
        kernel,
        grid=() if grid is None else grid,
        out_shape=shapes,
        in_specs=[SMEM] + [WHOLE] * (len(operands) - 1),
        out_specs=[WHOLE] * len(shapes) if many else WHOLE,
        scratch_shapes=list(scratch),
        compiler_params=PARAMS,
        name=name,
    )(*operands)


def shape(dims, dtype):
    return jax.ShapeDtypeStruct(tuple(dims), dtype)


def cut_halves(where, values, heads):
    block, width = values.shape
    part = block // heads

    def kernel(where_ref, ref, own, other):
        for out, half in ((own, where_ref[3]), (other, 1 - where_ref[3])):
            out[...] = ref[pl.ds(pl.multiple_of(half * part, part), part), :]

    return call(kernel, "cut_halves", [shape((part, width), values.dtype)] * 2, where, values)


def join_halves(where, own, other):
    part, width = own.shape

    def kernel(where_ref, own_ref, other_ref, out):
        for ref, half in ((own_ref, where_ref[3]), (other_ref, 1 - where_ref[3])):
            out[pl.ds(pl.multiple_of(half * part, part), part), :] = ref[...]

    return call(kernel, "join_halves", shape((2 * part, width), own.dtype), where, own, other)


def cut_heads(where, totals, first=0):
    nz, rows, _ = totals[0].shape
    width = sum(total.shape[2] for total in totals)

    def kernel(where_ref, *refs):
        ins, outs = refs[: len(totals)], refs[len(totals) :]
        targets = [outs[k] for k in range(nz)] if not first else steps(outs, first)
        for k in range(nz):
            at = 0
            for ref in ins:
                cols = ref.shape[2]
                targets[k][:, at : at + cols] = ref[where_ref[0] ^ k].astype(bf16)
                at += cols

    shapes = [shape((rows, width), bf16)] * nz
    if first:
        shapes = shapes[:2] + [shape((2, rows, width), bf16)]
    return call(kernel, "cut_heads", shapes, where, *totals)


def steps(refs, first):
    stay, second, firsts = refs
    return {0: stay, 4 - first: second, first: firsts.at[0], 2: firsts.at[1]}


def pack_weights(where, weights, nz, rows, extras=None, first=0):
    widths = [w.size // rows // nz for w in weights]
    total = sum(widths)
    count = 0
    if extras:
        gains, decays = extras
        block = decays.shape[1]
        extras = (jnp.pad(gains, ((0, 0), (0, total - gains.shape[1]))), decays)
        count = EXTRA

    def kernel(where_ref, *refs):
        ins, rest = refs[: len(weights)], refs[len(weights) :]
        outs = steps(rest, first) if first else rest[-nz:]
        for k in range(nz):
            target = where_ref[0] ^ k
            at = 0
            for ref, width in zip(ins, widths):
                start = pl.multiple_of(target * width, width)
                if ref.shape[0] == rows:
                    piece = ref[:, pl.ds(start, width)]
                else:
                    piece = ref[pl.ds(start, width), :].astype(f32).T.astype(bf16)
                outs[k][:rows, at : at + width] = piece
                at += width
            if extras:
                line = lax.broadcasted_iota(jnp.int32, (EXTRA, 1), 0)
                gain_rows = jnp.where(line == 0, rest[0][...].astype(f32), 0.0)
                parts = gain_rows[:, :block]
                left = rest[1][pl.ds(target, 1), :]
                for number in range(1, 4):
                    part = left.astype(bf16).astype(f32)
                    parts = jnp.where(line == number, part, parts)
                    left = left - part
                outs[k][rows:, :] = gain_rows.astype(bf16)
                outs[k][rows:, :block] = parts.astype(bf16)

    shapes = [shape((rows + count, total), bf16)] * nz
    if first:
        shapes = shapes[:2] + [shape((2, rows, total), bf16)]
    return call(kernel, "pack_weights", shapes, where, *weights, *(extras or ()))


def unpack_grads(where, pieces, outs):
    nz = len(pieces)
    rows = pieces[0].shape[0]

    def kernel(where_ref, *refs):
        ins, results = refs[:nz], refs[nz:]
        for k in range(nz):
            target = where_ref[0] ^ k
            at = 0
            for ref, (width, turned) in zip(results, outs):
                to = pl.ds(pl.multiple_of(target * width, width), width)
                piece = ins[k][:, at : at + width].astype(f32)
                if turned:
                    ref[to, :] = piece.T
                else:
                    ref[:, to] = piece
                at += width

    shapes = [shape((nz * w, rows) if turned else (rows, nz * w), f32) for w, turned in outs]
    return call(kernel, "unpack_grads", shapes, where, *pieces)


EXTRA = 16


def assemble(where, parts, ny, nb, widths, extra=0, block=0):
    nz, rows, _ = parts[0][0].shape
    rows -= extra
    count = nz * ny * nb
    total = sum(widths)
    sizes = [len(part) for part in parts]
    aligned = rows % 128 == 0

    def kernel(where_ref, *refs):
        ins, outs = refs[: sum(sizes)], refs[sum(sizes) :]
        for ky in range(ny):
            for kb in range(nb):
                pieces, ins = ins[: sizes[ky * nb + kb]], ins[sizes[ky * nb + kb] :]
                for kz in range(nz):
                    place = (where_ref[0] ^ kz) * ny + (where_ref[1] ^ ky)
                    device = place * nb + (where_ref[2] ^ kb)
                    at = pl.multiple_of(device * rows, rows)
                    column = 0
                    for piece in pieces:
                        cols = piece.shape[-1]
                        start = 0
                        for out, width in zip(outs, widths):
                            low, high = max(start, column), min(start + width, column + cols)
                            if low < high:
                                out[pl.ds(at, rows), low - start : high - start] = piece[
                                    kz, :rows, low - column : high - column
                                ]
                            start += width
                        column += cols
                    if extra:
                        tail = pieces[0][kz, rows:, :].astype(f32)
                        if aligned:
                            for number in range(4):
                                gain = tail[:1, number * rows : (number + 1) * rows]
                                outs[-2][number : number + 1, pl.ds(at, rows)] = gain
                        else:
                            outs[-2][pl.ds(device, 1), :] = tail[:1]
                        if kb == 0:
                            decay = (tail[1:2] + tail[2:3]) + tail[3:4]
                            outs[-1][pl.ds(place, 1), :] = decay[:, :block]

    shapes = [shape((count * rows, width), bf16) for width in widths]
    if extra:
        shapes.append(shape((4, count * rows) if aligned else (count, total), f32))
        shapes.append(shape((nz * ny, block), f32))
    outs = list(call(kernel, "assemble", shapes, where, *[p for part in parts for p in part]))
    if extra and not aligned:
        gains = outs[-2][:, : 4 * rows].reshape(count, 4, rows)
        outs[-2] = gains.transpose(1, 0, 2).reshape(4, count * rows)
    return outs


def row_groups(where, left, sizes):
    nz, ny, nb = sizes
    groups = left.reshape(left.shape[0], nz, ny, nb, -1)
    groups = jnp.take(groups, jnp.arange(ny) ^ where[1], axis=2)
    groups = jnp.take(groups, jnp.arange(nb) ^ where[2], axis=3)
    return groups.transpose(0, 3, 2, 1, 4).reshape(left.shape)


def weight_grads(where, lefts, rights, sizes, widths=None, got=None):
    nz, ny, nb = sizes
    width = lefts[0].shape[1]
    rows = width // (nz * ny * nb)
    group = nz * rows
    rights = [right if isinstance(right, tuple) else (right, 0, right.shape[1]) for right in rights]
    ranges = [right[1:] for right in rights]
    rights = [right[0] for right in rights]
    total = sum(high - low for low, high in ranges)
    kb = 1 if got is None else 0
    aligned = rows % 128 == 0
    if not aligned:
        lefts = [row_groups(where, left, sizes) for left in lefts]

    def columns(where_ref, left, step):
        if not aligned:
            return left[:, pl.ds(pl.multiple_of((kb * ny + step) * group, group), group)]
        tiles = []
        for z in range(nz):
            start = ((z * ny + (where_ref[1] ^ step)) * nb + (where_ref[2] ^ kb)) * rows
            tiles.append(left[:, pl.ds(pl.multiple_of(start, rows), rows)])
        return jnp.concatenate(tiles, axis=1)

    def kernel(where_ref, *refs):
        ins, rest = refs[: len(lefts)], refs[len(lefts) :]
        others, rest = rest[: len(rights)], rest[len(rights) :]
        step = pl.program_id(0)
        values = []
        for left, right, (low, high) in zip(ins, others, ranges):
            values.append(dot(columns(where_ref, left, step), right[:, low:high], TN))
        if got is None:
            at = 0
            for value in values:
                rest[0][:, at : at + value.shape[1]] = value.astype(bf16)
                at += value.shape[1]
            return
        value = jnp.concatenate(values, axis=1) + rest[0][...].astype(f32)
        keeps, sends = rest[1 : 1 + len(widths)], rest[1 + len(widths) :]
        at = 0
        for keep, send, cols in zip(keeps, sends, widths):
            part = value[:, at : at + cols]
            send[...] = part.astype(bf16)

            @pl.when(step == 0)
            def _():
                keep[...] = part

            at += cols

    moving = lambda cols: pl.BlockSpec((group, cols), lambda i: (i, 0))
    if got is None:
        specs = moving(total)
        shapes = shape((ny * group, total), bf16)
    else:
        specs = [pl.BlockSpec((group, cols), lambda i: (0, 0)) for cols in widths]
        specs += [moving(cols) for cols in widths]
        shapes = [shape((group, cols), f32) for cols in widths]
        shapes += [shape((ny * group, cols), bf16) for cols in widths]
    outs = pl.pallas_call(
        kernel,
        grid=(ny,),
        out_shape=shapes,
        in_specs=[SMEM]
        + [WHOLE] * (len(lefts) + len(rights))
        + ([] if got is None else [moving(total)]),
        out_specs=specs,
        compiler_params=PARAMS,
        name="weight_grads",
    )(where, *lefts, *rights, *(() if got is None else (got,)))
    return outs if got is None else (outs[: len(widths)], outs[len(widths) :])


def place_rows(where, pieces, gains=None):
    width = pieces[0].shape[-1]
    tokens = sum(piece.shape[0] for piece in pieces)

    def kernel(where_ref, *refs):
        ins, full = refs[: len(pieces)], refs[-1]
        at = 0
        for ref in ins:
            values = ref[...]
            if gains is not None:
                values, _ = normalize(values.astype(f32))
                params = refs[-2]
                values = (values * params[0:1, :] + params[1:2, :]).astype(bf16)
            full[at : at + ref.shape[0], :] = values
            at += ref.shape[0]

    more = () if gains is None else (gains,)
    return call(kernel, "place_rows", shape((tokens, width), bf16), where, *pieces, *more)


LOW = 16


def write_message(ref, values, part, columns=slice(None)):
    count = values.shape[0]
    high = values.astype(bf16)
    ref[:count, columns] = high
    low = values - high.astype(f32)
    line = lax.broadcasted_iota(jnp.int32, (LOW, 1), 0)
    rows = jnp.zeros((LOW, values.shape[1]), f32)
    for number in range(count // part):
        rows = jnp.where(line == number, low[number * part : number * part + 1], rows)
    ref[count:, columns] = rows.astype(bf16)


def read_message(ref, part):
    count = ref.shape[0] - LOW
    values = ref[:count, :].astype(f32)
    low = ref[count:, :].astype(f32)
    line = lax.broadcasted_iota(jnp.int32, (count, 1), 0)
    for number in range(count // part):
        values = values + jnp.where(line == number * part, low[number : number + 1], 0.0)
    return values


def far_messages(where, values, weight, part):
    half = values.shape[0] // 2
    quarter = half // 2
    width, depth = weight.shape
    step = width // 4

    def kernel(where_ref, value_ref, weight_ref, second, first):
        out = dot(value_ref[half:, :], weight_ref[...], NT)
        write_message(second, out[quarter:], part)
        write_message(first, out[:quarter], part)

    return pl.pallas_call(
        kernel,
        grid=(4,),
        out_shape=[shape((quarter + LOW, width), bf16)] * 2,
        in_specs=[SMEM, WHOLE, pl.BlockSpec((step, depth), lambda i: (i, 0))],
        out_specs=[pl.BlockSpec((quarter + LOW, step), lambda i: (0, i))] * 2,
        compiler_params=PARAMS,
        name="far_messages",
    )(where, values, weight)


def pass_message(where, near, got, part):
    def kernel(where_ref, near_ref, got_ref, out):
        write_message(out, near_ref[...] + read_message(got_ref, part), part)

    return call(kernel, "pass_message", shape(got.shape, bf16), where, near, got)


def keep_message(where, near, got_far, got, part):
    width = near.shape[1]

    def kernel(where_ref, near_ref, far_ref, got_ref, keep, out):
        total = near_ref[...] + read_message(far_ref, part) + read_message(got_ref, part)
        keep[...] = total[:part]
        write_message(out, total[part:], part)

    shapes = [shape((part, width), f32), shape((part + LOW, width), bf16)]
    return call(kernel, "keep_message", shapes, where, near, got_far, got)


def second_norm(where, inputs, keep, got, gains, part):
    width = keep.shape[1]

    def kernel(where_ref, in_ref, keep_ref, got_ref, gain_ref, middle, scaled, rstd, out):
        total = in_ref[...].astype(f32) + (keep_ref[...] + read_message(got_ref, part))
        middle[...] = total
        normed, factor = normalize(total)
        scaled[...] = normed
        rstd[...] = factor
        out[...] = (normed * gain_ref[2:3, :] + gain_ref[3:4, :]).astype(bf16)

    full = shape((part, width), f32)
    shapes = [full, full, shape((part, 1), f32), shape((part, width), bf16)]
    return call(kernel, "second_norm", shapes, where, inputs, keep, got, gains)


def second_norm_back(where, grad, keep, got, gains, scaled, rstd, part):
    width = keep.shape[1]

    def kernel(where_ref, g_ref, keep_ref, got_ref, gain_ref, scaled_ref, rstd_ref, two, mid, out):
        total = keep_ref[...] + read_message(got_ref, part)
        two[...] = total
        back = norm_back(total * gain_ref[2:3, :], scaled_ref[...], rstd_ref[...])
        back = g_ref[...].astype(f32) + back
        mid[...] = back
        out[...] = back.astype(bf16)

    full = shape((part, width), f32)
    shapes = [full, full, shape((part, width), bf16)]
    operands = (where, grad, keep, got, gains, scaled, rstd)
    return call(kernel, "second_norm_back", shapes, *operands)


def slot_of(k):
    return (((k & 1) ^ (k >> 1)) << 1) | (k >> 1)


def natural(ref, slot, flip, columns=slice(None)):
    first = ref[flip, slot, :, columns]
    second = ref[1 - flip, slot, :, columns]
    return jnp.concatenate([first, second], axis=0)


def choose(refs, ky, slot, flip, columns=slice(None)):
    values = natural(refs[0], slot, flip, columns)
    for k in range(1, len(refs)):
        values = jnp.where(ky == k, natural(refs[k], slot, flip, columns), values)
    return values


def dot(left, right, dims):
    return lax.dot_general(left, right, (dims, ((), ())), preferred_element_type=f32)


NN, NT, TN = ((1,), (0,)), ((1,), (1,)), ((0,), (0,))


def decays_of(row):
    block = row.shape[-1]
    at = lax.broadcasted_iota(jnp.int32, (block, block), 0)
    to = lax.broadcasted_iota(jnp.int32, (block, block), 1)
    turned = jnp.sum(jnp.where(at == to, row, 0.0), axis=1, keepdims=True)
    running = jnp.sum(jnp.where(at <= to, turned, 0.0), axis=0, keepdims=True)
    col = jnp.sum(jnp.where(at == to, running, 0.0), axis=1, keepdims=True)
    matrix = jnp.where(at >= to, jnp.exp(jnp.minimum(col - running, 0.0)), 0.0)
    return col, running[:, block - 1 :], matrix


def retention_forward(where, decays, keyvals, query_gate):
    ny = len(keyvals)
    halves, nz, part, _ = query_gate.shape

    def kernel(where_ref, decay_ref, *refs):
        kv_refs, (qg_ref, y_ref, n_ref, r_ref, s_ref, q_ref, state) = refs[:ny], refs[ny:]
        j = pl.program_id(0)

        @pl.when(j == 0)
        def _():
            state[...] = jnp.zeros_like(state)

        slot = slot_of((j // ny) ^ where_ref[0])
        ky = (j % ny) ^ where_ref[1]
        flip = where_ref[3]
        col, last, matrix = decays_of(decay_ref[pl.ds(j, 1), :])
        key = choose(kv_refs, ky, slot, flip, slice(0, DK))
        value = choose(kv_refs, ky, slot, flip, slice(DK, DK + DV))

        @pl.when(ky == 0)
        def _():
            q = natural(qg_ref, slot, flip, slice(0, DK)).astype(bf16)
            state_bf = state[...].astype(bf16)
            s_ref[slot] = state_bf
            weights = (dot(q, key, NT) * matrix).astype(bf16)
            out = dot(weights, value, NN) + jnp.exp(col) * dot(q, state_bf, NN)
            normed, rstd = normalize(out)
            g = natural(qg_ref, slot, flip, slice(DK, DK + DV))
            mixed = (g * jax.nn.sigmoid(g) * normed).astype(bf16)
            for half in range(2):
                rows = slice(half * part, (half + 1) * part)
                to = (1 - flip) if half else flip
                y_ref[to, slot] = mixed[rows]
                n_ref[to, slot] = normed[rows]
                r_ref[to, slot] = rstd[rows]
                q_ref[to, slot] = q[rows]

        key_tail = (key.astype(f32) * jnp.exp(last - col)).astype(bf16)
        state[...] = jnp.exp(last) * state[...] + dot(key_tail, value, TN)

    return call(
        kernel,
        "retention_forward",
        [
            shape((halves, nz, part, DV), bf16),
            shape((halves, nz, part, DV), f32),
            shape((halves, nz, part, 1), f32),
            shape((nz, DK, DV), bf16),
            shape((halves, nz, part, DK), bf16),
        ],
        where,
        decays,
        *keyvals,
        query_gate,
        grid=(nz * ny,),
        scratch=[pltpu.VMEM((DK, DV), f32)],
    )


def retention_backward(where, decays, keyval, queries, grads, states, cosines, sines, gate):
    ny = len(queries)
    halves, nz, part, _ = keyval.shape
    key_scale = DK ** (-0.5)

    def kernel(where_ref, decay_ref, *refs):
        q_refs, d_refs, rest = refs[:ny], refs[ny : 2 * ny], refs[2 * ny :]
        kv_ref, s_ref, cos_ref, sin_ref, gate_ref, kv_out, qg_out, state = rest
        step = pl.program_id(0)
        j = nz * ny - 1 - step

        @pl.when(step == 0)
        def _():
            state[...] = jnp.zeros_like(state)
            qg_out[:, :, :, DK:] = gate_ref[...]

        slot = slot_of((j // ny) ^ where_ref[0])
        ky = (j % ny) ^ where_ref[1]
        flip = where_ref[3]
        col, last, matrix = decays_of(decay_ref[pl.ds(j, 1), :])
        q = choose(q_refs, ky, slot, flip)
        grad = choose(d_refs, ky, slot, flip)
        entry = jnp.exp(col)

        @pl.when(ky == 0)
        def _():
            key = natural(kv_ref, slot, flip, slice(0, DK))
            value = natural(kv_ref, slot, flip, slice(DK, DK + DV))
            cos = natural(cos_ref, slot, flip)
            sin = natural(sin_ref, slot, flip)
            tail = jnp.exp(last - col)
            state_bf = state[...].astype(bf16)
            weights = (dot(q, key, NT) * matrix).astype(bf16)
            scores = (dot(grad, value, NT) * matrix).astype(bf16)
            grad_q = dot(scores, key, NN) + entry * dot(grad, s_ref[slot], NT)
            grad_k = dot(scores, q, TN) + tail * dot(value, state_bf, NT)
            grad_v = dot(weights, grad, TN) + tail * dot(key, state_bf, NN)
            grad_q = rotate(grad_q, cos, -sin).astype(bf16)
            grad_k = (rotate(grad_k, cos, -sin) * key_scale).astype(bf16)
            grad_v = grad_v.astype(bf16)
            for half in range(2):
                rows = slice(half * part, (half + 1) * part)
                to = (1 - flip) if half else flip
                kv_out[to, slot, :, :DK] = grad_k[rows]
                kv_out[to, slot, :, DK:] = grad_v[rows]
                qg_out[to, slot, :, :DK] = grad_q[rows]

        query_entry = (q.astype(f32) * entry).astype(bf16)
        state[...] = jnp.exp(last) * state[...] + dot(query_entry, grad, TN)

    return call(
        kernel,
        "retention_backward",
        [shape((halves, nz, part, DK + DV), bf16)] * 2,
        where,
        decays,
        *queries,
        *grads,
        keyval,
        states,
        cosines,
        sines,
        gate,
        grid=(nz * ny,),
        scratch=[pltpu.VMEM((DK, DV), f32)],
    )


def shards(
    hidden_in,
    log_decay,
    out_grad,
    ln1_gain,
    ln1_bias,
    w_query,
    w_key,
    w_value,
    w_gate,
    w_out,
    ln2_gain,
    ln2_bias,
    mlp_gate,
    mlp_up,
    mlp_down,
):
    nz, ny = lax.axis_size("row"), lax.axis_size("col")
    nb, nh = lax.axis_size("batch"), lax.axis_size("head")
    block, width = hidden_in.shape[1:]
    rows = ln1_gain.shape[0]
    part = block // nh
    tokens = nz * block
    half, quarter = tokens // 2, tokens // 4
    group = nz * rows
    sizes = (nz, ny, nb)
    where = jnp.stack([lax.axis_index(name) for name in ("row", "col", "batch", "head")])
    (where,) = tie(where.astype(jnp.int32))

    def trade(pieces, k):
        return swap(pieces[k], "row", k) if k else pieces[k]

    def over_col(own):
        return [own] + [swap(own, "col", k) for k in range(1, ny)]

    def over_batch(values):
        return [swap(value, "batch", 1) for value in values]

    def mirror(values):
        return swap(values, "head", 1)

    def pairs(own, other):
        return [(part,) for both in zip(own, other) for part in both]

    def split(values):
        return values.reshape(nh, nz, part, -1)

    def add(values, got):
        return values + got.astype(f32)

    def sum_col(keep, send):
        for k in range(1, ny):
            keep = add(keep, swap(send[k * group : (k + 1) * group], "col", k))
        return keep.reshape(nz, rows, -1)

    def reduce_far(*terms):
        far = sum(matmul_t(values[half:], weight) for values, weight in terms).astype(bf16)
        return far[quarter:], far[:quarter]

    def reduce_near(*terms):
        near = sum(matmul_t(values[:half], weight) for values, weight in terms)
        return near[quarter:], near[:quarter]

    def step_one(packed, first):
        return swap(packed[2], "row", first)

    def step_two(packed, got, first):
        return swap(jnp.stack([packed[1], got[1]]), "row", 4 - first)

    def in_order(packed, got, last, first):
        pieces = {0: packed[0], first: got[0], 4 - first: last[0], 2: last[1]}
        return [pieces[k] for k in range(4)]

    gains = jnp.concatenate([ln1_gain, ln1_bias, ln2_gain, ln2_bias])[None]
    own_in, other_in = cut_halves(where, hidden_in[0], nh)
    two_in = swap(own_in, "row", 3)
    kv = pack_weights(where, (w_key, w_value), nz, rows, (gains, log_decay[0]))
    kv = [trade(kv, k) for k in range(nz)]
    qg = pack_weights(where, (w_query, w_gate), nz, rows, first=1)
    qg_got = step_one(qg, 1)
    kv, two_in, qg_got, late_grad = tie(kv, two_in, qg_got, out_grad[0])
    kv = jnp.stack(kv)
    kv_cols, kv_mate = over_col(kv), swap(kv, "batch", 1)
    one_in = swap(jnp.concatenate([own_in, two_in]), "row", 1)
    qg_last = step_two(qg, qg_got, 1)
    own_grad, other_grad = cut_halves(where, late_grad, nh)
    half_dim = DK // 2
    freqs = 10000.0 ** (-jnp.arange(half_dim, dtype=f32) / half_dim)
    block_at = (jnp.array(ORDER, jnp.int32) ^ where[0:1]) * ny + where[1:2]
    half_at = jnp.arange(nh, dtype=jnp.int32) ^ where[3:4]
    positions = (
        block_at[None, :, None] * block + half_at[:, None, None] * part + jnp.arange(part)
    )
    angles = positions.astype(f32)[..., None] * freqs
    cosines, sines = jnp.cos(angles), jnp.sin(angles)
    out = pack_weights(where, (w_out,), nz, rows, first=3)
    kv_cols, kv_mate, one_in, qg_last, own_grad, out, cosines, sines = tie(
        kv_cols, kv_mate, one_in, qg_last, own_grad, out, cosines, sines
    )
    kv_mates = [kv_mate] + over_batch(kv_cols[1:])
    mirror_in = mirror(jnp.concatenate([two_in, one_in]))
    qg_cols = over_col(jnp.stack(in_order(qg, qg_got, qg_last, 1)))
    two_grad = swap(own_grad, "row", 3)
    out_got = step_one(out, 3)
    feed = pack_weights(where, (mlp_gate, mlp_up, mlp_down), nz, rows)
    kv_mates, mirror_in, qg_cols, two_grad, out_got, feed = tie(
        kv_mates, mirror_in, qg_cols, two_grad, out_got, feed
    )
    kv_w, gains, decays = assemble(
        where, pairs(kv_cols, kv_mates), ny, nb, (DK + DV,), EXTRA, block
    )

    first_bf = place_rows(where, (own_in, two_in, one_in, other_in, mirror_in), gains)
    key_scale = DK ** (-0.5)
    projected = split(matmul(first_bf, kv_w))
    key_bf = (rotate(projected[..., :DK], cosines, sines) * key_scale).astype(bf16)
    keyval = jnp.concatenate([key_bf, projected[..., DK:].astype(bf16)], axis=-1)

    keyval, qg_cols, out_got, feed = tie(keyval, qg_cols, out_got, feed)
    keyvals = over_col(keyval)
    out_last = step_two(out, out_got, 3)
    feed_two = trade(feed, 2)
    (qg_w,) = assemble(where, pairs(qg_cols, over_batch(qg_cols)), ny, nb, (DK + DV,))
    projected = split(matmul(first_bf, qg_w))
    query_gate = jnp.concatenate(
        [rotate(projected[..., :DK], cosines, sines), projected[..., DK:]], axis=-1
    )
    keyvals, query_gate, out_last, feed_two = tie(keyvals, query_gate, out_last, feed_two)
    out_cols = over_col(jnp.stack(in_order(out, out_got, out_last, 3)))
    late_grad, late_two = after((own_grad, two_grad), keyvals)
    one_grad = swap(jnp.concatenate([late_grad, late_two]), "row", 1)
    mixed, normed, rstd, states, query = retention_forward(where, decays, keyvals, query_gate)
    mixed, out_cols, one_grad = tie(mixed, out_cols, one_grad)
    (out_w,) = assemble(where, pairs(out_cols, over_batch(out_cols)), ny, nb, (DV,))
    mixed_bf = mixed.reshape(tokens, DV)

    far = far_messages(where, mixed_bf, out_w, part)
    got = mirror(far[0])
    near = reduce_near((mixed_bf, out_w))
    late_feed = after(feed, far)
    feed_three, feed_one = trade(late_feed, 3), trade(late_feed, 1)
    got, near, feed_three, feed_one = tie(got, near, feed_three, feed_one)
    got_far = mirror(after(far[1], got))
    got = swap(pass_message(where, near[0], got, part), "row", 1)
    feed = jnp.stack([feed[0], feed_one, feed_two, feed_three])
    units = feed.shape[-1] // 3
    feed_gates = over_col(feed[..., :units])[1:]
    feed_mate = swap(feed, "batch", 1)
    got, got_far, feed_gates, feed_mate, feed = tie(got, got_far, feed_gates, feed_mate, feed)
    keep, send = keep_message(where, near[1], got_far, got, part)
    got = swap(send, "row", 3)
    late_feed, late_two, late_gates = after((feed, two_grad, feed_gates), keep)
    feed_ups = over_col(late_feed[..., units : 2 * units])[1:]
    mirror_two = mirror(late_two)
    gate_mates = over_batch(late_gates)
    got, feed_ups, mirror_two, gate_mates = tie(got, feed_ups, mirror_two, gate_mates)
    middle, scaled_two, rstd_two, own = second_norm(where, own_in, keep, got, gains, part)
    two = swap(own, "row", 3)
    late_feed, late_one, late_ups = after((feed, one_grad, feed_ups), own)
    feed_downs = over_col(late_feed[..., 2 * units :])[1:]
    mirror_one = mirror(late_one)
    up_mates = over_batch(late_ups)
    two, feed_downs, mirror_one, up_mates, query = tie(
        two, feed_downs, mirror_one, up_mates, query
    )
    pair = jnp.concatenate([own, two])
    one, mirror_pair = swap(pair, "row", 1), mirror(pair)
    down_mates = over_batch(after(feed_downs, pair))
    one, mirror_pair, down_mates, query = tie(one, mirror_pair, down_mates, query)
    mirror_last = mirror(one)
    queries = over_col(query)
    parts = [(feed,), (feed_mate,)]
    for three in zip(feed_gates, feed_ups, feed_downs, gate_mates, up_mates, down_mates):
        parts += [three[:3], three[3:]]
    up_w, down_w = assemble(where, after(parts, one), ny, nb, (2 * units, units))
    down_bf = place_rows(
        where, after((own_grad, two_grad, one_grad, other_grad, mirror_two, mirror_one), one)
    )
    mirror_last, up_w, down_w, down_bf, queries = tie(mirror_last, up_w, down_w, down_bf, queries)
    second_bf = place_rows(where, (pair, one, mirror_pair, mirror_last))

    up = matmul(second_bf, up_w)
    up_gate, up_lin = up[:, :units], up[:, units:]
    gelu_cdf = 0.5 * (1.0 + lax.erf(up_gate * (0.5**0.5)))
    gelu_val = up_gate * gelu_cdf
    gelu_slope = gelu_cdf + up_gate * jnp.exp(-0.5 * up_gate * up_gate) * (2.0 * jnp.pi) ** -0.5
    hidden_bf = (gelu_val * up_lin).astype(bf16)
    grad_hidden = matmul(down_bf, down_w)
    grad_upgate = (grad_hidden * up_lin * gelu_slope).astype(bf16)
    grad_uplin = (grad_hidden * gelu_val).astype(bf16)
    grad_up = jnp.concatenate([grad_upgate, grad_uplin], axis=-1)
    far = far_messages(where, grad_up, up_w, part)
    got = mirror(far[0])
    near = reduce_near((grad_up, up_w))
    lefts, rights = (second_bf, down_bf), (grad_up, hidden_bf)
    feed_far = weight_grads(where, lefts, rights, sizes)
    got, near, feed_far, hidden_bf = tie(got, near, feed_far, hidden_bf)
    got_far = mirror(after(far[1], got))
    got = swap(pass_message(where, near[0], got, part), "row", 1)
    feed_got = swap(feed_far, "batch", 1)
    feed_keeps, feed_sends = weight_grads(where, lefts, rights, sizes, (units,) * 3, feed_got)
    result_far = reduce_far((hidden_bf, down_w))
    got, got_far, feed_sends, result_far, hidden_bf = tie(
        got, got_far, feed_sends, result_far, hidden_bf
    )
    keep, send = keep_message(where, near[1], got_far, got, part)
    got = swap(send, "row", 3)
    result_got = mirror(result_far[0])
    result_near = reduce_near((hidden_bf, down_w))
    sums = [sum_col(feed_keeps[0], feed_sends[0])]
    got, result_got, result_near, sums, feed_sends = tie(
        got, result_got, result_near, sums, feed_sends
    )
    grad_two, grad_middle, own = second_norm_back(
        where, own_grad, keep, got, gains, scaled_two, rstd_two, part
    )
    own, feed_sends, result_got = tie(own, feed_sends, result_got)
    two = swap(own, "row", 3)
    sums.append(sum_col(feed_keeps[1], feed_sends[1]))
    result_got_far = mirror(after(result_far[1], own))
    result_got = swap(add(result_near[0], result_got).astype(bf16), "row", 1)
    two, sums, feed_sends, result_got_far, result_got = tie(
        two, sums, feed_sends, result_got_far, result_got
    )
    pair = jnp.concatenate([own, two])
    one, mirror_pair = swap(pair, "row", 1), mirror(pair)
    down_sum = sum_col(feed_keeps[2], feed_sends[2])
    wide_grads = cut_heads(where, sums)
    result_keep = add(add(result_near[1], result_got_far), result_got)
    result_send = result_keep[part:].astype(bf16)
    one, mirror_pair, down_sum, wide_grads, result_send = tie(
        one, mirror_pair, down_sum, wide_grads, result_send
    )
    mirror_last = mirror(one)
    wide_two, wide_one = trade(wide_grads, 2), trade(wide_grads, 1)
    down_grads = cut_heads(where, (down_sum,))
    mirror_last, wide_two, wide_one, down_grads = tie(mirror_last, wide_two, wide_one, down_grads)
    attn_bf = place_rows(where, (pair, one, mirror_pair, mirror_last))

    grp_norm, grp_rstd = normed.reshape(tokens, DV), rstd.reshape(tokens, 1)
    gate = query_gate.reshape(tokens, -1)[:, DK:]
    gate_sig = jax.nn.sigmoid(gate)
    gate_act = gate * gate_sig
    grad_mixed = matmul(attn_bf, out_w)
    grad_gate = (grad_mixed * grp_norm * (gate_sig * (1.0 + gate * (1.0 - gate_sig)))).astype(bf16)
    ret_bf = norm_back(grad_mixed * gate_act, grp_norm, grp_rstd).astype(bf16)
    ret_bf, wide_grads, down_grads = tie(split(ret_bf), wide_grads, down_grads)
    ret_all = over_col(ret_bf)
    wide_three, down_one = trade(wide_grads, 3), trade(down_grads, 1)
    lefts, rights = (first_bf, attn_bf), (grad_gate, mixed_bf)
    both_got = swap(weight_grads(where, lefts, rights, sizes), "batch", 1)
    both_keeps, both_sends = weight_grads(where, lefts, rights, sizes, (DV, DV), both_got)
    ret_all, wide_three, down_one, both_sends = tie(ret_all, wide_three, down_one, both_sends)
    grad_kv, grad_qg = retention_backward(
        where, decays, keyval, queries, ret_all, states, cosines, sines, split(grad_gate)
    )
    grad_kv, grad_qg = grad_kv.reshape(tokens, -1), grad_qg.reshape(tokens, -1)
    terms = ((grad_kv, kv_w), (grad_qg, qg_w))
    far = reduce_far(*terms)
    got = mirror(far[0])
    late_kv, late_qg, late_send, late_down = after((grad_kv, grad_qg, both_sends, down_grads), far)
    kvq = ((first_bf, first_bf), (late_kv, (late_qg, 0, DK)))
    kvq_got = swap(weight_grads(where, *kvq, sizes), "batch", 1)
    down_two, down_three = trade(late_down, 2), trade(late_down, 3)
    out_sum = sum_col(both_keeps[1], late_send[1])
    near = reduce_near(*terms)
    kvq_keeps, kvq_sends = weight_grads(where, *kvq, sizes, (DV, 2 * DK), kvq_got)
    got, near, down_two, down_three, kvq_sends, out_sum, both_sends, result_send = tie(
        got, near, down_two, down_three, kvq_sends, out_sum, both_sends, result_send
    )
    got_far = mirror(after(far[1], got))
    got = swap(add(near[0], got).astype(bf16), "row", 1)
    gate_sum = sum_col(both_keeps[0], both_sends[0])
    result_got = swap(result_send, "row", 3)
    got, got_far, gate_sum, result_got, kvq_sends = tie(
        got, got_far, gate_sum, result_got, kvq_sends
    )
    keep = add(add(near[1], got_far), got)
    got = swap(keep[part:].astype(bf16), "row", 3)
    result = (middle + add(result_keep[:part], result_got)).astype(bf16)
    result_other = mirror(result)
    kvq_first = sum_col(kvq_keeps[0], kvq_sends[0])
    both_pieces = cut_heads(where, (gate_sum, out_sum))
    got, result_other, kvq_first, kvq_sends, both_pieces = tie(
        got, result_other, kvq_first, kvq_sends, both_pieces
    )
    both_pieces = [trade(both_pieces, k) for k in range(nz)]
    kvq_second = sum_col(kvq_keeps[1], kvq_sends[1])
    grad_one = add(keep[:part], got)
    scaled_own, rstd_own = normalize(own_in.astype(f32))
    grad_in = grad_middle + norm_back(grad_one * gains[0:1], scaled_own, rstd_own)
    grad_in_other = mirror(grad_in)
    wide_pieces = (wide_grads[0], wide_one, wide_two, wide_three)
    grad_gates, grad_ups = unpack_grads(where, wide_pieces, ((units, False), (units, False)))
    down_pieces = (down_grads[0], down_one, down_two, down_three)
    (grad_downs,) = unpack_grads(where, down_pieces, ((units, True),))
    kvq_pieces = cut_heads(where, (kvq_first, kvq_second))
    norm_sums = jnp.stack(
        [
            jnp.sum(grad_one * scaled_own, axis=0),
            jnp.sum(grad_one, axis=0),
            jnp.sum(grad_two * scaled_two, axis=0),
            jnp.sum(grad_two, axis=0),
        ]
    )
    norm_sums = norm_sums + mirror(norm_sums)
    norm_sums = norm_sums.reshape(4, nz, ny, nb, rows)

    def sum_over(values, name, axis):
        me = lax.axis_index(name)
        summed = pick(values, me, axis)
        for k in range(1, lax.axis_size(name)):
            summed = summed + swap(pick(values, me ^ k, axis), name, k)
        return summed

    norm_sums = sum_over(sum_over(norm_sums, "batch", 3), "col", 2)
    both_pieces, kvq_pieces, grad_in_other, norm_sums, grad_gates, grad_ups, grad_downs = tie(
        both_pieces, kvq_pieces, grad_in_other, norm_sums, grad_gates, grad_ups, grad_downs
    )
    norm_sums = sum_over(norm_sums, "row", 1)
    kvq_pieces = [trade(kvq_pieces, k) for k in range(nz)]
    grad_g, grad_outs = unpack_grads(where, both_pieces, ((DV, False), (DV, True)))
    grad_k, grad_v, grad_q = unpack_grads(
        where, kvq_pieces, ((DK, False), (DV, False), (DK, False))
    )

    def join(own, other):
        return join_halves(where, own, other).reshape(1, block, width)

    return (
        join(result, result_other),
        join(grad_in, grad_in_other),
        norm_sums[0],
        norm_sums[1],
        grad_q,
        grad_k,
        grad_v,
        grad_g,
        grad_outs,
        norm_sums[2],
        norm_sums[3],
        grad_gates,
        grad_ups,
        grad_downs,
    )


def solution(mesh):
    seq = ("row", "col")
    tokens = P("batch", seq, None)
    params = P((*seq, "batch"))
    by_rows = P((*seq, "batch"), "head")
    by_cols = P("head", (*seq, "batch"))

    def run(*arrays):
        rows = arrays[1].shape[1] // mesh.shape["head"]
        sizes = (rows, mesh.shape["seq"] // rows, mesh.shape["batch"], mesh.shape["head"])
        order = [mesh.axis_names.index(n) for n in ("seq", "batch", "head")]
        fine = Mesh(
            mesh.devices.transpose(order).reshape(sizes), ("row", "col", "batch", "head")
        )
        weights = (by_rows, by_rows, by_rows, by_rows, by_cols)
        feeds = (by_rows, by_rows, by_cols)
        return jax.shard_map(
            shards,
            mesh=fine,
            in_specs=(
                tokens,
                P("batch", "head", seq),
                tokens,
                params,
                params,
                *weights,
                params,
                params,
                *feeds,
            ),
            out_specs=(tokens, tokens, params, params, *weights, params, params, *feeds),
            check_vma=False,
        )(*arrays)

    return run
```

```python
import jax
import jax.numpy as jnp
from jax import lax
from jax.experimental import pallas as pl
from jax.experimental.pallas import tpu as pltpu
from jax.sharding import Mesh
from jax.sharding import PartitionSpec as P

DK = 256
DV = 512

epsilon = 1e-05
f32 = jnp.float32
bf16 = jnp.bfloat16
VMEM_LIMIT = 12 * 1024 * 1024

ORDER = (0, 3, 1, 2)


def swap(values, axis, k):
    count = lax.axis_size(axis)
    return lax.ppermute(values, axis, [(i, i ^ k) for i in range(count)])


def pick(values, index, axis):
    return lax.dynamic_index_in_dim(values, index, axis, keepdims=False)


def tie(*values):
    return lax.optimization_barrier(values)


def after(values, *others):
    return tie(values, others)[0]


def matmul(values, weight):
    return jnp.dot(values, weight, preferred_element_type=f32)


def matmul_t(values, weight):
    return lax.dot_general(values, weight, (((1,), (1,)), ((), ())), preferred_element_type=f32)


def outer_sum(values, other):
    return lax.dot_general(values, other, (((0,), (0,)), ((), ())), preferred_element_type=f32)


def normalize(values):
    center = values - jnp.mean(values, axis=-1, keepdims=True)
    rstd = lax.rsqrt(jnp.mean(center * center, axis=-1, keepdims=True) + epsilon)
    return center * rstd, rstd


def norm_back(scaled_grad, scaled, rstd):
    return rstd * (
        scaled_grad
        - jnp.mean(scaled_grad, axis=-1, keepdims=True)
        - scaled * jnp.mean(scaled_grad * scaled, axis=-1, keepdims=True)
    )


def rotate(values, cosines, sines):
    half_dim = values.shape[-1] // 2
    first_half = values[..., :half_dim]
    second_half = values[..., half_dim:]
    return jnp.concatenate(
        [first_half * cosines - second_half * sines, first_half * sines + second_half * cosines],
        axis=-1,
    )


SMEM = pl.BlockSpec(memory_space=pltpu.SMEM)
WHOLE = pl.BlockSpec(memory_space=pltpu.VMEM)
PARAMS = pltpu.CompilerParams(vmem_limit_bytes=VMEM_LIMIT)


def call(kernel, name, shapes, *operands, grid=None, scratch=()):
    many = isinstance(shapes, list)
    return pl.pallas_call(
        kernel,
        grid=() if grid is None else grid,
        out_shape=shapes,
        in_specs=[SMEM] + [WHOLE] * (len(operands) - 1),
        out_specs=[WHOLE] * len(shapes) if many else WHOLE,
        scratch_shapes=list(scratch),
        compiler_params=PARAMS,
        name=name,
    )(*operands)


def shape(dims, dtype):
    return jax.ShapeDtypeStruct(tuple(dims), dtype)


def cut_halves(where, values, heads):
    block, width = values.shape
    part = block // heads

    def kernel(where_ref, ref, own, other):
        for out, half in ((own, where_ref[3]), (other, 1 - where_ref[3])):
            out[...] = ref[pl.ds(pl.multiple_of(half * part, part), part), :]

    return call(kernel, "cut_halves", [shape((part, width), values.dtype)] * 2, where, values)


def join_halves(where, own, other):
    part, width = own.shape

    def kernel(where_ref, own_ref, other_ref, out):
        for ref, half in ((own_ref, where_ref[3]), (other_ref, 1 - where_ref[3])):
            out[pl.ds(pl.multiple_of(half * part, part), part), :] = ref[...]

    return call(kernel, "join_halves", shape((2 * part, width), own.dtype), where, own, other)


def cut_heads(where, totals, first=0):
    nz, rows, _ = totals[0].shape
    width = sum(total.shape[2] for total in totals)

    def kernel(where_ref, *refs):
        ins, outs = refs[: len(totals)], refs[len(totals) :]
        targets = [outs[k] for k in range(nz)] if not first else steps(outs, first)
        for k in range(nz):
            at = 0
            for ref in ins:
                cols = ref.shape[2]
                targets[k][:, at : at + cols] = ref[where_ref[0] ^ k].astype(bf16)
                at += cols

    shapes = [shape((rows, width), bf16)] * nz
    if first:
        shapes = shapes[:2] + [shape((2, rows, width), bf16)]
    return call(kernel, "cut_heads", shapes, where, *totals)


def steps(refs, first):
    stay, second, firsts = refs
    return {0: stay, 4 - first: second, first: firsts.at[0], 2: firsts.at[1]}


def pack_weights(where, weights, nz, rows, extras=None, first=0):
    widths = [w.size // rows // nz for w in weights]
    total = sum(widths)
    count = 0
    if extras:
        gains, decays = extras
        block = decays.shape[1]
        extras = (jnp.pad(gains, ((0, 0), (0, total - gains.shape[1]))), decays)
        count = EXTRA

    def kernel(where_ref, *refs):
        ins, rest = refs[: len(weights)], refs[len(weights) :]
        outs = steps(rest, first) if first else rest[-nz:]
        for k in range(nz):
            target = where_ref[0] ^ k
            at = 0
            for ref, width in zip(ins, widths):
                start = pl.multiple_of(target * width, width)
                if ref.shape[0] == rows:
                    piece = ref[:, pl.ds(start, width)]
                else:
                    piece = ref[pl.ds(start, width), :].astype(f32).T.astype(bf16)
                outs[k][:rows, at : at + width] = piece
                at += width
            if extras:
                line = lax.broadcasted_iota(jnp.int32, (EXTRA, 1), 0)
                gain_rows = jnp.where(line == 0, rest[0][...].astype(f32), 0.0)
                parts = gain_rows[:, :block]
                left = rest[1][pl.ds(target, 1), :]
                for number in range(1, 4):
                    part = left.astype(bf16).astype(f32)
                    parts = jnp.where(line == number, part, parts)
                    left = left - part
                outs[k][rows:, :] = gain_rows.astype(bf16)
                outs[k][rows:, :block] = parts.astype(bf16)

    shapes = [shape((rows + count, total), bf16)] * nz
    if first:
        shapes = shapes[:2] + [shape((2, rows, total), bf16)]
    return call(kernel, "pack_weights", shapes, where, *weights, *(extras or ()))


def unpack_grads(where, pieces, outs):
    nz = len(pieces)
    rows = pieces[0].shape[0]

    def kernel(where_ref, *refs):
        ins, results = refs[:nz], refs[nz:]
        for k in range(nz):
            target = where_ref[0] ^ k
            at = 0
            for ref, (width, turned) in zip(results, outs):
                to = pl.ds(pl.multiple_of(target * width, width), width)
                piece = ins[k][:, at : at + width].astype(f32)
                if turned:
                    ref[to, :] = piece.T
                else:
                    ref[:, to] = piece
                at += width

    shapes = [shape((nz * w, rows) if turned else (rows, nz * w), f32) for w, turned in outs]
    return call(kernel, "unpack_grads", shapes, where, *pieces)


EXTRA = 16


def assemble(where, parts, ny, nb, widths, extra=0, block=0):
    nz, rows, _ = parts[0][0].shape
    rows -= extra
    count = nz * ny * nb
    total = sum(widths)
    sizes = [len(part) for part in parts]
    aligned = rows % 128 == 0

    def kernel(where_ref, *refs):
        ins, outs = refs[: sum(sizes)], refs[sum(sizes) :]
        for ky in range(ny):
            for kb in range(nb):
                pieces, ins = ins[: sizes[ky * nb + kb]], ins[sizes[ky * nb + kb] :]
                for kz in range(nz):
                    place = (where_ref[0] ^ kz) * ny + (where_ref[1] ^ ky)
                    device = place * nb + (where_ref[2] ^ kb)
                    at = pl.multiple_of(device * rows, rows)
                    column = 0
                    for piece in pieces:
                        cols = piece.shape[-1]
                        start = 0
                        for out, width in zip(outs, widths):
                            low, high = max(start, column), min(start + width, column + cols)
                            if low < high:
                                out[pl.ds(at, rows), low - start : high - start] = piece[
                                    kz, :rows, low - column : high - column
                                ]
                            start += width
                        column += cols
                    if extra:
                        tail = pieces[0][kz, rows:, :].astype(f32)
                        if aligned:
                            for number in range(4):
                                gain = tail[:1, number * rows : (number + 1) * rows]
                                outs[-2][number : number + 1, pl.ds(at, rows)] = gain
                        else:
                            outs[-2][pl.ds(device, 1), :] = tail[:1]
                        if kb == 0:
                            decay = (tail[1:2] + tail[2:3]) + tail[3:4]
                            outs[-1][pl.ds(place, 1), :] = decay[:, :block]

    shapes = [shape((count * rows, width), bf16) for width in widths]
    if extra:
        shapes.append(shape((4, count * rows) if aligned else (count, total), f32))
        shapes.append(shape((nz * ny, block), f32))
    outs = list(call(kernel, "assemble", shapes, where, *[p for part in parts for p in part]))
    if extra and not aligned:
        gains = outs[-2][:, : 4 * rows].reshape(count, 4, rows)
        outs[-2] = gains.transpose(1, 0, 2).reshape(4, count * rows)
    return outs


def row_groups(where, left, sizes):
    nz, ny, nb = sizes
    groups = left.reshape(left.shape[0], nz, ny, nb, -1)
    groups = jnp.take(groups, jnp.arange(ny) ^ where[1], axis=2)
    groups = jnp.take(groups, jnp.arange(nb) ^ where[2], axis=3)
    return groups.transpose(0, 3, 2, 1, 4).reshape(left.shape)


def weight_grads(where, lefts, rights, sizes, widths=None, got=None):
    nz, ny, nb = sizes
    width = lefts[0].shape[1]
    rows = width // (nz * ny * nb)
    group = nz * rows
    rights = [right if isinstance(right, tuple) else (right, 0, right.shape[1]) for right in rights]
    ranges = [right[1:] for right in rights]
    rights = [right[0] for right in rights]
    total = sum(high - low for low, high in ranges)
    kb = 1 if got is None else 0
    aligned = rows % 128 == 0
    if not aligned:
        lefts = [row_groups(where, left, sizes) for left in lefts]

    def columns(where_ref, left, step):
        if not aligned:
            return left[:, pl.ds(pl.multiple_of((kb * ny + step) * group, group), group)]
        tiles = []
        for z in range(nz):
            start = ((z * ny + (where_ref[1] ^ step)) * nb + (where_ref[2] ^ kb)) * rows
            tiles.append(left[:, pl.ds(pl.multiple_of(start, rows), rows)])
        return jnp.concatenate(tiles, axis=1)

    def kernel(where_ref, *refs):
        ins, rest = refs[: len(lefts)], refs[len(lefts) :]
        others, rest = rest[: len(rights)], rest[len(rights) :]
        step = pl.program_id(0)
        values = []
        for left, right, (low, high) in zip(ins, others, ranges):
            values.append(dot(columns(where_ref, left, step), right[:, low:high], TN))
        if got is None:
            at = 0
            for value in values:
                rest[0][:, at : at + value.shape[1]] = value.astype(bf16)
                at += value.shape[1]
            return
        value = jnp.concatenate(values, axis=1) + rest[0][...].astype(f32)
        keeps, sends = rest[1 : 1 + len(widths)], rest[1 + len(widths) :]
        at = 0
        for keep, send, cols in zip(keeps, sends, widths):
            part = value[:, at : at + cols]
            send[...] = part.astype(bf16)

            @pl.when(step == 0)
            def _():
                keep[...] = part

            at += cols

    moving = lambda cols: pl.BlockSpec((group, cols), lambda i: (i, 0))
    if got is None:
        specs = moving(total)
        shapes = shape((ny * group, total), bf16)
    else:
        specs = [pl.BlockSpec((group, cols), lambda i: (0, 0)) for cols in widths]
        specs += [moving(cols) for cols in widths]
        shapes = [shape((group, cols), f32) for cols in widths]
        shapes += [shape((ny * group, cols), bf16) for cols in widths]
    outs = pl.pallas_call(
        kernel,
        grid=(ny,),
        out_shape=shapes,
        in_specs=[SMEM]
        + [WHOLE] * (len(lefts) + len(rights))
        + ([] if got is None else [moving(total)]),
        out_specs=specs,
        compiler_params=PARAMS,
        name="weight_grads",
    )(where, *lefts, *rights, *(() if got is None else (got,)))
    return outs if got is None else (outs[: len(widths)], outs[len(widths) :])


def place_rows(where, pieces, gains=None):
    width = pieces[0].shape[-1]
    tokens = sum(piece.shape[0] for piece in pieces)

    def kernel(where_ref, *refs):
        ins, full = refs[: len(pieces)], refs[-1]
        at = 0
        for ref in ins:
            values = ref[...]
            if gains is not None:
                values, _ = normalize(values.astype(f32))
                params = refs[-2]
                values = (values * params[0:1, :] + params[1:2, :]).astype(bf16)
            full[at : at + ref.shape[0], :] = values
            at += ref.shape[0]

    more = () if gains is None else (gains,)
    return call(kernel, "place_rows", shape((tokens, width), bf16), where, *pieces, *more)


LOW = 16


def write_message(ref, values, part, columns=slice(None)):
    count = values.shape[0]
    high = values.astype(bf16)
    ref[:count, columns] = high
    low = values - high.astype(f32)
    line = lax.broadcasted_iota(jnp.int32, (LOW, 1), 0)
    rows = jnp.zeros((LOW, values.shape[1]), f32)
    for number in range(count // part):
        rows = jnp.where(line == number, low[number * part : number * part + 1], rows)
    ref[count:, columns] = rows.astype(bf16)


def read_message(ref, part):
    count = ref.shape[0] - LOW
    values = ref[:count, :].astype(f32)
    low = ref[count:, :].astype(f32)
    line = lax.broadcasted_iota(jnp.int32, (count, 1), 0)
    for number in range(count // part):
        values = values + jnp.where(line == number * part, low[number : number + 1], 0.0)
    return values


def far_messages(where, values, weight, part):
    half = values.shape[0] // 2
    quarter = half // 2
    width, depth = weight.shape
    step = width // 4

    def kernel(where_ref, value_ref, weight_ref, second, first):
        out = dot(value_ref[half:, :], weight_ref[...], NT)
        write_message(second, out[quarter:], part)
        write_message(first, out[:quarter], part)

    return pl.pallas_call(
        kernel,
        grid=(4,),
        out_shape=[shape((quarter + LOW, width), bf16)] * 2,
        in_specs=[SMEM, WHOLE, pl.BlockSpec((step, depth), lambda i: (i, 0))],
        out_specs=[pl.BlockSpec((quarter + LOW, step), lambda i: (0, i))] * 2,
        compiler_params=PARAMS,
        name="far_messages",
    )(where, values, weight)


def pass_message(where, near, got, part):
    def kernel(where_ref, near_ref, got_ref, out):
        write_message(out, near_ref[...] + read_message(got_ref, part), part)

    return call(kernel, "pass_message", shape(got.shape, bf16), where, near, got)


def keep_message(where, near, got_far, got, part):
    width = near.shape[1]

    def kernel(where_ref, near_ref, far_ref, got_ref, keep, out):
        total = near_ref[...] + read_message(far_ref, part) + read_message(got_ref, part)
        keep[...] = total[:part]
        write_message(out, total[part:], part)

    shapes = [shape((part, width), f32), shape((part + LOW, width), bf16)]
    return call(kernel, "keep_message", shapes, where, near, got_far, got)


def second_norm(where, inputs, keep, got, gains, part):
    width = keep.shape[1]

    def kernel(where_ref, in_ref, keep_ref, got_ref, gain_ref, middle, scaled, rstd, out):
        total = in_ref[...].astype(f32) + (keep_ref[...] + read_message(got_ref, part))
        middle[...] = total
        normed, factor = normalize(total)
        scaled[...] = normed
        rstd[...] = factor
        out[...] = (normed * gain_ref[2:3, :] + gain_ref[3:4, :]).astype(bf16)

    full = shape((part, width), f32)
    shapes = [full, full, shape((part, 1), f32), shape((part, width), bf16)]
    return call(kernel, "second_norm", shapes, where, inputs, keep, got, gains)


def second_norm_back(where, grad, keep, got, gains, scaled, rstd, part):
    width = keep.shape[1]

    def kernel(where_ref, g_ref, keep_ref, got_ref, gain_ref, scaled_ref, rstd_ref, two, mid, out):
        total = keep_ref[...] + read_message(got_ref, part)
        two[...] = total
        back = norm_back(total * gain_ref[2:3, :], scaled_ref[...], rstd_ref[...])
        back = g_ref[...].astype(f32) + back
        mid[...] = back
        out[...] = back.astype(bf16)

    full = shape((part, width), f32)
    shapes = [full, full, shape((part, width), bf16)]
    operands = (where, grad, keep, got, gains, scaled, rstd)
    return call(kernel, "second_norm_back", shapes, *operands)


def slot_of(k):
    return (((k & 1) ^ (k >> 1)) << 1) | (k >> 1)


def natural(ref, slot, flip, columns=slice(None)):
    first = ref[flip, slot, :, columns]
    second = ref[1 - flip, slot, :, columns]
    return jnp.concatenate([first, second], axis=0)


def choose(refs, ky, slot, flip, columns=slice(None)):
    values = natural(refs[0], slot, flip, columns)
    for k in range(1, len(refs)):
        values = jnp.where(ky == k, natural(refs[k], slot, flip, columns), values)
    return values


def dot(left, right, dims):
    return lax.dot_general(left, right, (dims, ((), ())), preferred_element_type=f32)


NN, NT, TN = ((1,), (0,)), ((1,), (1,)), ((0,), (0,))


def decays_of(row):
    block = row.shape[-1]
    at = lax.broadcasted_iota(jnp.int32, (block, block), 0)
    to = lax.broadcasted_iota(jnp.int32, (block, block), 1)
    turned = jnp.sum(jnp.where(at == to, row, 0.0), axis=1, keepdims=True)
    running = jnp.sum(jnp.where(at <= to, turned, 0.0), axis=0, keepdims=True)
    col = jnp.sum(jnp.where(at == to, running, 0.0), axis=1, keepdims=True)
    matrix = jnp.where(at >= to, jnp.exp(jnp.minimum(col - running, 0.0)), 0.0)
    return col, running[:, block - 1 :], matrix


def retention_forward(where, decays, keyvals, query_gate):
    ny = len(keyvals)
    halves, nz, part, _ = query_gate.shape

    def kernel(where_ref, decay_ref, *refs):
        kv_refs, (qg_ref, y_ref, n_ref, r_ref, s_ref, q_ref, state) = refs[:ny], refs[ny:]
        j = pl.program_id(0)

        @pl.when(j == 0)
        def _():
            state[...] = jnp.zeros_like(state)

        slot = slot_of((j // ny) ^ where_ref[0])
        ky = (j % ny) ^ where_ref[1]
        flip = where_ref[3]
        col, last, matrix = decays_of(decay_ref[pl.ds(j, 1), :])
        key = choose(kv_refs, ky, slot, flip, slice(0, DK))
        value = choose(kv_refs, ky, slot, flip, slice(DK, DK + DV))

        @pl.when(ky == 0)
        def _():
            q = natural(qg_ref, slot, flip, slice(0, DK)).astype(bf16)
            state_bf = state[...].astype(bf16)
            s_ref[slot] = state_bf
            weights = (dot(q, key, NT) * matrix).astype(bf16)
            out = dot(weights, value, NN) + jnp.exp(col) * dot(q, state_bf, NN)
            normed, rstd = normalize(out)
            g = natural(qg_ref, slot, flip, slice(DK, DK + DV))
            mixed = (g * jax.nn.sigmoid(g) * normed).astype(bf16)
            for half in range(2):
                rows = slice(half * part, (half + 1) * part)
                to = (1 - flip) if half else flip
                y_ref[to, slot] = mixed[rows]
                n_ref[to, slot] = normed[rows]
                r_ref[to, slot] = rstd[rows]
                q_ref[to, slot] = q[rows]

        key_tail = (key.astype(f32) * jnp.exp(last - col)).astype(bf16)
        state[...] = jnp.exp(last) * state[...] + dot(key_tail, value, TN)

    return call(
        kernel,
        "retention_forward",
        [
            shape((halves, nz, part, DV), bf16),
            shape((halves, nz, part, DV), f32),
            shape((halves, nz, part, 1), f32),
            shape((nz, DK, DV), bf16),
            shape((halves, nz, part, DK), bf16),
        ],
        where,
        decays,
        *keyvals,
        query_gate,
        grid=(nz * ny,),
        scratch=[pltpu.VMEM((DK, DV), f32)],
    )


def retention_backward(where, decays, keyval, queries, grads, states, cosines, sines, gate):
    ny = len(queries)
    halves, nz, part, _ = keyval.shape
    key_scale = DK ** (-0.5)

    def kernel(where_ref, decay_ref, *refs):
        q_refs, d_refs, rest = refs[:ny], refs[ny : 2 * ny], refs[2 * ny :]
        kv_ref, s_ref, cos_ref, sin_ref, gate_ref, kv_out, qg_out, state = rest
        step = pl.program_id(0)
        j = nz * ny - 1 - step

        @pl.when(step == 0)
        def _():
            state[...] = jnp.zeros_like(state)
            qg_out[:, :, :, DK:] = gate_ref[...]

        slot = slot_of((j // ny) ^ where_ref[0])
        ky = (j % ny) ^ where_ref[1]
        flip = where_ref[3]
        col, last, matrix = decays_of(decay_ref[pl.ds(j, 1), :])
        q = choose(q_refs, ky, slot, flip)
        grad = choose(d_refs, ky, slot, flip)
        entry = jnp.exp(col)

        @pl.when(ky == 0)
        def _():
            key = natural(kv_ref, slot, flip, slice(0, DK))
            value = natural(kv_ref, slot, flip, slice(DK, DK + DV))
            cos = natural(cos_ref, slot, flip)
            sin = natural(sin_ref, slot, flip)
            tail = jnp.exp(last - col)
            state_bf = state[...].astype(bf16)
            weights = (dot(q, key, NT) * matrix).astype(bf16)
            scores = (dot(grad, value, NT) * matrix).astype(bf16)
            grad_q = dot(scores, key, NN) + entry * dot(grad, s_ref[slot], NT)
            grad_k = dot(scores, q, TN) + tail * dot(value, state_bf, NT)
            grad_v = dot(weights, grad, TN) + tail * dot(key, state_bf, NN)
            grad_q = rotate(grad_q, cos, -sin).astype(bf16)
            grad_k = (rotate(grad_k, cos, -sin) * key_scale).astype(bf16)
            grad_v = grad_v.astype(bf16)
            for half in range(2):
                rows = slice(half * part, (half + 1) * part)
                to = (1 - flip) if half else flip
                kv_out[to, slot, :, :DK] = grad_k[rows]
                kv_out[to, slot, :, DK:] = grad_v[rows]
                qg_out[to, slot, :, :DK] = grad_q[rows]

        query_entry = (q.astype(f32) * entry).astype(bf16)
        state[...] = jnp.exp(last) * state[...] + dot(query_entry, grad, TN)

    return call(
        kernel,
        "retention_backward",
        [shape((halves, nz, part, DK + DV), bf16)] * 2,
        where,
        decays,
        *queries,
        *grads,
        keyval,
        states,
        cosines,
        sines,
        gate,
        grid=(nz * ny,),
        scratch=[pltpu.VMEM((DK, DV), f32)],
    )


def shards(
    hidden_in,
    log_decay,
    out_grad,
    ln1_gain,
    ln1_bias,
    w_query,
    w_key,
    w_value,
    w_gate,
    w_out,
    ln2_gain,
    ln2_bias,
    mlp_gate,
    mlp_up,
    mlp_down,
):
    nz, ny = lax.axis_size("row"), lax.axis_size("col")
    nb, nh = lax.axis_size("batch"), lax.axis_size("head")
    block, width = hidden_in.shape[1:]
    rows = ln1_gain.shape[0]
    part = block // nh
    tokens = nz * block
    half, quarter = tokens // 2, tokens // 4
    group = nz * rows
    sizes = (nz, ny, nb)
    where = jnp.stack([lax.axis_index(name) for name in ("row", "col", "batch", "head")])
    (where,) = tie(where.astype(jnp.int32))

    def trade(pieces, k):
        return swap(pieces[k], "row", k) if k else pieces[k]

    def over_col(own):
        return [own] + [swap(own, "col", k) for k in range(1, ny)]

    def over_batch(values):
        return [swap(value, "batch", 1) for value in values]

    def mirror(values):
        return swap(values, "head", 1)

    def pairs(own, other):
        return [(part,) for both in zip(own, other) for part in both]

    def split(values):
        return values.reshape(nh, nz, part, -1)

    def add(values, got):
        return values + got.astype(f32)

    def sum_col(keep, send):
        for k in range(1, ny):
            keep = add(keep, swap(send[k * group : (k + 1) * group], "col", k))
        return keep.reshape(nz, rows, -1)

    def reduce_far(*terms):
        far = sum(matmul_t(values[half:], weight) for values, weight in terms).astype(bf16)
        return far[quarter:], far[:quarter]

    def reduce_near(*terms):
        near = sum(matmul_t(values[:half], weight) for values, weight in terms)
        return near[quarter:], near[:quarter]

    def step_one(packed, first):
        return swap(packed[2], "row", first)

    def step_two(packed, got, first):
        return swap(jnp.stack([packed[1], got[1]]), "row", 4 - first)

    def in_order(packed, got, last, first):
        pieces = {0: packed[0], first: got[0], 4 - first: last[0], 2: last[1]}
        return [pieces[k] for k in range(4)]

    gains = jnp.concatenate([ln1_gain, ln1_bias, ln2_gain, ln2_bias])[None]
    own_in, other_in = cut_halves(where, hidden_in[0], nh)
    two_in = swap(own_in, "row", 3)
    kv = pack_weights(where, (w_key, w_value), nz, rows, (gains, log_decay[0]))
    kv = [trade(kv, k) for k in range(nz)]
    qg = pack_weights(where, (w_query, w_gate), nz, rows, first=1)
    qg_got = step_one(qg, 1)
    kv, two_in, qg_got, late_grad = tie(kv, two_in, qg_got, out_grad[0])
    kv = jnp.stack(kv)
    kv_cols, kv_mate = over_col(kv), swap(kv, "batch", 1)
    one_in = swap(jnp.concatenate([own_in, two_in]), "row", 1)
    qg_last = step_two(qg, qg_got, 1)
    own_grad, other_grad = cut_halves(where, late_grad, nh)
    half_dim = DK // 2
    freqs = 10000.0 ** (-jnp.arange(half_dim, dtype=f32) / half_dim)
    block_at = (jnp.array(ORDER, jnp.int32) ^ where[0:1]) * ny + where[1:2]
    half_at = jnp.arange(nh, dtype=jnp.int32) ^ where[3:4]
    positions = (
        block_at[None, :, None] * block + half_at[:, None, None] * part + jnp.arange(part)
    )
    angles = positions.astype(f32)[..., None] * freqs
    cosines, sines = jnp.cos(angles), jnp.sin(angles)
    out = pack_weights(where, (w_out,), nz, rows, first=3)
    kv_cols, kv_mate, one_in, qg_last, own_grad, out, cosines, sines = tie(
        kv_cols, kv_mate, one_in, qg_last, own_grad, out, cosines, sines
    )
    kv_mates = [kv_mate] + over_batch(kv_cols[1:])
    mirror_in = mirror(jnp.concatenate([two_in, one_in]))
    qg_cols = over_col(jnp.stack(in_order(qg, qg_got, qg_last, 1)))
    two_grad = swap(own_grad, "row", 3)
    out_got = step_one(out, 3)
    feed = pack_weights(where, (mlp_gate, mlp_up, mlp_down), nz, rows)
    kv_mates, mirror_in, qg_cols, two_grad, out_got, feed = tie(
        kv_mates, mirror_in, qg_cols, two_grad, out_got, feed
    )
    kv_w, gains, decays = assemble(
        where, pairs(kv_cols, kv_mates), ny, nb, (DK + DV,), EXTRA, block
    )

    first_bf = place_rows(where, (own_in, two_in, one_in, other_in, mirror_in), gains)
    key_scale = DK ** (-0.5)
    projected = split(matmul(first_bf, kv_w))
    key_bf = (rotate(projected[..., :DK], cosines, sines) * key_scale).astype(bf16)
    keyval = jnp.concatenate([key_bf, projected[..., DK:].astype(bf16)], axis=-1)

    keyval, qg_cols, out_got, feed = tie(keyval, qg_cols, out_got, feed)
    keyvals = over_col(keyval)
    out_last = step_two(out, out_got, 3)
    feed_two = trade(feed, 2)
    (qg_w,) = assemble(where, pairs(qg_cols, over_batch(qg_cols)), ny, nb, (DK + DV,))
    projected = split(matmul(first_bf, qg_w))
    query_gate = jnp.concatenate(
        [rotate(projected[..., :DK], cosines, sines), projected[..., DK:]], axis=-1
    )
    keyvals, query_gate, out_last, feed_two = tie(keyvals, query_gate, out_last, feed_two)
    out_cols = over_col(jnp.stack(in_order(out, out_got, out_last, 3)))
    late_grad, late_two, late_three = after((own_grad, two_grad, feed[3]), keyvals)
    middle_col = late_three.shape[1] // 2
    feed_left = swap(late_three[:, :middle_col], "row", 3)
    one_grad = swap(jnp.concatenate([late_grad, late_two]), "row", 1)
    mixed, normed, rstd, states, query = retention_forward(where, decays, keyvals, query_gate)
    mixed, out_cols, one_grad, feed_left = tie(mixed, out_cols, one_grad, feed_left)
    (out_w,) = assemble(where, pairs(out_cols, over_batch(out_cols)), ny, nb, (DV,))
    mixed_bf = mixed.reshape(tokens, DV)

    far = far_messages(where, mixed_bf, out_w, part)
    got = mirror(far[0])
    near = reduce_near((mixed_bf, out_w))
    late_feed = after(feed, far)
    feed_right = swap(late_feed[3][:, middle_col:], "row", 3)
    feed_one = trade(late_feed, 1)
    got, near, feed_right, feed_one = tie(got, near, feed_right, feed_one)
    feed_three = jnp.concatenate([feed_left, feed_right], axis=-1)
    got_far = mirror(after(far[1], got))
    got = swap(pass_message(where, near[0], got, part), "row", 1)
    feed = jnp.stack([feed[0], feed_one, feed_two, feed_three])
    units = feed.shape[-1] // 3
    feed_gates = over_col(feed[..., :units])[1:]
    feed_mate = swap(feed, "batch", 1)
    got, got_far, feed_gates, feed_mate, feed = tie(got, got_far, feed_gates, feed_mate, feed)
    keep, send = keep_message(where, near[1], got_far, got, part)
    got = swap(send, "row", 3)
    late_feed, late_two, late_gates = after((feed, two_grad, feed_gates), keep)
    feed_ups = over_col(late_feed[..., units : 2 * units])[1:]
    mirror_two = mirror(late_two)
    gate_mates = over_batch(late_gates)
    got, feed_ups, mirror_two, gate_mates = tie(got, feed_ups, mirror_two, gate_mates)
    middle, scaled_two, rstd_two, own = second_norm(where, own_in, keep, got, gains, part)
    two = swap(own, "row", 3)
    late_feed, late_one, late_ups = after((feed, one_grad, feed_ups), own)
    feed_downs = over_col(late_feed[..., 2 * units :])[1:]
    mirror_one = mirror(late_one)
    up_mates = over_batch(late_ups)
    two, feed_downs, mirror_one, up_mates, query = tie(
        two, feed_downs, mirror_one, up_mates, query
    )
    pair = jnp.concatenate([own, two])
    one, mirror_pair = swap(pair, "row", 1), mirror(pair)
    down_mates = over_batch(after(feed_downs, pair))
    one, mirror_pair, down_mates, query = tie(one, mirror_pair, down_mates, query)
    mirror_last = mirror(one)
    queries = over_col(query)
    parts = [(feed,), (feed_mate,)]
    for three in zip(feed_gates, feed_ups, feed_downs, gate_mates, up_mates, down_mates):
        parts += [three[:3], three[3:]]
    up_w, down_w = assemble(where, after(parts, one), ny, nb, (2 * units, units))
    down_bf = place_rows(
        where, after((own_grad, two_grad, one_grad, other_grad, mirror_two, mirror_one), one)
    )
    mirror_last, up_w, down_w, down_bf, queries = tie(mirror_last, up_w, down_w, down_bf, queries)
    second_bf = place_rows(where, (pair, one, mirror_pair, mirror_last))

    up = matmul(second_bf, up_w)
    up_gate, up_lin = up[:, :units], up[:, units:]
    gelu_cdf = 0.5 * (1.0 + lax.erf(up_gate * (0.5**0.5)))
    gelu_val = up_gate * gelu_cdf
    gelu_slope = gelu_cdf + up_gate * jnp.exp(-0.5 * up_gate * up_gate) * (2.0 * jnp.pi) ** -0.5
    hidden_bf = (gelu_val * up_lin).astype(bf16)
    grad_hidden = matmul(down_bf, down_w)
    grad_upgate = (grad_hidden * up_lin * gelu_slope).astype(bf16)
    grad_uplin = (grad_hidden * gelu_val).astype(bf16)
    grad_up = jnp.concatenate([grad_upgate, grad_uplin], axis=-1)
    far = far_messages(where, grad_up, up_w, part)
    got = mirror(far[0])
    near = reduce_near((grad_up, up_w))
    lefts, rights = (second_bf, down_bf), (grad_up, hidden_bf)
    feed_far = weight_grads(where, lefts, rights, sizes)
    got, near, feed_far, hidden_bf = tie(got, near, feed_far, hidden_bf)
    got_far = mirror(after(far[1], got))
    got = swap(pass_message(where, near[0], got, part), "row", 1)
    feed_got = swap(feed_far, "batch", 1)
    feed_keeps, feed_sends = weight_grads(where, lefts, rights, sizes, (units,) * 3, feed_got)
    result_far = reduce_far((hidden_bf, down_w))
    got, got_far, feed_sends, result_far, hidden_bf = tie(
        got, got_far, feed_sends, result_far, hidden_bf
    )
    keep, send = keep_message(where, near[1], got_far, got, part)
    got = swap(send, "row", 3)
    result_got = mirror(result_far[0])
    result_near = reduce_near((hidden_bf, down_w))
    sums = [sum_col(feed_keeps[0], feed_sends[0])]
    got, result_got, result_near, sums, feed_sends = tie(
        got, result_got, result_near, sums, feed_sends
    )
    grad_two, grad_middle, own = second_norm_back(
        where, own_grad, keep, got, gains, scaled_two, rstd_two, part
    )
    own, feed_sends, result_got = tie(own, feed_sends, result_got)
    two = swap(own, "row", 3)
    sums.append(sum_col(feed_keeps[1], feed_sends[1]))
    result_got_far = mirror(after(result_far[1], own))
    result_got = swap(add(result_near[0], result_got).astype(bf16), "row", 1)
    two, sums, feed_sends, result_got_far, result_got = tie(
        two, sums, feed_sends, result_got_far, result_got
    )
    pair = jnp.concatenate([own, two])
    one, mirror_pair = swap(pair, "row", 1), mirror(pair)
    down_sum = sum_col(feed_keeps[2], feed_sends[2])
    wide_grads = cut_heads(where, sums)
    result_keep = add(add(result_near[1], result_got_far), result_got)
    result_send = result_keep[part:].astype(bf16)
    one, mirror_pair, down_sum, wide_grads, result_send = tie(
        one, mirror_pair, down_sum, wide_grads, result_send
    )
    mirror_last = mirror(one)
    wide_two, wide_one = trade(wide_grads, 2), trade(wide_grads, 1)
    down_grads = cut_heads(where, (down_sum,))
    mirror_last, wide_two, wide_one, down_grads = tie(mirror_last, wide_two, wide_one, down_grads)
    attn_bf = place_rows(where, (pair, one, mirror_pair, mirror_last))

    grp_norm, grp_rstd = normed.reshape(tokens, DV), rstd.reshape(tokens, 1)
    gate = query_gate.reshape(tokens, -1)[:, DK:]
    gate_sig = jax.nn.sigmoid(gate)
    gate_act = gate * gate_sig
    grad_mixed = matmul(attn_bf, out_w)
    grad_gate = (grad_mixed * grp_norm * (gate_sig * (1.0 + gate * (1.0 - gate_sig)))).astype(bf16)
    ret_bf = norm_back(grad_mixed * gate_act, grp_norm, grp_rstd).astype(bf16)
    ret_bf, wide_grads, down_grads = tie(split(ret_bf), wide_grads, down_grads)
    ret_all = over_col(ret_bf)
    wide_three, down_one = trade(wide_grads, 3), trade(down_grads, 1)
    lefts, rights = (first_bf, attn_bf), (grad_gate, mixed_bf)
    both_got = swap(weight_grads(where, lefts, rights, sizes), "batch", 1)
    both_keeps, both_sends = weight_grads(where, lefts, rights, sizes, (DV, DV), both_got)
    ret_all, wide_three, down_one, both_sends = tie(ret_all, wide_three, down_one, both_sends)
    grad_kv, grad_qg = retention_backward(
        where, decays, keyval, queries, ret_all, states, cosines, sines, split(grad_gate)
    )
    grad_kv, grad_qg = grad_kv.reshape(tokens, -1), grad_qg.reshape(tokens, -1)
    terms = ((grad_kv, kv_w), (grad_qg, qg_w))
    far = reduce_far(*terms)
    got = mirror(far[0])
    late_kv, late_qg, late_send, late_down = after((grad_kv, grad_qg, both_sends, down_grads), far)
    kvq = ((first_bf, first_bf), (late_kv, (late_qg, 0, DK)))
    kvq_got = swap(weight_grads(where, *kvq, sizes), "batch", 1)
    down_two, down_three = trade(late_down, 2), trade(late_down, 3)
    out_sum = sum_col(both_keeps[1], late_send[1])
    near = reduce_near(*terms)
    got, near, down_two, down_three, kvq_got, out_sum, both_sends, result_send = tie(
        got, near, down_two, down_three, kvq_got, out_sum, both_sends, result_send
    )
    got_far = mirror(after(far[1], got))
    got = swap(add(near[0], got).astype(bf16), "row", 1)
    gate_sum = sum_col(both_keeps[0], both_sends[0])
    result_got = swap(result_send, "row", 3)
    kvq_keeps, kvq_sends = weight_grads(where, *kvq, sizes, (DV, 2 * DK), kvq_got)
    wide_pieces = (wide_grads[0], wide_one, wide_two, wide_three)
    grad_gates, grad_ups = unpack_grads(where, wide_pieces, ((units, False), (units, False)))
    got, got_far, gate_sum, result_got, kvq_sends, grad_gates, grad_ups = tie(
        got, got_far, gate_sum, result_got, kvq_sends, grad_gates, grad_ups
    )
    keep = add(add(near[1], got_far), got)
    got = swap(keep[part:].astype(bf16), "row", 3)
    result = (middle + add(result_keep[:part], result_got)).astype(bf16)
    result_other = mirror(result)
    kvq_first = sum_col(kvq_keeps[0], kvq_sends[0])
    both_pieces = cut_heads(where, (gate_sum, out_sum))
    down_pieces = (down_grads[0], down_one, down_two, down_three)
    (grad_downs,) = unpack_grads(where, down_pieces, ((units, True),))
    got, result_other, kvq_first, kvq_sends, both_pieces, grad_downs = tie(
        got, result_other, kvq_first, kvq_sends, both_pieces, grad_downs
    )
    both_pieces = [trade(both_pieces, k) for k in range(nz)]
    kvq_second = sum_col(kvq_keeps[1], kvq_sends[1])
    grad_one = add(keep[:part], got)
    scaled_own, rstd_own = normalize(own_in.astype(f32))
    grad_in = grad_middle + norm_back(grad_one * gains[0:1], scaled_own, rstd_own)
    grad_in_other = mirror(grad_in)
    kvq_pieces = cut_heads(where, (kvq_first, kvq_second))
    both_pieces, kvq_pieces, grad_in_other, grad_one = tie(
        both_pieces, kvq_pieces, grad_in_other, grad_one
    )
    kvq_pieces = [trade(kvq_pieces, k) for k in range(nz)]
    norm_sums = jnp.stack(
        [
            jnp.sum(grad_one * scaled_own, axis=0),
            jnp.sum(grad_one, axis=0),
            jnp.sum(grad_two * scaled_two, axis=0),
            jnp.sum(grad_two, axis=0),
        ]
    )
    norm_sums = after(norm_sums, kvq_pieces[1])
    norm_sums = norm_sums + mirror(norm_sums)
    norm_sums = norm_sums.reshape(4, nz, ny, nb, rows)

    def sum_over(values, name, axis):
        me = lax.axis_index(name)
        summed = pick(values, me, axis)
        for k in range(1, lax.axis_size(name)):
            summed = summed + swap(pick(values, me ^ k, axis), name, k)
        return summed

    for name, axis in (("batch", 3), ("col", 2), ("row", 1)):
        norm_sums = sum_over(norm_sums, name, axis)
    grad_g, grad_outs = unpack_grads(where, both_pieces, ((DV, False), (DV, True)))
    grad_k, grad_v, grad_q = unpack_grads(
        where, kvq_pieces, ((DK, False), (DV, False), (DK, False))
    )

    def join(own, other):
        return join_halves(where, own, other).reshape(1, block, width)

    return (
        join(result, result_other),
        join(grad_in, grad_in_other),
        norm_sums[0],
        norm_sums[1],
        grad_q,
        grad_k,
        grad_v,
        grad_g,
        grad_outs,
        norm_sums[2],
        norm_sums[3],
        grad_gates,
        grad_ups,
        grad_downs,
    )


def solution(mesh):
    seq = ("row", "col")
    tokens = P("batch", seq, None)
    params = P((*seq, "batch"))
    by_rows = P((*seq, "batch"), "head")
    by_cols = P("head", (*seq, "batch"))

    def run(*arrays):
        rows = arrays[1].shape[1] // mesh.shape["head"]
        sizes = (rows, mesh.shape["seq"] // rows, mesh.shape["batch"], mesh.shape["head"])
        order = [mesh.axis_names.index(n) for n in ("seq", "batch", "head")]
        fine = Mesh(
            mesh.devices.transpose(order).reshape(sizes), ("row", "col", "batch", "head")
        )
        weights = (by_rows, by_rows, by_rows, by_rows, by_cols)
        feeds = (by_rows, by_rows, by_cols)
        return jax.shard_map(
            shards,
            mesh=fine,
            in_specs=(
                tokens,
                P("batch", "head", seq),
                tokens,
                params,
                params,
                *weights,
                params,
                params,
                *feeds,
            ),
            out_specs=(tokens, tokens, params, params, *weights, params, params, *feeds),
            check_vma=False,
        )(*arrays)

    return run
```

```python
import jax
import jax.numpy as jnp
from jax import lax
from jax.experimental import pallas as pl
from jax.experimental.pallas import tpu as pltpu
from jax.sharding import Mesh
from jax.sharding import PartitionSpec as P

DK = 256
DV = 512

epsilon = 1e-05
f32 = jnp.float32
bf16 = jnp.bfloat16
VMEM_LIMIT = 12 * 1024 * 1024

ORDER = (0, 3, 1, 2)


def swap(values, axis, k):
    count = lax.axis_size(axis)
    return lax.ppermute(values, axis, [(i, i ^ k) for i in range(count)])


def pick(values, index, axis):
    return lax.dynamic_index_in_dim(values, index, axis, keepdims=False)


def tie(*values):
    return lax.optimization_barrier(values)


def after(values, *others):
    return tie(values, others)[0]


def matmul(values, weight):
    return jnp.dot(values, weight, preferred_element_type=f32)


def matmul_t(values, weight):
    return lax.dot_general(values, weight, (((1,), (1,)), ((), ())), preferred_element_type=f32)


def outer_sum(values, other):
    return lax.dot_general(values, other, (((0,), (0,)), ((), ())), preferred_element_type=f32)


def normalize(values):
    center = values - jnp.mean(values, axis=-1, keepdims=True)
    rstd = lax.rsqrt(jnp.mean(center * center, axis=-1, keepdims=True) + epsilon)
    return center * rstd, rstd


def norm_back(scaled_grad, scaled, rstd):
    return rstd * (
        scaled_grad
        - jnp.mean(scaled_grad, axis=-1, keepdims=True)
        - scaled * jnp.mean(scaled_grad * scaled, axis=-1, keepdims=True)
    )


def rotate(values, cosines, sines):
    half_dim = values.shape[-1] // 2
    first_half = values[..., :half_dim]
    second_half = values[..., half_dim:]
    return jnp.concatenate(
        [first_half * cosines - second_half * sines, first_half * sines + second_half * cosines],
        axis=-1,
    )


SMEM = pl.BlockSpec(memory_space=pltpu.SMEM)
WHOLE = pl.BlockSpec(memory_space=pltpu.VMEM)
PARAMS = pltpu.CompilerParams(vmem_limit_bytes=VMEM_LIMIT)


def call(kernel, name, shapes, *operands, grid=None, scratch=()):
    many = isinstance(shapes, list)
    return pl.pallas_call(
        kernel,
        grid=() if grid is None else grid,
        out_shape=shapes,
        in_specs=[SMEM] + [WHOLE] * (len(operands) - 1),
        out_specs=[WHOLE] * len(shapes) if many else WHOLE,
        scratch_shapes=list(scratch),
        compiler_params=PARAMS,
        name=name,
    )(*operands)


def shape(dims, dtype):
    return jax.ShapeDtypeStruct(tuple(dims), dtype)


def cut_halves(where, values, heads):
    block, width = values.shape
    part = block // heads

    def kernel(where_ref, ref, own, other):
        for out, half in ((own, where_ref[3]), (other, 1 - where_ref[3])):
            out[...] = ref[pl.ds(pl.multiple_of(half * part, part), part), :]

    return call(kernel, "cut_halves", [shape((part, width), values.dtype)] * 2, where, values)


def join_halves(where, own, other):
    part, width = own.shape

    def kernel(where_ref, own_ref, other_ref, out):
        for ref, half in ((own_ref, where_ref[3]), (other_ref, 1 - where_ref[3])):
            out[pl.ds(pl.multiple_of(half * part, part), part), :] = ref[...]

    return call(kernel, "join_halves", shape((2 * part, width), own.dtype), where, own, other)


def cut_heads(where, totals, first=0):
    nz, rows, _ = totals[0].shape
    width = sum(total.shape[2] for total in totals)

    def kernel(where_ref, *refs):
        ins, outs = refs[: len(totals)], refs[len(totals) :]
        targets = [outs[k] for k in range(nz)] if not first else steps(outs, first)
        for k in range(nz):
            at = 0
            for ref in ins:
                cols = ref.shape[2]
                targets[k][:, at : at + cols] = ref[where_ref[0] ^ k].astype(bf16)
                at += cols

    shapes = [shape((rows, width), bf16)] * nz
    if first:
        shapes = shapes[:2] + [shape((2, rows, width), bf16)]
    return call(kernel, "cut_heads", shapes, where, *totals)


def steps(refs, first):
    stay, second, firsts = refs
    return {0: stay, 4 - first: second, first: firsts.at[0], 2: firsts.at[1]}


def pack_weights(where, weights, nz, rows, extras=None, first=0):
    widths = [w.size // rows // nz for w in weights]
    total = sum(widths)
    count = 0
    if extras:
        gains, decays = extras
        block = decays.shape[1]
        extras = (jnp.pad(gains, ((0, 0), (0, total - gains.shape[1]))), decays)
        count = EXTRA

    def kernel(where_ref, *refs):
        ins, rest = refs[: len(weights)], refs[len(weights) :]
        outs = steps(rest, first) if first else rest[-nz:]
        for k in range(nz):
            target = where_ref[0] ^ k
            at = 0
            for ref, width in zip(ins, widths):
                start = pl.multiple_of(target * width, width)
                if ref.shape[0] == rows:
                    piece = ref[:, pl.ds(start, width)]
                else:
                    piece = ref[pl.ds(start, width), :].astype(f32).T.astype(bf16)
                outs[k][:rows, at : at + width] = piece
                at += width
            if extras:
                line = lax.broadcasted_iota(jnp.int32, (EXTRA, 1), 0)
                gain_rows = jnp.where(line == 0, rest[0][...].astype(f32), 0.0)
                parts = gain_rows[:, :block]
                left = rest[1][pl.ds(target, 1), :]
                for number in range(1, 4):
                    part = left.astype(bf16).astype(f32)
                    parts = jnp.where(line == number, part, parts)
                    left = left - part
                outs[k][rows:, :] = gain_rows.astype(bf16)
                outs[k][rows:, :block] = parts.astype(bf16)

    shapes = [shape((rows + count, total), bf16)] * nz
    if first:
        shapes = shapes[:2] + [shape((2, rows, total), bf16)]
    return call(kernel, "pack_weights", shapes, where, *weights, *(extras or ()))


def unpack_grads(where, pieces, outs):
    nz = len(pieces)
    rows = pieces[0].shape[0]

    def kernel(where_ref, *refs):
        ins, results = refs[:nz], refs[nz:]
        for k in range(nz):
            target = where_ref[0] ^ k
            at = 0
            for ref, (width, turned) in zip(results, outs):
                to = pl.ds(pl.multiple_of(target * width, width), width)
                piece = ins[k][:, at : at + width].astype(f32)
                if turned:
                    ref[to, :] = piece.T
                else:
                    ref[:, to] = piece
                at += width

    shapes = [shape((nz * w, rows) if turned else (rows, nz * w), f32) for w, turned in outs]
    return call(kernel, "unpack_grads", shapes, where, *pieces)


EXTRA = 16


def assemble(where, parts, ny, nb, widths, extra=0, block=0):
    nz, rows, _ = parts[0][0].shape
    rows -= extra
    count = nz * ny * nb
    total = sum(widths)
    sizes = [len(part) for part in parts]
    aligned = rows % 128 == 0

    def kernel(where_ref, *refs):
        ins, outs = refs[: sum(sizes)], refs[sum(sizes) :]
        for ky in range(ny):
            for kb in range(nb):
                pieces, ins = ins[: sizes[ky * nb + kb]], ins[sizes[ky * nb + kb] :]
                for kz in range(nz):
                    place = (where_ref[0] ^ kz) * ny + (where_ref[1] ^ ky)
                    device = place * nb + (where_ref[2] ^ kb)
                    at = pl.multiple_of(device * rows, rows)
                    column = 0
                    for piece in pieces:
                        cols = piece.shape[-1]
                        start = 0
                        for out, width in zip(outs, widths):
                            low, high = max(start, column), min(start + width, column + cols)
                            if low < high:
                                out[pl.ds(at, rows), low - start : high - start] = piece[
                                    kz, :rows, low - column : high - column
                                ]
                            start += width
                        column += cols
                    if extra:
                        tail = pieces[0][kz, rows:, :].astype(f32)
                        if aligned:
                            for number in range(4):
                                gain = tail[:1, number * rows : (number + 1) * rows]
                                outs[-2][number : number + 1, pl.ds(at, rows)] = gain
                        else:
                            outs[-2][pl.ds(device, 1), :] = tail[:1]
                        if kb == 0:
                            decay = (tail[1:2] + tail[2:3]) + tail[3:4]
                            outs[-1][pl.ds(place, 1), :] = decay[:, :block]

    shapes = [shape((count * rows, width), bf16) for width in widths]
    if extra:
        shapes.append(shape((4, count * rows) if aligned else (count, total), f32))
        shapes.append(shape((nz * ny, block), f32))
    outs = list(call(kernel, "assemble", shapes, where, *[p for part in parts for p in part]))
    if extra and not aligned:
        gains = outs[-2][:, : 4 * rows].reshape(count, 4, rows)
        outs[-2] = gains.transpose(1, 0, 2).reshape(4, count * rows)
    return outs


def row_groups(where, left, sizes):
    nz, ny, nb = sizes
    groups = left.reshape(left.shape[0], nz, ny, nb, -1)
    groups = jnp.take(groups, jnp.arange(ny) ^ where[1], axis=2)
    groups = jnp.take(groups, jnp.arange(nb) ^ where[2], axis=3)
    return groups.transpose(0, 3, 2, 1, 4).reshape(left.shape)


def weight_grads(where, lefts, rights, sizes, widths=None, got=None):
    nz, ny, nb = sizes
    width = lefts[0].shape[1]
    rows = width // (nz * ny * nb)
    group = nz * rows
    rights = [right if isinstance(right, tuple) else (right, 0, right.shape[1]) for right in rights]
    ranges = [right[1:] for right in rights]
    rights = [right[0] for right in rights]
    total = sum(high - low for low, high in ranges)
    kb = 1 if got is None else 0
    aligned = rows % 128 == 0
    if not aligned:
        lefts = [row_groups(where, left, sizes) for left in lefts]

    def columns(where_ref, left, step):
        if not aligned:
            return left[:, pl.ds(pl.multiple_of((kb * ny + step) * group, group), group)]
        tiles = []
        for z in range(nz):
            start = ((z * ny + (where_ref[1] ^ step)) * nb + (where_ref[2] ^ kb)) * rows
            tiles.append(left[:, pl.ds(pl.multiple_of(start, rows), rows)])
        return jnp.concatenate(tiles, axis=1)

    def kernel(where_ref, *refs):
        ins, rest = refs[: len(lefts)], refs[len(lefts) :]
        others, rest = rest[: len(rights)], rest[len(rights) :]
        step = pl.program_id(0)
        values = []
        for left, right, (low, high) in zip(ins, others, ranges):
            values.append(dot(columns(where_ref, left, step), right[:, low:high], TN))
        if got is None:
            at = 0
            for value in values:
                rest[0][:, at : at + value.shape[1]] = value.astype(bf16)
                at += value.shape[1]
            return
        value = jnp.concatenate(values, axis=1) + rest[0][...].astype(f32)
        keeps, sends = rest[1 : 1 + len(widths)], rest[1 + len(widths) :]
        at = 0
        for keep, send, cols in zip(keeps, sends, widths):
            part = value[:, at : at + cols]
            send[...] = part.astype(bf16)

            @pl.when(step == 0)
            def _():
                keep[...] = part

            at += cols

    moving = lambda cols: pl.BlockSpec((group, cols), lambda i: (i, 0))
    if got is None:
        specs = moving(total)
        shapes = shape((ny * group, total), bf16)
    else:
        specs = [pl.BlockSpec((group, cols), lambda i: (0, 0)) for cols in widths]
        specs += [moving(cols) for cols in widths]
        shapes = [shape((group, cols), f32) for cols in widths]
        shapes += [shape((ny * group, cols), bf16) for cols in widths]
    outs = pl.pallas_call(
        kernel,
        grid=(ny,),
        out_shape=shapes,
        in_specs=[SMEM]
        + [WHOLE] * (len(lefts) + len(rights))
        + ([] if got is None else [moving(total)]),
        out_specs=specs,
        compiler_params=PARAMS,
        name="weight_grads",
    )(where, *lefts, *rights, *(() if got is None else (got,)))
    return outs if got is None else (outs[: len(widths)], outs[len(widths) :])


def place_rows(where, pieces, gains=None):
    width = pieces[0].shape[-1]
    tokens = sum(piece.shape[0] for piece in pieces)

    def kernel(where_ref, *refs):
        ins, full = refs[: len(pieces)], refs[-1]
        at = 0
        for ref in ins:
            values = ref[...]
            if gains is not None:
                values, _ = normalize(values.astype(f32))
                params = refs[-2]
                values = (values * params[0:1, :] + params[1:2, :]).astype(bf16)
            full[at : at + ref.shape[0], :] = values
            at += ref.shape[0]

    more = () if gains is None else (gains,)
    return call(kernel, "place_rows", shape((tokens, width), bf16), where, *pieces, *more)


LOW = 16


def write_message(ref, values, part, columns=slice(None)):
    count = values.shape[0]
    high = values.astype(bf16)
    ref[:count, columns] = high
    low = values - high.astype(f32)
    line = lax.broadcasted_iota(jnp.int32, (LOW, 1), 0)
    rows = jnp.zeros((LOW, values.shape[1]), f32)
    for number in range(count // part):
        rows = jnp.where(line == number, low[number * part : number * part + 1], rows)
    ref[count:, columns] = rows.astype(bf16)


def read_message(ref, part):
    count = ref.shape[0] - LOW
    values = ref[:count, :].astype(f32)
    low = ref[count:, :].astype(f32)
    line = lax.broadcasted_iota(jnp.int32, (count, 1), 0)
    for number in range(count // part):
        values = values + jnp.where(line == number * part, low[number : number + 1], 0.0)
    return values


def far_messages(where, values, weight, part):
    half = values.shape[0] // 2
    quarter = half // 2
    width, depth = weight.shape
    step = width // 4

    def kernel(where_ref, value_ref, weight_ref, second, first):
        out = dot(value_ref[half:, :], weight_ref[...], NT)
        write_message(second, out[quarter:], part)
        write_message(first, out[:quarter], part)

    return pl.pallas_call(
        kernel,
        grid=(4,),
        out_shape=[shape((quarter + LOW, width), bf16)] * 2,
        in_specs=[SMEM, WHOLE, pl.BlockSpec((step, depth), lambda i: (i, 0))],
        out_specs=[pl.BlockSpec((quarter + LOW, step), lambda i: (0, i))] * 2,
        compiler_params=PARAMS,
        name="far_messages",
    )(where, values, weight)


def pass_message(where, near, got, part):
    def kernel(where_ref, near_ref, got_ref, out):
        write_message(out, near_ref[...] + read_message(got_ref, part), part)

    return call(kernel, "pass_message", shape(got.shape, bf16), where, near, got)


def keep_message(where, near, got_far, got, part):
    width = near.shape[1]

    def kernel(where_ref, near_ref, far_ref, got_ref, keep, out):
        total = near_ref[...] + read_message(far_ref, part) + read_message(got_ref, part)
        keep[...] = total[:part]
        write_message(out, total[part:], part)

    shapes = [shape((part, width), f32), shape((part + LOW, width), bf16)]
    return call(kernel, "keep_message", shapes, where, near, got_far, got)


def second_norm(where, inputs, keep, got, gains, part):
    width = keep.shape[1]

    def kernel(where_ref, in_ref, keep_ref, got_ref, gain_ref, middle, scaled, rstd, out):
        total = in_ref[...].astype(f32) + (keep_ref[...] + read_message(got_ref, part))
        middle[...] = total
        normed, factor = normalize(total)
        scaled[...] = normed
        rstd[...] = factor
        out[...] = (normed * gain_ref[2:3, :] + gain_ref[3:4, :]).astype(bf16)

    full = shape((part, width), f32)
    shapes = [full, full, shape((part, 1), f32), shape((part, width), bf16)]
    return call(kernel, "second_norm", shapes, where, inputs, keep, got, gains)


def second_norm_back(where, grad, keep, got, gains, scaled, rstd, part):
    width = keep.shape[1]

    def kernel(where_ref, g_ref, keep_ref, got_ref, gain_ref, scaled_ref, rstd_ref, two, mid, out):
        total = keep_ref[...] + read_message(got_ref, part)
        two[...] = total
        back = norm_back(total * gain_ref[2:3, :], scaled_ref[...], rstd_ref[...])
        back = g_ref[...].astype(f32) + back
        mid[...] = back
        out[...] = back.astype(bf16)

    full = shape((part, width), f32)
    shapes = [full, full, shape((part, width), bf16)]
    operands = (where, grad, keep, got, gains, scaled, rstd)
    return call(kernel, "second_norm_back", shapes, *operands)


def slot_of(k):
    return (((k & 1) ^ (k >> 1)) << 1) | (k >> 1)


def natural(ref, slot, flip, columns=slice(None)):
    first = ref[flip, slot, :, columns]
    second = ref[1 - flip, slot, :, columns]
    return jnp.concatenate([first, second], axis=0)


def choose(refs, ky, slot, flip, columns=slice(None)):
    values = natural(refs[0], slot, flip, columns)
    for k in range(1, len(refs)):
        values = jnp.where(ky == k, natural(refs[k], slot, flip, columns), values)
    return values


def dot(left, right, dims):
    return lax.dot_general(left, right, (dims, ((), ())), preferred_element_type=f32)


NN, NT, TN = ((1,), (0,)), ((1,), (1,)), ((0,), (0,))


def decays_of(row):
    block = row.shape[-1]
    at = lax.broadcasted_iota(jnp.int32, (block, block), 0)
    to = lax.broadcasted_iota(jnp.int32, (block, block), 1)
    turned = jnp.sum(jnp.where(at == to, row, 0.0), axis=1, keepdims=True)
    running = jnp.sum(jnp.where(at <= to, turned, 0.0), axis=0, keepdims=True)
    col = jnp.sum(jnp.where(at == to, running, 0.0), axis=1, keepdims=True)
    matrix = jnp.where(at >= to, jnp.exp(jnp.minimum(col - running, 0.0)), 0.0)
    return col, running[:, block - 1 :], matrix


def retention_forward(where, decays, keyvals, query_gate):
    ny = len(keyvals)
    halves, nz, part, _ = query_gate.shape

    def kernel(where_ref, decay_ref, *refs):
        kv_refs, (qg_ref, y_ref, n_ref, r_ref, s_ref, q_ref, state) = refs[:ny], refs[ny:]
        j = pl.program_id(0)

        @pl.when(j == 0)
        def _():
            state[...] = jnp.zeros_like(state)

        slot = slot_of((j // ny) ^ where_ref[0])
        ky = (j % ny) ^ where_ref[1]
        flip = where_ref[3]
        col, last, matrix = decays_of(decay_ref[pl.ds(j, 1), :])
        key = choose(kv_refs, ky, slot, flip, slice(0, DK))
        value = choose(kv_refs, ky, slot, flip, slice(DK, DK + DV))

        @pl.when(ky == 0)
        def _():
            q = natural(qg_ref, slot, flip, slice(0, DK)).astype(bf16)
            state_bf = state[...].astype(bf16)
            s_ref[slot] = state_bf
            weights = (dot(q, key, NT) * matrix).astype(bf16)
            out = dot(weights, value, NN) + jnp.exp(col) * dot(q, state_bf, NN)
            normed, rstd = normalize(out)
            g = natural(qg_ref, slot, flip, slice(DK, DK + DV))
            mixed = (g * jax.nn.sigmoid(g) * normed).astype(bf16)
            for half in range(2):
                rows = slice(half * part, (half + 1) * part)
                to = (1 - flip) if half else flip
                y_ref[to, slot] = mixed[rows]
                n_ref[to, slot] = normed[rows]
                r_ref[to, slot] = rstd[rows]
                q_ref[to, slot] = q[rows]

        key_tail = (key.astype(f32) * jnp.exp(last - col)).astype(bf16)
        state[...] = jnp.exp(last) * state[...] + dot(key_tail, value, TN)

    return call(
        kernel,
        "retention_forward",
        [
            shape((halves, nz, part, DV), bf16),
            shape((halves, nz, part, DV), f32),
            shape((halves, nz, part, 1), f32),
            shape((nz, DK, DV), bf16),
            shape((halves, nz, part, DK), bf16),
        ],
        where,
        decays,
        *keyvals,
        query_gate,
        grid=(nz * ny,),
        scratch=[pltpu.VMEM((DK, DV), f32)],
    )


def retention_backward(where, decays, keyval, queries, grads, states, cosines, sines, gate):
    ny = len(queries)
    halves, nz, part, _ = keyval.shape
    key_scale = DK ** (-0.5)

    def kernel(where_ref, decay_ref, *refs):
        q_refs, d_refs, rest = refs[:ny], refs[ny : 2 * ny], refs[2 * ny :]
        kv_ref, s_ref, cos_ref, sin_ref, gate_ref, kv_out, qg_out, state = rest
        step = pl.program_id(0)
        j = nz * ny - 1 - step

        @pl.when(step == 0)
        def _():
            state[...] = jnp.zeros_like(state)
            qg_out[:, :, :, DK:] = gate_ref[...]

        slot = slot_of((j // ny) ^ where_ref[0])
        ky = (j % ny) ^ where_ref[1]
        flip = where_ref[3]
        col, last, matrix = decays_of(decay_ref[pl.ds(j, 1), :])
        q = choose(q_refs, ky, slot, flip)
        grad = choose(d_refs, ky, slot, flip)
        entry = jnp.exp(col)

        @pl.when(ky == 0)
        def _():
            key = natural(kv_ref, slot, flip, slice(0, DK))
            value = natural(kv_ref, slot, flip, slice(DK, DK + DV))
            cos = natural(cos_ref, slot, flip)
            sin = natural(sin_ref, slot, flip)
            tail = jnp.exp(last - col)
            state_bf = state[...].astype(bf16)
            weights = (dot(q, key, NT) * matrix).astype(bf16)
            scores = (dot(grad, value, NT) * matrix).astype(bf16)
            grad_q = dot(scores, key, NN) + entry * dot(grad, s_ref[slot], NT)
            grad_k = dot(scores, q, TN) + tail * dot(value, state_bf, NT)
            grad_v = dot(weights, grad, TN) + tail * dot(key, state_bf, NN)
            grad_q = rotate(grad_q, cos, -sin).astype(bf16)
            grad_k = (rotate(grad_k, cos, -sin) * key_scale).astype(bf16)
            grad_v = grad_v.astype(bf16)
            for half in range(2):
                rows = slice(half * part, (half + 1) * part)
                to = (1 - flip) if half else flip
                kv_out[to, slot, :, :DK] = grad_k[rows]
                kv_out[to, slot, :, DK:] = grad_v[rows]
                qg_out[to, slot, :, :DK] = grad_q[rows]

        query_entry = (q.astype(f32) * entry).astype(bf16)
        state[...] = jnp.exp(last) * state[...] + dot(query_entry, grad, TN)

    return call(
        kernel,
        "retention_backward",
        [shape((halves, nz, part, DK + DV), bf16)] * 2,
        where,
        decays,
        *queries,
        *grads,
        keyval,
        states,
        cosines,
        sines,
        gate,
        grid=(nz * ny,),
        scratch=[pltpu.VMEM((DK, DV), f32)],
    )


def shards(
    hidden_in,
    log_decay,
    out_grad,
    ln1_gain,
    ln1_bias,
    w_query,
    w_key,
    w_value,
    w_gate,
    w_out,
    ln2_gain,
    ln2_bias,
    mlp_gate,
    mlp_up,
    mlp_down,
):
    nz, ny = lax.axis_size("row"), lax.axis_size("col")
    nb, nh = lax.axis_size("batch"), lax.axis_size("head")
    block, width = hidden_in.shape[1:]
    rows = ln1_gain.shape[0]
    part = block // nh
    tokens = nz * block
    half, quarter = tokens // 2, tokens // 4
    group = nz * rows
    sizes = (nz, ny, nb)
    where = jnp.stack([lax.axis_index(name) for name in ("row", "col", "batch", "head")])
    (where,) = tie(where.astype(jnp.int32))

    def trade(pieces, k):
        return swap(pieces[k], "row", k) if k else pieces[k]

    def over_col(own):
        return [own] + [swap(own, "col", k) for k in range(1, ny)]

    def over_batch(values):
        return [swap(value, "batch", 1) for value in values]

    def mirror(values):
        return swap(values, "head", 1)

    def pairs(own, other):
        return [(part,) for both in zip(own, other) for part in both]

    def split(values):
        return values.reshape(nh, nz, part, -1)

    def add(values, got):
        return values + got.astype(f32)

    def sum_col(keep, send):
        for k in range(1, ny):
            keep = add(keep, swap(send[k * group : (k + 1) * group], "col", k))
        return keep.reshape(nz, rows, -1)

    def reduce_far(*terms):
        far = sum(matmul_t(values[half:], weight) for values, weight in terms).astype(bf16)
        return far[quarter:], far[:quarter]

    def reduce_near(*terms):
        near = sum(matmul_t(values[:half], weight) for values, weight in terms)
        return near[quarter:], near[:quarter]

    def step_one(packed, first):
        return swap(packed[2], "row", first)

    def step_two(packed, got, first):
        return swap(jnp.stack([packed[1], got[1]]), "row", 4 - first)

    def in_order(packed, got, last, first):
        pieces = {0: packed[0], first: got[0], 4 - first: last[0], 2: last[1]}
        return [pieces[k] for k in range(4)]

    gains = jnp.concatenate([ln1_gain, ln1_bias, ln2_gain, ln2_bias])[None]
    own_in, other_in = cut_halves(where, hidden_in[0], nh)
    two_in = swap(own_in, "row", 3)
    kv = pack_weights(where, (w_key, w_value), nz, rows, (gains, log_decay[0]))
    kv = [trade(kv, k) for k in range(nz)]
    qg = pack_weights(where, (w_query, w_gate), nz, rows, first=1)
    qg_got = step_one(qg, 1)
    kv, two_in, qg_got, late_grad = tie(kv, two_in, qg_got, out_grad[0])
    kv = jnp.stack(kv)
    kv_cols, kv_mate = over_col(kv), swap(kv, "batch", 1)
    one_in = swap(jnp.concatenate([own_in, two_in]), "row", 1)
    qg_last = step_two(qg, qg_got, 1)
    own_grad, other_grad = cut_halves(where, late_grad, nh)
    half_dim = DK // 2
    freqs = 10000.0 ** (-jnp.arange(half_dim, dtype=f32) / half_dim)
    block_at = (jnp.array(ORDER, jnp.int32) ^ where[0:1]) * ny + where[1:2]
    half_at = jnp.arange(nh, dtype=jnp.int32) ^ where[3:4]
    positions = (
        block_at[None, :, None] * block + half_at[:, None, None] * part + jnp.arange(part)
    )
    angles = positions.astype(f32)[..., None] * freqs
    cosines, sines = jnp.cos(angles), jnp.sin(angles)
    out = pack_weights(where, (w_out,), nz, rows, first=3)
    kv_cols, kv_mate, one_in, qg_last, own_grad, out, cosines, sines = tie(
        kv_cols, kv_mate, one_in, qg_last, own_grad, out, cosines, sines
    )
    kv_mates = [kv_mate] + over_batch(kv_cols[1:])
    mirror_in = mirror(jnp.concatenate([two_in, one_in]))
    qg_cols = over_col(jnp.stack(in_order(qg, qg_got, qg_last, 1)))
    two_grad = swap(own_grad, "row", 3)
    out_got = step_one(out, 3)
    feed = pack_weights(where, (mlp_gate, mlp_up, mlp_down), nz, rows)
    kv_mates, mirror_in, qg_cols, two_grad, out_got, feed = tie(
        kv_mates, mirror_in, qg_cols, two_grad, out_got, feed
    )
    kv_w, gains, decays = assemble(
        where, pairs(kv_cols, kv_mates), ny, nb, (DK + DV,), EXTRA, block
    )

    first_bf = place_rows(where, (own_in, two_in, one_in, other_in, mirror_in), gains)
    key_scale = DK ** (-0.5)
    projected = split(matmul(first_bf, kv_w))
    key_bf = (rotate(projected[..., :DK], cosines, sines) * key_scale).astype(bf16)
    keyval = jnp.concatenate([key_bf, projected[..., DK:].astype(bf16)], axis=-1)

    keyval, qg_cols, out_got, feed = tie(keyval, qg_cols, out_got, feed)
    keyvals = over_col(keyval)
    out_last = step_two(out, out_got, 3)
    feed_two = trade(feed, 2)
    (qg_w,) = assemble(where, pairs(qg_cols, over_batch(qg_cols)), ny, nb, (DK + DV,))
    projected = split(matmul(first_bf, qg_w))
    query_gate = jnp.concatenate(
        [rotate(projected[..., :DK], cosines, sines), projected[..., DK:]], axis=-1
    )
    keyvals, query_gate, out_last, feed_two = tie(keyvals, query_gate, out_last, feed_two)
    out_cols = over_col(jnp.stack(in_order(out, out_got, out_last, 3)))
    late_one, late_three = after((feed[1], feed[3]), keyvals)
    middle_col = late_three.shape[1] // 2
    feed_left = swap(late_three[:, :middle_col], "row", 3)
    feed_one = swap(late_one, "row", 1)
    mixed, normed, rstd, states, query = retention_forward(where, decays, keyvals, query_gate)
    mixed, out_cols, feed_one, feed_left = tie(mixed, out_cols, feed_one, feed_left)
    (out_w,) = assemble(where, pairs(out_cols, over_batch(out_cols)), ny, nb, (DV,))
    mixed_bf = mixed.reshape(tokens, DV)

    far = far_messages(where, mixed_bf, out_w, part)
    got = mirror(far[0])
    near = reduce_near((mixed_bf, out_w))
    late_three, late_grad, late_two = after((feed[3], own_grad, two_grad), far)
    feed_right = swap(late_three[:, middle_col:], "row", 3)
    one_grad = swap(jnp.concatenate([late_grad, late_two]), "row", 1)
    got, near, feed_right, one_grad = tie(got, near, feed_right, one_grad)
    feed_three = jnp.concatenate([feed_left, feed_right], axis=-1)
    got_far = mirror(after(far[1], got))
    got = swap(pass_message(where, near[0], got, part), "row", 1)
    feed = jnp.stack([feed[0], feed_one, feed_two, feed_three])
    units = feed.shape[-1] // 3
    feed_gates = over_col(feed[..., :units])[1:]
    feed_mate = swap(feed, "batch", 1)
    got, got_far, feed_gates, feed_mate, feed = tie(got, got_far, feed_gates, feed_mate, feed)
    keep, send = keep_message(where, near[1], got_far, got, part)
    got = swap(send, "row", 3)
    late_feed, late_two, late_gates = after((feed, two_grad, feed_gates), keep)
    feed_ups = over_col(late_feed[..., units : 2 * units])[1:]
    mirror_two = mirror(late_two)
    gate_mates = over_batch(late_gates)
    got, feed_ups, mirror_two, gate_mates = tie(got, feed_ups, mirror_two, gate_mates)
    middle, scaled_two, rstd_two, own = second_norm(where, own_in, keep, got, gains, part)
    two = swap(own, "row", 3)
    late_feed, late_one, late_ups = after((feed, one_grad, feed_ups), own)
    feed_downs = over_col(late_feed[..., 2 * units :])[1:]
    mirror_one = mirror(late_one)
    up_mates = over_batch(late_ups)
    two, feed_downs, mirror_one, up_mates, query = tie(
        two, feed_downs, mirror_one, up_mates, query
    )
    pair = jnp.concatenate([own, two])
    one, mirror_pair = swap(pair, "row", 1), mirror(pair)
    down_mates = over_batch(after(feed_downs, pair))
    one, mirror_pair, down_mates, query = tie(one, mirror_pair, down_mates, query)
    mirror_last = mirror(one)
    queries = over_col(query)
    parts = [(feed,), (feed_mate,)]
    for three in zip(feed_gates, feed_ups, feed_downs, gate_mates, up_mates, down_mates):
        parts += [three[:3], three[3:]]
    up_w, down_w = assemble(where, after(parts, one), ny, nb, (2 * units, units))
    down_bf = place_rows(
        where, after((own_grad, two_grad, one_grad, other_grad, mirror_two, mirror_one), one)
    )
    mirror_last, up_w, down_w, down_bf, queries = tie(mirror_last, up_w, down_w, down_bf, queries)
    second_bf = place_rows(where, (pair, one, mirror_pair, mirror_last))

    up = matmul(second_bf, up_w)
    up_gate, up_lin = up[:, :units], up[:, units:]
    gelu_cdf = 0.5 * (1.0 + lax.erf(up_gate * (0.5**0.5)))
    gelu_val = up_gate * gelu_cdf
    gelu_slope = gelu_cdf + up_gate * jnp.exp(-0.5 * up_gate * up_gate) * (2.0 * jnp.pi) ** -0.5
    hidden_bf = (gelu_val * up_lin).astype(bf16)
    grad_hidden = matmul(down_bf, down_w)
    grad_upgate = (grad_hidden * up_lin * gelu_slope).astype(bf16)
    grad_uplin = (grad_hidden * gelu_val).astype(bf16)
    grad_up = jnp.concatenate([grad_upgate, grad_uplin], axis=-1)
    far = far_messages(where, grad_up, up_w, part)
    got = mirror(far[0])
    near = reduce_near((grad_up, up_w))
    lefts, rights = (second_bf, down_bf), (grad_up, hidden_bf)
    feed_far = weight_grads(where, lefts, rights, sizes)
    got, near, feed_far, hidden_bf = tie(got, near, feed_far, hidden_bf)
    got_far = mirror(after(far[1], got))
    got = swap(pass_message(where, near[0], got, part), "row", 1)
    feed_got = swap(feed_far, "batch", 1)
    feed_keeps, feed_sends = weight_grads(where, lefts, rights, sizes, (units,) * 3, feed_got)
    result_far = reduce_far((hidden_bf, down_w))
    got, got_far, feed_sends, result_far, hidden_bf = tie(
        got, got_far, feed_sends, result_far, hidden_bf
    )
    keep, send = keep_message(where, near[1], got_far, got, part)
    got = swap(send, "row", 3)
    result_got = mirror(result_far[0])
    result_near = reduce_near((hidden_bf, down_w))
    sums = [sum_col(feed_keeps[0], feed_sends[0])]
    got, result_got, result_near, sums, feed_sends = tie(
        got, result_got, result_near, sums, feed_sends
    )
    grad_two, grad_middle, own = second_norm_back(
        where, own_grad, keep, got, gains, scaled_two, rstd_two, part
    )
    own, feed_sends, result_got = tie(own, feed_sends, result_got)
    two = swap(own, "row", 3)
    sums.append(sum_col(feed_keeps[1], feed_sends[1]))
    result_got_far = mirror(after(result_far[1], own))
    result_got = swap(add(result_near[0], result_got).astype(bf16), "row", 1)
    two, sums, feed_sends, result_got_far, result_got = tie(
        two, sums, feed_sends, result_got_far, result_got
    )
    pair = jnp.concatenate([own, two])
    one, mirror_pair = swap(pair, "row", 1), mirror(pair)
    down_sum = sum_col(feed_keeps[2], feed_sends[2])
    wide_grads = cut_heads(where, sums)
    result_keep = add(add(result_near[1], result_got_far), result_got)
    result_send = result_keep[part:].astype(bf16)
    one, mirror_pair, down_sum, wide_grads, result_send = tie(
        one, mirror_pair, down_sum, wide_grads, result_send
    )
    mirror_last = mirror(one)
    wide_two, wide_one = trade(wide_grads, 2), trade(wide_grads, 1)
    down_grads = cut_heads(where, (down_sum,))
    mirror_last, wide_two, wide_one, down_grads = tie(mirror_last, wide_two, wide_one, down_grads)
    attn_bf = place_rows(where, (pair, one, mirror_pair, mirror_last))

    grp_norm, grp_rstd = normed.reshape(tokens, DV), rstd.reshape(tokens, 1)
    gate = query_gate.reshape(tokens, -1)[:, DK:]
    gate_sig = jax.nn.sigmoid(gate)
    gate_act = gate * gate_sig
    grad_mixed = matmul(attn_bf, out_w)
    grad_gate = (grad_mixed * grp_norm * (gate_sig * (1.0 + gate * (1.0 - gate_sig)))).astype(bf16)
    ret_bf = norm_back(grad_mixed * gate_act, grp_norm, grp_rstd).astype(bf16)
    ret_bf, wide_grads, down_grads, late_gate, late_mixed = tie(
        split(ret_bf), wide_grads, down_grads, grad_gate, mixed_bf
    )
    ret_all = over_col(ret_bf)
    wide_three, down_one = trade(wide_grads, 3), trade(down_grads, 1)
    lefts, rights = (first_bf, attn_bf), (late_gate, late_mixed)
    both_got = swap(weight_grads(where, lefts, rights, sizes), "batch", 1)
    both_keeps, both_sends = weight_grads(where, lefts, rights, sizes, (DV, DV), both_got)
    ret_all, wide_three, down_one, both_sends = tie(ret_all, wide_three, down_one, both_sends)
    grad_kv, grad_qg = retention_backward(
        where, decays, keyval, queries, ret_all, states, cosines, sines, split(grad_gate)
    )
    grad_kv, grad_qg = grad_kv.reshape(tokens, -1), grad_qg.reshape(tokens, -1)
    terms = ((grad_kv, kv_w), (grad_qg, qg_w))
    far = reduce_far(*terms)
    got = mirror(far[0])
    late_kv, late_qg, late_send, late_down = after((grad_kv, grad_qg, both_sends, down_grads), far)
    kvq = ((first_bf, first_bf), (late_kv, (late_qg, 0, DK)))
    kvq_got = swap(weight_grads(where, *kvq, sizes), "batch", 1)
    down_two, down_three = trade(late_down, 2), trade(late_down, 3)
    out_sum = sum_col(both_keeps[1], late_send[1])
    near = reduce_near(*terms)
    got, near, down_two, down_three, kvq_got, out_sum, both_sends, result_send = tie(
        got, near, down_two, down_three, kvq_got, out_sum, both_sends, result_send
    )
    got_far = mirror(after(far[1], got))
    got = swap(add(near[0], got).astype(bf16), "row", 1)
    gate_sum = sum_col(both_keeps[0], both_sends[0])
    result_got = swap(result_send, "row", 3)
    kvq_keeps, kvq_sends = weight_grads(where, *kvq, sizes, (DV, 2 * DK), kvq_got)
    wide_pieces = (wide_grads[0], wide_one, wide_two, wide_three)
    grad_gates, grad_ups = unpack_grads(where, wide_pieces, ((units, False), (units, False)))
    got, got_far, gate_sum, result_got, kvq_sends, grad_gates, grad_ups = tie(
        got, got_far, gate_sum, result_got, kvq_sends, grad_gates, grad_ups
    )
    keep = add(add(near[1], got_far), got)
    got = swap(keep[part:].astype(bf16), "row", 3)
    result = (middle + add(result_keep[:part], result_got)).astype(bf16)
    result_other = mirror(result)
    kvq_first = sum_col(kvq_keeps[0], kvq_sends[0])
    both_pieces = cut_heads(where, (gate_sum, out_sum))
    down_pieces = (down_grads[0], down_one, down_two, down_three)
    (grad_downs,) = unpack_grads(where, down_pieces, ((units, True),))
    got, result_other, kvq_first, kvq_sends, both_pieces, grad_downs = tie(
        got, result_other, kvq_first, kvq_sends, both_pieces, grad_downs
    )
    both_pieces = [trade(both_pieces, k) for k in range(nz)]
    kvq_second = sum_col(kvq_keeps[1], kvq_sends[1])
    grad_one = add(keep[:part], got)
    scaled_own, rstd_own = normalize(own_in.astype(f32))
    grad_in = grad_middle + norm_back(grad_one * gains[0:1], scaled_own, rstd_own)
    grad_in_other = mirror(grad_in)
    kvq_pieces = cut_heads(where, (kvq_first, kvq_second))
    both_pieces, kvq_pieces, grad_in_other, grad_one = tie(
        both_pieces, kvq_pieces, grad_in_other, grad_one
    )
    kvq_pieces = [trade(kvq_pieces, k) for k in range(nz)]
    norm_sums = jnp.stack(
        [
            jnp.sum(grad_one * scaled_own, axis=0),
            jnp.sum(grad_one, axis=0),
            jnp.sum(grad_two * scaled_two, axis=0),
            jnp.sum(grad_two, axis=0),
        ]
    )
    norm_sums = after(norm_sums, kvq_pieces[1:3])
    norm_sums = norm_sums + mirror(norm_sums)
    norm_sums = norm_sums.reshape(4, nz, ny, nb, rows)

    def sum_over(values, name, axis):
        me = lax.axis_index(name)
        summed = pick(values, me, axis)
        for k in range(1, lax.axis_size(name)):
            summed = summed + swap(pick(values, me ^ k, axis), name, k)
        return summed

    for name, axis in (("batch", 3), ("col", 2), ("row", 1)):
        norm_sums = sum_over(norm_sums, name, axis)
    grad_g, grad_outs = unpack_grads(where, both_pieces, ((DV, False), (DV, True)))
    grad_k, grad_v, grad_q = unpack_grads(
        where, kvq_pieces, ((DK, False), (DV, False), (DK, False))
    )

    def join(own, other):
        return join_halves(where, own, other).reshape(1, block, width)

    return (
        join(result, result_other),
        join(grad_in, grad_in_other),
        norm_sums[0],
        norm_sums[1],
        grad_q,
        grad_k,
        grad_v,
        grad_g,
        grad_outs,
        norm_sums[2],
        norm_sums[3],
        grad_gates,
        grad_ups,
        grad_downs,
    )


def solution(mesh):
    seq = ("row", "col")
    tokens = P("batch", seq, None)
    params = P((*seq, "batch"))
    by_rows = P((*seq, "batch"), "head")
    by_cols = P("head", (*seq, "batch"))

    def run(*arrays):
        rows = arrays[1].shape[1] // mesh.shape["head"]
        sizes = (rows, mesh.shape["seq"] // rows, mesh.shape["batch"], mesh.shape["head"])
        order = [mesh.axis_names.index(n) for n in ("seq", "batch", "head")]
        fine = Mesh(
            mesh.devices.transpose(order).reshape(sizes), ("row", "col", "batch", "head")
        )
        weights = (by_rows, by_rows, by_rows, by_rows, by_cols)
        feeds = (by_rows, by_rows, by_cols)
        return jax.shard_map(
            shards,
            mesh=fine,
            in_specs=(
                tokens,
                P("batch", "head", seq),
                tokens,
                params,
                params,
                *weights,
                params,
                params,
                *feeds,
            ),
            out_specs=(tokens, tokens, params, params, *weights, params, params, *feeds),
            check_vma=False,
        )(*arrays)

    return run
```

```python
import jax
import jax.numpy as jnp
from jax import lax
from jax.experimental import pallas as pl
from jax.experimental.pallas import tpu as pltpu
from jax.sharding import Mesh
from jax.sharding import PartitionSpec as P

DK = 256
DV = 512

epsilon = 1e-05
f32 = jnp.float32
bf16 = jnp.bfloat16
VMEM_LIMIT = 12 * 1024 * 1024

ORDER = (0, 3, 1, 2)


def swap(values, axis, k):
    count = lax.axis_size(axis)
    return lax.ppermute(values, axis, [(i, i ^ k) for i in range(count)])


def pick(values, index, axis):
    return lax.dynamic_index_in_dim(values, index, axis, keepdims=False)


def tie(*values):
    return lax.optimization_barrier(values)


def after(values, *others):
    return tie(values, others)[0]


def matmul(values, weight):
    return jnp.dot(values, weight, preferred_element_type=f32)


def matmul_t(values, weight):
    return lax.dot_general(values, weight, (((1,), (1,)), ((), ())), preferred_element_type=f32)


def outer_sum(values, other):
    return lax.dot_general(values, other, (((0,), (0,)), ((), ())), preferred_element_type=f32)


def normalize(values):
    center = values - jnp.mean(values, axis=-1, keepdims=True)
    rstd = lax.rsqrt(jnp.mean(center * center, axis=-1, keepdims=True) + epsilon)
    return center * rstd, rstd


def norm_back(scaled_grad, scaled, rstd):
    return rstd * (
        scaled_grad
        - jnp.mean(scaled_grad, axis=-1, keepdims=True)
        - scaled * jnp.mean(scaled_grad * scaled, axis=-1, keepdims=True)
    )


def rotate(values, cosines, sines):
    half_dim = values.shape[-1] // 2
    first_half = values[..., :half_dim]
    second_half = values[..., half_dim:]
    return jnp.concatenate(
        [first_half * cosines - second_half * sines, first_half * sines + second_half * cosines],
        axis=-1,
    )


SMEM = pl.BlockSpec(memory_space=pltpu.SMEM)
WHOLE = pl.BlockSpec(memory_space=pltpu.VMEM)
PARAMS = pltpu.CompilerParams(vmem_limit_bytes=VMEM_LIMIT)


def call(kernel, name, shapes, *operands, grid=None, scratch=()):
    many = isinstance(shapes, list)
    return pl.pallas_call(
        kernel,
        grid=() if grid is None else grid,
        out_shape=shapes,
        in_specs=[SMEM] + [WHOLE] * (len(operands) - 1),
        out_specs=[WHOLE] * len(shapes) if many else WHOLE,
        scratch_shapes=list(scratch),
        compiler_params=PARAMS,
        name=name,
    )(*operands)


def shape(dims, dtype):
    return jax.ShapeDtypeStruct(tuple(dims), dtype)


def cut_halves(where, values, heads):
    block, width = values.shape
    part = block // heads

    def kernel(where_ref, ref, own, other):
        for out, half in ((own, where_ref[3]), (other, 1 - where_ref[3])):
            out[...] = ref[pl.ds(pl.multiple_of(half * part, part), part), :]

    return call(kernel, "cut_halves", [shape((part, width), values.dtype)] * 2, where, values)


def join_halves(where, own, other):
    part, width = own.shape

    def kernel(where_ref, own_ref, other_ref, out):
        for ref, half in ((own_ref, where_ref[3]), (other_ref, 1 - where_ref[3])):
            out[pl.ds(pl.multiple_of(half * part, part), part), :] = ref[...]

    return call(kernel, "join_halves", shape((2 * part, width), own.dtype), where, own, other)


def cut_heads(where, totals, first=0):
    nz, rows, _ = totals[0].shape
    width = sum(total.shape[2] for total in totals)

    def kernel(where_ref, *refs):
        ins, outs = refs[: len(totals)], refs[len(totals) :]
        targets = [outs[k] for k in range(nz)] if not first else steps(outs, first)
        for k in range(nz):
            at = 0
            for ref in ins:
                cols = ref.shape[2]
                targets[k][:, at : at + cols] = ref[where_ref[0] ^ k].astype(bf16)
                at += cols

    shapes = [shape((rows, width), bf16)] * nz
    if first:
        shapes = shapes[:2] + [shape((2, rows, width), bf16)]
    return call(kernel, "cut_heads", shapes, where, *totals)


def steps(refs, first):
    stay, second, firsts = refs
    return {0: stay, 4 - first: second, first: firsts.at[0], 2: firsts.at[1]}


def pack_weights(where, weights, nz, rows, extras=None, first=0):
    widths = [w.size // rows // nz for w in weights]
    total = sum(widths)
    count = 0
    if extras:
        gains, decays = extras
        block = decays.shape[1]
        extras = (jnp.pad(gains, ((0, 0), (0, total - gains.shape[1]))), decays)
        count = EXTRA

    def kernel(where_ref, *refs):
        ins, rest = refs[: len(weights)], refs[len(weights) :]
        outs = steps(rest, first) if first else rest[-nz:]
        for k in range(nz):
            target = where_ref[0] ^ k
            at = 0
            for ref, width in zip(ins, widths):
                start = pl.multiple_of(target * width, width)
                if ref.shape[0] == rows:
                    piece = ref[:, pl.ds(start, width)]
                else:
                    piece = ref[pl.ds(start, width), :].astype(f32).T.astype(bf16)
                outs[k][:rows, at : at + width] = piece
                at += width
            if extras:
                line = lax.broadcasted_iota(jnp.int32, (EXTRA, 1), 0)
                gain_rows = jnp.where(line == 0, rest[0][...].astype(f32), 0.0)
                parts = gain_rows[:, :block]
                left = rest[1][pl.ds(target, 1), :]
                for number in range(1, 4):
                    part = left.astype(bf16).astype(f32)
                    parts = jnp.where(line == number, part, parts)
                    left = left - part
                outs[k][rows:, :] = gain_rows.astype(bf16)
                outs[k][rows:, :block] = parts.astype(bf16)

    shapes = [shape((rows + count, total), bf16)] * nz
    if first:
        shapes = shapes[:2] + [shape((2, rows, total), bf16)]
    return call(kernel, "pack_weights", shapes, where, *weights, *(extras or ()))


def unpack_grads(where, pieces, outs):
    nz = len(pieces)
    rows = pieces[0].shape[0]

    def kernel(where_ref, *refs):
        ins, results = refs[:nz], refs[nz:]
        for k in range(nz):
            target = where_ref[0] ^ k
            at = 0
            for ref, (width, turned) in zip(results, outs):
                to = pl.ds(pl.multiple_of(target * width, width), width)
                piece = ins[k][:, at : at + width].astype(f32)
                if turned:
                    ref[to, :] = piece.T
                else:
                    ref[:, to] = piece
                at += width

    shapes = [shape((nz * w, rows) if turned else (rows, nz * w), f32) for w, turned in outs]
    return call(kernel, "unpack_grads", shapes, where, *pieces)


EXTRA = 16


def assemble(where, parts, ny, nb, widths, extra=0, block=0):
    nz, rows, _ = parts[0][0].shape
    rows -= extra
    count = nz * ny * nb
    total = sum(widths)
    sizes = [len(part) for part in parts]
    aligned = rows % 128 == 0

    def kernel(where_ref, *refs):
        ins, outs = refs[: sum(sizes)], refs[sum(sizes) :]
        for ky in range(ny):
            for kb in range(nb):
                pieces, ins = ins[: sizes[ky * nb + kb]], ins[sizes[ky * nb + kb] :]
                for kz in range(nz):
                    place = (where_ref[0] ^ kz) * ny + (where_ref[1] ^ ky)
                    device = place * nb + (where_ref[2] ^ kb)
                    at = pl.multiple_of(device * rows, rows)
                    column = 0
                    for piece in pieces:
                        cols = piece.shape[-1]
                        start = 0
                        for out, width in zip(outs, widths):
                            low, high = max(start, column), min(start + width, column + cols)
                            if low < high:
                                out[pl.ds(at, rows), low - start : high - start] = piece[
                                    kz, :rows, low - column : high - column
                                ]
                            start += width
                        column += cols
                    if extra:
                        tail = pieces[0][kz, rows:, :].astype(f32)
                        if aligned:
                            for number in range(4):
                                gain = tail[:1, number * rows : (number + 1) * rows]
                                outs[-2][number : number + 1, pl.ds(at, rows)] = gain
                        else:
                            outs[-2][pl.ds(device, 1), :] = tail[:1]
                        if kb == 0:
                            decay = (tail[1:2] + tail[2:3]) + tail[3:4]
                            outs[-1][pl.ds(place, 1), :] = decay[:, :block]

    shapes = [shape((count * rows, width), bf16) for width in widths]
    if extra:
        shapes.append(shape((4, count * rows) if aligned else (count, total), f32))
        shapes.append(shape((nz * ny, block), f32))
    outs = list(call(kernel, "assemble", shapes, where, *[p for part in parts for p in part]))
    if extra and not aligned:
        gains = outs[-2][:, : 4 * rows].reshape(count, 4, rows)
        outs[-2] = gains.transpose(1, 0, 2).reshape(4, count * rows)
    return outs


def row_groups(where, left, sizes):
    nz, ny, nb = sizes
    groups = left.reshape(left.shape[0], nz, ny, nb, -1)
    groups = jnp.take(groups, jnp.arange(ny) ^ where[1], axis=2)
    groups = jnp.take(groups, jnp.arange(nb) ^ where[2], axis=3)
    return groups.transpose(0, 3, 2, 1, 4).reshape(left.shape)


def weight_grads(where, lefts, rights, sizes, widths=None, got=None):
    nz, ny, nb = sizes
    width = lefts[0].shape[1]
    rows = width // (nz * ny * nb)
    group = nz * rows
    rights = [right if isinstance(right, tuple) else (right, 0, right.shape[1]) for right in rights]
    ranges = [right[1:] for right in rights]
    rights = [right[0] for right in rights]
    total = sum(high - low for low, high in ranges)
    kb = 1 if got is None else 0
    aligned = rows % 128 == 0
    if not aligned:
        lefts = [row_groups(where, left, sizes) for left in lefts]

    def columns(where_ref, left, step):
        if not aligned:
            return left[:, pl.ds(pl.multiple_of((kb * ny + step) * group, group), group)]
        tiles = []
        for z in range(nz):
            start = ((z * ny + (where_ref[1] ^ step)) * nb + (where_ref[2] ^ kb)) * rows
            tiles.append(left[:, pl.ds(pl.multiple_of(start, rows), rows)])
        return jnp.concatenate(tiles, axis=1)

    def kernel(where_ref, *refs):
        ins, rest = refs[: len(lefts)], refs[len(lefts) :]
        others, rest = rest[: len(rights)], rest[len(rights) :]
        step = pl.program_id(0)
        values = []
        for left, right, (low, high) in zip(ins, others, ranges):
            values.append(dot(columns(where_ref, left, step), right[:, low:high], TN))
        if got is None:
            at = 0
            for value in values:
                rest[0][:, at : at + value.shape[1]] = value.astype(bf16)
                at += value.shape[1]
            return
        value = jnp.concatenate(values, axis=1) + rest[0][...].astype(f32)
        keeps, sends = rest[1 : 1 + len(widths)], rest[1 + len(widths) :]
        at = 0
        for keep, send, cols in zip(keeps, sends, widths):
            part = value[:, at : at + cols]
            send[...] = part.astype(bf16)

            @pl.when(step == 0)
            def _():
                keep[...] = part

            at += cols

    moving = lambda cols: pl.BlockSpec((group, cols), lambda i: (i, 0))
    if got is None:
        specs = moving(total)
        shapes = shape((ny * group, total), bf16)
    else:
        specs = [pl.BlockSpec((group, cols), lambda i: (0, 0)) for cols in widths]
        specs += [moving(cols) for cols in widths]
        shapes = [shape((group, cols), f32) for cols in widths]
        shapes += [shape((ny * group, cols), bf16) for cols in widths]
    outs = pl.pallas_call(
        kernel,
        grid=(ny,),
        out_shape=shapes,
        in_specs=[SMEM]
        + [WHOLE] * (len(lefts) + len(rights))
        + ([] if got is None else [moving(total)]),
        out_specs=specs,
        compiler_params=PARAMS,
        name="weight_grads",
    )(where, *lefts, *rights, *(() if got is None else (got,)))
    return outs if got is None else (outs[: len(widths)], outs[len(widths) :])


def place_rows(where, pieces, gains=None):
    width = pieces[0].shape[-1]
    tokens = sum(piece.shape[0] for piece in pieces)

    def kernel(where_ref, *refs):
        ins, full = refs[: len(pieces)], refs[-1]
        at = 0
        for ref in ins:
            values = ref[...]
            if gains is not None:
                values, _ = normalize(values.astype(f32))
                params = refs[-2]
                values = (values * params[0:1, :] + params[1:2, :]).astype(bf16)
            full[at : at + ref.shape[0], :] = values
            at += ref.shape[0]

    more = () if gains is None else (gains,)
    return call(kernel, "place_rows", shape((tokens, width), bf16), where, *pieces, *more)


LOW = 16


def write_message(ref, values, part, columns=slice(None)):
    count = values.shape[0]
    high = values.astype(bf16)
    ref[:count, columns] = high
    low = values - high.astype(f32)
    line = lax.broadcasted_iota(jnp.int32, (LOW, 1), 0)
    rows = jnp.zeros((LOW, values.shape[1]), f32)
    for number in range(count // part):
        rows = jnp.where(line == number, low[number * part : number * part + 1], rows)
    ref[count:, columns] = rows.astype(bf16)


def read_message(ref, part):
    count = ref.shape[0] - LOW
    values = ref[:count, :].astype(f32)
    low = ref[count:, :].astype(f32)
    line = lax.broadcasted_iota(jnp.int32, (count, 1), 0)
    for number in range(count // part):
        values = values + jnp.where(line == number * part, low[number : number + 1], 0.0)
    return values


def far_messages(where, values, weight, part):
    half = values.shape[0] // 2
    quarter = half // 2
    width, depth = weight.shape
    step = width // 4

    def kernel(where_ref, value_ref, weight_ref, second, first):
        out = dot(value_ref[half:, :], weight_ref[...], NT)
        write_message(second, out[quarter:], part)
        write_message(first, out[:quarter], part)

    return pl.pallas_call(
        kernel,
        grid=(4,),
        out_shape=[shape((quarter + LOW, width), bf16)] * 2,
        in_specs=[SMEM, WHOLE, pl.BlockSpec((step, depth), lambda i: (i, 0))],
        out_specs=[pl.BlockSpec((quarter + LOW, step), lambda i: (0, i))] * 2,
        compiler_params=PARAMS,
        name="far_messages",
    )(where, values, weight)


def pass_message(where, near, got, part):
    def kernel(where_ref, near_ref, got_ref, out):
        write_message(out, near_ref[...] + read_message(got_ref, part), part)

    return call(kernel, "pass_message", shape(got.shape, bf16), where, near, got)


def keep_message(where, near, got_far, got, part):
    width = near.shape[1]

    def kernel(where_ref, near_ref, far_ref, got_ref, keep, out):
        total = near_ref[...] + read_message(far_ref, part) + read_message(got_ref, part)
        keep[...] = total[:part]
        write_message(out, total[part:], part)

    shapes = [shape((part, width), f32), shape((part + LOW, width), bf16)]
    return call(kernel, "keep_message", shapes, where, near, got_far, got)


def second_norm(where, inputs, keep, got, gains, part):
    width = keep.shape[1]

    def kernel(where_ref, in_ref, keep_ref, got_ref, gain_ref, middle, scaled, rstd, out):
        total = in_ref[...].astype(f32) + (keep_ref[...] + read_message(got_ref, part))
        middle[...] = total
        normed, factor = normalize(total)
        scaled[...] = normed
        rstd[...] = factor
        out[...] = (normed * gain_ref[2:3, :] + gain_ref[3:4, :]).astype(bf16)

    full = shape((part, width), f32)
    shapes = [full, full, shape((part, 1), f32), shape((part, width), bf16)]
    return call(kernel, "second_norm", shapes, where, inputs, keep, got, gains)


def second_norm_back(where, grad, keep, got, gains, scaled, rstd, part):
    width = keep.shape[1]

    def kernel(where_ref, g_ref, keep_ref, got_ref, gain_ref, scaled_ref, rstd_ref, two, mid, out):
        total = keep_ref[...] + read_message(got_ref, part)
        two[...] = total
        back = norm_back(total * gain_ref[2:3, :], scaled_ref[...], rstd_ref[...])
        back = g_ref[...].astype(f32) + back
        mid[...] = back
        out[...] = back.astype(bf16)

    full = shape((part, width), f32)
    shapes = [full, full, shape((part, width), bf16)]
    operands = (where, grad, keep, got, gains, scaled, rstd)
    return call(kernel, "second_norm_back", shapes, *operands)


def slot_of(k):
    return (((k & 1) ^ (k >> 1)) << 1) | (k >> 1)


def natural(ref, slot, flip, columns=slice(None)):
    first = ref[flip, slot, :, columns]
    second = ref[1 - flip, slot, :, columns]
    return jnp.concatenate([first, second], axis=0)


def choose(refs, ky, slot, flip, columns=slice(None)):
    values = natural(refs[0], slot, flip, columns)
    for k in range(1, len(refs)):
        values = jnp.where(ky == k, natural(refs[k], slot, flip, columns), values)
    return values


def dot(left, right, dims):
    return lax.dot_general(left, right, (dims, ((), ())), preferred_element_type=f32)


NN, NT, TN = ((1,), (0,)), ((1,), (1,)), ((0,), (0,))


def decays_of(row):
    block = row.shape[-1]
    at = lax.broadcasted_iota(jnp.int32, (block, block), 0)
    to = lax.broadcasted_iota(jnp.int32, (block, block), 1)
    turned = jnp.sum(jnp.where(at == to, row, 0.0), axis=1, keepdims=True)
    running = jnp.sum(jnp.where(at <= to, turned, 0.0), axis=0, keepdims=True)
    col = jnp.sum(jnp.where(at == to, running, 0.0), axis=1, keepdims=True)
    matrix = jnp.where(at >= to, jnp.exp(jnp.minimum(col - running, 0.0)), 0.0)
    return col, running[:, block - 1 :], matrix


def retention_forward(where, decays, keyvals, query_gate):
    ny = len(keyvals)
    halves, nz, part, _ = query_gate.shape

    def kernel(where_ref, decay_ref, *refs):
        kv_refs, (qg_ref, y_ref, n_ref, r_ref, s_ref, q_ref, state) = refs[:ny], refs[ny:]
        j = pl.program_id(0)

        @pl.when(j == 0)
        def _():
            state[...] = jnp.zeros_like(state)

        slot = slot_of((j // ny) ^ where_ref[0])
        ky = (j % ny) ^ where_ref[1]
        flip = where_ref[3]
        col, last, matrix = decays_of(decay_ref[pl.ds(j, 1), :])
        key = choose(kv_refs, ky, slot, flip, slice(0, DK))
        value = choose(kv_refs, ky, slot, flip, slice(DK, DK + DV))

        @pl.when(ky == 0)
        def _():
            q = natural(qg_ref, slot, flip, slice(0, DK)).astype(bf16)
            state_bf = state[...].astype(bf16)
            s_ref[slot] = state_bf
            weights = (dot(q, key, NT) * matrix).astype(bf16)
            out = dot(weights, value, NN) + jnp.exp(col) * dot(q, state_bf, NN)
            normed, rstd = normalize(out)
            g = natural(qg_ref, slot, flip, slice(DK, DK + DV))
            mixed = (g * jax.nn.sigmoid(g) * normed).astype(bf16)
            for half in range(2):
                rows = slice(half * part, (half + 1) * part)
                to = (1 - flip) if half else flip
                y_ref[to, slot] = mixed[rows]
                n_ref[to, slot] = normed[rows]
                r_ref[to, slot] = rstd[rows]
                q_ref[to, slot] = q[rows]

        key_tail = (key.astype(f32) * jnp.exp(last - col)).astype(bf16)
        state[...] = jnp.exp(last) * state[...] + dot(key_tail, value, TN)

    return call(
        kernel,
        "retention_forward",
        [
            shape((halves, nz, part, DV), bf16),
            shape((halves, nz, part, DV), f32),
            shape((halves, nz, part, 1), f32),
            shape((nz, DK, DV), bf16),
            shape((halves, nz, part, DK), bf16),
        ],
        where,
        decays,
        *keyvals,
        query_gate,
        grid=(nz * ny,),
        scratch=[pltpu.VMEM((DK, DV), f32)],
    )


def retention_backward(where, decays, keyval, queries, grads, states, cosines, sines, gate):
    ny = len(queries)
    halves, nz, part, _ = keyval.shape
    key_scale = DK ** (-0.5)

    def kernel(where_ref, decay_ref, *refs):
        q_refs, d_refs, rest = refs[:ny], refs[ny : 2 * ny], refs[2 * ny :]
        kv_ref, s_ref, cos_ref, sin_ref, gate_ref, kv_out, qg_out, state = rest
        step = pl.program_id(0)
        j = nz * ny - 1 - step

        @pl.when(step == 0)
        def _():
            state[...] = jnp.zeros_like(state)
            qg_out[:, :, :, DK:] = gate_ref[...]

        slot = slot_of((j // ny) ^ where_ref[0])
        ky = (j % ny) ^ where_ref[1]
        flip = where_ref[3]
        col, last, matrix = decays_of(decay_ref[pl.ds(j, 1), :])
        q = choose(q_refs, ky, slot, flip)
        grad = choose(d_refs, ky, slot, flip)
        entry = jnp.exp(col)

        @pl.when(ky == 0)
        def _():
            key = natural(kv_ref, slot, flip, slice(0, DK))
            value = natural(kv_ref, slot, flip, slice(DK, DK + DV))
            cos = natural(cos_ref, slot, flip)
            sin = natural(sin_ref, slot, flip)
            tail = jnp.exp(last - col)
            state_bf = state[...].astype(bf16)
            weights = (dot(q, key, NT) * matrix).astype(bf16)
            scores = (dot(grad, value, NT) * matrix).astype(bf16)
            grad_q = dot(scores, key, NN) + entry * dot(grad, s_ref[slot], NT)
            grad_k = dot(scores, q, TN) + tail * dot(value, state_bf, NT)
            grad_v = dot(weights, grad, TN) + tail * dot(key, state_bf, NN)
            grad_q = rotate(grad_q, cos, -sin).astype(bf16)
            grad_k = (rotate(grad_k, cos, -sin) * key_scale).astype(bf16)
            grad_v = grad_v.astype(bf16)
            for half in range(2):
                rows = slice(half * part, (half + 1) * part)
                to = (1 - flip) if half else flip
                kv_out[to, slot, :, :DK] = grad_k[rows]
                kv_out[to, slot, :, DK:] = grad_v[rows]
                qg_out[to, slot, :, :DK] = grad_q[rows]

        query_entry = (q.astype(f32) * entry).astype(bf16)
        state[...] = jnp.exp(last) * state[...] + dot(query_entry, grad, TN)

    return call(
        kernel,
        "retention_backward",
        [shape((halves, nz, part, DK + DV), bf16)] * 2,
        where,
        decays,
        *queries,
        *grads,
        keyval,
        states,
        cosines,
        sines,
        gate,
        grid=(nz * ny,),
        scratch=[pltpu.VMEM((DK, DV), f32)],
    )


def shards(
    hidden_in,
    log_decay,
    out_grad,
    ln1_gain,
    ln1_bias,
    w_query,
    w_key,
    w_value,
    w_gate,
    w_out,
    ln2_gain,
    ln2_bias,
    mlp_gate,
    mlp_up,
    mlp_down,
):
    nz, ny = lax.axis_size("row"), lax.axis_size("col")
    nb, nh = lax.axis_size("batch"), lax.axis_size("head")
    block, width = hidden_in.shape[1:]
    rows = ln1_gain.shape[0]
    part = block // nh
    tokens = nz * block
    half, quarter = tokens // 2, tokens // 4
    group = nz * rows
    sizes = (nz, ny, nb)
    where = jnp.stack([lax.axis_index(name) for name in ("row", "col", "batch", "head")])
    (where,) = tie(where.astype(jnp.int32))

    def trade(pieces, k):
        return swap(pieces[k], "row", k) if k else pieces[k]

    def over_col(own):
        return [own] + [swap(own, "col", k) for k in range(1, ny)]

    def over_batch(values):
        return [swap(value, "batch", 1) for value in values]

    def mirror(values):
        return swap(values, "head", 1)

    def pairs(own, other):
        return [(part,) for both in zip(own, other) for part in both]

    def split(values):
        return values.reshape(nh, nz, part, -1)

    def add(values, got):
        return values + got.astype(f32)

    def sum_col(keep, send):
        for k in range(1, ny):
            keep = add(keep, swap(send[k * group : (k + 1) * group], "col", k))
        return keep.reshape(nz, rows, -1)

    def reduce_far(*terms):
        far = sum(matmul_t(values[half:], weight) for values, weight in terms).astype(bf16)
        return far[quarter:], far[:quarter]

    def reduce_near(*terms):
        near = sum(matmul_t(values[:half], weight) for values, weight in terms)
        return near[quarter:], near[:quarter]

    def step_one(packed, first):
        return swap(packed[2], "row", first)

    def step_two(packed, got, first):
        return swap(jnp.stack([packed[1], got[1]]), "row", 4 - first)

    def in_order(packed, got, last, first):
        pieces = {0: packed[0], first: got[0], 4 - first: last[0], 2: last[1]}
        return [pieces[k] for k in range(4)]

    gains = jnp.concatenate([ln1_gain, ln1_bias, ln2_gain, ln2_bias])[None]
    own_in, other_in = cut_halves(where, hidden_in[0], nh)
    two_in = swap(own_in, "row", 3)
    kv = pack_weights(where, (w_key, w_value), nz, rows, (gains, log_decay[0]))
    kv = [trade(kv, k) for k in range(nz)]
    qg = pack_weights(where, (w_query, w_gate), nz, rows, first=1)
    qg_got = step_one(qg, 1)
    kv, two_in, qg_got, late_grad = tie(kv, two_in, qg_got, out_grad[0])
    kv = jnp.stack(kv)
    kv_cols, kv_mate = over_col(kv), swap(kv, "batch", 1)
    one_in = swap(jnp.concatenate([own_in, two_in]), "row", 1)
    qg_last = step_two(qg, qg_got, 1)
    own_grad, other_grad = cut_halves(where, late_grad, nh)
    half_dim = DK // 2
    freqs = 10000.0 ** (-jnp.arange(half_dim, dtype=f32) / half_dim)
    block_at = (jnp.array(ORDER, jnp.int32) ^ where[0:1]) * ny + where[1:2]
    half_at = jnp.arange(nh, dtype=jnp.int32) ^ where[3:4]
    positions = (
        block_at[None, :, None] * block + half_at[:, None, None] * part + jnp.arange(part)
    )
    angles = positions.astype(f32)[..., None] * freqs
    cosines, sines = jnp.cos(angles), jnp.sin(angles)
    out = pack_weights(where, (w_out,), nz, rows, first=3)
    kv_cols, kv_mate, one_in, qg_last, own_grad, out, cosines, sines = tie(
        kv_cols, kv_mate, one_in, qg_last, own_grad, out, cosines, sines
    )
    kv_mates = [kv_mate] + over_batch(kv_cols[1:])
    mirror_in = mirror(jnp.concatenate([two_in, one_in]))
    qg_cols = over_col(jnp.stack(in_order(qg, qg_got, qg_last, 1)))
    two_grad = swap(own_grad, "row", 3)
    out_got = step_one(out, 3)
    feed = pack_weights(where, (mlp_gate, mlp_up, mlp_down), nz, rows)
    kv_mates, mirror_in, qg_cols, two_grad, out_got, feed = tie(
        kv_mates, mirror_in, qg_cols, two_grad, out_got, feed
    )
    kv_w, gains, decays = assemble(
        where, pairs(kv_cols, kv_mates), ny, nb, (DK + DV,), EXTRA, block
    )

    first_bf = place_rows(where, (own_in, two_in, one_in, other_in, mirror_in), gains)
    key_scale = DK ** (-0.5)
    projected = split(matmul(first_bf, kv_w))
    key_bf = (rotate(projected[..., :DK], cosines, sines) * key_scale).astype(bf16)
    keyval = jnp.concatenate([key_bf, projected[..., DK:].astype(bf16)], axis=-1)

    keyval, qg_cols, out_got, feed = tie(keyval, qg_cols, out_got, feed)
    keyvals = over_col(keyval)
    out_last = step_two(out, out_got, 3)
    feed_two = trade(feed, 2)
    (qg_w,) = assemble(where, pairs(qg_cols, over_batch(qg_cols)), ny, nb, (DK + DV,))
    projected = split(matmul(first_bf, qg_w))
    query_gate = jnp.concatenate(
        [rotate(projected[..., :DK], cosines, sines), projected[..., DK:]], axis=-1
    )
    keyvals, query_gate, out_last, feed_two = tie(keyvals, query_gate, out_last, feed_two)
    out_cols = over_col(jnp.stack(in_order(out, out_got, out_last, 3)))
    late_grad, late_two, late_three = after((own_grad, two_grad, feed[3]), keyvals)
    middle_col = late_three.shape[1] // 2
    feed_left = swap(late_three[:, :middle_col], "row", 3)
    one_grad = swap(jnp.concatenate([late_grad, late_two]), "row", 1)
    mixed, normed, rstd, states, query = retention_forward(where, decays, keyvals, query_gate)
    mixed, out_cols, one_grad, feed_left = tie(mixed, out_cols, one_grad, feed_left)
    (out_w,) = assemble(where, pairs(out_cols, over_batch(out_cols)), ny, nb, (DV,))
    mixed_bf = mixed.reshape(tokens, DV)

    far = far_messages(where, mixed_bf, out_w, part)
    got = mirror(far[0])
    near = reduce_near((mixed_bf, out_w))
    late_feed = after(feed, far)
    feed_right = swap(late_feed[3][:, middle_col:], "row", 3)
    feed_one = trade(late_feed, 1)
    got, near, feed_right, feed_one = tie(got, near, feed_right, feed_one)
    feed_three = jnp.concatenate([feed_left, feed_right], axis=-1)
    got_far = mirror(after(far[1], got))
    got = swap(pass_message(where, near[0], got, part), "row", 1)
    feed = jnp.stack([feed[0], feed_one, feed_two, feed_three])
    units = feed.shape[-1] // 3
    feed_gates = over_col(feed[..., :units])[1:]
    feed_mate = swap(feed, "batch", 1)
    got, got_far, feed_gates, feed_mate, feed = tie(got, got_far, feed_gates, feed_mate, feed)
    keep, send = keep_message(where, near[1], got_far, got, part)
    got = swap(send, "row", 3)
    late_feed, late_two, late_gates = after((feed, two_grad, feed_gates), keep)
    feed_ups = over_col(late_feed[..., units : 2 * units])[1:]
    mirror_two = mirror(late_two)
    gate_mates = over_batch(late_gates)
    got, feed_ups, mirror_two, gate_mates = tie(got, feed_ups, mirror_two, gate_mates)
    middle, scaled_two, rstd_two, own = second_norm(where, own_in, keep, got, gains, part)
    two = swap(own, "row", 3)
    late_feed, late_one, late_ups = after((feed, one_grad, feed_ups), own)
    feed_downs = over_col(late_feed[..., 2 * units :])[1:]
    mirror_one = mirror(late_one)
    up_mates = over_batch(late_ups)
    two, feed_downs, mirror_one, up_mates, query = tie(
        two, feed_downs, mirror_one, up_mates, query
    )
    pair = jnp.concatenate([own, two])
    one, mirror_pair = swap(pair, "row", 1), mirror(pair)
    down_mates = over_batch(after(feed_downs, pair))
    one, mirror_pair, down_mates, query = tie(one, mirror_pair, down_mates, query)
    mirror_last = mirror(one)
    queries = over_col(query)
    parts = [(feed,), (feed_mate,)]
    for three in zip(feed_gates, feed_ups, feed_downs, gate_mates, up_mates, down_mates):
        parts += [three[:3], three[3:]]
    up_w, down_w = assemble(where, after(parts, one), ny, nb, (2 * units, units))
    down_bf = place_rows(
        where, after((own_grad, two_grad, one_grad, other_grad, mirror_two, mirror_one), one)
    )
    mirror_last, up_w, down_w, down_bf, queries = tie(mirror_last, up_w, down_w, down_bf, queries)
    second_bf = place_rows(where, (pair, one, mirror_pair, mirror_last))

    up = matmul(second_bf, up_w)
    up_gate, up_lin = up[:, :units], up[:, units:]
    gelu_cdf = 0.5 * (1.0 + lax.erf(up_gate * (0.5**0.5)))
    gelu_val = up_gate * gelu_cdf
    gelu_slope = gelu_cdf + up_gate * jnp.exp(-0.5 * up_gate * up_gate) * (2.0 * jnp.pi) ** -0.5
    hidden_bf = (gelu_val * up_lin).astype(bf16)
    grad_hidden = matmul(down_bf, down_w)
    grad_upgate = (grad_hidden * up_lin * gelu_slope).astype(bf16)
    grad_uplin = (grad_hidden * gelu_val).astype(bf16)
    grad_up = jnp.concatenate([grad_upgate, grad_uplin], axis=-1)
    far = far_messages(where, grad_up, up_w, part)
    got = mirror(far[0])
    near = reduce_near((grad_up, up_w))
    lefts, rights = (second_bf, down_bf), (grad_up, hidden_bf)
    feed_far = weight_grads(where, lefts, rights, sizes)
    got, near, feed_far, hidden_bf = tie(got, near, feed_far, hidden_bf)
    got_far = mirror(after(far[1], got))
    got = swap(pass_message(where, near[0], got, part), "row", 1)
    feed_got = swap(feed_far, "batch", 1)
    feed_keeps, feed_sends = weight_grads(where, lefts, rights, sizes, (units,) * 3, feed_got)
    result_far = reduce_far((hidden_bf, down_w))
    got, got_far, feed_sends, result_far, hidden_bf = tie(
        got, got_far, feed_sends, result_far, hidden_bf
    )
    keep, send = keep_message(where, near[1], got_far, got, part)
    got = swap(send, "row", 3)
    result_got = mirror(result_far[0])
    result_near = reduce_near((hidden_bf, down_w))
    sums = [sum_col(feed_keeps[0], feed_sends[0])]
    got, result_got, result_near, sums, feed_sends = tie(
        got, result_got, result_near, sums, feed_sends
    )
    grad_two, grad_middle, own = second_norm_back(
        where, own_grad, keep, got, gains, scaled_two, rstd_two, part
    )
    own, feed_sends, result_got = tie(own, feed_sends, result_got)
    two = swap(own, "row", 3)
    sums.append(sum_col(feed_keeps[1], feed_sends[1]))
    result_got_far = mirror(after(result_far[1], own))
    result_got = swap(add(result_near[0], result_got).astype(bf16), "row", 1)
    two, sums, feed_sends, result_got_far, result_got = tie(
        two, sums, feed_sends, result_got_far, result_got
    )
    pair = jnp.concatenate([own, two])
    one, mirror_pair = swap(pair, "row", 1), mirror(pair)
    down_sum = sum_col(feed_keeps[2], feed_sends[2])
    wide_grads = cut_heads(where, sums)
    result_keep = add(add(result_near[1], result_got_far), result_got)
    result_send = result_keep[part:].astype(bf16)
    one, mirror_pair, down_sum, wide_grads, result_send = tie(
        one, mirror_pair, down_sum, wide_grads, result_send
    )
    mirror_last = mirror(one)
    wide_two, wide_one = trade(wide_grads, 2), trade(wide_grads, 1)
    down_grads = cut_heads(where, (down_sum,))
    mirror_last, wide_two, wide_one, down_grads = tie(mirror_last, wide_two, wide_one, down_grads)
    attn_bf = place_rows(where, (pair, one, mirror_pair, mirror_last))

    grp_norm, grp_rstd = normed.reshape(tokens, DV), rstd.reshape(tokens, 1)
    gate = query_gate.reshape(tokens, -1)[:, DK:]
    gate_sig = jax.nn.sigmoid(gate)
    gate_act = gate * gate_sig
    grad_mixed = matmul(attn_bf, out_w)
    grad_gate = (grad_mixed * grp_norm * (gate_sig * (1.0 + gate * (1.0 - gate_sig)))).astype(bf16)
    ret_bf = norm_back(grad_mixed * gate_act, grp_norm, grp_rstd).astype(bf16)
    ret_bf, wide_grads, down_grads = tie(split(ret_bf), wide_grads, down_grads)
    ret_all = over_col(ret_bf)
    wide_three, down_one = trade(wide_grads, 3), trade(down_grads, 1)
    lefts, rights = (first_bf, attn_bf), (grad_gate, mixed_bf)
    both_got = swap(weight_grads(where, lefts, rights, sizes), "batch", 1)
    both_keeps, both_sends = weight_grads(where, lefts, rights, sizes, (DV, DV), both_got)
    ret_all, wide_three, down_one, both_sends = tie(ret_all, wide_three, down_one, both_sends)
    grad_kv, grad_qg = retention_backward(
        where, decays, keyval, queries, ret_all, states, cosines, sines, split(grad_gate)
    )
    grad_kv, grad_qg = grad_kv.reshape(tokens, -1), grad_qg.reshape(tokens, -1)
    terms = ((grad_kv, kv_w), (grad_qg, qg_w))
    far = reduce_far(*terms)
    got = mirror(far[0])
    late_kv, late_qg, late_send, late_down = after((grad_kv, grad_qg, both_sends, down_grads), far)
    kvq = ((first_bf, first_bf), (late_kv, (late_qg, 0, DK)))
    kvq_got = swap(weight_grads(where, *kvq, sizes), "batch", 1)
    down_two, down_three = trade(late_down, 2), trade(late_down, 3)
    out_sum = sum_col(both_keeps[1], late_send[1])
    near = reduce_near(*terms)
    got, near, down_two, down_three, kvq_got, out_sum, both_sends, result_send = tie(
        got, near, down_two, down_three, kvq_got, out_sum, both_sends, result_send
    )
    got_far = mirror(after(far[1], got))
    got = swap(add(near[0], got).astype(bf16), "row", 1)
    gate_sum = sum_col(both_keeps[0], both_sends[0])
    result_got = swap(result_send, "row", 3)
    kvq_keeps, kvq_sends = weight_grads(where, *kvq, sizes, (DV, 2 * DK), kvq_got)
    wide_pieces = (wide_grads[0], wide_one, wide_two, wide_three)
    grad_gates, grad_ups = unpack_grads(where, wide_pieces, ((units, False), (units, False)))
    got, got_far, gate_sum, result_got, kvq_sends, grad_gates, grad_ups = tie(
        got, got_far, gate_sum, result_got, kvq_sends, grad_gates, grad_ups
    )
    keep = add(add(near[1], got_far), got)
    got = swap(keep[part:].astype(bf16), "row", 3)
    result = (middle + add(result_keep[:part], result_got)).astype(bf16)
    result_other = mirror(result)
    kvq_first = sum_col(kvq_keeps[0], kvq_sends[0])
    both_pieces = cut_heads(where, (gate_sum, out_sum))
    down_pieces = (down_grads[0], down_one, down_two, down_three)
    (grad_downs,) = unpack_grads(where, down_pieces, ((units, True),))
    got, result_other, kvq_first, kvq_sends, both_pieces, grad_downs = tie(
        got, result_other, kvq_first, kvq_sends, both_pieces, grad_downs
    )
    both_pieces = [trade(both_pieces, k) for k in range(nz)]
    kvq_second = sum_col(kvq_keeps[1], kvq_sends[1])
    grad_one = add(keep[:part], got)
    scaled_own, rstd_own = normalize(own_in.astype(f32))
    grad_in = grad_middle + norm_back(grad_one * gains[0:1], scaled_own, rstd_own)
    grad_in_other = mirror(grad_in)
    kvq_pieces = cut_heads(where, (kvq_first, kvq_second))
    both_pieces, kvq_pieces, grad_in_other, grad_one = tie(
        both_pieces, kvq_pieces, grad_in_other, grad_one
    )
    top = swap(kvq_pieces[1][:LOW], "row", 1)
    rest = swap(kvq_pieces[1][LOW:], "row", 1)
    kvq_pieces = [
        kvq_pieces[0],
        jnp.concatenate([top, rest]),
        trade(kvq_pieces, 2),
        trade(kvq_pieces, 3),
    ]
    norm_sums = jnp.stack(
        [
            jnp.sum(grad_one * scaled_own, axis=0),
            jnp.sum(grad_one, axis=0),
            jnp.sum(grad_two * scaled_two, axis=0),
            jnp.sum(grad_two, axis=0),
        ]
    )
    norm_sums = after(norm_sums, top)
    norm_sums = norm_sums + mirror(norm_sums)
    norm_sums = norm_sums.reshape(4, nz, ny, nb, rows)

    def sum_over(values, name, axis):
        me = lax.axis_index(name)
        summed = pick(values, me, axis)
        for k in range(1, lax.axis_size(name)):
            summed = summed + swap(pick(values, me ^ k, axis), name, k)
        return summed

    for name, axis in (("batch", 3), ("col", 2), ("row", 1)):
        norm_sums = sum_over(norm_sums, name, axis)
    grad_g, grad_outs = unpack_grads(where, both_pieces, ((DV, False), (DV, True)))
    grad_k, grad_v, grad_q = unpack_grads(
        where, kvq_pieces, ((DK, False), (DV, False), (DK, False))
    )

    def join(own, other):
        return join_halves(where, own, other).reshape(1, block, width)

    return (
        join(result, result_other),
        join(grad_in, grad_in_other),
        norm_sums[0],
        norm_sums[1],
        grad_q,
        grad_k,
        grad_v,
        grad_g,
        grad_outs,
        norm_sums[2],
        norm_sums[3],
        grad_gates,
        grad_ups,
        grad_downs,
    )


def solution(mesh):
    seq = ("row", "col")
    tokens = P("batch", seq, None)
    params = P((*seq, "batch"))
    by_rows = P((*seq, "batch"), "head")
    by_cols = P("head", (*seq, "batch"))

    def run(*arrays):
        rows = arrays[1].shape[1] // mesh.shape["head"]
        sizes = (rows, mesh.shape["seq"] // rows, mesh.shape["batch"], mesh.shape["head"])
        order = [mesh.axis_names.index(n) for n in ("seq", "batch", "head")]
        fine = Mesh(
            mesh.devices.transpose(order).reshape(sizes), ("row", "col", "batch", "head")
        )
        weights = (by_rows, by_rows, by_rows, by_rows, by_cols)
        feeds = (by_rows, by_rows, by_cols)
        return jax.shard_map(
            shards,
            mesh=fine,
            in_specs=(
                tokens,
                P("batch", "head", seq),
                tokens,
                params,
                params,
                *weights,
                params,
                params,
                *feeds,
            ),
            out_specs=(tokens, tokens, params, params, *weights, params, params, *feeds),
            check_vma=False,
        )(*arrays)

    return run
```
